32 devices in a mesh: dp: 8 (over z, core), ctx: 4 (over y, x).
Axes of the slice: x: 2, y: 2, z: 4, core: 2. Of those that a mesh axis runs over, the one named last changes fastest.
Arguments:
- residual_in: bfloat16 [8, 512, 1536], P('dp', 'ctx'), may hold values from -64 to 64
- query_rows: bfloat16 [8, 512, 1536], P('dp', 'ctx'), may hold values from -6 to 6
- key_rows: bfloat16 [8, 512, 1536], P('dp', 'ctx'), may hold values from -6 to 6
- value_rows: bfloat16 [8, 512, 1536], P('dp', 'ctx'), may hold values from -6 to 6
- lengths: int32 [8], P('dp'), may hold values from 128 to 512, as said below
- out_weight: bfloat16 [1536, 1536], replicated, may hold values from -0.15625 to 0.15625
- norm_gain: float32 [1536], replicated, may hold values from 0.25 to 1.75
- conv_kernel: float32 [31, 1536], replicated, may hold values from -1 to 1
- conv_bias: float32 [1536], replicated, may hold values from -3 to 3
- conv_gain: float32 [1536], replicated, may hold values from 0.25 to 1.75
- point_weight: bfloat16 [1536, 1536], replicated, may hold values from -0.15625 to 0.15625
- grad_out: bfloat16 [8, 512, 1536], P('dp', 'ctx'), may hold values from -6 to 6
Outputs:
- block_out: bfloat16 [8, 512, 1536], P('dp', 'ctx')
- grad_residual: bfloat16 [8, 512, 1536], P('dp', 'ctx')
- grad_query: bfloat16 [8, 512, 1536], P('dp', 'ctx')
- grad_key: bfloat16 [8, 512, 1536], P('dp', 'ctx')
- grad_value: bfloat16 [8, 512, 1536], P('dp', 'ctx')
- grad_out_weight: float32 [1536, 1536], P(None, ('dp', 'ctx'))
- grad_point_weight: float32 [1536, 1536], P(None, ('dp', 'ctx'))
- grad_kernel: float32 [31, 1536], P(None, ('dp', 'ctx'))
- grad_vectors: float32 [3, 1536], P(None, ('dp', 'ctx'))
The draws below stay inside these ranges and needn't reach their ends.
Inputs may be any that keep to these rules, and one draw needn't show every extreme that they name: `lengths`: in every draw some utterance has all 512 frames.
All inputs are finite; a program needn't handle non-finite values.
Results may differ from the reference program's by a relative error of at most 0.028.
Values may be sent and summed in bfloat16 or wider, within the bound.
No kernel may reach another device: no remote copies, remote signals or barrier semaphores. Data moves between devices by JAX's collectives and lax.ppermute only.
A program may use at most 192 MiB of HBM per device.

```python
import jax
import jax.numpy as jnp
from jax import lax

D = 1536
HEADS = 24
HEAD_DIM = 64
KERN = 31
ATT = 1536
HALF = 15
S = 512
B = 8


def draw_query_rows(key, part):
    own_key = jax.random.fold_in(key, 5)
    return jnp.clip(jax.random.normal(own_key, (B, S, ATT), jnp.float32), -4.0, 4.0).astype(jnp.bfloat16)


def draw_key_rows(key, part):
    own_key = jax.random.fold_in(key, 6)
    return jnp.clip(jax.random.normal(own_key, (B, S, ATT), jnp.float32), -4.0, 4.0).astype(jnp.bfloat16)


def draw_residual_in(key, part):
    own_key = jax.random.fold_in(key, 7)
    row_key, column_key, base_key = jax.random.split(own_key, 3)
    row_scale = jnp.exp(jax.random.uniform(row_key, (B, S, 1), jnp.float32, -0.916, 1.386))
    column_scale = jnp.exp(jax.random.uniform(column_key, (1, 1, D), jnp.float32, -0.916, 1.386))
    base = jnp.clip(jax.random.normal(base_key, (B, S, D), jnp.float32), -4.0, 4.0)
    return (base * column_scale * row_scale).astype(jnp.bfloat16)


def draw_lengths(key, part):
    own_key = jax.random.fold_in(key, 9)
    length_key, pick_key = jax.random.split(own_key)
    drawn = jax.random.randint(length_key, (B,), S // 4, S + 1)
    fullest = jax.random.randint(pick_key, (), 0, B)
    return jnp.where(jnp.arange(B, dtype=jnp.int32) == fullest, S, drawn).astype(jnp.int32)


def spiked(values, key, source, target, parts, factor):
    def block_of(position):
        return (jnp.arange(values.shape[position]) // (values.shape[position] // parts)).reshape((-1,) + (1,) * (values.ndim - 1 - position))

    one_side = jax.random.permutation(key, parts)[block_of(target)]
    other_side = (block_of(target) + parts // 2) % parts
    return jnp.where((block_of(source) == one_side) | (block_of(source) == other_side), factor * values, values)


def level_of(stream_key, shape, cuts, least, largest):
    level = 1.0
    for axis_at, parts in cuts:
        steps = jax.random.uniform(jax.random.fold_in(jax.random.fold_in(stream_key, 6), axis_at), (parts,), jnp.float32, least / len(cuts), largest / len(cuts))
        level = level * jnp.repeat(jnp.exp(steps), shape[axis_at] // parts).reshape((-1,) + (1,) * (len(shape) - 1 - axis_at))
    return level


def normal_values(rng, extent, scale, bound, cuts=(), held_as=jnp.bfloat16):
    result = jax.random.normal(rng, extent, jnp.float32) * scale
    if len(cuts) > 0:
        result = level_of(rng, extent, cuts, -0.22, 0.18) * result
    return jnp.clip(result, min=-bound, max=bound).astype(held_as)


def bell_draw_with(rng, extent, width, most, pieces, heavy, kind=jnp.bfloat16):
    array = width * jax.random.normal(rng, extent, jnp.float32)
    if pieces:
        array = array * level_of(rng, extent, pieces, -0.22, 0.18)
    return jnp.clip(spiked(array, jax.random.fold_in(rng, 3), *heavy), -most, most).astype(kind)


def setup_inputs(seed: int = 0) -> dict:
    key_of = jax.random.split(jax.random.key(seed), 13)
    return {
        "residual_in": draw_residual_in(jax.random.fold_in(key_of[12], 71), 0),
        "query_rows": draw_query_rows(jax.random.fold_in(key_of[12], 71), 0),
        "key_rows": draw_key_rows(jax.random.fold_in(key_of[12], 71), 0),
        "value_rows": normal_values(key_of[3], (B, S, ATT), 1.0, 6.0, ((0, 8), (1, 4))),
        "lengths": draw_lengths(jax.random.fold_in(key_of[12], 71), 0),
        "out_weight": normal_values(key_of[5], (ATT, D), ATT ** -0.5, 0.15625),
        "norm_gain": jnp.clip(1.0 + 0.15 * jax.random.normal(key_of[6], (D,), jnp.float32), 0.25, 1.75),
        "conv_kernel": normal_values(key_of[7], (KERN, D), KERN ** -0.5, 1.0, (), jnp.float32),
        "conv_bias": normal_values(key_of[8], (D,), 0.5, 3.0, (), jnp.float32),
        "conv_gain": jnp.clip(1.0 + 0.15 * jax.random.normal(key_of[9], (D,), jnp.float32), 0.25, 1.75),
        "point_weight": normal_values(key_of[10], (D, D), D ** -0.5, 0.15625),
        "grad_out": bell_draw_with(key_of[11], (B, S, D), 1.0, 6.0, ((0, 8), (1, 4)), (0, 2, 8, 2.0)),
    }


NEG_FILL = -1e+30
EPSILON = 1e-05

def low_float(values):
    return lax.optimization_barrier(values.astype(jnp.bfloat16)).astype(jnp.float32)

def layer_norm(rows, gain):
    centre = lax.optimization_barrier(jnp.mean(rows, axis=-1, keepdims=True))
    centred = rows - centre
    inv_scale = lax.rsqrt(lax.optimization_barrier(jnp.mean(centred * centred, axis=-1, keepdims=True)) + EPSILON)
    normed = centred * inv_scale
    return (normed * gain, normed, inv_scale)

def layer_norm_back(grad_scaled, normed, inv_scale, gain):
    grad_normed = grad_scaled * gain
    first_mean = lax.optimization_barrier(jnp.mean(grad_normed, axis=-1, keepdims=True))
    second_mean = lax.optimization_barrier(jnp.mean(grad_normed * normed, axis=-1, keepdims=True))
    grad_rows = inv_scale * (grad_normed - first_mean - normed * second_mean)
    grad_gain = lax.optimization_barrier(jnp.sum((grad_scaled * normed).reshape(-1, normed.shape[-1]), axis=0))
    return (grad_rows, grad_gain)

def depthwise(padded, taps, count):
    total = jnp.zeros((padded.shape[0], count, padded.shape[2]), jnp.float32)
    for offset in range(taps.shape[0]):
        total = total + padded[:, offset:offset + count, :].astype(jnp.float32) * taps[offset]
    return total

def kernel_grad(padded, grad_conv, count, tap_count):
    rows_list = []
    for offset in range(tap_count):
        product = padded[:, offset:offset + count, :].astype(jnp.float32) * grad_conv
        rows_list.append(lax.optimization_barrier(jnp.sum(product.reshape(-1, grad_conv.shape[2]), axis=0)))
    return jnp.stack(rows_list)

def masked_scores(query_one, key_one, valid_one):
    score_scale = HEAD_DIM ** (-0.5)
    scores = jnp.einsum('qhd,khd->hqk', query_one.astype(jnp.float32), key_one.astype(jnp.float32)) * score_scale
    return jnp.where(valid_one[None, None, :], scores, NEG_FILL)

def attend_one(inputs):
    query_one, key_one, value_one, valid_one = inputs
    scores = masked_scores(query_one, key_one, valid_one)
    row_max = lax.optimization_barrier(jnp.max(scores, axis=-1))
    weights = jnp.exp(scores - row_max[..., None]) * valid_one[None, None, :].astype(jnp.float32)
    total = lax.optimization_barrier(jnp.sum(weights, axis=-1))
    summed = jnp.einsum('hqk,khd->qhd', low_float(weights), value_one.astype(jnp.float32))
    attended_one = (summed / jnp.transpose(total)[:, :, None]).astype(jnp.bfloat16)
    return (attended_one, row_max + jnp.log(total))

def attend_back(inputs):
    query_one, key_one, value_one, valid_one, grad_one, log_one, delta_one = inputs
    score_scale = HEAD_DIM ** (-0.5)
    scores = masked_scores(query_one, key_one, valid_one)
    probs = jnp.where(valid_one[None, None, :], jnp.exp(scores - log_one[..., None]), 0.0)
    grad_float = grad_one.astype(jnp.float32)
    value_grad = jnp.einsum('hqk,qhd->khd', low_float(probs), grad_float)
    prob_grad = jnp.einsum('qhd,khd->hqk', grad_float, value_one.astype(jnp.float32))
    score_grad = low_float(probs * (prob_grad - delta_one[..., None]) * score_scale)
    query_grad = jnp.einsum('hqk,khd->qhd', score_grad, key_one.astype(jnp.float32))
    key_grad = jnp.einsum('hqk,qhd->khd', score_grad, query_one.astype(jnp.float32))
    return (query_grad.astype(jnp.bfloat16), key_grad.astype(jnp.bfloat16), value_grad.astype(jnp.bfloat16))

def reference(residual_in, query_rows, key_rows, value_rows, lengths, out_weight, norm_gain, conv_kernel, conv_bias, conv_gain, point_weight, grad_out):
    positions = jnp.arange(S, dtype=jnp.int32)
    frame_valid = positions[None, :] < lengths[:, None]
    valid_rows = frame_valid[..., None].astype(jnp.float32)
    heads_shape = (B, S, HEADS, HEAD_DIM)
    query_heads = query_rows.reshape(heads_shape)
    key_heads = key_rows.reshape(heads_shape)
    value_heads = value_rows.reshape(heads_shape)
    attended_heads, log_total = lax.map(attend_one, (query_heads, key_heads, value_heads, frame_valid))
    attended = attended_heads.reshape(B, S, ATT)
    mixed = residual_in.astype(jnp.float32) + jnp.dot(attended.reshape(-1, ATT), out_weight, preferred_element_type=jnp.float32).reshape(B, S, D)
    scaled_one, normed_one, inv_one = layer_norm(mixed, norm_gain)
    conv_in = (scaled_one * valid_rows).astype(jnp.bfloat16)
    conv_padded = jnp.pad(conv_in, ((0, 0), (HALF, HALF), (0, 0)))
    conv_sum = depthwise(conv_padded, conv_kernel, S) + conv_bias
    scaled_two, normed_two, inv_two = layer_norm(conv_sum, conv_gain)
    gate_value = jax.nn.sigmoid(scaled_two)
    conv_act = (scaled_two * gate_value).astype(jnp.bfloat16)
    block_out = (mixed + jnp.dot(conv_act.reshape(-1, D), point_weight, preferred_element_type=jnp.float32).reshape(B, S, D)).astype(jnp.bfloat16)
    grad_masked = jnp.where(frame_valid[..., None], grad_out, jnp.zeros_like(grad_out))
    grad_act = jnp.dot(grad_masked.reshape(-1, D), point_weight.T, preferred_element_type=jnp.float32).reshape(B, S, D)
    grad_point_weight = jnp.dot(conv_act.reshape(-1, D).T, grad_masked.reshape(-1, D), preferred_element_type=jnp.float32)
    grad_scaled_two = grad_act * gate_value * (1.0 + scaled_two * (1.0 - gate_value))
    grad_conv, conv_gain_grad = layer_norm_back(grad_scaled_two, normed_two, inv_two, conv_gain)
    bias_grad = lax.optimization_barrier(jnp.sum(grad_conv.reshape(-1, D), axis=0))
    grad_kernel = kernel_grad(conv_padded, grad_conv, S, KERN)
    grad_conv_low = grad_conv.astype(jnp.bfloat16)
    grad_padded = jnp.pad(grad_conv_low, ((0, 0), (HALF, HALF), (0, 0)))
    grad_conv_in = depthwise(grad_padded, conv_kernel[::-1], S) * valid_rows
    grad_mixed, norm_gain_grad = layer_norm_back(grad_conv_in, normed_one, inv_one, norm_gain)
    grad_vectors = jnp.stack([bias_grad, norm_gain_grad, conv_gain_grad])
    grad_residual = (grad_masked.astype(jnp.float32) + grad_mixed).astype(jnp.bfloat16)
    grad_out_weight = jnp.dot(attended.reshape(-1, ATT).T, grad_residual.reshape(-1, D), preferred_element_type=jnp.float32)
    grad_attended = jnp.dot(grad_residual.reshape(-1, D), out_weight.T, preferred_element_type=jnp.float32).astype(jnp.bfloat16)
    grad_heads = grad_attended.reshape(heads_shape)
    delta = jnp.einsum('bqhd,bqhd->bhq', grad_heads.astype(jnp.float32), attended_heads.astype(jnp.float32))
    grad_query, grad_key, grad_value = lax.map(attend_back, (query_heads, key_heads, value_heads, frame_valid, grad_heads, log_total, delta))
    return (block_out, grad_residual, grad_query.reshape(B, S, ATT), grad_key.reshape(B, S, ATT), grad_value.reshape(B, S, ATT), grad_out_weight, grad_point_weight, grad_kernel, grad_vectors)
```

```python
import jax
import jax.numpy as jnp
from jax import lax
from jax.sharding import PartitionSpec as P

HEADS = 24
HEAD_DIM = 64
SCALE = HEAD_DIM ** (-0.5)

NEG_FILL = -1e30
EPSILON = 1e-05


def swap(block, axis, by):
    return lax.ppermute(block, axis, [(i, i ^ by) for i in range(lax.axis_size(axis))])


def pick(stack, index, axis=0):
    return lax.dynamic_index_in_dim(stack, index, axis, keepdims=False)


def layer_norm(rows, gain):
    centre = jnp.mean(rows, axis=-1, keepdims=True)
    centred = rows - centre
    inv_scale = lax.rsqrt(jnp.mean(centred * centred, axis=-1, keepdims=True) + EPSILON)
    normed = centred * inv_scale
    return (normed * gain, normed, inv_scale)


def layer_norm_back(grad_scaled, normed, inv_scale, gain):
    grad_normed = grad_scaled * gain
    first_mean = jnp.mean(grad_normed, axis=-1, keepdims=True)
    second_mean = jnp.mean(grad_normed * normed, axis=-1, keepdims=True)
    grad_rows = inv_scale * (grad_normed - first_mean - normed * second_mean)
    return (grad_rows, jnp.sum(grad_scaled * normed, axis=0))


def extended(cells, width):
    count = lax.axis_size("ctx")
    steps = [(i, i + 1) for i in range(count - 1)]
    before = lax.ppermute(cells[-width:], "ctx", steps)
    after = lax.ppermute(cells[:width], "ctx", [(j, i) for i, j in steps])
    return jnp.concatenate([before, cells, after], axis=0)


def depthwise(padded, taps, count):
    total = jnp.zeros((count, padded.shape[1]), jnp.float32)
    for offset in range(taps.shape[0]):
        total = total + padded[offset : offset + count].astype(jnp.float32) * taps[offset]
    return total


def kernel_grad(padded, grad_conv, count, tap_count):
    rows = []
    for offset in range(tap_count):
        rows.append(jnp.sum(padded[offset : offset + count].astype(jnp.float32) * grad_conv, axis=0))
    return jnp.stack(rows)


def to_heads(rows):
    return rows.reshape(rows.shape[0], -1, HEAD_DIM)


def masked_scores(query, key, valid):
    scores = jnp.einsum("qhd,khd->hqk", query, key, preferred_element_type=jnp.float32) * SCALE
    return jnp.where(valid[None, None, :], scores, NEG_FILL)


def attend(query, key, value, valid):
    scores = masked_scores(query, key, valid)
    row_max = jnp.max(scores, axis=-1)
    weights = jnp.exp(scores - row_max[..., None]) * valid[None, None, :].astype(jnp.float32)
    total = jnp.sum(weights, axis=-1)
    summed = jnp.einsum(
        "hqk,khd->qhd", weights.astype(jnp.bfloat16), value, preferred_element_type=jnp.float32
    )
    attended = (summed / jnp.transpose(total)[:, :, None]).astype(jnp.bfloat16)
    return attended, row_max + jnp.log(total)


def attend_back(query, key, value, valid, grad, attended, log_total):
    delta = jnp.einsum("qhd,qhd->hq", grad.astype(jnp.float32), attended.astype(jnp.float32))
    scores = masked_scores(query, key, valid)
    probs = jnp.where(valid[None, None, :], jnp.exp(scores - log_total[..., None]), 0.0)
    value_grad = jnp.einsum(
        "hqk,qhd->khd", probs.astype(jnp.bfloat16), grad, preferred_element_type=jnp.float32
    )
    prob_grad = jnp.einsum("qhd,khd->hqk", grad, value, preferred_element_type=jnp.float32)
    score_grad = (probs * (prob_grad - delta[..., None]) * SCALE).astype(jnp.bfloat16)
    query_grad = jnp.einsum("hqk,khd->qhd", score_grad, key, preferred_element_type=jnp.float32)
    key_grad = jnp.einsum("hqk,qhd->khd", score_grad, query, preferred_element_type=jnp.float32)
    return query_grad, key_grad, value_grad


def reduce_dp(terms):
    count = terms.shape[0]
    own = lax.axis_index("dp")
    core, place = own % 2, own // 2
    paired = terms.reshape((count // 2, 2) + terms.shape[1:])
    sent = pick(paired, 1 - core, 1).astype(jnp.bfloat16)
    half = pick(paired, core, 1) + swap(sent, "dp", 1).astype(jnp.float32)
    low = half.astype(jnp.bfloat16)
    total = pick(half, place)
    for by in range(1, count // 2):
        total = total + swap(pick(low, place ^ by), "dp", 2 * by).astype(jnp.float32)
    return total


def local(
    residual_in,
    query_rows,
    key_rows,
    value_rows,
    lengths,
    out_weight,
    norm_gain,
    conv_kernel,
    conv_bias,
    conv_gain,
    point_weight,
    grad_out,
):
    ways = lax.axis_size("ctx")
    parts = lax.axis_size("dp")
    own = lax.axis_index("ctx")
    frames, width = residual_in.shape[1:]
    share = width // ways
    slim = share // parts
    tap_count = conv_kernel.shape[0]
    rim = (tap_count - 1) // 2

    within = jnp.arange(frames, dtype=jnp.int32)
    frame_valid = own * frames + within < lengths[0]
    valid_rows = frame_valid[:, None].astype(jnp.float32)
    key_valid = jnp.concatenate(
        [(own ^ by) * frames + within < lengths[0] for by in range(ways)]
    )

    def feature_blocks(rows):
        return jnp.moveaxis(rows.reshape(rows.shape[:-1] + (ways, share)), -2, 0)

    def to_features(rows):
        blocks = feature_blocks(rows)
        parts_list = [pick(blocks, own)]
        parts_list += [swap(pick(blocks, own ^ by), "ctx", by) for by in range(1, ways)]
        return jnp.concatenate(parts_list, axis=-2)

    def to_frames(rows):
        blocks = rows.reshape(rows.shape[:-2] + (ways, frames, share))
        back = [blocks[..., 0, :, :]]
        back += [swap(blocks[..., by, :, :], "ctx", by) for by in range(1, ways)]
        stack = jnp.stack(back)
        return jnp.concatenate([pick(stack, own ^ at) for at in range(ways)], axis=-1)

    def all_frames(rows):
        return jnp.concatenate([rows] + [swap(rows, "ctx", by) for by in range(1, ways)], axis=0)

    def columns_turned(rows):
        turned = rows.T.reshape(parts, ways, slim, frames)
        blocks = [pick(turned, own, 1)]
        blocks += [swap(pick(turned, own ^ by, 1), "ctx", by) for by in range(1, ways)]
        return jnp.concatenate(blocks, axis=-1).reshape(share, ways * frames)

    grad_masked = jnp.where(frame_valid[:, None], grad_out[0], jnp.zeros_like(grad_out[0]))

    packed = to_features(jnp.concatenate([query_rows, key_rows, value_rows], axis=0))
    query, key, value = to_heads(packed[0]), to_heads(packed[1]), to_heads(packed[2])
    attended_heads, log_total = attend(query, key, value, key_valid)
    attended = to_frames(attended_heads.reshape(ways * frames, share))
    attended_all = all_frames(attended)
    masked_turned = columns_turned(grad_masked)

    mixed = residual_in[0].astype(jnp.float32) + jnp.dot(
        attended, out_weight, preferred_element_type=jnp.float32
    )
    scaled_one, normed_one, inv_one = layer_norm(mixed, norm_gain)
    conv_in = (scaled_one * valid_rows).astype(jnp.bfloat16)
    conv_padded = extended(conv_in, rim)
    conv_sum = depthwise(conv_padded, conv_kernel, frames) + conv_bias
    scaled_two, normed_two, inv_two = layer_norm(conv_sum, conv_gain)
    gate_value = jax.nn.sigmoid(scaled_two)
    conv_act = (scaled_two * gate_value).astype(jnp.bfloat16)
    block_out = (
        mixed + jnp.dot(conv_act, point_weight, preferred_element_type=jnp.float32)
    ).astype(jnp.bfloat16)
    grad_act = jnp.einsum(
        "fe,de->fd", grad_masked, point_weight, preferred_element_type=jnp.float32
    )
    act_all = all_frames(conv_act)
    point_term = jnp.dot(masked_turned, act_all, preferred_element_type=jnp.float32)
    point_total = reduce_dp(point_term.reshape(parts, slim, width))

    grad_scaled_two = grad_act * gate_value * (1.0 + scaled_two * (1.0 - gate_value))
    grad_conv, conv_gain_term = layer_norm_back(grad_scaled_two, normed_two, inv_two, conv_gain)
    bias_term = jnp.sum(grad_conv, axis=0)
    kernel_term = kernel_grad(conv_padded, grad_conv, frames, tap_count)
    grad_padded = extended(grad_conv.astype(jnp.bfloat16), rim)
    grad_conv_in = depthwise(grad_padded, conv_kernel[::-1], frames) * valid_rows
    grad_mixed, norm_gain_term = layer_norm_back(grad_conv_in, normed_one, inv_one, norm_gain)
    grad_residual = (grad_masked.astype(jnp.float32) + grad_mixed).astype(jnp.bfloat16)
    grad_attended = jnp.einsum(
        "fd,ad->fa", grad_residual, out_weight, preferred_element_type=jnp.float32
    ).astype(jnp.bfloat16)

    grad_heads = to_heads(to_features(grad_attended))
    grads = attend_back(query, key, value, key_valid, grad_heads, attended_heads, log_total)
    grad_rows = jnp.stack([g.reshape(ways * frames, share).astype(jnp.bfloat16) for g in grads])
    grad_rows = to_frames(grad_rows)

    small = jnp.concatenate(
        [kernel_term, jnp.stack([bias_term, norm_gain_term, conv_gain_term])], axis=0
    )
    small = jnp.transpose(small.reshape(small.shape[0], parts, ways, slim), (2, 1, 3, 0))
    small_sum = pick(small, own)
    for by in range(1, ways):
        small_sum = small_sum + swap(pick(small, own ^ by), "ctx", by)
    residual_turned = columns_turned(grad_residual)
    out_term = jnp.dot(residual_turned, attended_all, preferred_element_type=jnp.float32)
    out_total = reduce_dp(
        jnp.concatenate([out_term.reshape(parts, slim, width), small_sum], axis=-1)
    )
    small_total = out_total[:, width:].T
    return (
        block_out[None],
        grad_residual[None],
        grad_rows[0][None],
        grad_rows[1][None],
        grad_rows[2][None],
        out_total[:, :width].T,
        point_total.T,
        small_total[:tap_count],
        small_total[tap_count:],
    )


def solution(mesh):
    rows = P("dp", "ctx", None)
    columns = P(None, ("dp", "ctx"))
    in_specs = (rows, rows, rows, rows, P("dp"), P(), P(), P(), P(), P(), P(), rows)
    out_specs = (rows,) * 5 + (columns,) * 4
    return jax.shard_map(local, mesh=mesh, in_specs=in_specs, out_specs=out_specs, check_vma=False)
```

```python
import functools

import jax
import jax.numpy as jnp
from jax import lax
from jax.experimental import pallas as pl
from jax.experimental.pallas import tpu as pltpu
from jax.sharding import PartitionSpec as P

HEADS = 24
HEAD_DIM = 64
SCALE = HEAD_DIM ** (-0.5)

NEG_FILL = -1e30
EPSILON = 1e-05

LANES = 128
EDGE = 16
BAND = 16
EXTRA = 48

NN = (((1,), (0,)), ((), ()))
NT = (((1,), (1,)), ((), ()))
TN = (((0,), (0,)), ((), ()))


def dot(left, right, dims=NN):
    return lax.dot_general(left, right, dims, preferred_element_type=jnp.float32)


def call(kernel, name, outs, scratch=(), megabytes=28, flops=0, moved=0, exps=0):
    vmem = pl.BlockSpec(memory_space=pltpu.VMEM)
    smem = pl.BlockSpec(memory_space=pltpu.SMEM)

    def run(info, *arrays):
        return pl.pallas_call(
            kernel,
            name=name,
            in_specs=[smem] + [vmem] * len(arrays),
            out_specs=[vmem] * len(outs),
            out_shape=[jax.ShapeDtypeStruct(shape, kind) for shape, kind in outs],
            scratch_shapes=[pltpu.VMEM(shape, kind) for shape, kind in scratch],
            compiler_params=pltpu.CompilerParams(vmem_limit_bytes=megabytes << 20),
            cost_estimate=pl.CostEstimate(flops=flops, bytes_accessed=moved, transcendentals=exps),
        )(info, *arrays)

    return run


def valid_of(first, rows, length):
    return first + lax.broadcasted_iota(jnp.int32, (rows, 1), 0) < length


def moments(rows):
    centre = jnp.mean(rows, axis=-1, keepdims=True)
    centred = rows - centre
    inv_scale = lax.rsqrt(jnp.mean(centred * centred, axis=-1, keepdims=True) + EPSILON)
    return centred * inv_scale, inv_scale


def norm_back(grad_normed, normed, inv_scale):
    first_mean = jnp.mean(grad_normed, axis=-1, keepdims=True)
    second_mean = jnp.mean(grad_normed * normed, axis=-1, keepdims=True)
    return inv_scale * (grad_normed - first_mean - normed * second_mean)


def fold(rows):
    total = rows[:8]
    for at in range(8, rows.shape[0], 8):
        total = total + rows[at : at + 8]
    return total


def pack_kernel(ways, info, query, key, value, *blocks):
    share = query.shape[1] // ways
    for by in range(ways):
        for at in range(ways):

            @pl.when((info[0] ^ by) == at)
            def _():
                for slot, rows in enumerate((query, key, value)):
                    blocks[by][slot] = rows[:, at * share : (at + 1) * share]


def unpack_kernel(ways, info, *refs):
    blocks, outs = refs[:ways], refs[ways:]
    share = blocks[0].shape[2]
    for by in range(ways):
        for at in range(ways):

            @pl.when((info[0] ^ by) == at)
            def _():
                for slot, rows in enumerate(outs):
                    rows[:, at * share : (at + 1) * share] = blocks[by][slot]


def selector(columns, slim, position, width):
    wanted = columns + position * slim
    rows = lax.broadcasted_iota(jnp.int32, (width, columns.shape[1]), 0)
    return jnp.where(rows == wanted, 1.0, 0.0).astype(jnp.bfloat16)


def mask_kernel(ways, slim, info, grad_out, point_weight, columns, masked, grad_act, *blocks):
    frames, width = grad_out.shape
    valid = valid_of(info[0] * frames, frames, info[1])
    masked[...] = jnp.where(valid, grad_out[...].astype(jnp.float32), 0.0).astype(jnp.bfloat16)
    step = width // 3
    for at in range(0, width, step):
        grad_act[:, at : at + step] = dot(masked[...], point_weight[at : at + step, :], NT)
    for by in range(ways):
        chosen = selector(columns[...], slim, info[0] ^ by, width)
        blocks[by][...] = dot(masked[...], chosen).astype(jnp.bfloat16)


def gather_heads(info, blocks, query, key, value, bias):
    frames = blocks[0].shape[1]
    for by, block in enumerate(blocks):
        rows = slice(by * frames, (by + 1) * frames)
        query[rows] = block[0] * jnp.bfloat16(SCALE)
        key[rows] = block[1]
        value[rows] = block[2]
        valid = valid_of((info[0] ^ by) * frames, frames, info[1])
        bias[rows] = jnp.broadcast_to(jnp.where(valid, 0.0, NEG_FILL), (frames, LANES))


def attend_kernel(ways, info, *refs):
    blocks, outs = refs[:ways], refs[ways : 2 * ways]
    log_total, query, key, value, bias, turned = refs[2 * ways :]
    gather_heads(info, blocks, query, key, value, bias)
    total_frames, share = query.shape
    frames = total_frames // ways
    for head in range(share // HEAD_DIM):
        part = slice(head * HEAD_DIM, (head + 1) * HEAD_DIM)
        spread = jnp.concatenate([bias[...]] * (total_frames // LANES), axis=1)
        scores = dot(key[:, part], query[:, part], NT) + spread
        row_max = jnp.max(scores, axis=0, keepdims=True)
        weights = jnp.exp(scores - row_max)
        total = jnp.sum(weights, axis=0, keepdims=True)
        turned[part, :] = dot(value[:, part], weights.astype(jnp.bfloat16), TN) / total
        log_total[head : head + 1, :] = row_max + jnp.log(total)
    attended = turned[...].T.astype(jnp.bfloat16)
    for by in range(ways):
        outs[by][...] = attended[by * frames : (by + 1) * frames]


def attend_back_kernel(ways, info, *refs):
    blocks, attended, grads = refs[:ways], refs[ways : 2 * ways], refs[2 * ways : 3 * ways]
    log_total = refs[3 * ways]
    outs = refs[3 * ways + 1 : 4 * ways + 1]
    query, key, value, bias, grad, turned = refs[4 * ways + 1 :]
    gather_heads(info, blocks, query, key, value, bias)
    total_frames, share = query.shape
    frames = total_frames // ways
    products = []
    for by in range(ways):
        grad[by * frames : (by + 1) * frames] = grads[by][...]
        products.append(grads[by][...].astype(jnp.float32) * attended[by][...].astype(jnp.float32))
    turned[...] = jnp.concatenate(products, axis=0).T
    for head in range(share // HEAD_DIM):
        part = slice(head * HEAD_DIM, (head + 1) * HEAD_DIM)
        delta = jnp.sum(turned[part, :], axis=0, keepdims=True)
        spread = jnp.concatenate([bias[...]] * (total_frames // LANES), axis=1)
        scores = dot(key[:, part], query[:, part], NT) + spread
        probs = jnp.exp(scores - log_total[head : head + 1, :])
        value_grad = dot(probs.astype(jnp.bfloat16), grad[:, part])
        prob_grad = dot(value[:, part], grad[:, part], NT)
        score_grad = (probs * (prob_grad - delta)).astype(jnp.bfloat16)
        key_grad = dot(score_grad, query[:, part])
        turned[part, :] = dot(key[:, part], score_grad, TN) * SCALE
        for by in range(ways):
            rows = slice(by * frames, (by + 1) * frames)
            outs[by][1, :, part] = key_grad[rows].astype(jnp.bfloat16)
            outs[by][2, :, part] = value_grad[rows].astype(jnp.bfloat16)
    query_grad = turned[...].T.astype(jnp.bfloat16)
    for by in range(ways):
        outs[by][0] = query_grad[by * frames : (by + 1) * frames]


def project_kernel(ways, info, *refs):
    blocks = refs[:ways]
    residual, out_weight, params, attended, mixed, conv_in, head, tail = refs[ways:]
    frames, width = residual.shape
    share = width // ways
    for by in range(ways):
        for at in range(ways):

            @pl.when((info[0] ^ by) == at)
            def _():
                attended[:, at * share : (at + 1) * share] = blocks[by][...]

    step = width // 3
    for at in range(0, width, step):
        part = slice(at, at + step)
        mixed[:, part] = residual[:, part].astype(jnp.float32) + dot(
            attended[...], out_weight[:, part]
        )

    gain = params[31:32, :]

    def band(index, carry):
        rows = pl.ds(pl.multiple_of(index * BAND, BAND), BAND)
        normed, _ = moments(mixed[rows, :])
        valid = valid_of(info[0] * frames + index * BAND, BAND, info[1])
        conv_in[rows, :] = jnp.where(valid, normed * gain, 0.0).astype(jnp.bfloat16)
        return carry

    lax.fori_loop(0, frames // BAND, band, 0)
    head[...] = conv_in[:EDGE, :]
    tail[...] = conv_in[frames - EDGE :, :]


def pad_rows(padded, before, rows, after):
    frames = rows.shape[0]
    padded[:EDGE] = before[...].astype(jnp.float32)
    padded[EDGE : EDGE + frames] = rows[...].astype(jnp.float32)
    padded[EDGE + frames :] = after[...].astype(jnp.float32)


def slide(padded, part, frames, visit):
    for residue in range(8):
        reach = frames + 2 * EDGE - 8
        shifted = padded[residue : residue + reach, part]
        for offset in range(residue, 2 * EDGE, 8):
            if offset:
                start = offset - residue
                visit(offset, shifted[start : start + frames])


def depthwise(padded, taps, tap_of, out):
    frames, width = out.shape

    def column(index, carry):
        part = pl.ds(pl.multiple_of(index * LANES, LANES), LANES)
        total = [jnp.zeros((frames, LANES), jnp.float32)]

        def visit(offset, rows):
            tap = tap_of(offset)
            total[0] = total[0] + rows * taps[tap : tap + 1, part]

        slide(padded, part, frames, visit)
        out[:, part] = total[0]
        return carry

    lax.fori_loop(0, width // LANES, column, 0)


def conv_kernel_body(info, conv_in, before, after, params, grad_act, *refs):
    conv_act, grad_conv, head, tail, sums, padded, conv, bias_sum, gain_sum = refs
    frames = conv_in.shape[0]
    pad_rows(padded, before, conv_in, after)
    depthwise(padded, params, lambda offset: offset - 1, conv)
    bias, gain = params[32:33, :], params[33:34, :]
    bias_sum[...] = jnp.zeros_like(bias_sum)
    gain_sum[...] = jnp.zeros_like(gain_sum)

    def band(index, carry):
        rows = pl.ds(pl.multiple_of(index * BAND, BAND), BAND)
        normed, inv_scale = moments(conv[rows, :] + bias)
        scaled = normed * gain
        gate = 1.0 / (1.0 + jnp.exp(-scaled))
        conv_act[rows, :] = (scaled * gate).astype(jnp.bfloat16)
        grad_scaled = grad_act[rows, :] * gate * (1.0 + scaled * (1.0 - gate))
        grad_rows = norm_back(grad_scaled * gain, normed, inv_scale)
        grad_conv[rows, :] = grad_rows
        bias_sum[...] += fold(grad_rows)
        gain_sum[...] += fold(grad_scaled * normed)
        return carry

    lax.fori_loop(0, frames // BAND, band, 0)
    head[...] = grad_conv[:EDGE, :].astype(jnp.bfloat16)
    tail[...] = grad_conv[frames - EDGE :, :].astype(jnp.bfloat16)
    sums[0:1, :] = jnp.sum(bias_sum[...], axis=0, keepdims=True)
    sums[1:2, :] = jnp.sum(gain_sum[...], axis=0, keepdims=True)


def taps_kernel(info, conv_in, before, after, grad_conv, conv_act, mixed, point_weight, *refs):
    block_out, taps, padded = refs
    frames, width = conv_in.shape
    pad_rows(padded, before, conv_in, after)

    def column(index, carry):
        part = pl.ds(pl.multiple_of(index * LANES, LANES), LANES)
        grad = grad_conv[:, part]

        def visit(offset, rows):
            taps[offset - 1 : offset, part] = jnp.sum(fold(rows * grad), axis=0, keepdims=True)

        slide(padded, part, frames, visit)
        return carry

    lax.fori_loop(0, width // LANES, column, 0)
    step = width // 3
    for at in range(0, width, step):
        part = slice(at, at + step)
        block_out[:, part] = (mixed[:, part] + dot(conv_act[...], point_weight[:, part])).astype(
            jnp.bfloat16
        )


def conv_back_kernel(ways, info, grad_conv, before, after, params, masked, mixed, out_weight, *refs):
    grad_residual, sums, blocks = refs[0], refs[1], refs[2 : 2 + ways]
    padded, conv, gain_sum = refs[2 + ways :]
    frames, width = grad_conv.shape
    share = width // ways
    pad_rows(padded, before, grad_conv[...].astype(jnp.bfloat16), after)
    depthwise(padded, params, lambda offset: 31 - offset, conv)
    gain = params[31:32, :]
    gain_sum[...] = jnp.zeros_like(gain_sum)

    def band(index, carry):
        rows = pl.ds(pl.multiple_of(index * BAND, BAND), BAND)
        valid = valid_of(info[0] * frames + index * BAND, BAND, info[1])
        grad_in = jnp.where(valid, conv[rows, :], 0.0)
        normed, inv_scale = moments(mixed[rows, :])
        grad_mixed = norm_back(grad_in * gain, normed, inv_scale)
        gain_sum[...] += fold(grad_in * normed)
        grad_residual[rows, :] = (masked[rows, :].astype(jnp.float32) + grad_mixed).astype(
            jnp.bfloat16
        )
        return carry

    lax.fori_loop(0, frames // BAND, band, 0)
    sums[...] = jnp.sum(gain_sum[...], axis=0, keepdims=True)
    for by in range(ways):
        rows = pl.ds(pl.multiple_of((info[0] ^ by) * share, share), share)
        blocks[by][...] = dot(grad_residual[...], out_weight[rows, :], NT).astype(jnp.bfloat16)


def columns_kernel(ways, slim, info, grad_residual, taps, conv_sums, norm_sums, columns, *refs):
    blocks, packed = refs[:ways], refs[ways]
    frames, width = grad_residual.shape
    small = jnp.concatenate(
        [taps[:31, :], norm_sums[...], conv_sums[0:2, :], jnp.zeros((14, width), jnp.float32)], axis=0
    )
    high = small.astype(jnp.bfloat16)
    low = (small - high.astype(jnp.float32)).astype(jnp.bfloat16)
    packed[:frames] = grad_residual[...]
    packed[frames : frames + EXTRA] = high
    packed[frames + EXTRA :] = low
    for by in range(ways):
        chosen = selector(columns[...], slim, info[0] ^ by, width)
        blocks[by][...] = dot(packed[...], chosen).astype(jnp.bfloat16)


def weight_kernel(ways, parts, info, *refs):
    grads, rows = refs[:ways], refs[ways : 2 * ways]
    sent, kept, terms = refs[2 * ways :]
    frames, width = rows[0].shape
    slim = terms.shape[0] // parts
    left = jnp.concatenate([grad[:frames] for grad in grads], axis=0)
    step = width // 3
    for at in range(0, width, step):
        part = slice(at, at + step)
        right = jnp.concatenate([block[:, part] for block in rows], axis=0)
        terms[:, part] = dot(left, right, TN)
    if terms.shape[1] > width:
        small = jnp.zeros((EXTRA, terms.shape[0]), jnp.float32)
        for grad in grads:
            small = small + grad[frames : frames + EXTRA].astype(jnp.float32)
            small = small + grad[frames + EXTRA :].astype(jnp.float32)
        filler = jnp.zeros((LANES - EXTRA, terms.shape[0]), jnp.float32)
        terms[:, width:] = jnp.concatenate([small, filler], axis=0).T
    for core in range(2):

        @pl.when(info[2] == core)
        def _():
            for at in range(parts // 2):
                own = (2 * at + core) * slim
                other = (2 * at + 1 - core) * slim
                kept[at] = terms[own : own + slim, :]
                sent[at] = terms[other : other + slim, :].astype(jnp.bfloat16)


def halve_kernel(info, kept, received, total, *blocks):
    total[...] = kept[info[3]] + received[info[3]].astype(jnp.float32)
    for by, block in enumerate(blocks, 1):
        place = info[3] ^ by
        block[...] = (kept[place] + received[place].astype(jnp.float32)).astype(jnp.bfloat16)


def finish_kernel(info, *refs):
    blocks, outs = refs[: -1], refs[-1]
    total = blocks[0][...]
    for block in blocks[1:]:
        total = total + block[...].astype(jnp.float32)
    outs[...] = total


def swap(block, axis, by):
    return lax.ppermute(block, axis, [(i, i ^ by) for i in range(lax.axis_size(axis))])


def swap_all(blocks, axis, step=1):
    return [blocks[0]] + [swap(block, axis, step * by) for by, block in enumerate(blocks[1:], 1)]


def edges(head, tail):
    count = lax.axis_size("ctx")
    steps = [(i, i + 1) for i in range(count - 1)]
    before = lax.ppermute(tail, "ctx", steps)
    after = lax.ppermute(head, "ctx", [(j, i) for i, j in steps])
    return before, after


def local(
    residual_in,
    query_rows,
    key_rows,
    value_rows,
    lengths,
    out_weight,
    norm_gain,
    conv_kernel,
    conv_bias,
    conv_gain,
    point_weight,
    grad_out,
):
    ways = lax.axis_size("ctx")
    parts = lax.axis_size("dp")
    place = lax.axis_index("dp")
    frames, width = residual_in.shape[1:]
    share = width // ways
    slim = share // parts
    heads = HEADS // ways
    every = ways * frames
    bf16, f32 = jnp.bfloat16, jnp.float32
    square = 2 * frames * width * width
    rows_bytes = 2 * frames * width

    info = jnp.stack(
        [lax.axis_index("ctx"), lengths[0], place % 2, place // 2]
    ).astype(jnp.int32)
    params = jnp.concatenate(
        [conv_kernel, norm_gain[None], conv_bias[None], conv_gain[None]], axis=0
    )
    owned = jnp.arange(share, dtype=jnp.int32)
    columns = ((owned // slim) * (ways * slim) + owned % slim)[None]

    def reduce_dp(sent, kept):
        received = swap(sent, "dp", 1)
        extent = kept.shape[1:]
        size = extent[0] * extent[1]
        halves = call(
            halve_kernel,
            "halve",
            [(extent, f32)] + [(extent, bf16)] * (parts // 2 - 1),
            moved=size * 5 * parts,
        )(info, kept, received)
        pieces = swap_all(halves, "dp", 2)
        return call(finish_kernel, "finish", [(extent, f32)], moved=size * (parts + 8))(
            info, *pieces
        )[0]

    packed = call(
        functools.partial(pack_kernel, ways),
        "pack",
        [((3, frames, share), bf16)] * ways,
        moved=6 * rows_bytes,
    )(info, query_rows[0], key_rows[0], value_rows[0])
    packed = swap_all(packed, "ctx")

    masked, grad_act, *masked_columns = call(
        functools.partial(mask_kernel, ways, slim),
        "mask",
        [((frames, width), bf16), ((frames, width), f32)] + [((frames, share), bf16)] * ways,
        flops=2 * square,
        moved=6 * rows_bytes + 2 * width * width,
    )(info, grad_out[0], point_weight, columns)

    head_scratch = [((every, share), bf16)] * 3 + [((every, LANES), f32)]
    pair_flops = 2 * heads * every * every * HEAD_DIM
    *attended_heads, log_total = call(
        functools.partial(attend_kernel, ways),
        "attend",
        [((frames, share), bf16)] * ways + [((heads, every), f32)],
        scratch=head_scratch + [((share, every), f32)],
        flops=8 * pair_flops,
        moved=4 * rows_bytes,
        exps=heads * every * every,
    )(info, *packed)
    returned = swap_all(attended_heads, "ctx")

    attended, mixed, conv_in, head, tail = call(
        functools.partial(project_kernel, ways),
        "project",
        [((frames, width), bf16), ((frames, width), f32), ((frames, width), bf16)]
        + [((EDGE, width), bf16)] * 2,
        flops=square,
        moved=6 * rows_bytes + 2 * width * width,
    )(info, *returned, residual_in[0], out_weight, params)
    before, after = edges(head, tail)
    attended_all = swap_all([attended] * ways, "ctx")
    masked_columns = swap_all(masked_columns, "ctx")

    pad_scratch = [((frames + 2 * EDGE, width), f32)]
    conv_act, grad_conv, grad_head, grad_tail, conv_sums = call(
        conv_kernel_body,
        "conv",
        [((frames, width), bf16), ((frames, width), f32)]
        + [((EDGE, width), bf16)] * 2
        + [((2, width), f32)],
        scratch=pad_scratch + [((frames, width), f32)] + [((8, width), f32)] * 2,
        flops=frames * width * 4000,
        moved=6 * rows_bytes,
        exps=frames * width,
    )(info, conv_in, before, after, params, grad_act)
    grad_before, grad_after = edges(grad_head, grad_tail)
    act_all = swap_all([conv_act] * ways, "ctx")

    block_out, taps = call(
        taps_kernel,
        "taps",
        [((frames, width), bf16), ((31, width), f32)],
        scratch=pad_scratch,
        flops=frames * width * 4000,
        moved=8 * rows_bytes + 2 * width * width,
    )(info, conv_in, before, after, grad_conv, conv_act, mixed, point_weight)

    grad_residual, norm_sums, *grad_blocks = call(
        functools.partial(conv_back_kernel, ways),
        "conv_back",
        [((frames, width), bf16), ((1, width), f32)] + [((frames, share), bf16)] * ways,
        scratch=pad_scratch + [((frames, width), f32), ((8, width), f32)],
        flops=frames * width * 4000,
        moved=8 * rows_bytes + 2 * width * width,
    )(info, grad_conv, grad_before, grad_after, params, masked, mixed, out_weight)
    grad_blocks = swap_all(grad_blocks, "ctx")

    residual_columns = call(
        functools.partial(columns_kernel, ways, slim),
        "columns",
        [((frames + 2 * EXTRA, share), bf16)] * ways,
        scratch=[((frames + 2 * EXTRA, width), bf16)],
        flops=square,
        moved=3 * rows_bytes,
    )(info, grad_residual, taps, conv_sums, norm_sums, columns)
    residual_columns = swap_all(residual_columns, "ctx")

    def weight_terms(name, extent, grads, rows):
        half = (parts // 2, slim, extent)
        return call(
            functools.partial(weight_kernel, ways, parts),
            name,
            [(half, bf16), (half, f32)],
            scratch=[((share, extent), f32)],
            flops=square,
            moved=10 * rows_bytes,
        )(info, *grads, *rows)

    point_total = reduce_dp(*weight_terms("point_terms", width, masked_columns, act_all))
    out_total = reduce_dp(
        *weight_terms("out_terms", width + LANES, residual_columns, attended_all)
    )

    grad_packed = call(
        functools.partial(attend_back_kernel, ways),
        "attend_back",
        [((3, frames, share), bf16)] * ways,
        scratch=head_scratch + [((every, share), bf16), ((share, every), f32)],
        flops=20 * pair_flops,
        moved=8 * rows_bytes,
        exps=heads * every * every,
    )(info, *packed, *attended_heads, *grad_blocks, log_total)
    grad_packed = swap_all(grad_packed, "ctx")
    grad_query, grad_key, grad_value = call(
        functools.partial(unpack_kernel, ways),
        "unpack",
        [((frames, width), bf16)] * 3,
        moved=6 * rows_bytes,
    )(info, *grad_packed)

    small = out_total[:, width:].T
    return (
        block_out[None],
        grad_residual[None],
        grad_query[None],
        grad_key[None],
        grad_value[None],
        out_total[:, :width].T,
        point_total.T,
        small[:31],
        jnp.concatenate([small[32:33], small[31:32], small[33:34]], axis=0),
    )


def solution(mesh):
    rows = P("dp", "ctx", None)
    columns = P(None, ("dp", "ctx"))
    in_specs = (rows, rows, rows, rows, P("dp"), P(), P(), P(), P(), P(), P(), rows)
    out_specs = (rows,) * 5 + (columns,) * 4
    return jax.shard_map(local, mesh=mesh, in_specs=in_specs, out_specs=out_specs, check_vma=False)
```

```python
import functools

import jax
import jax.numpy as jnp
from jax import lax
from jax.experimental import pallas as pl
from jax.experimental.pallas import tpu as pltpu
from jax.sharding import PartitionSpec as P

HEADS = 24
HEAD_DIM = 64
SCALE = HEAD_DIM ** (-0.5)

NEG_FILL = -1e30
EPSILON = 1e-05

LANES = 128
EDGE = 16
BAND = 16
EXTRA = 48

NN = (((1,), (0,)), ((), ()))
NT = (((1,), (1,)), ((), ()))
TN = (((0,), (0,)), ((), ()))


def dot(left, right, dims=NN):
    return lax.dot_general(left, right, dims, preferred_element_type=jnp.float32)


def call(kernel, name, outs, scratch=(), megabytes=28, flops=0, moved=0, exps=0):
    vmem = pl.BlockSpec(memory_space=pltpu.VMEM)
    smem = pl.BlockSpec(memory_space=pltpu.SMEM)

    def run(info, *arrays):
        return pl.pallas_call(
            kernel,
            name=name,
            in_specs=[smem] + [vmem] * len(arrays),
            out_specs=[vmem] * len(outs),
            out_shape=[jax.ShapeDtypeStruct(shape, kind) for shape, kind in outs],
            scratch_shapes=[pltpu.VMEM(shape, kind) for shape, kind in scratch],
            compiler_params=pltpu.CompilerParams(vmem_limit_bytes=megabytes << 20),
            cost_estimate=pl.CostEstimate(flops=flops, bytes_accessed=moved, transcendentals=exps),
        )(info, *arrays)

    return run


def valid_of(first, rows, length):
    return first + lax.broadcasted_iota(jnp.int32, (rows, 1), 0) < length


def moments(rows):
    centre = jnp.mean(rows, axis=-1, keepdims=True)
    centred = rows - centre
    inv_scale = lax.rsqrt(jnp.mean(centred * centred, axis=-1, keepdims=True) + EPSILON)
    return centred * inv_scale, inv_scale


def norm_back(grad_normed, normed, inv_scale):
    first_mean = jnp.mean(grad_normed, axis=-1, keepdims=True)
    second_mean = jnp.mean(grad_normed * normed, axis=-1, keepdims=True)
    return inv_scale * (grad_normed - first_mean - normed * second_mean)


def fold(rows):
    total = rows[:8]
    for at in range(8, rows.shape[0], 8):
        total = total + rows[at : at + 8]
    return total


def pack_kernel(ways, info, query, key, value, blocks):
    share = query.shape[1] // ways
    for at in range(ways):
        for slot, rows in enumerate((query, key, value)):
            blocks[at, slot] = rows[:, at * share : (at + 1) * share]


def unpack_kernel(ways, info, blocks, *outs):
    share = blocks.shape[3]
    for at in range(ways):
        for slot, rows in enumerate(outs):
            rows[:, at * share : (at + 1) * share] = blocks[at, slot]


def selector(columns, slim, position, width):
    wanted = columns + position * slim
    rows = lax.broadcasted_iota(jnp.int32, (width, columns.shape[1]), 0)
    return jnp.where(rows == wanted, 1.0, 0.0).astype(jnp.bfloat16)


def mask_kernel(ways, slim, info, grad_out, point_weight, columns, masked, grad_act, blocks):
    frames, width = grad_out.shape
    valid = valid_of(info[0] * frames, frames, info[1])
    masked[...] = jnp.where(valid, grad_out[...].astype(jnp.float32), 0.0).astype(jnp.bfloat16)
    step = width // 3
    for at in range(0, width, step):
        grad_act[:, at : at + step] = dot(masked[...], point_weight[at : at + step, :], NT)
    for by in range(ways):
        chosen = selector(columns[...], slim, by, width)
        blocks[by] = dot(masked[...], chosen).astype(jnp.bfloat16)


def gather_heads(info, blocks, query, key, value, bias):
    ways, _, frames, _ = blocks.shape
    for by in range(ways):
        rows = slice(by * frames, (by + 1) * frames)
        query[rows] = blocks[by, 0] * jnp.bfloat16(SCALE)
        key[rows] = blocks[by, 1]
        value[rows] = blocks[by, 2]
        valid = valid_of(by * frames, frames, info[1])
        bias[rows] = jnp.broadcast_to(jnp.where(valid, 0.0, NEG_FILL), (frames, LANES))


def attend_kernel(ways, info, blocks, outs, log_total, query, key, value, bias, turned):
    gather_heads(info, blocks, query, key, value, bias)
    total_frames, share = query.shape
    frames = total_frames // ways
    for head in range(share // HEAD_DIM):
        part = slice(head * HEAD_DIM, (head + 1) * HEAD_DIM)
        spread = jnp.concatenate([bias[...]] * (total_frames // LANES), axis=1)
        scores = dot(key[:, part], query[:, part], NT) + spread
        row_max = jnp.max(scores, axis=0, keepdims=True)
        weights = jnp.exp(scores - row_max)
        total = jnp.sum(weights, axis=0, keepdims=True)
        turned[part, :] = dot(value[:, part], weights.astype(jnp.bfloat16), TN) / total
        log_total[head : head + 1, :] = row_max + jnp.log(total)
    attended = turned[...].T.astype(jnp.bfloat16)
    for by in range(ways):
        outs[by] = attended[by * frames : (by + 1) * frames]


def attend_back_kernel(ways, info, blocks, attended, grads, log_total, outs, *scratch):
    query, key, value, bias, grad, turned = scratch
    gather_heads(info, blocks, query, key, value, bias)
    total_frames, share = query.shape
    frames = total_frames // ways
    products = []
    for by in range(ways):
        grad[by * frames : (by + 1) * frames] = grads[by]
        products.append(grads[by].astype(jnp.float32) * attended[by].astype(jnp.float32))
    turned[...] = jnp.concatenate(products, axis=0).T
    for head in range(share // HEAD_DIM):
        part = slice(head * HEAD_DIM, (head + 1) * HEAD_DIM)
        delta = jnp.sum(turned[part, :], axis=0, keepdims=True)
        spread = jnp.concatenate([bias[...]] * (total_frames // LANES), axis=1)
        scores = dot(key[:, part], query[:, part], NT) + spread
        probs = jnp.exp(scores - log_total[head : head + 1, :])
        value_grad = dot(probs.astype(jnp.bfloat16), grad[:, part])
        prob_grad = dot(value[:, part], grad[:, part], NT)
        score_grad = (probs * (prob_grad - delta)).astype(jnp.bfloat16)
        key_grad = dot(score_grad, query[:, part])
        turned[part, :] = dot(key[:, part], score_grad, TN) * SCALE
        for by in range(ways):
            rows = slice(by * frames, (by + 1) * frames)
            outs[by, 1, :, part] = key_grad[rows].astype(jnp.bfloat16)
            outs[by, 2, :, part] = value_grad[rows].astype(jnp.bfloat16)
    query_grad = turned[...].T.astype(jnp.bfloat16)
    for by in range(ways):
        outs[by, 0] = query_grad[by * frames : (by + 1) * frames]


def project_kernel(ways, info, blocks, residual, out_weight, params, *outs):
    attended, mixed, conv_in, head, tail = outs
    frames, width = residual.shape
    share = width // ways
    for at in range(ways):
        attended[:, at * share : (at + 1) * share] = blocks[at]

    step = width // 3
    for at in range(0, width, step):
        part = slice(at, at + step)
        mixed[:, part] = residual[:, part].astype(jnp.float32) + dot(
            attended[...], out_weight[:, part]
        )

    gain = params[31:32, :]

    def band(index, carry):
        rows = pl.ds(pl.multiple_of(index * BAND, BAND), BAND)
        normed, _ = moments(mixed[rows, :])
        valid = valid_of(info[0] * frames + index * BAND, BAND, info[1])
        conv_in[rows, :] = jnp.where(valid, normed * gain, 0.0).astype(jnp.bfloat16)
        return carry

    lax.fori_loop(0, frames // BAND, band, 0)
    head[...] = conv_in[:EDGE, :]
    tail[...] = conv_in[frames - EDGE :, :]


def pad_rows(padded, before, rows, after):
    frames = rows.shape[0]
    padded[:EDGE] = before[...].astype(jnp.float32)
    padded[EDGE : EDGE + frames] = rows[...].astype(jnp.float32)
    padded[EDGE + frames :] = after[...].astype(jnp.float32)


def slide(padded, part, frames, visit):
    for residue in range(8):
        reach = frames + 2 * EDGE - 8
        shifted = padded[residue : residue + reach, part]
        for offset in range(residue, 2 * EDGE, 8):
            if offset:
                start = offset - residue
                visit(offset, shifted[start : start + frames])


def depthwise(padded, taps, tap_of, out):
    frames, width = out.shape

    def column(index, carry):
        part = pl.ds(pl.multiple_of(index * LANES, LANES), LANES)
        total = [jnp.zeros((frames, LANES), jnp.float32)]

        def visit(offset, rows):
            tap = tap_of(offset)
            total[0] = total[0] + rows * taps[tap : tap + 1, part]

        slide(padded, part, frames, visit)
        out[:, part] = total[0]
        return carry

    lax.fori_loop(0, width // LANES, column, 0)


def conv_kernel_body(info, conv_in, before, after, params, grad_act, *refs):
    conv_act, grad_conv, head, tail, sums, padded, conv, bias_sum, gain_sum = refs
    frames = conv_in.shape[0]
    pad_rows(padded, before, conv_in, after)
    depthwise(padded, params, lambda offset: offset - 1, conv)
    bias, gain = params[32:33, :], params[33:34, :]
    bias_sum[...] = jnp.zeros_like(bias_sum)
    gain_sum[...] = jnp.zeros_like(gain_sum)

    def band(index, carry):
        rows = pl.ds(pl.multiple_of(index * BAND, BAND), BAND)
        normed, inv_scale = moments(conv[rows, :] + bias)
        scaled = normed * gain
        gate = 1.0 / (1.0 + jnp.exp(-scaled))
        conv_act[rows, :] = (scaled * gate).astype(jnp.bfloat16)
        grad_scaled = grad_act[rows, :] * gate * (1.0 + scaled * (1.0 - gate))
        grad_rows = norm_back(grad_scaled * gain, normed, inv_scale)
        grad_conv[rows, :] = grad_rows
        bias_sum[...] += fold(grad_rows)
        gain_sum[...] += fold(grad_scaled * normed)
        return carry

    lax.fori_loop(0, frames // BAND, band, 0)
    head[...] = grad_conv[:EDGE, :].astype(jnp.bfloat16)
    tail[...] = grad_conv[frames - EDGE :, :].astype(jnp.bfloat16)
    sums[0:1, :] = jnp.sum(bias_sum[...], axis=0, keepdims=True)
    sums[1:2, :] = jnp.sum(gain_sum[...], axis=0, keepdims=True)


def taps_kernel(info, conv_in, before, after, grad_conv, conv_act, mixed, point_weight, *refs):
    block_out, taps, padded = refs
    frames, width = conv_in.shape
    pad_rows(padded, before, conv_in, after)

    def column(index, carry):
        part = pl.ds(pl.multiple_of(index * LANES, LANES), LANES)
        grad = grad_conv[:, part]

        def visit(offset, rows):
            taps[offset - 1 : offset, part] = jnp.sum(fold(rows * grad), axis=0, keepdims=True)

        slide(padded, part, frames, visit)
        return carry

    lax.fori_loop(0, width // LANES, column, 0)
    step = width // 3
    for at in range(0, width, step):
        part = slice(at, at + step)
        block_out[:, part] = (mixed[:, part] + dot(conv_act[...], point_weight[:, part])).astype(
            jnp.bfloat16
        )


def conv_back_kernel(ways, info, grad_conv, before, after, params, masked, mixed, out_weight, *refs):
    grad_residual, sums, blocks = refs[:3]
    padded, conv, gain_sum = refs[3:]
    frames, width = grad_conv.shape
    share = width // ways
    pad_rows(padded, before, grad_conv[...].astype(jnp.bfloat16), after)
    depthwise(padded, params, lambda offset: 31 - offset, conv)
    gain = params[31:32, :]
    gain_sum[...] = jnp.zeros_like(gain_sum)

    def band(index, carry):
        rows = pl.ds(pl.multiple_of(index * BAND, BAND), BAND)
        valid = valid_of(info[0] * frames + index * BAND, BAND, info[1])
        grad_in = jnp.where(valid, conv[rows, :], 0.0)
        normed, inv_scale = moments(mixed[rows, :])
        grad_mixed = norm_back(grad_in * gain, normed, inv_scale)
        gain_sum[...] += fold(grad_in * normed)
        grad_residual[rows, :] = (masked[rows, :].astype(jnp.float32) + grad_mixed).astype(
            jnp.bfloat16
        )
        return carry

    lax.fori_loop(0, frames // BAND, band, 0)
    sums[...] = jnp.sum(gain_sum[...], axis=0, keepdims=True)
    for by in range(ways):
        rows = slice(by * share, (by + 1) * share)
        blocks[by] = dot(grad_residual[...], out_weight[rows, :], NT).astype(jnp.bfloat16)


def columns_kernel(ways, slim, info, grad_residual, taps, conv_sums, norm_sums, columns, blocks, packed):
    frames, width = grad_residual.shape
    small = jnp.concatenate(
        [taps[:31, :], norm_sums[...], conv_sums[0:2, :], jnp.zeros((14, width), jnp.float32)], axis=0
    )
    high = small.astype(jnp.bfloat16)
    low = (small - high.astype(jnp.float32)).astype(jnp.bfloat16)
    packed[:frames] = grad_residual[...]
    packed[frames : frames + EXTRA] = high
    packed[frames + EXTRA :] = low
    for by in range(ways):
        chosen = selector(columns[...], slim, by, width)
        blocks[by] = dot(packed[...], chosen).astype(jnp.bfloat16)


def weight_kernel(ways, parts, info, grads, rows, sent, kept, terms):
    _, frames, width = rows.shape
    slim = terms.shape[0] // parts
    left = jnp.concatenate([grads[at, :frames] for at in range(ways)], axis=0)
    step = width // 3
    for at in range(0, width, step):
        part = slice(at, at + step)
        right = jnp.concatenate([rows[at, :, part] for at in range(ways)], axis=0)
        terms[:, part] = dot(left, right, TN)
    if terms.shape[1] > width:
        small = jnp.zeros((EXTRA, terms.shape[0]), jnp.float32)
        for at in range(ways):
            small = small + grads[at, frames : frames + EXTRA].astype(jnp.float32)
            small = small + grads[at, frames + EXTRA :].astype(jnp.float32)
        filler = jnp.zeros((LANES - EXTRA, terms.shape[0]), jnp.float32)
        terms[:, width:] = jnp.concatenate([small, filler], axis=0).T
    for core in range(2):

        @pl.when(info[2] == core)
        def _():
            for at in range(parts // 2):
                own = (2 * at + core) * slim
                other = (2 * at + 1 - core) * slim
                kept[at] = terms[own : own + slim, :]
                sent[at] = terms[other : other + slim, :].astype(jnp.bfloat16)


def halve_kernel(info, kept, received, total, *blocks):
    total[...] = kept[info[3]] + received[info[3]].astype(jnp.float32)
    for by, block in enumerate(blocks, 1):
        place = info[3] ^ by
        block[...] = (kept[place] + received[place].astype(jnp.float32)).astype(jnp.bfloat16)


def finish_kernel(info, *refs):
    blocks, outs = refs[: -1], refs[-1]
    total = blocks[0][...]
    for block in blocks[1:]:
        total = total + block[...].astype(jnp.float32)
    outs[...] = total


def swap(block, axis, by):
    return lax.ppermute(block, axis, [(i, i ^ by) for i in range(lax.axis_size(axis))])


def swap_all(blocks, axis, step=1):
    return [blocks[0]] + [swap(block, axis, step * by) for by, block in enumerate(blocks[1:], 1)]


def trade(blocks):
    return lax.all_to_all(blocks, "ctx", 0, 0)


def edges(head, tail):
    count = lax.axis_size("ctx")
    steps = [(i, i + 1) for i in range(count - 1)]
    before = lax.ppermute(tail, "ctx", steps)
    after = lax.ppermute(head, "ctx", [(j, i) for i, j in steps])
    return before, after


def local(
    residual_in,
    query_rows,
    key_rows,
    value_rows,
    lengths,
    out_weight,
    norm_gain,
    conv_kernel,
    conv_bias,
    conv_gain,
    point_weight,
    grad_out,
):
    ways = lax.axis_size("ctx")
    parts = lax.axis_size("dp")
    place = lax.axis_index("dp")
    frames, width = residual_in.shape[1:]
    share = width // ways
    slim = share // parts
    heads = HEADS // ways
    every = ways * frames
    bf16, f32 = jnp.bfloat16, jnp.float32
    square = 2 * frames * width * width
    rows_bytes = 2 * frames * width

    info = jnp.stack(
        [lax.axis_index("ctx"), lengths[0], place % 2, place // 2]
    ).astype(jnp.int32)
    params = jnp.concatenate(
        [conv_kernel, norm_gain[None], conv_bias[None], conv_gain[None]], axis=0
    )
    owned = jnp.arange(share, dtype=jnp.int32)
    columns = ((owned // slim) * (ways * slim) + owned % slim)[None]

    def reduce_dp(sent, kept):
        received = swap(sent, "dp", 1)
        extent = kept.shape[1:]
        size = extent[0] * extent[1]
        halves = call(
            halve_kernel,
            "halve",
            [(extent, f32)] + [(extent, bf16)] * (parts // 2 - 1),
            moved=size * 5 * parts,
        )(info, kept, received)
        pieces = swap_all(halves, "dp", 2)
        return call(finish_kernel, "finish", [(extent, f32)], moved=size * (parts + 8))(
            info, *pieces
        )[0]

    packed = call(
        functools.partial(pack_kernel, ways),
        "pack",
        [((ways, 3, frames, share), bf16)],
        moved=6 * rows_bytes,
    )(info, query_rows[0], key_rows[0], value_rows[0])
    packed = trade(packed[0])

    masked, grad_act, masked_columns = call(
        functools.partial(mask_kernel, ways, slim),
        "mask",
        [((frames, width), bf16), ((frames, width), f32)] + [((ways, frames, share), bf16)],
        flops=2 * square,
        moved=6 * rows_bytes + 2 * width * width,
    )(info, grad_out[0], point_weight, columns)

    head_scratch = [((every, share), bf16)] * 3 + [((every, LANES), f32)]
    pair_flops = 2 * heads * every * every * HEAD_DIM
    attended_heads, log_total = call(
        functools.partial(attend_kernel, ways),
        "attend",
        [((ways, frames, share), bf16)] + [((heads, every), f32)],
        scratch=head_scratch + [((share, every), f32)],
        flops=8 * pair_flops,
        moved=4 * rows_bytes,
        exps=heads * every * every,
    )(info, packed)
    returned = trade(attended_heads)

    attended, mixed, conv_in, head, tail = call(
        functools.partial(project_kernel, ways),
        "project",
        [((frames, width), bf16), ((frames, width), f32), ((frames, width), bf16)]
        + [((EDGE, width), bf16)] * 2,
        flops=square,
        moved=6 * rows_bytes + 2 * width * width,
    )(info, returned, residual_in[0], out_weight, params)
    before, after = edges(head, tail)
    attended_all = lax.all_gather(attended, "ctx")
    masked_columns = trade(masked_columns)

    pad_scratch = [((frames + 2 * EDGE, width), f32)]
    conv_act, grad_conv, grad_head, grad_tail, conv_sums = call(
        conv_kernel_body,
        "conv",
        [((frames, width), bf16), ((frames, width), f32)]
        + [((EDGE, width), bf16)] * 2
        + [((2, width), f32)],
        scratch=pad_scratch + [((frames, width), f32)] + [((8, width), f32)] * 2,
        flops=frames * width * 4000,
        moved=6 * rows_bytes,
        exps=frames * width,
    )(info, conv_in, before, after, params, grad_act)
    grad_before, grad_after = edges(grad_head, grad_tail)
    act_all = lax.all_gather(conv_act, "ctx")

    block_out, taps = call(
        taps_kernel,
        "taps",
        [((frames, width), bf16), ((31, width), f32)],
        scratch=pad_scratch,
        flops=frames * width * 4000,
        moved=8 * rows_bytes + 2 * width * width,
    )(info, conv_in, before, after, grad_conv, conv_act, mixed, point_weight)

    grad_residual, norm_sums, grad_blocks = call(
        functools.partial(conv_back_kernel, ways),
        "conv_back",
        [((frames, width), bf16), ((1, width), f32)] + [((ways, frames, share), bf16)],
        scratch=pad_scratch + [((frames, width), f32), ((8, width), f32)],
        flops=frames * width * 4000,
        moved=8 * rows_bytes + 2 * width * width,
    )(info, grad_conv, grad_before, grad_after, params, masked, mixed, out_weight)
    grad_blocks = trade(grad_blocks)

    residual_columns = call(
        functools.partial(columns_kernel, ways, slim),
        "columns",
        [((ways, frames + 2 * EXTRA, share), bf16)],
        scratch=[((frames + 2 * EXTRA, width), bf16)],
        flops=square,
        moved=3 * rows_bytes,
    )(info, grad_residual, taps, conv_sums, norm_sums, columns)
    residual_columns = trade(residual_columns[0])

    def weight_terms(name, extent, grads, rows):
        half = (parts // 2, slim, extent)
        return call(
            functools.partial(weight_kernel, ways, parts),
            name,
            [(half, bf16), (half, f32)],
            scratch=[((share, extent), f32)],
            flops=square,
            moved=10 * rows_bytes,
        )(info, grads, rows)

    point_total = reduce_dp(*weight_terms("point_terms", width, masked_columns, act_all))
    out_total = reduce_dp(
        *weight_terms("out_terms", width + LANES, residual_columns, attended_all)
    )

    grad_packed = call(
        functools.partial(attend_back_kernel, ways),
        "attend_back",
        [((ways, 3, frames, share), bf16)],
        scratch=head_scratch + [((every, share), bf16), ((share, every), f32)],
        flops=20 * pair_flops,
        moved=8 * rows_bytes,
        exps=heads * every * every,
    )(info, packed, attended_heads, grad_blocks, log_total)
    grad_packed = trade(grad_packed[0])
    grad_query, grad_key, grad_value = call(
        functools.partial(unpack_kernel, ways),
        "unpack",
        [((frames, width), bf16)] * 3,
        moved=6 * rows_bytes,
    )(info, grad_packed)

    small = out_total[:, width:].T
    return (
        block_out[None],
        grad_residual[None],
        grad_query[None],
        grad_key[None],
        grad_value[None],
        out_total[:, :width].T,
        point_total.T,
        small[:31],
        jnp.concatenate([small[32:33], small[31:32], small[33:34]], axis=0),
    )


def solution(mesh):
    rows = P("dp", "ctx", None)
    columns = P(None, ("dp", "ctx"))
    in_specs = (rows, rows, rows, rows, P("dp"), P(), P(), P(), P(), P(), P(), rows)
    out_specs = (rows,) * 5 + (columns,) * 4
    return jax.shard_map(local, mesh=mesh, in_specs=in_specs, out_specs=out_specs, check_vma=False)
```

```python
import functools

import jax
import jax.numpy as jnp
from jax import lax
from jax.experimental import pallas as pl
from jax.experimental.pallas import tpu as pltpu
from jax.sharding import PartitionSpec as P

HEADS = 24
HEAD_DIM = 64
SCALE = HEAD_DIM ** (-0.5)

NEG_FILL = -1e30
EPSILON = 1e-05

LANES = 128
EDGE = 16
BAND = 16
EXTRA = 48

NN = (((1,), (0,)), ((), ()))
NT = (((1,), (1,)), ((), ()))
TN = (((0,), (0,)), ((), ()))


def dot(left, right, dims=NN):
    return lax.dot_general(left, right, dims, preferred_element_type=jnp.float32)


def call(kernel, name, outs, scratch=(), megabytes=28, flops=0, moved=0, exps=0):
    vmem = pl.BlockSpec(memory_space=pltpu.VMEM)
    smem = pl.BlockSpec(memory_space=pltpu.SMEM)

    def run(info, *arrays):
        return pl.pallas_call(
            kernel,
            name=name,
            in_specs=[smem] + [vmem] * len(arrays),
            out_specs=[vmem] * len(outs),
            out_shape=[jax.ShapeDtypeStruct(shape, kind) for shape, kind in outs],
            scratch_shapes=[pltpu.VMEM(shape, kind) for shape, kind in scratch],
            compiler_params=pltpu.CompilerParams(vmem_limit_bytes=megabytes << 20),
            cost_estimate=pl.CostEstimate(flops=flops, bytes_accessed=moved, transcendentals=exps),
        )(info, *arrays)

    return run


def valid_of(first, rows, length):
    return first + lax.broadcasted_iota(jnp.int32, (rows, 1), 0) < length


def moments(rows):
    centre = jnp.mean(rows, axis=-1, keepdims=True)
    centred = rows - centre
    inv_scale = lax.rsqrt(jnp.mean(centred * centred, axis=-1, keepdims=True) + EPSILON)
    return centred * inv_scale, inv_scale


def norm_back(grad_normed, normed, inv_scale):
    first_mean = jnp.mean(grad_normed, axis=-1, keepdims=True)
    second_mean = jnp.mean(grad_normed * normed, axis=-1, keepdims=True)
    return inv_scale * (grad_normed - first_mean - normed * second_mean)


def fold(rows):
    total = rows[:8]
    for at in range(8, rows.shape[0], 8):
        total = total + rows[at : at + 8]
    return total


def pack_kernel(ways, info, query, key, value, *blocks):
    share = query.shape[1] // ways
    for by in range(ways):
        for at in range(ways):

            @pl.when((info[0] ^ by) == at)
            def _():
                for slot, rows in enumerate((query, key, value)):
                    blocks[by][slot] = rows[:, at * share : (at + 1) * share]


def unpack_kernel(ways, info, *refs):
    blocks, outs = refs[:ways], refs[ways:]
    share = blocks[0].shape[2]
    for by in range(ways):
        for at in range(ways):

            @pl.when((info[0] ^ by) == at)
            def _():
                for slot, rows in enumerate(outs):
                    rows[:, at * share : (at + 1) * share] = blocks[by][slot]


def selector(columns, slim, position, width):
    wanted = columns + position * slim
    rows = lax.broadcasted_iota(jnp.int32, (width, columns.shape[1]), 0)
    return jnp.where(rows == wanted, 1.0, 0.0).astype(jnp.bfloat16)


def mask_kernel(slim, info, grad_out, before, after, point_weight, columns, masked, grad_act, *halves):
    frames, width = grad_out.shape
    rows = frames + 2 * EDGE
    first = info[0] * frames
    masked[:EDGE] = before[2 * EDGE :]
    masked[EDGE : EDGE + frames] = grad_out[...]
    masked[EDGE + frames :] = after[2 * EDGE :]
    valid = valid_of(first - EDGE, rows, info[1])
    masked[...] = jnp.where(valid, masked[...].astype(jnp.float32), 0.0).astype(jnp.bfloat16)
    step = width // 3
    for at in range(0, width, step):
        grad_act[:, at : at + step] = dot(masked[...], point_weight[at : at + step, :], NT)
    across = len(halves)
    for by in range(across):
        chosen = selector(columns[...], slim, (info[0] % across) ^ by, width)
        halves[by][...] = dot(masked[EDGE : EDGE + frames, :], chosen).astype(jnp.bfloat16)


def gather_heads(info, blocks, query, key, value, bias):
    frames = blocks[0].shape[1]
    for by, block in enumerate(blocks):
        rows = slice(by * frames, (by + 1) * frames)
        query[rows] = block[0] * jnp.bfloat16(SCALE)
        key[rows] = block[1]
        value[rows] = block[2]
        valid = valid_of((info[0] ^ by) * frames, frames, info[1])
        bias[rows] = jnp.broadcast_to(jnp.where(valid, 0.0, NEG_FILL), (frames, LANES))


def attend_kernel(ways, info, *refs):
    blocks, outs = refs[:ways], refs[ways : 2 * ways]
    attended, log_total, query, key, value, bias, turned = refs[2 * ways :]
    gather_heads(info, blocks, query, key, value, bias)
    total_frames, share = query.shape
    frames = total_frames // ways
    for head in range(share // HEAD_DIM):
        part = slice(head * HEAD_DIM, (head + 1) * HEAD_DIM)
        spread = jnp.concatenate([bias[...]] * (total_frames // LANES), axis=1)
        scores = dot(key[:, part], query[:, part], NT) + spread
        row_max = jnp.max(scores, axis=0, keepdims=True)
        weights = jnp.exp(scores - row_max)
        total = jnp.sum(weights, axis=0, keepdims=True)
        turned[part, :] = dot(value[:, part], weights.astype(jnp.bfloat16), TN) / total
        log_total[head : head + 1, :] = row_max + jnp.log(total)
    attended[...] = turned[...].T.astype(jnp.bfloat16)
    reach = 2 * EDGE
    for by in range(ways):
        other = info[0] ^ by
        before = (info[0] ^ jnp.maximum(other - 1, 0)) * frames + frames - reach
        after = (info[0] ^ jnp.minimum(other + 1, ways - 1)) * frames
        outs[by][:reach] = attended[pl.ds(pl.multiple_of(before, reach), reach), :]
        outs[by][reach : reach + frames] = attended[by * frames : (by + 1) * frames, :]
        outs[by][reach + frames :] = attended[pl.ds(pl.multiple_of(after, reach), reach), :]


def attend_back_kernel(ways, info, *refs):
    blocks, messages = refs[:ways], refs[ways : 2 * ways]
    attended, log_total = refs[2 * ways : 2 * ways + 2]
    outs = refs[2 * ways + 2 : 3 * ways + 2]
    query, key, value, bias, grad, turned = refs[3 * ways + 2 :]
    gather_heads(info, blocks, query, key, value, bias)
    total_frames, share = query.shape
    frames = total_frames // ways
    for by in range(ways):
        grad[by * frames : (by + 1) * frames] = messages[by][:frames, :]
    turned[...] = (grad[...].astype(jnp.float32) * attended[...].astype(jnp.float32)).T
    for head in range(share // HEAD_DIM):
        part = slice(head * HEAD_DIM, (head + 1) * HEAD_DIM)
        delta = jnp.sum(turned[part, :], axis=0, keepdims=True)
        spread = jnp.concatenate([bias[...]] * (total_frames // LANES), axis=1)
        scores = dot(key[:, part], query[:, part], NT) + spread
        probs = jnp.exp(scores - log_total[head : head + 1, :])
        value_grad = dot(probs.astype(jnp.bfloat16), grad[:, part])
        prob_grad = dot(value[:, part], grad[:, part], NT)
        score_grad = (probs * (prob_grad - delta)).astype(jnp.bfloat16)
        key_grad = dot(score_grad, query[:, part])
        turned[part, :] = dot(key[:, part], score_grad, TN) * SCALE
        for by in range(ways):
            rows = slice(by * frames, (by + 1) * frames)
            outs[by][1, :, part] = key_grad[rows].astype(jnp.bfloat16)
            outs[by][2, :, part] = value_grad[rows].astype(jnp.bfloat16)
    query_grad = turned[...].T.astype(jnp.bfloat16)
    for by in range(ways):
        outs[by][0] = query_grad[by * frames : (by + 1) * frames]


def project_kernel(ways, info, *refs):
    blocks = refs[:ways]
    residual, before, after, out_weight, params = refs[ways : ways + 5]
    mixed, conv_in = refs[-3 - ways : -1 - ways]
    messages, attended = refs[-1 - ways : -1], refs[-1]
    halves = refs[ways + 5 : -3 - ways]
    frames, width = residual.shape
    share = width // ways
    reach = 2 * EDGE
    rows = frames + 2 * reach
    for by in range(ways):
        for at in range(ways):

            @pl.when((info[0] ^ by) == at)
            def _():
                attended[:, at * share : (at + 1) * share] = blocks[by][...]

    step = width // 3
    for at in range(0, width, step):
        part = slice(at, at + step)
        mixed[:reach, part] = before[:reach, part].astype(jnp.float32)
        mixed[reach : reach + frames, part] = residual[:, part].astype(jnp.float32)
        mixed[reach + frames :, part] = after[:reach, part].astype(jnp.float32)
        mixed[:, part] += dot(attended[...], out_weight[:, part])

    gain = params[31:32, :]
    first = info[0] * frames - reach

    def band(index, carry):
        at = pl.ds(pl.multiple_of(index * BAND, BAND), BAND)
        normed, _ = moments(mixed[at, :])
        position = first + index * BAND + lax.broadcasted_iota(jnp.int32, (BAND, 1), 0)
        valid = (position >= 0) & (position < info[1])
        conv_in[at, :] = jnp.where(valid, normed * gain, 0.0).astype(jnp.bfloat16)
        return carry

    lax.fori_loop(0, rows // BAND, band, 0)
    for by, message in enumerate(messages):
        lacking = [slot for slot in range(ways) if slot != by]
        for at, slot in enumerate(lacking):
            message[:, at * share : (at + 1) * share] = blocks[slot][reach : reach + frames, :]
        message[:, (ways - 1) * share :] = halves[by % len(halves)][...]


def slide(padded, start, part, frames, visit):
    for residue in range(8):
        reach = frames + 2 * EDGE - 8
        shifted = padded[start + residue : start + residue + reach, part]
        for offset in range(residue, 2 * EDGE, 8):
            if offset:
                at = offset - residue
                visit(offset, shifted[at : at + frames])


def depthwise(padded, taps, tap_of, out):
    frames, width = out.shape

    def column(index, carry):
        part = pl.ds(pl.multiple_of(index * LANES, LANES), LANES)
        total = [jnp.zeros((frames, LANES), jnp.float32)]

        def visit(offset, rows):
            tap = tap_of(offset)
            total[0] = total[0] + rows * taps[tap : tap + 1, part]

        slide(padded, 0, part, frames, visit)
        out[:, part] = total[0]
        return carry

    lax.fori_loop(0, width // LANES, column, 0)


def conv_kernel_body(across, info, conv_in, params, grad_act, conv_act, grad_conv, sums, *refs):
    halves = refs[:-4]
    padded, conv, bias_sum, gain_sum = refs[-4:]
    rows, width = conv.shape
    frames = rows - 2 * EDGE
    padded[...] = conv_in[...].astype(jnp.float32)
    depthwise(padded, params, lambda offset: offset - 1, conv)
    bias, gain = params[32:33, :], params[33:34, :]
    bias_sum[...] = jnp.zeros_like(bias_sum)
    gain_sum[...] = jnp.zeros_like(gain_sum)

    def band(index, carry):
        at = pl.ds(pl.multiple_of(index * BAND, BAND), BAND)
        normed, inv_scale = moments(conv[at, :] + bias)
        scaled = normed * gain
        gate = 1.0 / (1.0 + jnp.exp(-scaled))
        conv_act[at, :] = (scaled * gate).astype(jnp.bfloat16)
        grad_scaled = grad_act[at, :] * gate * (1.0 + scaled * (1.0 - gate))
        grad_rows = norm_back(grad_scaled * gain, normed, inv_scale)
        grad_conv[at, :] = grad_rows

        @pl.when((index >= EDGE // BAND) & (index < (EDGE + frames) // BAND))
        def _():
            bias_sum[...] += fold(grad_rows)
            gain_sum[...] += fold(grad_scaled * normed)

        return carry

    lax.fori_loop(0, rows // BAND, band, 0)
    sums[0:1, :] = jnp.sum(bias_sum[...], axis=0, keepdims=True)
    sums[1:2, :] = jnp.sum(gain_sum[...], axis=0, keepdims=True)
    half = width // 2
    for by, block in enumerate(halves):
        for at in range(2):

            @pl.when((info[0] ^ by) // across == at)
            def _():
                block[...] = conv_act[EDGE : EDGE + frames, at * half : (at + 1) * half]


def block_out_kernel(info, conv_act, mixed, point_weight, block_out):
    frames, width = block_out.shape
    step = width // 3
    for at in range(0, width, step):
        part = slice(at, at + step)
        block_out[:, part] = (
            mixed[2 * EDGE : 2 * EDGE + frames, part]
            + dot(conv_act[EDGE : EDGE + frames, :], point_weight[:, part])
        ).astype(jnp.bfloat16)


def conv_back_kernel(ways, slim, info, grad_conv, conv_in, params, masked, mixed, out_weight, *refs):
    conv_sums, columns, grad_residual = refs[:3]
    messages = refs[3 : 3 + ways]
    padded, padded_in, conv, gain_sum, taps, packed = refs[3 + ways :]
    frames, width = grad_residual.shape
    share = width // ways
    padded[...] = grad_conv[...].astype(jnp.bfloat16).astype(jnp.float32)
    depthwise(padded, params, lambda offset: 31 - offset, conv)
    gain = params[31:32, :]
    gain_sum[...] = jnp.zeros_like(gain_sum)

    def band(index, carry):
        at = pl.ds(pl.multiple_of(index * BAND, BAND), BAND)
        own_mixed = pl.ds(pl.multiple_of(index * BAND + 2 * EDGE, BAND), BAND)
        own_masked = pl.ds(pl.multiple_of(index * BAND + EDGE, BAND), BAND)
        valid = valid_of(info[0] * frames + index * BAND, BAND, info[1])
        grad_in = jnp.where(valid, conv[at, :], 0.0)
        normed, inv_scale = moments(mixed[own_mixed, :])
        grad_mixed = norm_back(grad_in * gain, normed, inv_scale)
        gain_sum[...] += fold(grad_in * normed)
        grad_residual[at, :] = (masked[own_masked, :].astype(jnp.float32) + grad_mixed).astype(
            jnp.bfloat16
        )
        return carry

    lax.fori_loop(0, frames // BAND, band, 0)
    for by in range(ways):
        at = pl.ds(pl.multiple_of((info[0] ^ by) * share, share), share)
        messages[by][:frames] = dot(grad_residual[...], out_weight[at, :], NT).astype(jnp.bfloat16)

    padded_in[...] = conv_in[...].astype(jnp.float32)

    def column(index, carry):
        part = pl.ds(pl.multiple_of(index * LANES, LANES), LANES)
        grad = grad_conv[EDGE : EDGE + frames, part]

        def visit(offset, rows):
            taps[offset - 1 : offset, part] = jnp.sum(fold(rows * grad), axis=0, keepdims=True)

        slide(padded_in, EDGE, part, frames, visit)
        return carry

    lax.fori_loop(0, width // LANES, column, 0)
    taps[31:32, :] = conv_sums[0:1, :]
    taps[32:33, :] = jnp.sum(gain_sum[...], axis=0, keepdims=True)
    taps[33:34, :] = conv_sums[1:2, :]
    taps[34:, :] = jnp.zeros((EXTRA - 34, width), jnp.float32)
    high = taps[...].astype(jnp.bfloat16)
    packed[:frames] = grad_residual[...]
    packed[frames : frames + EXTRA] = high
    packed[frames + EXTRA :] = (taps[...] - high.astype(jnp.float32)).astype(jnp.bfloat16)
    for by in range(ways):
        chosen = selector(columns[...], slim, info[0] ^ by, width)
        messages[by][frames:] = dot(packed[...], chosen).astype(jnp.bfloat16)


def point_kernel(ways, info, *refs):
    messages, halves, terms = refs[:ways], refs[ways : 2 * ways], refs[2 * ways]
    extent = terms.shape[0]
    left = jnp.concatenate([block[:, block.shape[1] - extent :] for block in messages], axis=0)
    right = jnp.concatenate([half[...] for half in halves], axis=0)
    step = terms.shape[1] // 2
    for at in range(0, 2 * step, step):
        part = slice(at, at + step)
        terms[:, part] = dot(left, right[:, part], TN).astype(jnp.bfloat16)


def weight_kernel(ways, parts, info, *refs):
    grads, rows = refs[:ways], refs[ways : 2 * ways]
    attended, sent, kept, terms = refs[2 * ways :]
    total_frames, share = attended.shape
    frames = total_frames // ways
    width = ways * share
    slim = share // parts
    left = jnp.concatenate([grad[frames : 2 * frames, :] for grad in grads], axis=0)
    for slot in range(ways):
        if slot == 0:
            right = attended[...]
        else:
            pieces = []
            for by in range(ways):
                at = (by ^ slot) - (1 if (by ^ slot) > by else 0)
                pieces.append(rows[by][:, at * share : (at + 1) * share])
            right = jnp.concatenate(pieces, axis=0)
        terms[:, slot * share : (slot + 1) * share] = dot(left, right, TN)
    small = jnp.zeros((EXTRA, share), jnp.float32)
    for grad in grads:
        small = small + grad[2 * frames : 2 * frames + EXTRA, :].astype(jnp.float32)
        small = small + grad[2 * frames + EXTRA :, :].astype(jnp.float32)
    filler = jnp.zeros((LANES - EXTRA, share), jnp.float32)
    terms[:, width:] = jnp.concatenate([small, filler], axis=0).T
    for core in range(2):

        @pl.when(info[2] == core)
        def _():
            for at in range(parts // 2):
                own = (2 * at + core) * slim
                other = (2 * at + 1 - core) * slim
                kept[at] = terms[own : own + slim, :]
                sent[at] = terms[other : other + slim, :].astype(jnp.bfloat16)


def halve_kernel(info, kept, received, total, *blocks):
    total[...] = kept[info[3]] + received[info[3]].astype(jnp.float32)
    for by, block in enumerate(blocks, 1):
        place = info[3] ^ by
        block[...] = (kept[place] + received[place].astype(jnp.float32)).astype(jnp.bfloat16)


def finish_kernel(ways, info, *refs):
    blocks = refs[:-3]
    weight, taps, vectors = refs[-3:]
    width = weight.shape[1]
    share = width // ways
    total = blocks[0][...]
    for block in blocks[1:]:
        total = total + block[...].astype(jnp.float32)
    for by in range(ways):
        for at in range(ways):

            @pl.when((info[0] ^ by) == at)
            def _():
                weight[:, at * share : (at + 1) * share] = total[:, by * share : (by + 1) * share]

    small = total[:, width:].T
    taps[...] = small[:31]
    vectors[...] = small[31:34]


def swap(block, axis, by):
    return lax.ppermute(block, axis, [(i, i ^ by) for i in range(lax.axis_size(axis))])


def swap_all(blocks, axis, step=1):
    return [blocks[0]] + [swap(block, axis, step * by) for by, block in enumerate(blocks[1:], 1)]


def edges(head, tail):
    count = lax.axis_size("ctx")
    steps = [(i, i + 1) for i in range(count - 1)]
    before = lax.ppermute(tail, "ctx", steps)
    after = lax.ppermute(head, "ctx", [(j, i) for i, j in steps])
    return before, after


def local(
    residual_in,
    query_rows,
    key_rows,
    value_rows,
    lengths,
    out_weight,
    norm_gain,
    conv_kernel,
    conv_bias,
    conv_gain,
    point_weight,
    grad_out,
):
    ways = lax.axis_size("ctx")
    parts = lax.axis_size("dp")
    own = lax.axis_index("ctx")
    place = lax.axis_index("dp")
    frames, width = residual_in.shape[1:]
    share = width // ways
    slim = share // parts
    heads = HEADS // ways
    every = ways * frames
    across = ways // 2
    broad = width // across
    half = width // 2
    bf16, f32 = jnp.bfloat16, jnp.float32
    square = 2 * frames * width * width
    rows_bytes = 2 * frames * width
    reached, wide = frames + 2 * EDGE, frames + 4 * EDGE

    info = jnp.stack([own, lengths[0], place % 2, place // 2]).astype(jnp.int32)
    params = jnp.concatenate(
        [conv_kernel, norm_gain[None], conv_bias[None], conv_gain[None]], axis=0
    )

    def strided(count, group):
        at = jnp.arange(count, dtype=jnp.int32)
        return ((at // slim) * (group * slim) + at % slim)[None]

    packed = call(
        functools.partial(pack_kernel, ways),
        "pack",
        [((3, frames, share), bf16)] * ways,
        moved=6 * rows_bytes,
    )(info, query_rows[0], key_rows[0], value_rows[0])
    packed = swap_all(packed, "ctx")

    residual, grad = residual_in[0], grad_out[0]
    before, after = edges(
        jnp.concatenate([residual[: 2 * EDGE], grad[:EDGE]], axis=0),
        jnp.concatenate([residual[frames - 2 * EDGE :], grad[frames - EDGE :]], axis=0),
    )
    masked, grad_act, *masked_halves = call(
        functools.partial(mask_kernel, slim),
        "mask",
        [((reached, width), bf16), ((reached, width), f32)] + [((frames, broad), bf16)] * across,
        flops=2 * square,
        moved=6 * rows_bytes + 2 * width * width,
    )(info, grad, before, after, point_weight, strided(broad, across))

    head_scratch = [((every, share), bf16)] * 3 + [((every, LANES), f32)]
    pair_flops = 2 * heads * every * every * HEAD_DIM
    *returned, attended, log_total = call(
        functools.partial(attend_kernel, ways),
        "attend",
        [((wide, share), bf16)] * ways + [((every, share), bf16), ((heads, every), f32)],
        scratch=head_scratch + [((share, every), f32)],
        flops=8 * pair_flops,
        moved=4 * rows_bytes,
        exps=heads * every * every,
    )(info, *packed)
    returned = swap_all(returned, "ctx")

    mixed, conv_in, *messages = call(
        functools.partial(project_kernel, ways),
        "project",
        [((wide, width), f32), ((wide, width), bf16)]
        + [((frames, width - share + broad), bf16)] * ways,
        scratch=[((wide, width), bf16)],
        flops=square,
        moved=6 * rows_bytes + 2 * width * width,
    )(info, *returned, residual, before, after, out_weight, params, *masked_halves)
    messages = swap_all(messages, "ctx")

    conv_act, grad_conv, conv_sums, *act_halves = call(
        functools.partial(conv_kernel_body, across),
        "conv",
        [((reached, width), bf16), ((reached, width), f32), ((2, width), f32)]
        + [((frames, half), bf16)] * ways,
        scratch=[((wide, width), f32), ((reached, width), f32)] + [((8, width), f32)] * 2,
        flops=frames * width * 4000,
        moved=6 * rows_bytes,
        exps=frames * width,
    )(info, conv_in, params, grad_act)
    act_halves = swap_all(act_halves, "ctx")

    grad_residual, *grad_messages = call(
        functools.partial(conv_back_kernel, ways, slim),
        "conv_back",
        [((frames, width), bf16)] + [((2 * frames + 2 * EXTRA, share), bf16)] * ways,
        scratch=[
            ((reached, width), f32),
            ((wide, width), f32),
            ((frames, width), f32),
            ((8, width), f32),
            ((EXTRA, width), f32),
            ((frames + 2 * EXTRA, width), bf16),
        ],
        flops=frames * width * 8000,
        moved=8 * rows_bytes + 2 * width * width,
    )(
        info,
        grad_conv,
        conv_in,
        params,
        masked,
        mixed,
        out_weight,
        conv_sums,
        strided(share, ways),
    )
    grad_messages = swap_all(grad_messages, "ctx")

    block_out = call(
        block_out_kernel,
        "block_out",
        [((frames, width), bf16)],
        flops=square,
        moved=4 * rows_bytes + 2 * width * width,
    )(info, conv_act, mixed, point_weight)[0]

    point_terms = call(
        functools.partial(point_kernel, ways),
        "point_terms",
        [((broad, half), bf16)],
        flops=square,
        moved=8 * rows_bytes,
    )(info, *messages, *act_halves)[0]
    point_part = lax.psum_scatter(point_terms, "dp", scatter_dimension=0, tiled=True)
    point_part = point_part.reshape(2, slim, half)
    row = own // across
    point_kept = lax.dynamic_index_in_dim(point_part, row, 0, keepdims=False)
    point_sent = lax.dynamic_index_in_dim(point_part, 1 - row, 0, keepdims=False)
    point_back = swap(point_sent, "ctx", across)
    point_total = jnp.concatenate(
        [
            jnp.where(row == 0, point_kept, point_back),
            jnp.where(row == 0, point_back, point_kept),
        ],
        axis=1,
    ).astype(f32)

    extent = width + LANES
    core_half = (parts // 2, slim, extent)
    sent, kept = call(
        functools.partial(weight_kernel, ways, parts),
        "out_terms",
        [(core_half, bf16), (core_half, f32)],
        scratch=[((share, extent), f32)],
        flops=square,
        moved=10 * rows_bytes,
    )(info, *grad_messages, *messages, attended)
    received = swap(sent, "dp", 1)
    pieces = call(
        halve_kernel,
        "halve",
        [((slim, extent), f32)] + [((slim, extent), bf16)] * (parts // 2 - 1),
        moved=slim * extent * 5 * parts,
    )(info, kept, received)
    pieces = swap_all(pieces, "dp", 2)
    out_total, taps, vectors = call(
        functools.partial(finish_kernel, ways),
        "finish",
        [((slim, width), f32), ((31, slim), f32), ((3, slim), f32)],
        moved=slim * extent * (parts + 8),
    )(info, *pieces)

    grad_packed = call(
        functools.partial(attend_back_kernel, ways),
        "attend_back",
        [((3, frames, share), bf16)] * ways,
        scratch=head_scratch + [((every, share), bf16), ((share, every), f32)],
        flops=20 * pair_flops,
        moved=8 * rows_bytes,
        exps=heads * every * every,
    )(info, *packed, *grad_messages, attended, log_total)
    grad_packed = swap_all(grad_packed, "ctx")
    grad_query, grad_key, grad_value = call(
        functools.partial(unpack_kernel, ways),
        "unpack",
        [((frames, width), bf16)] * 3,
        moved=6 * rows_bytes,
    )(info, *grad_packed)

    return (
        block_out[None],
        grad_residual[None],
        grad_query[None],
        grad_key[None],
        grad_value[None],
        out_total.T,
        point_total.T,
        taps,
        vectors,
    )


def solution(mesh):
    rows = P("dp", "ctx", None)
    columns = P(None, ("dp", "ctx"))
    in_specs = (rows, rows, rows, rows, P("dp"), P(), P(), P(), P(), P(), P(), rows)
    out_specs = (rows,) * 5 + (columns,) * 4
    return jax.shard_map(local, mesh=mesh, in_specs=in_specs, out_specs=out_specs, check_vma=False)
```

```python
import functools

import jax
import jax.numpy as jnp
from jax import lax
from jax.experimental import pallas as pl
from jax.experimental.pallas import tpu as pltpu
from jax.sharding import PartitionSpec as P

HEADS = 24
HEAD_DIM = 64
SCALE = HEAD_DIM ** (-0.5)

NEG_FILL = -1e30
EPSILON = 1e-05

LANES = 128
EDGE = 16
BAND = 16
EXTRA = 48

NN = (((1,), (0,)), ((), ()))
NT = (((1,), (1,)), ((), ()))
TN = (((0,), (0,)), ((), ()))


def dot(left, right, dims=NN):
    return lax.dot_general(left, right, dims, preferred_element_type=jnp.float32)


def call(
    kernel, name, outs, scratch=(), semaphores=0, far=(), megabytes=28, flops=0, moved=0, exps=0
):
    vmem = pl.BlockSpec(memory_space=pltpu.VMEM)
    smem = pl.BlockSpec(memory_space=pltpu.SMEM)
    anywhere = pl.BlockSpec(memory_space=pl.ANY)

    def run(info, *arrays):
        scratches = [pltpu.VMEM(shape, kind) for shape, kind in scratch]
        if semaphores:
            scratches.append(pltpu.SemaphoreType.DMA((semaphores,)))
        return pl.pallas_call(
            kernel,
            name=name,
            in_specs=[smem] + [anywhere if "in" in far else vmem] * len(arrays),
            out_specs=[anywhere if "out" in far else vmem] * len(outs),
            out_shape=[jax.ShapeDtypeStruct(shape, kind) for shape, kind in outs],
            scratch_shapes=scratches,
            compiler_params=pltpu.CompilerParams(vmem_limit_bytes=megabytes << 20),
            cost_estimate=pl.CostEstimate(flops=flops, bytes_accessed=moved, transcendentals=exps),
        )(info, *arrays)

    return run


def valid_of(first, rows, length):
    return first + lax.broadcasted_iota(jnp.int32, (rows, 1), 0) < length


def moments(rows):
    centre = jnp.mean(rows, axis=-1, keepdims=True)
    centred = rows - centre
    inv_scale = lax.rsqrt(jnp.mean(centred * centred, axis=-1, keepdims=True) + EPSILON)
    return centred * inv_scale, inv_scale


def norm_back(grad_normed, normed, inv_scale):
    first_mean = jnp.mean(grad_normed, axis=-1, keepdims=True)
    second_mean = jnp.mean(grad_normed * normed, axis=-1, keepdims=True)
    return inv_scale * (grad_normed - first_mean - normed * second_mean)


def fold(rows):
    total = rows[:8]
    for at in range(8, rows.shape[0], 8):
        total = total + rows[at : at + 8]
    return total


def own_lanes(info, by, share):
    return pl.ds(pl.multiple_of((info[0] ^ by) * share, LANES), share)


def pack_kernel(ways, info, query, key, value, *refs):
    blocks, arrived = refs[:ways], refs[ways]
    share = query.shape[1] // ways
    copies = []
    for by in range(1, ways + 1):
        for slot, rows in enumerate((query, key, value)):
            copy = pltpu.make_async_copy(
                rows.at[:, own_lanes(info, by % ways, share)],
                blocks[by % ways].at[slot],
                arrived.at[len(copies)],
            )
            copy.start()
            copies.append(copy)
    for copy in copies:
        copy.wait()


def unpack_kernel(ways, info, *refs):
    blocks, outs, arrived = refs[:ways], refs[ways:-1], refs[-1]
    share = blocks[0].shape[2]
    copies = []
    for by in range(ways):
        for slot, rows in enumerate(outs):
            copy = pltpu.make_async_copy(
                blocks[by].at[slot],
                rows.at[:, own_lanes(info, by, share)],
                arrived.at[len(copies)],
            )
            copy.start()
            copies.append(copy)
    for copy in copies:
        copy.wait()


def pack_parts_kernel(ways, info, query, key, value, *blocks):
    share = query.shape[1] // ways
    for by in range(ways):
        for at in range(ways):

            @pl.when((info[0] ^ by) == at)
            def _():
                for slot, rows in enumerate((query, key, value)):
                    blocks[by][slot] = rows[:, at * share : (at + 1) * share]


def unpack_parts_kernel(ways, info, *refs):
    blocks, outs = refs[:ways], refs[ways:]
    share = blocks[0].shape[2]
    for by in range(ways):
        for at in range(ways):

            @pl.when((info[0] ^ by) == at)
            def _():
                for slot, rows in enumerate(outs):
                    rows[:, at * share : (at + 1) * share] = blocks[by][slot]


def selector(columns, slim, position, width):
    wanted = columns + position * slim
    rows = lax.broadcasted_iota(jnp.int32, (width, columns.shape[1]), 0)
    return jnp.where(rows == wanted, 1.0, 0.0).astype(jnp.bfloat16)


def mask_kernel(slim, info, grad_out, before, after, point_weight, columns, masked, grad_act, *halves):
    frames, width = grad_out.shape
    rows = frames + 2 * EDGE
    first = info[0] * frames
    masked[:EDGE] = before[2 * EDGE :]
    masked[EDGE : EDGE + frames] = grad_out[...]
    masked[EDGE + frames :] = after[2 * EDGE :]
    valid = valid_of(first - EDGE, rows, info[1])
    masked[...] = jnp.where(valid, masked[...].astype(jnp.float32), 0.0).astype(jnp.bfloat16)
    step = width // 3
    for at in range(0, width, step):
        grad_act[:, at : at + step] = dot(masked[...], point_weight[at : at + step, :], NT)
    across = len(halves)
    for by in range(across):
        chosen = selector(columns[...], slim, (info[0] % across) ^ by, width)
        halves[by][...] = dot(masked[EDGE : EDGE + frames, :], chosen).astype(jnp.bfloat16)


def gather_heads(info, blocks, query, key, value, bias):
    frames = blocks[0].shape[1]
    for by, block in enumerate(blocks):
        rows = slice(by * frames, (by + 1) * frames)
        query[rows] = block[0] * jnp.bfloat16(SCALE)
        key[rows] = block[1]
        value[rows] = block[2]
        valid = valid_of((info[0] ^ by) * frames, frames, info[1])
        bias[rows] = jnp.broadcast_to(jnp.where(valid, 0.0, NEG_FILL), (frames, LANES))


def attend_kernel(ways, info, *refs):
    blocks, outs = refs[:ways], refs[ways : 2 * ways]
    attended, log_total, query, key, value, bias, turned = refs[2 * ways :]
    gather_heads(info, blocks, query, key, value, bias)
    total_frames, share = query.shape
    frames = total_frames // ways
    for head in range(share // HEAD_DIM):
        part = slice(head * HEAD_DIM, (head + 1) * HEAD_DIM)
        spread = jnp.concatenate([bias[...]] * (total_frames // LANES), axis=1)
        scores = dot(key[:, part], query[:, part], NT) + spread
        row_max = jnp.max(scores, axis=0, keepdims=True)
        weights = jnp.exp(scores - row_max)
        total = jnp.sum(weights, axis=0, keepdims=True)
        turned[part, :] = dot(value[:, part], weights.astype(jnp.bfloat16), TN) / total
        log_total[head : head + 1, :] = row_max + jnp.log(total)
    attended[...] = turned[...].T.astype(jnp.bfloat16)
    reach = 2 * EDGE
    for by in range(ways):
        other = info[0] ^ by
        before = (info[0] ^ jnp.maximum(other - 1, 0)) * frames + frames - reach
        after = (info[0] ^ jnp.minimum(other + 1, ways - 1)) * frames
        outs[by][:reach] = attended[pl.ds(pl.multiple_of(before, reach), reach), :]
        outs[by][reach : reach + frames] = attended[by * frames : (by + 1) * frames, :]
        outs[by][reach + frames :] = attended[pl.ds(pl.multiple_of(after, reach), reach), :]


def attend_back_kernel(ways, info, *refs):
    blocks, messages = refs[:ways], refs[ways : 2 * ways]
    attended, log_total = refs[2 * ways : 2 * ways + 2]
    outs = refs[2 * ways + 2 : 3 * ways + 2]
    query, key, value, bias, grad, turned = refs[3 * ways + 2 :]
    gather_heads(info, blocks, query, key, value, bias)
    total_frames, share = query.shape
    frames = total_frames // ways
    for by in range(ways):
        grad[by * frames : (by + 1) * frames] = messages[by][:frames, :]
    turned[...] = (grad[...].astype(jnp.float32) * attended[...].astype(jnp.float32)).T
    for head in range(share // HEAD_DIM):
        part = slice(head * HEAD_DIM, (head + 1) * HEAD_DIM)
        delta = jnp.sum(turned[part, :], axis=0, keepdims=True)
        spread = jnp.concatenate([bias[...]] * (total_frames // LANES), axis=1)
        scores = dot(key[:, part], query[:, part], NT) + spread
        probs = jnp.exp(scores - log_total[head : head + 1, :])
        value_grad = dot(probs.astype(jnp.bfloat16), grad[:, part])
        prob_grad = dot(value[:, part], grad[:, part], NT)
        score_grad = (probs * (prob_grad - delta)).astype(jnp.bfloat16)
        key_grad = dot(score_grad, query[:, part])
        turned[part, :] = dot(key[:, part], score_grad, TN) * SCALE
        for by in range(ways):
            rows = slice(by * frames, (by + 1) * frames)
            outs[by][1, :, part] = key_grad[rows].astype(jnp.bfloat16)
            outs[by][2, :, part] = value_grad[rows].astype(jnp.bfloat16)
    query_grad = turned[...].T.astype(jnp.bfloat16)
    for by in range(ways):
        outs[by][0] = query_grad[by * frames : (by + 1) * frames]


def project_kernel(ways, info, *refs):
    blocks = refs[:ways]
    residual, before, after, out_weight, params = refs[ways : ways + 5]
    mixed, conv_in = refs[ways + 5 : ways + 7]
    messages, attended = refs[ways + 7 : -1], refs[-1]
    frames, width = residual.shape
    share = width // ways
    reach = 2 * EDGE
    rows = frames + 2 * reach
    for by in range(ways):
        for at in range(ways):

            @pl.when((info[0] ^ by) == at)
            def _():
                attended[:, at * share : (at + 1) * share] = blocks[by][...]

    step = width // 3
    for at in range(0, width, step):
        part = slice(at, at + step)
        mixed[:reach, part] = before[:reach, part].astype(jnp.float32)
        mixed[reach : reach + frames, part] = residual[:, part].astype(jnp.float32)
        mixed[reach + frames :, part] = after[:reach, part].astype(jnp.float32)
        mixed[:, part] += dot(attended[...], out_weight[:, part])

    gain = params[31:32, :]
    first = info[0] * frames - reach

    def band(index, carry):
        at = pl.ds(pl.multiple_of(index * BAND, BAND), BAND)
        normed, _ = moments(mixed[at, :])
        position = first + index * BAND + lax.broadcasted_iota(jnp.int32, (BAND, 1), 0)
        valid = (position >= 0) & (position < info[1])
        conv_in[at, :] = jnp.where(valid, normed * gain, 0.0).astype(jnp.bfloat16)
        return carry

    lax.fori_loop(0, rows // BAND, band, 0)
    for by, message in enumerate(messages):
        lacking = [slot for slot in range(ways) if slot != by]
        for at, slot in enumerate(lacking):
            message[:, at * share : (at + 1) * share] = blocks[slot][reach : reach + frames, :]


def slide(padded, start, part, frames, visit):
    for residue in range(8):
        reach = frames + 2 * EDGE - 8
        shifted = padded[start + residue : start + residue + reach, part]
        for offset in range(residue, 2 * EDGE, 8):
            if offset:
                at = offset - residue
                visit(offset, shifted[at : at + frames])


def depthwise(padded, taps, tap_of, out):
    frames, width = out.shape

    def column(index, carry):
        part = pl.ds(pl.multiple_of(index * LANES, LANES), LANES)
        total = [jnp.zeros((frames, LANES), jnp.float32)]

        def visit(offset, rows):
            tap = tap_of(offset)
            total[0] = total[0] + rows * taps[tap : tap + 1, part]

        slide(padded, 0, part, frames, visit)
        out[:, part] = total[0]
        return carry

    lax.fori_loop(0, width // LANES, column, 0)


def conv_kernel_body(across, info, conv_in, params, grad_act, *refs):
    masked_halves = refs[:across]
    conv_act, grad_conv, sums = refs[across : across + 3]
    messages = refs[across + 3 : -4]
    padded, conv, bias_sum, gain_sum = refs[-4:]
    rows, width = conv.shape
    frames = rows - 2 * EDGE
    padded[...] = conv_in[...].astype(jnp.float32)
    depthwise(padded, params, lambda offset: offset - 1, conv)
    bias, gain = params[32:33, :], params[33:34, :]
    bias_sum[...] = jnp.zeros_like(bias_sum)
    gain_sum[...] = jnp.zeros_like(gain_sum)

    def band(index, carry):
        at = pl.ds(pl.multiple_of(index * BAND, BAND), BAND)
        normed, inv_scale = moments(conv[at, :] + bias)
        scaled = normed * gain
        gate = 1.0 / (1.0 + jnp.exp(-scaled))
        conv_act[at, :] = (scaled * gate).astype(jnp.bfloat16)
        grad_scaled = grad_act[at, :] * gate * (1.0 + scaled * (1.0 - gate))
        grad_rows = norm_back(grad_scaled * gain, normed, inv_scale)
        grad_conv[at, :] = grad_rows

        @pl.when((index >= EDGE // BAND) & (index < (EDGE + frames) // BAND))
        def _():
            bias_sum[...] += fold(grad_rows)
            gain_sum[...] += fold(grad_scaled * normed)

        return carry

    lax.fori_loop(0, rows // BAND, band, 0)
    sums[0:1, :] = jnp.sum(bias_sum[...], axis=0, keepdims=True)
    sums[1:2, :] = jnp.sum(gain_sum[...], axis=0, keepdims=True)
    half = width // 2
    for by, message in enumerate(messages):
        message[:, half:] = masked_halves[by % across][...]
        for at in range(2):

            @pl.when((info[0] ^ by) // across == at)
            def _():
                message[:, :half] = conv_act[EDGE : EDGE + frames, at * half : (at + 1) * half]


def block_out_kernel(info, conv_act, mixed, point_weight, block_out):
    frames, width = block_out.shape
    step = width // 3
    for at in range(0, width, step):
        part = slice(at, at + step)
        block_out[:, part] = (
            mixed[2 * EDGE : 2 * EDGE + frames, part]
            + dot(conv_act[EDGE : EDGE + frames, :], point_weight[:, part])
        ).astype(jnp.bfloat16)


def conv_back_kernel(ways, slim, info, grad_conv, conv_in, params, masked, mixed, out_weight, *refs):
    conv_sums, columns, grad_residual = refs[:3]
    messages = refs[3 : 3 + ways]
    padded, padded_in, conv, gain_sum, taps, packed = refs[3 + ways :]
    frames, width = grad_residual.shape
    share = width // ways
    padded[...] = grad_conv[...].astype(jnp.bfloat16).astype(jnp.float32)
    depthwise(padded, params, lambda offset: 31 - offset, conv)
    gain = params[31:32, :]
    gain_sum[...] = jnp.zeros_like(gain_sum)

    def band(index, carry):
        at = pl.ds(pl.multiple_of(index * BAND, BAND), BAND)
        own_mixed = pl.ds(pl.multiple_of(index * BAND + 2 * EDGE, BAND), BAND)
        own_masked = pl.ds(pl.multiple_of(index * BAND + EDGE, BAND), BAND)
        valid = valid_of(info[0] * frames + index * BAND, BAND, info[1])
        grad_in = jnp.where(valid, conv[at, :], 0.0)
        normed, inv_scale = moments(mixed[own_mixed, :])
        grad_mixed = norm_back(grad_in * gain, normed, inv_scale)
        gain_sum[...] += fold(grad_in * normed)
        grad_residual[at, :] = (masked[own_masked, :].astype(jnp.float32) + grad_mixed).astype(
            jnp.bfloat16
        )
        return carry

    lax.fori_loop(0, frames // BAND, band, 0)
    for by in range(ways):
        at = pl.ds(pl.multiple_of((info[0] ^ by) * share, share), share)
        messages[by][:frames] = dot(grad_residual[...], out_weight[at, :], NT).astype(jnp.bfloat16)

    padded_in[...] = conv_in[...].astype(jnp.float32)

    def column(index, carry):
        part = pl.ds(pl.multiple_of(index * LANES, LANES), LANES)
        grad = grad_conv[EDGE : EDGE + frames, part]

        def visit(offset, rows):
            taps[offset - 1 : offset, part] = jnp.sum(fold(rows * grad), axis=0, keepdims=True)

        slide(padded_in, EDGE, part, frames, visit)
        return carry

    lax.fori_loop(0, width // LANES, column, 0)
    taps[31:32, :] = conv_sums[0:1, :]
    taps[32:33, :] = jnp.sum(gain_sum[...], axis=0, keepdims=True)
    taps[33:34, :] = conv_sums[1:2, :]
    taps[34:, :] = jnp.zeros((EXTRA - 34, width), jnp.float32)
    high = taps[...].astype(jnp.bfloat16)
    packed[:frames] = grad_residual[...]
    packed[frames : frames + EXTRA] = high
    packed[frames + EXTRA :] = (taps[...] - high.astype(jnp.float32)).astype(jnp.bfloat16)
    for by in range(ways):
        chosen = selector(columns[...], slim, info[0] ^ by, width)
        messages[by][frames:] = dot(packed[...], chosen).astype(jnp.bfloat16)


def split_rows(info, parts, terms, sent, kept):
    rows = terms.shape[0] // parts
    for bit in range(2):

        @pl.when(info[2] % 2 == bit)
        def _():
            for at in range(parts // 2):
                own = (2 * at + bit) * rows
                other = (2 * at + 1 - bit) * rows
                kept[at] = terms[own : own + rows, :]
                sent[at] = terms[other : other + rows, :].astype(jnp.bfloat16)


def point_kernel(ways, parts, info, *refs):
    messages, (sent, kept, terms) = refs[:ways], refs[ways:]
    half = terms.shape[1]
    left = jnp.concatenate([message[:, half:] for message in messages], axis=0)
    right = jnp.concatenate([message[:, :half] for message in messages], axis=0)
    step = half // 2
    for at in range(0, 2 * step, step):
        part = slice(at, at + step)
        terms[:, part] = dot(left, right[:, part], TN)
    split_rows(info, parts, terms, sent, kept)


def point_sum_kernel(across, info, kept, received, own, other):
    rows = own.shape[0]
    total = kept[0] + received[0].astype(jnp.float32)
    for at in range(2):

        @pl.when(info[0] // across == at)
        def _():
            own[...] = total[at * rows : (at + 1) * rows, :]
            other[...] = total[(1 - at) * rows : (2 - at) * rows, :].astype(jnp.bfloat16)


def point_finish_kernel(across, info, own, other, out):
    half = own.shape[1]
    for at in range(2):

        @pl.when(info[0] // across == at)
        def _():
            out[:, at * half : (at + 1) * half] = own[...]
            out[:, (1 - at) * half : (2 - at) * half] = other[...].astype(jnp.float32)


def weight_kernel(ways, parts, info, *refs):
    grads, rows = refs[:ways], refs[ways : 2 * ways]
    attended, sent, kept, terms = refs[2 * ways :]
    total_frames, share = attended.shape
    frames = total_frames // ways
    width = ways * share
    slim = share // parts
    left = jnp.concatenate([grad[frames : 2 * frames, :] for grad in grads], axis=0)
    for slot in range(ways):
        if slot == 0:
            right = attended[...]
        else:
            pieces = []
            for by in range(ways):
                at = (by ^ slot) - (1 if (by ^ slot) > by else 0)
                pieces.append(rows[by][:, at * share : (at + 1) * share])
            right = jnp.concatenate(pieces, axis=0)
        terms[:, slot * share : (slot + 1) * share] = dot(left, right, TN)
    small = jnp.zeros((EXTRA, share), jnp.float32)
    for grad in grads:
        small = small + grad[2 * frames : 2 * frames + EXTRA, :].astype(jnp.float32)
        small = small + grad[2 * frames + EXTRA :, :].astype(jnp.float32)
    filler = jnp.zeros((LANES - EXTRA, share), jnp.float32)
    terms[:, width:] = jnp.concatenate([small, filler], axis=0).T
    split_rows(info, parts, terms, sent, kept)


def halve_kernel(level, info, kept, received, sent, still_kept):
    bit = (info[2] >> level) & 1
    for at in range(sent.shape[0]):
        own, other = 2 * at + bit, 2 * at + 1 - bit
        still_kept[at] = kept[own] + received[own].astype(jnp.float32)
        sent[at] = (kept[other] + received[other].astype(jnp.float32)).astype(jnp.bfloat16)


def finish_kernel(ways, info, kept, received, weight, taps, vectors):
    width = weight.shape[1]
    share = width // ways
    total = kept[0] + received[0].astype(jnp.float32)
    for by in range(ways):
        for at in range(ways):

            @pl.when((info[0] ^ by) == at)
            def _():
                weight[:, at * share : (at + 1) * share] = total[:, by * share : (by + 1) * share]

    small = total[:, width:].T
    taps[...] = small[:31]
    vectors[...] = small[31:34]


def swap(block, axis, by):
    return lax.ppermute(block, axis, [(i, i ^ by) for i in range(lax.axis_size(axis))])


def swap_all(blocks, axis, step=1):
    return [blocks[0]] + [swap(block, axis, step * by) for by, block in enumerate(blocks[1:], 1)]


def edges(head, tail):
    count = lax.axis_size("ctx")
    steps = [(i, i + 1) for i in range(count - 1)]
    before = lax.ppermute(tail, "ctx", steps)
    after = lax.ppermute(head, "ctx", [(j, i) for i, j in steps])
    return before, after


def local(
    residual_in,
    query_rows,
    key_rows,
    value_rows,
    lengths,
    out_weight,
    norm_gain,
    conv_kernel,
    conv_bias,
    conv_gain,
    point_weight,
    grad_out,
):
    ways = lax.axis_size("ctx")
    parts = lax.axis_size("dp")
    own = lax.axis_index("ctx")
    place = lax.axis_index("dp")
    frames, width = residual_in.shape[1:]
    share = width // ways
    slim = share // parts
    heads = HEADS // ways
    every = ways * frames
    across = ways // 2
    broad = width // across
    half = width // 2
    bf16, f32 = jnp.bfloat16, jnp.float32
    square = 2 * frames * width * width
    rows_bytes = 2 * frames * width
    reached, wide = frames + 2 * EDGE, frames + 4 * EDGE

    info = jnp.stack([own, lengths[0], place]).astype(jnp.int32)
    params = jnp.concatenate(
        [conv_kernel, norm_gain[None], conv_bias[None], conv_gain[None]], axis=0
    )

    def strided(count, group):
        at = jnp.arange(count, dtype=jnp.int32)
        return ((at // slim) * (group * slim) + at % slim)[None]

    by_tiles = share % LANES == 0
    packed = call(
        functools.partial(pack_kernel if by_tiles else pack_parts_kernel, ways),
        "pack",
        [((3, frames, share), bf16)] * ways,
        semaphores=3 * ways if by_tiles else 0,
        far=("in",) if by_tiles else (),
        megabytes=58,
        moved=6 * rows_bytes,
    )(info, query_rows[0], key_rows[0], value_rows[0])
    packed = swap_all(packed, "ctx")

    residual, grad = residual_in[0], grad_out[0]
    before, after = edges(
        jnp.concatenate([residual[: 2 * EDGE], grad[:EDGE]], axis=0),
        jnp.concatenate([residual[frames - 2 * EDGE :], grad[frames - EDGE :]], axis=0),
    )
    masked, grad_act, *masked_halves = call(
        functools.partial(mask_kernel, slim),
        "mask",
        [((reached, width), bf16), ((reached, width), f32)] + [((frames, broad), bf16)] * across,
        flops=2 * square,
        moved=6 * rows_bytes + 2 * width * width,
    )(info, grad, before, after, point_weight, strided(broad, across))

    packed, masked = lax.optimization_barrier((packed, masked))
    head_scratch = [((every, share), bf16)] * 3 + [((every, LANES), f32)]
    pair_flops = 2 * heads * every * every * HEAD_DIM
    *returned, attended, log_total = call(
        functools.partial(attend_kernel, ways),
        "attend",
        [((wide, share), bf16)] * ways + [((every, share), bf16), ((heads, every), f32)],
        scratch=head_scratch + [((share, every), f32)],
        flops=8 * pair_flops,
        moved=4 * rows_bytes,
        exps=heads * every * every,
    )(info, *packed)
    returned = swap_all(returned, "ctx")

    mixed, conv_in, *messages = call(
        functools.partial(project_kernel, ways),
        "project",
        [((wide, width), f32), ((wide, width), bf16)] + [((frames, width - share), bf16)] * ways,
        scratch=[((wide, width), bf16)],
        flops=square,
        moved=6 * rows_bytes + 2 * width * width,
    )(info, *returned, residual, before, after, out_weight, params)
    messages = swap_all(messages, "ctx")

    conv_act, grad_conv, conv_sums, *point_messages = call(
        functools.partial(conv_kernel_body, across),
        "conv",
        [((reached, width), bf16), ((reached, width), f32), ((2, width), f32)]
        + [((frames, half + broad), bf16)] * ways,
        scratch=[((wide, width), f32), ((reached, width), f32)] + [((8, width), f32)] * 2,
        flops=frames * width * 4000,
        moved=6 * rows_bytes,
        exps=frames * width,
    )(info, conv_in, params, grad_act, *masked_halves)
    messages, point_messages, grad_conv = lax.optimization_barrier(
        (messages, point_messages, grad_conv)
    )
    point_messages = swap_all(point_messages, "ctx")

    grad_residual, *grad_messages = call(
        functools.partial(conv_back_kernel, ways, slim),
        "conv_back",
        [((frames, width), bf16)] + [((2 * frames + 2 * EXTRA, share), bf16)] * ways,
        scratch=[
            ((reached, width), f32),
            ((wide, width), f32),
            ((frames, width), f32),
            ((8, width), f32),
            ((EXTRA, width), f32),
            ((frames + 2 * EXTRA, width), bf16),
        ],
        flops=frames * width * 8000,
        moved=8 * rows_bytes + 2 * width * width,
    )(
        info,
        grad_conv,
        conv_in,
        params,
        masked,
        mixed,
        out_weight,
        conv_sums,
        strided(share, ways),
    )
    point_messages, grad_messages = lax.optimization_barrier((point_messages, grad_messages))
    grad_messages = swap_all(grad_messages, "ctx")

    block_out = call(
        block_out_kernel,
        "block_out",
        [((frames, width), bf16)],
        flops=square,
        moved=4 * rows_bytes + 2 * width * width,
    )(info, conv_act, mixed, point_weight)[0]

    def reduce_dp(sent, kept):
        received = swap(sent, "dp", 1)
        level, blocks = 1, parts // 2
        while blocks > 1:
            blocks //= 2
            extent = (blocks,) + kept.shape[1:]
            sent, kept = call(
                functools.partial(halve_kernel, level),
                "halve",
                [(extent, bf16), (extent, f32)],
                moved=16 * blocks * extent[1] * extent[2],
            )(info, kept, received)
            received = swap(sent, "dp", 2**level)
            level += 1
        return kept, received

    core_half = (parts // 2, 2 * slim, half)
    point_sent, point_kept = call(
        functools.partial(point_kernel, ways, parts),
        "point_terms",
        [(core_half, bf16), (core_half, f32)],
        scratch=[((broad, half), f32)],
        flops=square,
        moved=8 * rows_bytes,
    )(info, *point_messages)
    grad_messages, point_sent, block_out = lax.optimization_barrier(
        (grad_messages, point_sent, block_out)
    )
    point_pieces = reduce_dp(point_sent, point_kept)
    point_own, point_other = call(
        functools.partial(point_sum_kernel, across),
        "point_sum",
        [((slim, half), f32), ((slim, half), bf16)],
        moved=slim * width * (parts + 8),
    )(info, *point_pieces)
    point_other = swap(point_other, "ctx", across)
    point_total = call(
        functools.partial(point_finish_kernel, across),
        "point_finish",
        [((slim, width), f32)],
        moved=slim * width * 8,
    )(info, point_own, point_other)[0]

    extent = width + LANES
    core_half = (parts // 2, slim, extent)
    sent, kept = call(
        functools.partial(weight_kernel, ways, parts),
        "out_terms",
        [(core_half, bf16), (core_half, f32)],
        scratch=[((share, extent), f32)],
        flops=square,
        moved=10 * rows_bytes,
    )(info, *grad_messages, *messages, attended)
    pieces = reduce_dp(sent, kept)
    out_total, taps, vectors = call(
        functools.partial(finish_kernel, ways),
        "finish",
        [((slim, width), f32), ((31, slim), f32), ((3, slim), f32)],
        moved=slim * extent * (parts + 8),
    )(info, *pieces)

    grad_packed = call(
        functools.partial(attend_back_kernel, ways),
        "attend_back",
        [((3, frames, share), bf16)] * ways,
        scratch=head_scratch + [((every, share), bf16), ((share, every), f32)],
        flops=20 * pair_flops,
        moved=8 * rows_bytes,
        exps=heads * every * every,
    )(info, *packed, *grad_messages, attended, log_total)
    grad_packed = swap_all(grad_packed, "ctx")
    grad_query, grad_key, grad_value = call(
        functools.partial(unpack_kernel if by_tiles else unpack_parts_kernel, ways),
        "unpack",
        [((frames, width), bf16)] * 3,
        semaphores=3 * ways if by_tiles else 0,
        far=("out",) if by_tiles else (),
        moved=6 * rows_bytes,
    )(info, *grad_packed)

    return (
        block_out[None],
        grad_residual[None],
        grad_query[None],
        grad_key[None],
        grad_value[None],
        out_total.T,
        point_total.T,
        taps,
        vectors,
    )


def solution(mesh):
    rows = P("dp", "ctx", None)
    columns = P(None, ("dp", "ctx"))
    in_specs = (rows, rows, rows, rows, P("dp"), P(), P(), P(), P(), P(), P(), rows)
    out_specs = (rows,) * 5 + (columns,) * 4
    return jax.shard_map(local, mesh=mesh, in_specs=in_specs, out_specs=out_specs, check_vma=False)
```

```python
import functools

import jax
import jax.numpy as jnp
from jax import lax
from jax.experimental import pallas as pl
from jax.experimental.pallas import tpu as pltpu
from jax.sharding import PartitionSpec as P

HEADS = 24
HEAD_DIM = 64
SCALE = HEAD_DIM ** (-0.5)

NEG_FILL = -1e30
EPSILON = 1e-05

LANES = 128
EDGE = 16
BAND = 16
EXTRA = 48

NN = (((1,), (0,)), ((), ()))
NT = (((1,), (1,)), ((), ()))
TN = (((0,), (0,)), ((), ()))


def dot(left, right, dims=NN):
    return lax.dot_general(left, right, dims, preferred_element_type=jnp.float32)


def call(
    kernel, name, outs, scratch=(), semaphores=0, far=(), megabytes=28, flops=0, moved=0, exps=0
):
    vmem = pl.BlockSpec(memory_space=pltpu.VMEM)
    smem = pl.BlockSpec(memory_space=pltpu.SMEM)
    anywhere = pl.BlockSpec(memory_space=pl.ANY)

    def run(info, *arrays):
        scratches = [pltpu.VMEM(shape, kind) for shape, kind in scratch]
        if semaphores:
            scratches.append(pltpu.SemaphoreType.DMA((semaphores,)))
        return pl.pallas_call(
            kernel,
            name=name,
            in_specs=[smem] + [anywhere if "in" in far else vmem] * len(arrays),
            out_specs=[anywhere if "out" in far else vmem] * len(outs),
            out_shape=[jax.ShapeDtypeStruct(shape, kind) for shape, kind in outs],
            scratch_shapes=scratches,
            compiler_params=pltpu.CompilerParams(vmem_limit_bytes=megabytes << 20),
            cost_estimate=pl.CostEstimate(flops=flops, bytes_accessed=moved, transcendentals=exps),
        )(info, *arrays)

    return run


def valid_of(first, rows, length):
    return first + lax.broadcasted_iota(jnp.int32, (rows, 1), 0) < length


def moments(rows):
    centre = jnp.mean(rows, axis=-1, keepdims=True)
    centred = rows - centre
    inv_scale = lax.rsqrt(jnp.mean(centred * centred, axis=-1, keepdims=True) + EPSILON)
    return centred * inv_scale, inv_scale


def norm_back(grad_normed, normed, inv_scale):
    first_mean = jnp.mean(grad_normed, axis=-1, keepdims=True)
    second_mean = jnp.mean(grad_normed * normed, axis=-1, keepdims=True)
    return inv_scale * (grad_normed - first_mean - normed * second_mean)


def fold(rows):
    total = rows[:8]
    for at in range(8, rows.shape[0], 8):
        total = total + rows[at : at + 8]
    return total


def own_lanes(info, by, share):
    return pl.ds(pl.multiple_of((info[0] ^ by) * share, LANES), share)


def pack_kernel(ways, info, query, key, value, *refs):
    blocks, whole, arrived = refs[:ways], refs[ways], refs[ways + 1]
    share = query.shape[1] // ways
    copies = []
    for slot, rows in enumerate((query, key, value)):
        copies.append(pltpu.make_async_copy(rows, whole.at[slot], arrived.at[slot]))
        copies[slot].start()
    for slot, copy in enumerate(copies):
        copy.wait()
        for by in range(ways):
            blocks[by][slot] = whole[slot, :, own_lanes(info, by, share)]


def unpack_kernel(ways, info, *refs):
    blocks, outs, arrived = refs[:ways], refs[ways:-1], refs[-1]
    share = blocks[0].shape[2]
    copies = []
    for by in range(ways):
        for slot, rows in enumerate(outs):
            copy = pltpu.make_async_copy(
                blocks[by].at[slot],
                rows.at[:, own_lanes(info, by, share)],
                arrived.at[len(copies)],
            )
            copy.start()
            copies.append(copy)
    for copy in copies:
        copy.wait()


def pack_parts_kernel(ways, info, query, key, value, *blocks):
    share = query.shape[1] // ways
    for by in range(ways):
        for at in range(ways):

            @pl.when((info[0] ^ by) == at)
            def _():
                for slot, rows in enumerate((query, key, value)):
                    blocks[by][slot] = rows[:, at * share : (at + 1) * share]


def unpack_parts_kernel(ways, info, *refs):
    blocks, outs = refs[:ways], refs[ways:]
    share = blocks[0].shape[2]
    for by in range(ways):
        for at in range(ways):

            @pl.when((info[0] ^ by) == at)
            def _():
                for slot, rows in enumerate(outs):
                    rows[:, at * share : (at + 1) * share] = blocks[by][slot]


def selector(columns, slim, position, width):
    wanted = columns + position * slim
    rows = lax.broadcasted_iota(jnp.int32, (width, columns.shape[1]), 0)
    return jnp.where(rows == wanted, 1.0, 0.0).astype(jnp.bfloat16)


def mask_kernel(info, grad_out, point_weight, masked, grad_act):
    frames, width = grad_out.shape
    valid = valid_of(info[0] * frames, frames, info[1])
    masked[...] = jnp.where(valid, grad_out[...].astype(jnp.float32), 0.0).astype(jnp.bfloat16)
    step = width // 3
    for at in range(0, width, step):
        grad_act[:, at : at + step] = dot(masked[...], point_weight[at : at + step, :], NT)


def mask_edges_kernel(frames, info, before, after, point_weight, grad_act):
    width = grad_act.shape[1]
    first = info[0] * frames
    sides = []
    for side, start in ((before, first - EDGE), (after, first + frames)):
        valid = valid_of(start, EDGE, info[1])
        rows = side[2 * EDGE :, :].astype(jnp.float32)
        sides.append(jnp.where(valid, rows, 0.0).astype(jnp.bfloat16))
    masked = jnp.concatenate(sides, axis=0)
    step = width // 3
    for at in range(0, width, step):
        grad_act[:, at : at + step] = dot(masked, point_weight[at : at + step, :], NT)


def gather_heads(info, blocks, query, key, value, bias):
    frames = blocks[0].shape[1]
    for by, block in enumerate(blocks):
        rows = slice(by * frames, (by + 1) * frames)
        query[rows] = block[0] * jnp.bfloat16(SCALE)
        key[rows] = block[1]
        value[rows] = block[2]
        valid = valid_of((info[0] ^ by) * frames, frames, info[1])
        bias[rows] = jnp.broadcast_to(jnp.where(valid, 0.0, NEG_FILL), (frames, LANES))


def attend_kernel(ways, info, *refs):
    blocks, outs = refs[:ways], refs[ways : 2 * ways]
    attended, log_total, query, key, value, bias, turned = refs[2 * ways :]
    gather_heads(info, blocks, query, key, value, bias)
    total_frames, share = query.shape
    frames = total_frames // ways
    for head in range(share // HEAD_DIM):
        part = slice(head * HEAD_DIM, (head + 1) * HEAD_DIM)
        spread = jnp.concatenate([bias[...]] * (total_frames // LANES), axis=1)
        scores = dot(key[:, part], query[:, part], NT) + spread
        row_max = jnp.max(scores, axis=0, keepdims=True)
        weights = jnp.exp(scores - row_max)
        total = jnp.sum(weights, axis=0, keepdims=True)
        turned[part, :] = dot(value[:, part], weights.astype(jnp.bfloat16), TN) / total
        log_total[head : head + 1, :] = row_max + jnp.log(total)
    attended[...] = turned[...].T.astype(jnp.bfloat16)
    reach = 2 * EDGE
    for by in range(ways):
        other = info[0] ^ by
        before = (info[0] ^ jnp.maximum(other - 1, 0)) * frames + frames - reach
        after = (info[0] ^ jnp.minimum(other + 1, ways - 1)) * frames
        outs[by][:reach] = attended[pl.ds(pl.multiple_of(before, reach), reach), :]
        outs[by][reach : reach + frames] = attended[by * frames : (by + 1) * frames, :]
        outs[by][reach + frames :] = attended[pl.ds(pl.multiple_of(after, reach), reach), :]


def attend_back_kernel(ways, info, *refs):
    blocks, messages = refs[:ways], refs[ways : 2 * ways]
    attended, log_total = refs[2 * ways : 2 * ways + 2]
    outs = refs[2 * ways + 2 : 3 * ways + 2]
    query, key, value, bias, grad, turned = refs[3 * ways + 2 :]
    gather_heads(info, blocks, query, key, value, bias)
    total_frames, share = query.shape
    frames = total_frames // ways
    for by in range(ways):
        grad[by * frames : (by + 1) * frames] = messages[by][:frames, :]
    turned[...] = (grad[...].astype(jnp.float32) * attended[...].astype(jnp.float32)).T
    for head in range(share // HEAD_DIM):
        part = slice(head * HEAD_DIM, (head + 1) * HEAD_DIM)
        delta = jnp.sum(turned[part, :], axis=0, keepdims=True)
        spread = jnp.concatenate([bias[...]] * (total_frames // LANES), axis=1)
        scores = dot(key[:, part], query[:, part], NT) + spread
        probs = jnp.exp(scores - log_total[head : head + 1, :])
        value_grad = dot(probs.astype(jnp.bfloat16), grad[:, part])
        prob_grad = dot(value[:, part], grad[:, part], NT)
        score_grad = (probs * (prob_grad - delta)).astype(jnp.bfloat16)
        key_grad = dot(score_grad, query[:, part])
        turned[part, :] = dot(key[:, part], score_grad, TN) * SCALE
        for by in range(ways):
            rows = slice(by * frames, (by + 1) * frames)
            outs[by][1, :, part] = key_grad[rows].astype(jnp.bfloat16)
            outs[by][2, :, part] = value_grad[rows].astype(jnp.bfloat16)
    query_grad = turned[...].T.astype(jnp.bfloat16)
    for by in range(ways):
        outs[by][0] = query_grad[by * frames : (by + 1) * frames]


def project_kernel(ways, info, *refs):
    blocks = refs[:ways]
    residual, before, after, out_weight, params = refs[ways : ways + 5]
    mixed, conv_in = refs[ways + 5 : ways + 7]
    messages, attended = refs[ways + 7 : -1], refs[-1]
    frames, width = residual.shape
    share = width // ways
    reach = 2 * EDGE
    rows = frames + 2 * reach
    for by in range(ways):
        for at in range(ways):

            @pl.when((info[0] ^ by) == at)
            def _():
                attended[:, at * share : (at + 1) * share] = blocks[by][...]

    step = width // 3
    for at in range(0, width, step):
        part = slice(at, at + step)
        mixed[:reach, part] = before[:reach, part].astype(jnp.float32)
        mixed[reach : reach + frames, part] = residual[:, part].astype(jnp.float32)
        mixed[reach + frames :, part] = after[:reach, part].astype(jnp.float32)
        mixed[:, part] += dot(attended[...], out_weight[:, part])

    gain = params[31:32, :]
    first = info[0] * frames - reach

    def band(index, carry):
        at = pl.ds(pl.multiple_of(index * BAND, BAND), BAND)
        normed, _ = moments(mixed[at, :])
        position = first + index * BAND + lax.broadcasted_iota(jnp.int32, (BAND, 1), 0)
        valid = (position >= 0) & (position < info[1])
        conv_in[at, :] = jnp.where(valid, normed * gain, 0.0).astype(jnp.bfloat16)
        return carry

    lax.fori_loop(0, rows // BAND, band, 0)
    for by, message in enumerate(messages):
        lacking = [slot for slot in range(ways) if slot != by]
        for at, slot in enumerate(lacking):
            message[:, at * share : (at + 1) * share] = blocks[slot][reach : reach + frames, :]


def stride_of(rows):
    return rows // 8 + 1


def in_columns(ref, rows):
    for at in range(ref.shape[0]):
        ref[at, : rows.shape[0]] = rows[:, at * LANES : (at + 1) * LANES].astype(jnp.float32)


def from_columns(ref, rows):
    return jnp.concatenate([ref[at, rows, :] for at in range(ref.shape[0])], axis=1)


def strided(ref, index, start, stride):
    return ref[index, pl.ds(start, 8, stride=stride), :]


def depthwise(padded, taps, tap_of, out, rows):
    stride = stride_of(rows)

    def column(index, carry):
        part = pl.ds(pl.multiple_of(index * LANES, LANES), LANES)
        cells = [strided(padded, index, at + 1, stride) for at in range(stride + 2 * EDGE - 2)]
        total = [None] * stride
        for offset in range(1, 2 * EDGE):
            tap = tap_of(offset)
            scale = jnp.broadcast_to(taps[tap : tap + 1, part], (8, LANES))
            for at in range(stride):
                term = cells[at + offset - 1] * scale
                total[at] = term if total[at] is None else total[at] + term
        for at in range(stride):
            out[index, pl.ds(at, 8, stride=stride), :] = total[at]
        return carry

    lax.fori_loop(0, out.shape[0], column, 0)


def tap_grads(padded, grad, start, rows, taps):
    stride = rows // 8

    def column(index, carry):
        part = pl.ds(pl.multiple_of(index * LANES, LANES), LANES)
        cells = [
            strided(padded, index, start + at + 1, stride) for at in range(stride + 2 * EDGE - 2)
        ]
        grads = [strided(grad, index, start + at, stride) for at in range(stride)]
        for tap in range(2 * EDGE - 1):
            total = cells[tap] * grads[0]
            for at in range(1, stride):
                total = total + cells[at + tap] * grads[at]
            taps[tap : tap + 1, part] = jnp.sum(total, axis=0, keepdims=True)
        return carry

    lax.fori_loop(0, grad.shape[0], column, 0)


def conv_kernel_body(info, conv_in, params, grad_own, grad_edges, masked, *refs):
    conv_act, grad_conv, sums, messages, padded, conv, grad_act, bias_sum, gain_sum = refs
    frames, width = grad_own.shape
    rows, wide = frames + 2 * EDGE, frames + 4 * EDGE
    in_columns(padded, conv_in[...])
    padded[:, wide:, :] = jnp.zeros((width // LANES, padded.shape[1] - wide, LANES), jnp.float32)
    grad_act[:EDGE] = grad_edges[:EDGE]
    grad_act[EDGE : EDGE + frames] = grad_own[...]
    grad_act[EDGE + frames :] = grad_edges[EDGE:]
    depthwise(padded, params, lambda offset: offset - 1, conv, rows)
    bias, gain = params[32:33, :], params[33:34, :]
    bias_sum[...] = jnp.zeros_like(bias_sum)
    gain_sum[...] = jnp.zeros_like(gain_sum)

    def band(index, carry):
        at = pl.ds(pl.multiple_of(index * BAND, BAND), BAND)
        normed, inv_scale = moments(from_columns(conv, at) + bias)
        scaled = normed * gain
        gate = 0.5 + 0.5 * jnp.tanh(0.5 * scaled)
        conv_act[at, :] = (scaled * gate).astype(jnp.bfloat16)
        grad_scaled = grad_act[at, :] * gate * (1.0 + scaled * (1.0 - gate))
        grad_rows = norm_back(grad_scaled * gain, normed, inv_scale)
        for column in range(width // LANES):
            grad_conv[column, at, :] = grad_rows[:, column * LANES : (column + 1) * LANES]

        @pl.when((index >= EDGE // BAND) & (index < (EDGE + frames) // BAND))
        def _():
            bias_sum[...] += fold(grad_rows)
            gain_sum[...] += fold(grad_scaled * normed)

        return carry

    lax.fori_loop(0, rows // BAND, band, 0)
    sums[0:1, :] = jnp.sum(bias_sum[...], axis=0, keepdims=True)
    sums[1:2, :] = jnp.sum(gain_sum[...], axis=0, keepdims=True)
    half, quarter = width // 2, width // 4
    for layer in range(4):
        high, low = layer // 2, layer % 2
        messages[layer, :, :half] = conv_act[EDGE : EDGE + frames, high * half : (high + 1) * half]
        for at in range(2):
            start = (2 * at + low) * quarter
            lanes = slice(half + at * quarter, half + (at + 1) * quarter)
            messages[layer, :, lanes] = masked[:, start : start + quarter]


def block_out_kernel(info, conv_act, mixed, point_weight, block_out):
    frames, width = block_out.shape
    step = width // 3
    for at in range(0, width, step):
        part = slice(at, at + step)
        block_out[:, part] = (
            mixed[2 * EDGE : 2 * EDGE + frames, part]
            + dot(conv_act[EDGE : EDGE + frames, :], point_weight[:, part])
        ).astype(jnp.bfloat16)


def conv_back_kernel(ways, slim, info, grad_conv, conv_in, params, masked, mixed, out_weight, *refs):
    conv_sums, columns, grad_residual = refs[:3]
    messages = refs[3 : 3 + ways]
    padded, padded_in, conv, gain_sum, taps, packed = refs[3 + ways :]
    frames, width = grad_residual.shape
    share = width // ways
    reached = frames + 2 * EDGE
    padded[:, :reached, :] = grad_conv[...].astype(jnp.bfloat16).astype(jnp.float32)
    padded[:, reached:, :] = jnp.zeros(
        (width // LANES, padded.shape[1] - reached, LANES), jnp.float32
    )
    depthwise(padded, params, lambda offset: 31 - offset, conv, frames)
    gain = params[31:32, :]
    gain_sum[...] = jnp.zeros_like(gain_sum)

    def band(index, carry):
        at = pl.ds(pl.multiple_of(index * BAND, BAND), BAND)
        own_mixed = pl.ds(pl.multiple_of(index * BAND + 2 * EDGE, BAND), BAND)
        valid = valid_of(info[0] * frames + index * BAND, BAND, info[1])
        grad_in = jnp.where(valid, from_columns(conv, at), 0.0)
        normed, inv_scale = moments(mixed[own_mixed, :])
        grad_mixed = norm_back(grad_in * gain, normed, inv_scale)
        gain_sum[...] += fold(grad_in * normed)
        grad_residual[at, :] = (masked[at, :].astype(jnp.float32) + grad_mixed).astype(
            jnp.bfloat16
        )
        return carry

    lax.fori_loop(0, frames // BAND, band, 0)
    for by in range(ways):
        at = pl.ds(pl.multiple_of((info[0] ^ by) * share, share), share)
        messages[by][:frames] = dot(grad_residual[...], out_weight[at, :], NT).astype(jnp.bfloat16)

    in_columns(padded_in, conv_in[...])
    tap_grads(padded_in, grad_conv, EDGE, frames, taps)
    taps[31:32, :] = conv_sums[0:1, :]
    taps[32:33, :] = jnp.sum(gain_sum[...], axis=0, keepdims=True)
    taps[33:34, :] = conv_sums[1:2, :]
    taps[34:, :] = jnp.zeros((EXTRA - 34, width), jnp.float32)
    packed[:frames] = grad_residual[...]
    packed[frames:] = taps[...].astype(jnp.bfloat16)
    for by in range(ways):
        chosen = selector(columns[...], slim, info[0] ^ by, width)
        messages[by][frames:] = dot(packed[...], chosen).astype(jnp.bfloat16)


def split_rows(info, parts, terms, sent, kept):
    rows = terms.shape[0] // parts
    for bit in range(2):

        @pl.when(info[2] % 2 == bit)
        def _():
            for at in range(parts // 2):
                own = (2 * at + bit) * rows
                other = (2 * at + 1 - bit) * rows
                kept[at] = terms[own : own + rows, :]
                sent[at] = terms[other : other + rows, :].astype(jnp.bfloat16)


def point_kernel(shift, info, messages, sent, kept, terms):
    half = terms.shape[1]
    left = jnp.concatenate([messages[layer, :, half:] for layer in range(4)], axis=0)
    right = jnp.concatenate([messages[layer, :, :half] for layer in range(4)], axis=0)
    step = half // 2
    for at in range(0, 2 * step, step):
        part = slice(at, at + step)
        terms[:, part] = dot(left, right[:, part], TN)
    pieces, slim = kept.shape[0], kept.shape[1] // 2
    for bit in range(2):

        @pl.when(((info[2] >> shift) & 1) == bit)
        def _():
            for at in range(pieces):
                for side in range(2):
                    base = side * 2 * pieces * slim
                    own = base + (bit * pieces + at) * slim
                    other = base + ((1 - bit) * pieces + at) * slim
                    rows = slice(side * slim, (side + 1) * slim)
                    kept[at, rows, :] = terms[own : own + slim, :]
                    sent[at, rows, :] = terms[other : other + slim, :].astype(jnp.bfloat16)


def point_sum_kernel(shift, info, kept, received, own, other):
    rows = own.shape[0]
    total = kept[0] + received[0].astype(jnp.float32)
    for at in range(2):

        @pl.when(((info[2] >> shift) & 1) == at)
        def _():
            own[...] = total[at * rows : (at + 1) * rows, :]
            other[...] = total[(1 - at) * rows : (2 - at) * rows, :].astype(jnp.bfloat16)


def weight_kernel(ways, parts, info, *refs):
    grads, rows = refs[:ways], refs[ways : 2 * ways]
    attended, sent, kept, terms = refs[2 * ways :]
    total_frames, share = attended.shape
    frames = total_frames // ways
    width = ways * share
    slim = share // parts
    left = jnp.concatenate([grad[frames : 2 * frames, :] for grad in grads], axis=0)
    for slot in range(ways):
        if slot == 0:
            right = attended[...]
        else:
            pieces = []
            for by in range(ways):
                at = (by ^ slot) - (1 if (by ^ slot) > by else 0)
                pieces.append(rows[by][:, at * share : (at + 1) * share])
            right = jnp.concatenate(pieces, axis=0)
        terms[:, slot * share : (slot + 1) * share] = dot(left, right, TN)
    small = jnp.zeros((EXTRA, share), jnp.float32)
    for grad in grads:
        small = small + grad[2 * frames :, :].astype(jnp.float32)
    filler = jnp.zeros((LANES - EXTRA, share), jnp.float32)
    terms[:, width:] = jnp.concatenate([small, filler], axis=0).T
    split_rows(info, parts, terms, sent, kept)


def halve_kernel(axis, shift, alternate, info, kept, received, sent, still_kept):
    bit = (info[axis] >> shift) & 1
    count = sent.shape[0]
    for at in range(count):
        if alternate:
            own, other = 2 * at + bit, 2 * at + 1 - bit
        else:
            own, other = bit * count + at, (1 - bit) * count + at
        still_kept[at] = kept[own] + received[own].astype(jnp.float32)
        sent[at] = (kept[other] + received[other].astype(jnp.float32)).astype(jnp.bfloat16)


def finish_kernel(ways, shift, info, kept, received, own, other, weight, taps, vectors, point):
    width = weight.shape[1]
    share, half = width // ways, width // 2
    for at in range(2):

        @pl.when(((info[2] >> shift) & 1) == at)
        def _():
            point[:, at * half : (at + 1) * half] = own[...]
            point[:, (1 - at) * half : (2 - at) * half] = other[...].astype(jnp.float32)

    total = kept[0] + received[0].astype(jnp.float32)
    for by in range(ways):
        for at in range(ways):

            @pl.when((info[0] ^ by) == at)
            def _():
                weight[:, at * share : (at + 1) * share] = total[:, by * share : (by + 1) * share]

    small = total[:, width:].T
    taps[...] = small[:31]
    vectors[...] = small[31:34]


def swap(block, axis, by):
    return lax.ppermute(block, axis, [(i, i ^ by) for i in range(lax.axis_size(axis))])


def swap_all(blocks, axis, step=1):
    return [blocks[0]] + [swap(block, axis, step * by) for by, block in enumerate(blocks[1:], 1)]


def edges(head, tail):
    count = lax.axis_size("ctx")
    steps = [(i, i + 1) for i in range(count - 1)]
    before = lax.ppermute(tail, "ctx", steps)
    after = lax.ppermute(head, "ctx", [(j, i) for i, j in steps])
    return before, after


def local(
    residual_in,
    query_rows,
    key_rows,
    value_rows,
    lengths,
    out_weight,
    norm_gain,
    conv_kernel,
    conv_bias,
    conv_gain,
    point_weight,
    grad_out,
):
    ways = lax.axis_size("ctx")
    parts = lax.axis_size("dp")
    own = lax.axis_index("ctx")
    place = lax.axis_index("dp")
    frames, width = residual_in.shape[1:]
    share = width // ways
    slim = share // parts
    heads = HEADS // ways
    every = ways * frames
    lower = parts // 4
    half = width // 2
    tiles = width // LANES
    bf16, f32 = jnp.bfloat16, jnp.float32
    square = 2 * frames * width * width
    rows_bytes = 2 * frames * width
    reached, wide = frames + 2 * EDGE, frames + 4 * EDGE

    info = jnp.stack([own, lengths[0], place]).astype(jnp.int32)
    params = jnp.concatenate(
        [conv_kernel, norm_gain[None], conv_bias[None], conv_gain[None]], axis=0
    )

    at = jnp.arange(share, dtype=jnp.int32)
    columns = ((at // slim) * (ways * slim) + at % slim)[None]

    by_tiles = share % LANES == 0
    packed = call(
        functools.partial(pack_kernel if by_tiles else pack_parts_kernel, ways),
        "pack",
        [((3, frames, share), bf16)] * ways,
        scratch=[((3, frames, width), bf16)] if by_tiles else (),
        semaphores=3 if by_tiles else 0,
        far=("in",) if by_tiles else (),
        megabytes=58,
        moved=6 * rows_bytes,
    )(info, query_rows[0], key_rows[0], value_rows[0])
    residual, grad = residual_in[0], grad_out[0]
    packed, residual, grad = lax.optimization_barrier((packed, residual, grad))
    packed = swap_all(packed, "ctx")
    before, after = edges(
        jnp.concatenate([residual[: 2 * EDGE], grad[:EDGE]], axis=0),
        jnp.concatenate([residual[frames - 2 * EDGE :], grad[frames - EDGE :]], axis=0),
    )
    masked, grad_own = call(
        mask_kernel,
        "mask",
        [((frames, width), bf16), ((frames, width), f32)],
        flops=square,
        moved=6 * rows_bytes + 2 * width * width,
    )(info, grad, point_weight)

    packed, masked = lax.optimization_barrier((packed, masked))
    head_scratch = [((every, share), bf16)] * 3 + [((every, LANES), f32)]
    pair_flops = 2 * heads * every * every * HEAD_DIM
    *returned, attended, log_total = call(
        functools.partial(attend_kernel, ways),
        "attend",
        [((wide, share), bf16)] * ways + [((every, share), bf16), ((heads, every), f32)],
        scratch=head_scratch + [((share, every), f32)],
        flops=8 * pair_flops,
        moved=4 * rows_bytes,
        exps=heads * every * every,
    )(info, *packed)
    returned = swap_all(returned, "ctx")
    grad_edges = call(
        functools.partial(mask_edges_kernel, frames),
        "mask_edges",
        [((2 * EDGE, width), f32)],
        flops=square,
        moved=2 * width * width,
    )(info, before, after, point_weight)[0]
    returned, grad_edges = lax.optimization_barrier((returned, grad_edges))

    mixed, conv_in, *messages = call(
        functools.partial(project_kernel, ways),
        "project",
        [((wide, width), f32), ((wide, width), bf16)] + [((frames, width - share), bf16)] * ways,
        scratch=[((wide, width), bf16)],
        flops=square,
        moved=6 * rows_bytes + 2 * width * width,
    )(info, *returned, residual, before, after, out_weight, params)
    messages = swap_all(messages, "ctx")

    spread = 8 * stride_of(reached)
    conv_act, grad_conv, conv_sums, point_messages = call(
        conv_kernel_body,
        "conv",
        [
            ((reached, width), bf16),
            ((tiles, reached, LANES), f32),
            ((2, width), f32),
            ((4, frames, width), bf16),
        ],
        scratch=[
            ((tiles, spread + 2 * EDGE, LANES), f32),
            ((tiles, spread, LANES), f32),
            ((reached, width), f32),
            ((8, width), f32),
            ((8, width), f32),
        ],
        flops=frames * width * 4000,
        moved=6 * rows_bytes,
        exps=frames * width,
    )(info, conv_in, params, grad_own, grad_edges, masked)
    layers = [[layer * lower + at for layer in range(4)] for at in range(lower)]
    point_messages = lax.all_to_all(point_messages, "dp", 0, 0, axis_index_groups=layers)

    spread = 8 * stride_of(frames)
    grad_residual, *grad_messages = call(
        functools.partial(conv_back_kernel, ways, slim),
        "conv_back",
        [((frames, width), bf16)] + [((2 * frames + EXTRA, share), bf16)] * ways,
        scratch=[
            ((tiles, spread + 2 * EDGE, LANES), f32),
            ((tiles, wide, LANES), f32),
            ((tiles, spread, LANES), f32),
            ((8, width), f32),
            ((EXTRA, width), f32),
            ((frames + EXTRA, width), bf16),
        ],
        flops=frames * width * 8000,
        moved=8 * rows_bytes + 2 * width * width,
    )(
        info,
        grad_conv,
        conv_in,
        params,
        masked,
        mixed,
        out_weight,
        conv_sums,
        columns,
    )
    messages, grad_messages = lax.optimization_barrier((messages, grad_messages))
    grad_messages = swap_all(grad_messages, "ctx")

    block_out = call(
        block_out_kernel,
        "block_out",
        [((frames, width), bf16)],
        flops=square,
        moved=4 * rows_bytes + 2 * width * width,
    )(info, conv_act, mixed, point_weight)[0]

    def halve(kept, received, bit, alternate):
        axis, shift = bit
        extent = (kept.shape[0] // 2,) + kept.shape[1:]
        return call(
            functools.partial(halve_kernel, 0 if axis == "ctx" else 2, shift, alternate),
            "halve",
            [(extent, bf16), (extent, f32)],
            moved=16 * extent[0] * extent[1] * extent[2],
        )(info, kept, received)

    def reduce(sent, kept, bits, alternate):
        received = swap(sent, bits[0][0], 2 ** bits[0][1])
        for axis, shift in bits[1:]:
            sent, kept = halve(kept, received, (axis, shift), alternate)
            received = swap(sent, axis, 2**shift)
        return kept, received

    def falling(axis, count):
        return [(axis, shift) for shift in reversed(range(count.bit_length() - 1))]

    point_bits = falling("dp", lower) + falling("ctx", ways)
    point_half = (lower * ways // 2, 2 * slim, half)
    point_sent, point_kept = call(
        functools.partial(point_kernel, point_bits[0][1]),
        "point_terms",
        [(point_half, bf16), (point_half, f32)],
        scratch=[((half, half), f32)],
        flops=square,
        moved=8 * rows_bytes,
    )(info, point_messages)
    point_received = swap(point_sent, point_bits[0][0], 2 ** point_bits[0][1])
    point_sent, point_kept = halve(point_kept, point_received, point_bits[1], False)
    grad_messages, point_sent, block_out = lax.optimization_barrier(
        (grad_messages, point_sent, block_out)
    )
    layer_bit = (parts // 2).bit_length() - 1
    point_own, point_other = call(
        functools.partial(point_sum_kernel, layer_bit),
        "point_sum",
        [((slim, half), f32), ((slim, half), bf16)],
        moved=slim * width * (parts + 8),
    )(info, *reduce(point_sent, point_kept, point_bits[1:], False))
    point_other = swap(point_other, "dp", parts // 2)

    extent = width + LANES
    core_half = (parts // 2, slim, extent)
    sent, kept = call(
        functools.partial(weight_kernel, ways, parts),
        "out_terms",
        [(core_half, bf16), (core_half, f32)],
        scratch=[((share, extent), f32)],
        flops=square,
        moved=10 * rows_bytes,
    )(info, *grad_messages, *messages, attended)
    pieces = reduce(sent, kept, falling("dp", parts)[::-1], True)
    out_total, taps, vectors, point_total = call(
        functools.partial(finish_kernel, ways, layer_bit),
        "finish",
        [((slim, width), f32), ((31, slim), f32), ((3, slim), f32), ((slim, width), f32)],
        moved=slim * extent * (parts + 8),
    )(info, *pieces, point_own, point_other)

    grad_packed = call(
        functools.partial(attend_back_kernel, ways),
        "attend_back",
        [((3, frames, share), bf16)] * ways,
        scratch=head_scratch + [((every, share), bf16), ((share, every), f32)],
        flops=20 * pair_flops,
        moved=8 * rows_bytes,
        exps=heads * every * every,
    )(info, *packed, *grad_messages, attended, log_total)
    grad_packed = swap_all(grad_packed, "ctx")
    grad_query, grad_key, grad_value = call(
        functools.partial(unpack_kernel if by_tiles else unpack_parts_kernel, ways),
        "unpack",
        [((frames, width), bf16)] * 3,
        semaphores=3 * ways if by_tiles else 0,
        far=("out",) if by_tiles else (),
        moved=6 * rows_bytes,
    )(info, *grad_packed)

    return (
        block_out[None],
        grad_residual[None],
        grad_query[None],
        grad_key[None],
        grad_value[None],
        out_total.T,
        point_total.T,
        taps,
        vectors,
    )


def solution(mesh):
    rows = P("dp", "ctx", None)
    columns = P(None, ("dp", "ctx"))
    in_specs = (rows, rows, rows, rows, P("dp"), P(), P(), P(), P(), P(), P(), rows)
    out_specs = (rows,) * 5 + (columns,) * 4
    return jax.shard_map(local, mesh=mesh, in_specs=in_specs, out_specs=out_specs, check_vma=False)
```

```python
import functools

import jax
import jax.numpy as jnp
from jax import lax
from jax.experimental import pallas as pl
from jax.experimental.pallas import tpu as pltpu
from jax.sharding import PartitionSpec as P

HEADS = 24
HEAD_DIM = 64
SCALE = HEAD_DIM ** (-0.5)

NEG_FILL = -1e30
EPSILON = 1e-05

LANES = 128
EDGE = 16
BAND = 16
EXTRA = 48

NN = (((1,), (0,)), ((), ()))
NT = (((1,), (1,)), ((), ()))
TN = (((0,), (0,)), ((), ()))


def dot(left, right, dims=NN):
    return lax.dot_general(left, right, dims, preferred_element_type=jnp.float32)


def call(
    kernel, name, outs, scratch=(), semaphores=0, far=(), megabytes=28, flops=0, moved=0, exps=0
):
    vmem = pl.BlockSpec(memory_space=pltpu.VMEM)
    smem = pl.BlockSpec(memory_space=pltpu.SMEM)
    anywhere = pl.BlockSpec(memory_space=pl.ANY)

    def run(info, *arrays):
        scratches = [pltpu.VMEM(shape, kind) for shape, kind in scratch]
        if semaphores:
            scratches.append(pltpu.SemaphoreType.DMA((semaphores,)))
        return pl.pallas_call(
            kernel,
            name=name,
            in_specs=[smem] + [anywhere if "in" in far else vmem] * len(arrays),
            out_specs=[anywhere if "out" in far else vmem] * len(outs),
            out_shape=[jax.ShapeDtypeStruct(shape, kind) for shape, kind in outs],
            scratch_shapes=scratches,
            compiler_params=pltpu.CompilerParams(vmem_limit_bytes=megabytes << 20),
            cost_estimate=pl.CostEstimate(flops=flops, bytes_accessed=moved, transcendentals=exps),
        )(info, *arrays)

    return run


def valid_of(first, rows, length):
    return first + lax.broadcasted_iota(jnp.int32, (rows, 1), 0) < length


def moments(rows):
    centre = jnp.mean(rows, axis=-1, keepdims=True)
    centred = rows - centre
    inv_scale = lax.rsqrt(jnp.mean(centred * centred, axis=-1, keepdims=True) + EPSILON)
    return centred * inv_scale, inv_scale


def norm_back(grad_normed, normed, inv_scale):
    first_mean = jnp.mean(grad_normed, axis=-1, keepdims=True)
    second_mean = jnp.mean(grad_normed * normed, axis=-1, keepdims=True)
    return inv_scale * (grad_normed - first_mean - normed * second_mean)


def fold(rows):
    total = rows[:8]
    for at in range(8, rows.shape[0], 8):
        total = total + rows[at : at + 8]
    return total


def at_group(info, by, ways, share, visit):
    if share % LANES == 0:
        visit(pl.ds(pl.multiple_of((info[0] ^ by) * share, LANES), share))
        return
    for at in range(ways):

        @pl.when((info[0] ^ by) == at)
        def _():
            visit(slice(at * share, (at + 1) * share))


def neighbours(ways):
    return [by for by in (1, 3, 7, 15) if by < ways]


def pack_kernel(ways, info, query, key, value, residual, grad_out, *refs):
    blocks, whole, ends, arrived = refs[:ways], refs[ways], refs[ways + 1], refs[ways + 2]
    frames, width = query.shape
    share, reach = width // ways, 2 * EDGE
    pairs = [(rows, whole.at[slot]) for slot, rows in enumerate((query, key, value))]
    for side, tail in enumerate((False, True)):
        for rows, start, count in ((residual, 0, reach), (grad_out, reach, EDGE)):
            first = frames - count if tail else 0
            pairs.append(
                (rows.at[pl.ds(first, count)], ends.at[side, pl.ds(start, count)])
            )
    copies = [
        pltpu.make_async_copy(source, target, arrived.at[at])
        for at, (source, target) in enumerate(pairs)
    ]
    for copy in copies:
        copy.start()
    for copy in copies[3:]:
        copy.wait()
    for by in neighbours(ways):
        side = jnp.where((info[0] ^ by) > info[0], 1, 0)
        for at in range(ways):
            rows = slice(3 * frames + at * 3 * EDGE, 3 * frames + (at + 1) * 3 * EDGE)
            blocks[by][rows, :] = ends[side, :, at * share : (at + 1) * share]
    for slot, copy in enumerate(copies[:3]):
        copy.wait()
        for by in range(ways):

            def visit(lanes):
                blocks[by][slot * frames : (slot + 1) * frames, :] = whole[slot, :, lanes]

            at_group(info, by, ways, share, visit)


def unpack_kernel(ways, info, *refs):
    blocks, outs, arrived = refs[:ways], refs[ways:-1], refs[-1]
    share = blocks[0].shape[2]
    copies = []
    for by in range(ways):
        for slot, rows in enumerate(outs):
            lanes = pl.ds(pl.multiple_of((info[0] ^ by) * share, LANES), share)
            copy = pltpu.make_async_copy(
                blocks[by].at[slot], rows.at[:, lanes], arrived.at[len(copies)]
            )
            copy.start()
            copies.append(copy)
    for copy in copies:
        copy.wait()


def unpack_parts_kernel(ways, info, *refs):
    blocks, outs = refs[:ways], refs[ways:]
    share = blocks[0].shape[2]
    for by in range(ways):
        for slot, rows in enumerate(outs):

            def visit(lanes):
                rows[:, lanes] = blocks[by][slot]

            at_group(info, by, ways, share, visit)


def selector(columns, slim, position, width):
    wanted = columns + position * slim
    rows = lax.broadcasted_iota(jnp.int32, (width, columns.shape[1]), 0)
    return jnp.where(rows == wanted, 1.0, 0.0).astype(jnp.bfloat16)


def mask_kernel(slim, info, grad_out, point_weight, columns, masked, grad_act, *halves):
    frames, width = grad_out.shape
    valid = valid_of(info[0] * frames, frames, info[1])
    masked[...] = jnp.where(valid, grad_out[...].astype(jnp.float32), 0.0).astype(jnp.bfloat16)
    step = width // 3
    for at in range(0, width, step):
        grad_act[:, at : at + step] = dot(masked[...], point_weight[at : at + step, :], NT)
    across = len(halves)
    for by in range(across):
        chosen = selector(columns[...], slim, (info[0] % across) ^ by, width)
        halves[by][...] = dot(masked[...], chosen).astype(jnp.bfloat16)


def select_kernel(slim, info, columns, *outs):
    for by, out in enumerate(outs):
        out[...] = selector(columns[...], slim, info[0] ^ by, out.shape[0])


def mask_edges_kernel(frames, info, before, after, point_weight, grad_act):
    width = grad_act.shape[1]
    first = info[0] * frames
    sides = []
    for side, start in ((before, first - EDGE), (after, first + frames)):
        valid = valid_of(start, EDGE, info[1])
        rows = side[2 * EDGE :, :].astype(jnp.float32)
        sides.append(jnp.where(valid, rows, 0.0).astype(jnp.bfloat16))
    masked = jnp.concatenate(sides, axis=0)
    step = width // 3
    for at in range(0, width, step):
        grad_act[:, at : at + step] = dot(masked, point_weight[at : at + step, :], NT)


def gather_heads(info, blocks, query, key, value, bias):
    frames = query.shape[0] // len(blocks)
    for by, block in enumerate(blocks):
        rows = slice(by * frames, (by + 1) * frames)
        query[rows] = block[:frames, :] * jnp.bfloat16(SCALE)
        key[rows] = block[frames : 2 * frames, :]
        value[rows] = block[2 * frames : 3 * frames, :]
        valid = valid_of((info[0] ^ by) * frames, frames, info[1])
        bias[rows] = jnp.broadcast_to(jnp.where(valid, 0.0, NEG_FILL), (frames, LANES))


def attend_kernel(ways, info, *refs):
    blocks, outs = refs[:ways], refs[ways : 2 * ways]
    attended, log_total, before, after, query, key, value, bias, turned = refs[2 * ways :]
    gather_heads(info, blocks, query, key, value, bias)
    total_frames, share = query.shape
    frames = total_frames // ways
    for side, other in ((before, info[0] - 1), (after, info[0] + 1)):
        side[...] = jnp.zeros_like(side)
        for by in neighbours(ways):

            @pl.when((info[0] ^ other) == by)
            def _():
                for at in range(ways):
                    rows = slice(3 * frames + at * 3 * EDGE, 3 * frames + (at + 1) * 3 * EDGE)
                    side[:, at * share : (at + 1) * share] = blocks[by][rows, :]

    for head in range(share // HEAD_DIM):
        part = slice(head * HEAD_DIM, (head + 1) * HEAD_DIM)
        spread = jnp.concatenate([bias[...]] * (total_frames // LANES), axis=1)
        scores = dot(key[:, part], query[:, part], NT) + spread
        row_max = jnp.max(scores, axis=0, keepdims=True)
        weights = jnp.exp(scores - row_max)
        total = jnp.sum(weights, axis=0, keepdims=True)
        turned[part, :] = dot(value[:, part], weights.astype(jnp.bfloat16), TN) / total
        log_total[head : head + 1, :] = row_max + jnp.log(total)
    attended[...] = turned[...].T.astype(jnp.bfloat16)
    reach = 2 * EDGE
    for by in range(ways):
        other = info[0] ^ by
        before = (info[0] ^ jnp.maximum(other - 1, 0)) * frames + frames - reach
        after = (info[0] ^ jnp.minimum(other + 1, ways - 1)) * frames
        outs[by][:reach] = attended[pl.ds(pl.multiple_of(before, reach), reach), :]
        outs[by][reach : reach + frames] = attended[by * frames : (by + 1) * frames, :]
        outs[by][reach + frames :] = attended[pl.ds(pl.multiple_of(after, reach), reach), :]


def attend_back_kernel(ways, info, *refs):
    blocks, messages = refs[:ways], refs[ways : 2 * ways]
    attended, log_total = refs[2 * ways : 2 * ways + 2]
    outs = refs[2 * ways + 2 : 3 * ways + 2]
    query, key, value, bias, grad, turned = refs[3 * ways + 2 :]
    gather_heads(info, blocks, query, key, value, bias)
    total_frames, share = query.shape
    frames = total_frames // ways
    for by in range(ways):
        grad[by * frames : (by + 1) * frames] = messages[by][:frames, :]
    turned[...] = (grad[...].astype(jnp.float32) * attended[...].astype(jnp.float32)).T
    for head in range(share // HEAD_DIM):
        part = slice(head * HEAD_DIM, (head + 1) * HEAD_DIM)
        delta = jnp.sum(turned[part, :], axis=0, keepdims=True)
        spread = jnp.concatenate([bias[...]] * (total_frames // LANES), axis=1)
        scores = dot(key[:, part], query[:, part], NT) + spread
        probs = jnp.exp(scores - log_total[head : head + 1, :])
        value_grad = dot(probs.astype(jnp.bfloat16), grad[:, part])
        prob_grad = dot(value[:, part], grad[:, part], NT)
        score_grad = (probs * (prob_grad - delta)).astype(jnp.bfloat16)
        key_grad = dot(score_grad, query[:, part])
        turned[part, :] = dot(key[:, part], score_grad, TN) * SCALE
        for by in range(ways):
            rows = slice(by * frames, (by + 1) * frames)
            outs[by][1, :, part] = key_grad[rows].astype(jnp.bfloat16)
            outs[by][2, :, part] = value_grad[rows].astype(jnp.bfloat16)
    query_grad = turned[...].T.astype(jnp.bfloat16)
    for by in range(ways):
        outs[by][0] = query_grad[by * frames : (by + 1) * frames]


def project_kernel(ways, info, *refs):
    blocks = refs[:ways]
    residual, before, after, out_weight, params = refs[ways : ways + 5]
    mixed, conv_in = refs[ways + 5 : ways + 7]
    messages, attended = refs[ways + 7 : -1], refs[-1]
    frames, width = residual.shape
    share = width // ways
    reach = 2 * EDGE
    rows = frames + 2 * reach
    for by in range(ways):
        for at in range(ways):

            @pl.when((info[0] ^ by) == at)
            def _():
                attended[:, at * share : (at + 1) * share] = blocks[by][...]

    step = width // 3
    for at in range(0, width, step):
        part = slice(at, at + step)
        mixed[:reach, part] = before[:reach, part].astype(jnp.float32)
        mixed[reach : reach + frames, part] = residual[:, part].astype(jnp.float32)
        mixed[reach + frames :, part] = after[:reach, part].astype(jnp.float32)
        mixed[:, part] += dot(attended[...], out_weight[:, part])

    gain = params[31:32, :]
    first = info[0] * frames - reach

    def band(index, carry):
        at = pl.ds(pl.multiple_of(index * BAND, BAND), BAND)
        normed, _ = moments(mixed[at, :])
        position = first + index * BAND + lax.broadcasted_iota(jnp.int32, (BAND, 1), 0)
        valid = (position >= 0) & (position < info[1])
        conv_in[at, :] = jnp.where(valid, normed * gain, 0.0).astype(jnp.bfloat16)
        return carry

    lax.fori_loop(0, rows // BAND, band, 0)
    for by, message in enumerate(messages):
        lacking = [slot for slot in range(ways) if slot != by]
        for at, slot in enumerate(lacking):
            message[:, at * share : (at + 1) * share] = blocks[slot][reach : reach + frames, :]


def stride_of(rows):
    return rows // 8 + 1


def in_columns(ref, rows):
    for at in range(ref.shape[0]):
        ref[at, : rows.shape[0]] = rows[:, at * LANES : (at + 1) * LANES].astype(jnp.float32)


def from_columns(ref, rows):
    return jnp.concatenate([ref[at, rows, :] for at in range(ref.shape[0])], axis=1)


def strided(ref, index, start, stride):
    return ref[index, pl.ds(start, 8, stride=stride), :]


def depthwise(padded, taps, tap_of, out, rows):
    stride = stride_of(rows)

    def column(index, carry):
        part = pl.ds(pl.multiple_of(index * LANES, LANES), LANES)
        cells = [strided(padded, index, at + 1, stride) for at in range(stride + 2 * EDGE - 2)]
        total = [None] * stride
        for offset in range(1, 2 * EDGE):
            tap = tap_of(offset)
            scale = jnp.broadcast_to(taps[tap : tap + 1, part], (8, LANES))
            for at in range(stride):
                term = cells[at + offset - 1] * scale
                total[at] = term if total[at] is None else total[at] + term
        for at in range(stride):
            out[index, pl.ds(at, 8, stride=stride), :] = total[at]
        return carry

    lax.fori_loop(0, out.shape[0], column, 0)


def tap_grads(padded, grad, start, rows, taps):
    stride = rows // 8

    def column(index, carry):
        part = pl.ds(pl.multiple_of(index * LANES, LANES), LANES)
        cells = [
            strided(padded, index, start + at + 1, stride) for at in range(stride + 2 * EDGE - 2)
        ]
        grads = [strided(grad, index, start + at, stride) for at in range(stride)]
        for tap in range(2 * EDGE - 1):
            total = cells[tap] * grads[0]
            for at in range(1, stride):
                total = total + cells[at + tap] * grads[at]
            taps[tap : tap + 1, part] = jnp.sum(total, axis=0, keepdims=True)
        return carry

    lax.fori_loop(0, grad.shape[0], column, 0)


def conv_kernel_body(across, info, conv_in, params, grad_own, grad_edges, *refs):
    conv_act, grad_conv, sums = refs[:3]
    halves = refs[3:-5]
    padded, conv, grad_act, bias_sum, gain_sum = refs[-5:]
    frames, width = grad_own.shape
    rows, wide = frames + 2 * EDGE, frames + 4 * EDGE
    in_columns(padded, conv_in[...])
    padded[:, wide:, :] = jnp.zeros((width // LANES, padded.shape[1] - wide, LANES), jnp.float32)
    grad_act[:EDGE] = grad_edges[:EDGE]
    grad_act[EDGE : EDGE + frames] = grad_own[...]
    grad_act[EDGE + frames :] = grad_edges[EDGE:]
    depthwise(padded, params, lambda offset: offset - 1, conv, rows)
    bias, gain = params[32:33, :], params[33:34, :]
    bias_sum[...] = jnp.zeros_like(bias_sum)
    gain_sum[...] = jnp.zeros_like(gain_sum)

    def band(index, carry):
        at = pl.ds(pl.multiple_of(index * BAND, BAND), BAND)
        normed, inv_scale = moments(from_columns(conv, at) + bias)
        scaled = normed * gain
        gate = 0.5 + 0.5 * jnp.tanh(0.5 * scaled)
        conv_act[at, :] = (scaled * gate).astype(jnp.bfloat16)
        grad_scaled = grad_act[at, :] * gate * (1.0 + scaled * (1.0 - gate))
        grad_rows = norm_back(grad_scaled * gain, normed, inv_scale)
        for column in range(width // LANES):
            grad_conv[column, at, :] = grad_rows[:, column * LANES : (column + 1) * LANES]

        @pl.when((index >= EDGE // BAND) & (index < (EDGE + frames) // BAND))
        def _():
            bias_sum[...] += fold(grad_rows)
            gain_sum[...] += fold(grad_scaled * normed)

        return carry

    lax.fori_loop(0, rows // BAND, band, 0)
    sums[0:1, :] = jnp.sum(bias_sum[...], axis=0, keepdims=True)
    sums[1:2, :] = jnp.sum(gain_sum[...], axis=0, keepdims=True)
    half = width // 2
    for by, block in enumerate(halves):
        for at in range(2):

            @pl.when((info[0] ^ by) // across == at)
            def _():
                block[...] = conv_act[EDGE : EDGE + frames, at * half : (at + 1) * half]


def block_out_kernel(info, conv_act, mixed, point_weight, block_out):
    frames, width = block_out.shape
    step = width // 3
    for at in range(0, width, step):
        part = slice(at, at + step)
        block_out[:, part] = (
            mixed[2 * EDGE : 2 * EDGE + frames, part]
            + dot(conv_act[EDGE : EDGE + frames, :], point_weight[:, part])
        ).astype(jnp.bfloat16)


def conv_back_kernel(ways, info, grad_conv, conv_in, params, masked, mixed, out_weight, *refs):
    conv_sums, selectors, grad_residual = refs[0], refs[1 : 1 + ways], refs[1 + ways]
    messages = refs[2 + ways : 2 + 2 * ways]
    padded, padded_in, conv, gain_sum, taps, packed = refs[2 + 2 * ways :]
    frames, width = grad_residual.shape
    share = width // ways
    reached = frames + 2 * EDGE
    padded[:, :reached, :] = grad_conv[...].astype(jnp.bfloat16).astype(jnp.float32)
    padded[:, reached:, :] = jnp.zeros(
        (width // LANES, padded.shape[1] - reached, LANES), jnp.float32
    )
    depthwise(padded, params, lambda offset: 31 - offset, conv, frames)
    gain = params[31:32, :]
    gain_sum[...] = jnp.zeros_like(gain_sum)

    def band(index, carry):
        at = pl.ds(pl.multiple_of(index * BAND, BAND), BAND)
        own_mixed = pl.ds(pl.multiple_of(index * BAND + 2 * EDGE, BAND), BAND)
        valid = valid_of(info[0] * frames + index * BAND, BAND, info[1])
        grad_in = jnp.where(valid, from_columns(conv, at), 0.0)
        normed, inv_scale = moments(mixed[own_mixed, :])
        grad_mixed = norm_back(grad_in * gain, normed, inv_scale)
        gain_sum[...] += fold(grad_in * normed)
        grad_residual[at, :] = (masked[at, :].astype(jnp.float32) + grad_mixed).astype(
            jnp.bfloat16
        )
        return carry

    lax.fori_loop(0, frames // BAND, band, 0)
    for by in range(ways):
        at = pl.ds(pl.multiple_of((info[0] ^ by) * share, share), share)
        messages[by][:frames] = dot(grad_residual[...], out_weight[at, :], NT).astype(jnp.bfloat16)

    in_columns(padded_in, conv_in[...])
    tap_grads(padded_in, grad_conv, EDGE, frames, taps)
    taps[31:32, :] = conv_sums[0:1, :]
    taps[32:33, :] = jnp.sum(gain_sum[...], axis=0, keepdims=True)
    taps[33:34, :] = conv_sums[1:2, :]
    taps[34:, :] = jnp.zeros((EXTRA - 34, width), jnp.float32)
    packed[:frames] = grad_residual[...]
    packed[frames:] = taps[...].astype(jnp.bfloat16)
    for by in range(ways):
        messages[by][frames:] = dot(packed[...], selectors[by][...]).astype(jnp.bfloat16)


def split_rows(info, parts, terms, sent, kept):
    rows = terms.shape[0] // parts
    for bit in range(2):

        @pl.when(info[2] % 2 == bit)
        def _():
            for at in range(parts // 2):
                own = (2 * at + bit) * rows
                other = (2 * at + 1 - bit) * rows
                kept[at] = terms[own : own + rows, :]
                sent[at] = terms[other : other + rows, :].astype(jnp.bfloat16)


def point_kernel(ways, parts, info, *refs):
    grads, acts, (sent, kept, terms) = refs[:ways], refs[ways : 2 * ways], refs[2 * ways :]
    left = jnp.concatenate([grad[...] for grad in grads], axis=0)
    right = jnp.concatenate([act[...] for act in acts], axis=0)
    step = terms.shape[1] // 2
    for at in range(0, 2 * step, step):
        part = slice(at, at + step)
        terms[:, part] = dot(left, right[:, part], TN)
    split_rows(info, parts, terms, sent, kept)


def point_sum_kernel(across, info, kept, received, own, other):
    rows = own.shape[0]
    total = kept[0] + received[0].astype(jnp.float32)
    for at in range(2):

        @pl.when(info[0] // across == at)
        def _():
            own[...] = total[at * rows : (at + 1) * rows, :]
            other[...] = total[(1 - at) * rows : (2 - at) * rows, :].astype(jnp.bfloat16)


def weight_kernel(ways, parts, info, *refs):
    grads, rows = refs[:ways], refs[ways : 2 * ways]
    attended, sent, kept, terms = refs[2 * ways :]
    total_frames, share = attended.shape
    frames = total_frames // ways
    width = ways * share
    slim = share // parts
    left = jnp.concatenate([grad[frames : 2 * frames, :] for grad in grads], axis=0)
    for slot in range(ways):
        if slot == 0:
            right = attended[...]
        else:
            pieces = []
            for by in range(ways):
                at = (by ^ slot) - (1 if (by ^ slot) > by else 0)
                pieces.append(rows[by][:, at * share : (at + 1) * share])
            right = jnp.concatenate(pieces, axis=0)
        terms[:, slot * share : (slot + 1) * share] = dot(left, right, TN)
    small = jnp.zeros((EXTRA, share), jnp.float32)
    for grad in grads:
        small = small + grad[2 * frames :, :].astype(jnp.float32)
    filler = jnp.zeros((LANES - EXTRA, share), jnp.float32)
    terms[:, width:] = jnp.concatenate([small, filler], axis=0).T
    split_rows(info, parts, terms, sent, kept)


def halve_kernel(shift, info, kept, received, sent, still_kept):
    bit = (info[2] >> shift) & 1
    for at in range(sent.shape[0]):
        own, other = 2 * at + bit, 2 * at + 1 - bit
        still_kept[at] = kept[own] + received[own].astype(jnp.float32)
        sent[at] = (kept[other] + received[other].astype(jnp.float32)).astype(jnp.bfloat16)


def finish_kernel(ways, info, kept, received, own, other, weight, taps, vectors, point):
    width = weight.shape[1]
    share, half = width // ways, width // 2
    for at in range(2):

        @pl.when(info[0] // (ways // 2) == at)
        def _():
            point[:, at * half : (at + 1) * half] = own[...]
            point[:, (1 - at) * half : (2 - at) * half] = other[...].astype(jnp.float32)

    total = kept[0] + received[0].astype(jnp.float32)
    for by in range(ways):
        for at in range(ways):

            @pl.when((info[0] ^ by) == at)
            def _():
                weight[:, at * share : (at + 1) * share] = total[:, by * share : (by + 1) * share]

    small = total[:, width:].T
    taps[...] = small[:31]
    vectors[...] = small[31:34]


def swap(block, axis, by):
    return lax.ppermute(block, axis, [(i, i ^ by) for i in range(lax.axis_size(axis))])


def swap_all(blocks, axis, step=1):
    return [blocks[0]] + [swap(block, axis, step * by) for by, block in enumerate(blocks[1:], 1)]


def local(
    residual_in,
    query_rows,
    key_rows,
    value_rows,
    lengths,
    out_weight,
    norm_gain,
    conv_kernel,
    conv_bias,
    conv_gain,
    point_weight,
    grad_out,
):
    ways = lax.axis_size("ctx")
    parts = lax.axis_size("dp")
    own = lax.axis_index("ctx")
    place = lax.axis_index("dp")
    frames, width = residual_in.shape[1:]
    share = width // ways
    slim = share // parts
    heads = HEADS // ways
    every = ways * frames
    across = ways // 2
    broad = width // across
    half = width // 2
    tiles = width // LANES
    bf16, f32 = jnp.bfloat16, jnp.float32
    square = 2 * frames * width * width
    rows_bytes = 2 * frames * width
    reached, wide = frames + 2 * EDGE, frames + 4 * EDGE

    info = jnp.stack([own, lengths[0], place]).astype(jnp.int32)
    params = jnp.concatenate(
        [conv_kernel, norm_gain[None], conv_bias[None], conv_gain[None]], axis=0
    )

    def every_nth(count, group):
        at = jnp.arange(count, dtype=jnp.int32)
        return ((at // slim) * (group * slim) + at % slim)[None]

    by_tiles = share % LANES == 0
    packed_rows = [3 * frames + 3 * EDGE * ways * (by in neighbours(ways)) for by in range(ways)]
    packed = call(
        functools.partial(pack_kernel, ways),
        "pack",
        [((rows, share), bf16) for rows in packed_rows],
        scratch=[((3, frames, width), bf16), ((2, 3 * EDGE, width), bf16)],
        semaphores=7,
        far=("in",),
        megabytes=58,
        moved=6 * rows_bytes,
    )(info, query_rows[0], key_rows[0], value_rows[0], residual_in[0], grad_out[0])
    packed = swap_all(packed, "ctx")

    masked, grad_own, *masked_halves = call(
        functools.partial(mask_kernel, slim),
        "mask",
        [((frames, width), bf16), ((frames, width), f32)] + [((frames, broad), bf16)] * across,
        flops=2 * square,
        moved=6 * rows_bytes + 2 * width * width,
    )(info, grad_out[0], point_weight, every_nth(broad, across))
    packed[1], masked_halves = lax.optimization_barrier((packed[1], masked_halves))
    masked_halves = swap_all([masked_halves[by % across] for by in range(ways)], "ctx")

    packed, masked = lax.optimization_barrier((packed, masked))
    head_scratch = [((every, share), bf16)] * 3 + [((every, LANES), f32)]
    pair_flops = 2 * heads * every * every * HEAD_DIM
    *returned, attended, log_total, before, after = call(
        functools.partial(attend_kernel, ways),
        "attend",
        [((wide, share), bf16)] * ways + [((every, share), bf16), ((heads, every), f32)]
        + [((3 * EDGE, width), bf16)] * 2,
        scratch=head_scratch + [((share, every), f32)],
        flops=8 * pair_flops,
        moved=4 * rows_bytes,
        exps=heads * every * every,
    )(info, *packed)
    returned, masked_halves[1:3] = lax.optimization_barrier((returned, masked_halves[1:3]))
    returned = swap_all(returned, "ctx")
    grad_edges = call(
        functools.partial(mask_edges_kernel, frames),
        "mask_edges",
        [((2 * EDGE, width), f32)],
        flops=square,
        moved=2 * width * width,
    )(info, before, after, point_weight)[0]
    selectors = call(
        functools.partial(select_kernel, slim),
        "select",
        [((width, share), bf16)] * ways,
        moved=2 * width * width,
    )(info, every_nth(share, ways))
    returned, grad_edges, selectors, masked_halves = lax.optimization_barrier(
        (returned, grad_edges, selectors, masked_halves)
    )

    mixed, conv_in, *messages = call(
        functools.partial(project_kernel, ways),
        "project",
        [((wide, width), f32), ((wide, width), bf16)] + [((frames, width - share), bf16)] * ways,
        scratch=[((wide, width), bf16)],
        flops=square,
        moved=6 * rows_bytes + 2 * width * width,
    )(info, *returned, residual_in[0], before, after, out_weight, params)
    near = 3
    arrived = swap_all(messages[:near], "ctx")

    spread = 8 * stride_of(reached)
    conv_act, grad_conv, conv_sums, *act_halves = call(
        functools.partial(conv_kernel_body, across),
        "conv",
        [
            ((reached, width), bf16),
            ((tiles, reached, LANES), f32),
            ((2, width), f32),
        ]
        + [((frames, half), bf16)] * ways,
        scratch=[
            ((tiles, spread + 2 * EDGE, LANES), f32),
            ((tiles, spread, LANES), f32),
            ((reached, width), f32),
            ((8, width), f32),
            ((8, width), f32),
        ],
        flops=frames * width * 4000,
        moved=6 * rows_bytes,
        exps=frames * width,
    )(info, conv_in, params, grad_own, grad_edges)
    arrived, act_halves, grad_conv, far = lax.optimization_barrier(
        (arrived, act_halves, grad_conv, messages[near:])
    )
    far = [swap(block, "ctx", by) for by, block in enumerate(far, near)]
    act_halves = swap_all(act_halves, "ctx")

    spread = 8 * stride_of(frames)
    grad_residual, *grad_messages = call(
        functools.partial(conv_back_kernel, ways),
        "conv_back",
        [((frames, width), bf16)] + [((2 * frames + EXTRA, share), bf16)] * ways,
        scratch=[
            ((tiles, spread + 2 * EDGE, LANES), f32),
            ((tiles, wide, LANES), f32),
            ((tiles, spread, LANES), f32),
            ((8, width), f32),
            ((EXTRA, width), f32),
            ((frames + EXTRA, width), bf16),
        ],
        flops=frames * width * 8000,
        moved=8 * rows_bytes + 2 * width * width,
    )(
        info,
        grad_conv,
        conv_in,
        params,
        masked,
        mixed,
        out_weight,
        conv_sums,
        *selectors,
    )
    far, act_halves, grad_messages = lax.optimization_barrier((far, act_halves, grad_messages))
    messages = arrived + far
    grad_messages = swap_all(grad_messages, "ctx")

    block_out = call(
        block_out_kernel,
        "block_out",
        [((frames, width), bf16)],
        flops=square,
        moved=4 * rows_bytes + 2 * width * width,
    )(info, conv_act, mixed, point_weight)[0]

    def halve(kept, received, shift):
        extent = (kept.shape[0] // 2,) + kept.shape[1:]
        return call(
            functools.partial(halve_kernel, shift),
            "halve",
            [(extent, bf16), (extent, f32)],
            moved=16 * extent[0] * extent[1] * extent[2],
        )(info, kept, received)

    def reduce(sent, kept, first):
        received = swap(sent, "dp", 2**first)
        for shift in range(first + 1, parts.bit_length() - 1):
            sent, kept = halve(kept, received, shift)
            received = swap(sent, "dp", 2**shift)
        return kept, received

    grad_messages[1], act_halves = lax.optimization_barrier((grad_messages[1], act_halves))
    point_half = (parts // 2, 2 * slim, half)
    point_sent, point_kept = call(
        functools.partial(point_kernel, ways, parts),
        "point_terms",
        [(point_half, bf16), (point_half, f32)],
        scratch=[((broad, half), f32)],
        flops=square,
        moved=8 * rows_bytes,
    )(info, *masked_halves, *act_halves)
    grad_messages, point_sent, block_out = lax.optimization_barrier(
        (grad_messages, point_sent, block_out)
    )
    point_sent, point_kept = halve(point_kept, swap(point_sent, "dp", 1), 1)
    point_own, point_other = call(
        functools.partial(point_sum_kernel, across),
        "point_sum",
        [((slim, half), f32), ((slim, half), bf16)],
        moved=slim * width * (parts + 8),
    )(info, *reduce(point_sent, point_kept, 1))
    point_other = swap(point_other, "ctx", across)

    extent = width + LANES
    core_half = (parts // 2, slim, extent)
    sent, kept = call(
        functools.partial(weight_kernel, ways, parts),
        "out_terms",
        [(core_half, bf16), (core_half, f32)],
        scratch=[((share, extent), f32)],
        flops=square,
        moved=10 * rows_bytes,
    )(info, *grad_messages, *messages, attended)
    pieces = reduce(sent, kept, 0)
    out_total, taps, vectors, point_total = call(
        functools.partial(finish_kernel, ways),
        "finish",
        [((slim, width), f32), ((31, slim), f32), ((3, slim), f32), ((slim, width), f32)],
        moved=slim * extent * (parts + 8),
    )(info, *pieces, point_own, point_other)

    grad_packed = call(
        functools.partial(attend_back_kernel, ways),
        "attend_back",
        [((3, frames, share), bf16)] * ways,
        scratch=head_scratch + [((every, share), bf16), ((share, every), f32)],
        flops=20 * pair_flops,
        moved=8 * rows_bytes,
        exps=heads * every * every,
    )(info, *packed, *grad_messages, attended, log_total)
    grad_packed = swap_all(grad_packed, "ctx")
    grad_query, grad_key, grad_value = call(
        functools.partial(unpack_kernel if by_tiles else unpack_parts_kernel, ways),
        "unpack",
        [((frames, width), bf16)] * 3,
        semaphores=3 * ways if by_tiles else 0,
        far=("out",) if by_tiles else (),
        moved=6 * rows_bytes,
    )(info, *grad_packed)

    return (
        block_out[None],
        grad_residual[None],
        grad_query[None],
        grad_key[None],
        grad_value[None],
        out_total.T,
        point_total.T,
        taps,
        vectors,
    )


def solution(mesh):
    rows = P("dp", "ctx", None)
    columns = P(None, ("dp", "ctx"))
    in_specs = (rows, rows, rows, rows, P("dp"), P(), P(), P(), P(), P(), P(), rows)
    out_specs = (rows,) * 5 + (columns,) * 4
    return jax.shard_map(local, mesh=mesh, in_specs=in_specs, out_specs=out_specs, check_vma=False)
```

```python
import functools

import jax
import jax.numpy as jnp
from jax import lax
from jax.experimental import pallas as pl
from jax.experimental.pallas import tpu as pltpu
from jax.sharding import PartitionSpec as P

HEADS = 24
HEAD_DIM = 64
SCALE = HEAD_DIM ** (-0.5)

NEG_FILL = -1e30
EPSILON = 1e-05

LANES = 128
EDGE = 16
NEAR = 3
BAND = 16
EXTRA = 48

NN = (((1,), (0,)), ((), ()))
NT = (((1,), (1,)), ((), ()))
TN = (((0,), (0,)), ((), ()))


def dot(left, right, dims=NN):
    return lax.dot_general(left, right, dims, preferred_element_type=jnp.float32)


def call(
    kernel, name, outs, scratch=(), semaphores=0, far=(), megabytes=28, flops=0, moved=0, exps=0
):
    vmem = pl.BlockSpec(memory_space=pltpu.VMEM)
    smem = pl.BlockSpec(memory_space=pltpu.SMEM)
    anywhere = pl.BlockSpec(memory_space=pl.ANY)

    def run(*arrays):
        scratches = [pltpu.VMEM(shape, kind) for shape, kind in scratch]
        if semaphores:
            scratches.append(pltpu.SemaphoreType.DMA((semaphores,)))
        return pl.pallas_call(
            kernel,
            name=name,
            in_specs=[smem if a.ndim == 1 else anywhere if "in" in far else vmem for a in arrays],
            out_specs=[anywhere if "out" in far else vmem] * len(outs),
            out_shape=[jax.ShapeDtypeStruct(shape, kind) for shape, kind in outs],
            scratch_shapes=scratches,
            compiler_params=pltpu.CompilerParams(vmem_limit_bytes=megabytes << 20),
            cost_estimate=pl.CostEstimate(flops=flops, bytes_accessed=moved, transcendentals=exps),
        )(*arrays)

    return run


def valid_of(first, rows, length):
    return first + lax.broadcasted_iota(jnp.int32, (rows, 1), 0) < length


def moments(rows):
    centre = jnp.mean(rows, axis=-1, keepdims=True)
    centred = rows - centre
    inv_scale = lax.rsqrt(jnp.mean(centred * centred, axis=-1, keepdims=True) + EPSILON)
    return centred * inv_scale, inv_scale


def norm_back(grad_normed, normed, inv_scale):
    first_mean = jnp.mean(grad_normed, axis=-1, keepdims=True)
    second_mean = jnp.mean(grad_normed * normed, axis=-1, keepdims=True)
    return inv_scale * (grad_normed - first_mean - normed * second_mean)


def fold(rows):
    total = rows[:8]
    for at in range(8, rows.shape[0], 8):
        total = total + rows[at : at + 8]
    return total


def at_group(info, by, ways, share, visit):
    if share % LANES == 0:
        visit(pl.ds(pl.multiple_of((info[0] ^ by) * share, LANES), share))
        return
    for at in range(ways):

        @pl.when((info[0] ^ by) == at)
        def _():
            visit(slice(at * share, (at + 1) * share))


def pack_kernel(ways, query, key, value, residual, grad_out, *refs):
    blocks, ends, whole, arrived = refs[:ways], refs[ways : ways + 2], refs[-2], refs[-1]
    info = [lax.axis_index("ctx")]
    frames, width = query.shape
    share, reach = width // ways, 2 * EDGE
    pairs = [(rows, whole.at[slot]) for slot, rows in enumerate((query, key, value))]
    for end, tail in zip(ends, (False, True)):
        for rows, start, count in ((residual, 0, reach), (grad_out, reach, EDGE)):
            first = frames - count if tail else 0
            pairs.append((rows.at[pl.ds(first, count)], end.at[pl.ds(start, count)]))
    copies = [
        pltpu.make_async_copy(source, target, arrived.at[at])
        for at, (source, target) in enumerate(pairs)
    ]
    for copy in copies:
        copy.start()
    for slot, copy in enumerate(copies[:3]):
        copy.wait()
        for by in range(ways):

            def visit(lanes):
                blocks[by][slot] = whole[slot, :, lanes]

            at_group(info, by, ways, share, visit)
    for copy in copies[3:]:
        copy.wait()


def unpack_kernel(ways, info, *refs):
    blocks, outs, arrived = refs[:ways], refs[ways:-1], refs[-1]
    share = blocks[0].shape[2]
    copies = []
    for by in range(ways):
        for slot, rows in enumerate(outs):
            lanes = pl.ds(pl.multiple_of((info[0] ^ by) * share, LANES), share)
            copy = pltpu.make_async_copy(
                blocks[by].at[slot], rows.at[:, lanes], arrived.at[len(copies)]
            )
            copy.start()
            copies.append(copy)
    for copy in copies:
        copy.wait()


def unpack_parts_kernel(ways, info, *refs):
    blocks, outs = refs[:ways], refs[ways:]
    share = blocks[0].shape[2]
    for by in range(ways):
        for slot, rows in enumerate(outs):

            def visit(lanes):
                rows[:, lanes] = blocks[by][slot]

            at_group(info, by, ways, share, visit)


def selector(columns, slim, position, width):
    wanted = columns + position * slim
    rows = lax.broadcasted_iota(jnp.int32, (width, columns.shape[1]), 0)
    return jnp.where(rows == wanted, 1.0, 0.0).astype(jnp.bfloat16)


def mask_kernel(slim, info, grad_out, point_weight, columns, masked, grad_act, *halves):
    frames, width = grad_out.shape
    valid = valid_of(info[0] * frames, frames, info[1])
    masked[...] = jnp.where(valid, grad_out[...].astype(jnp.float32), 0.0).astype(jnp.bfloat16)
    step = width // 3
    for at in range(0, width, step):
        grad_act[:, at : at + step] = dot(masked[...], point_weight[at : at + step, :], NT)
    across = len(halves)
    for by in range(across):
        chosen = selector(columns[...], slim, (info[0] % across) ^ by, width)
        halves[by][...] = dot(masked[...], chosen).astype(jnp.bfloat16)


def mask_edges_kernel(frames, info, before, after, point_weight, grad_act):
    width = grad_act.shape[1]
    first = info[0] * frames
    sides = []
    for side, start in ((before, first - EDGE), (after, first + frames)):
        valid = valid_of(start, EDGE, info[1])
        rows = side[2 * EDGE :, :].astype(jnp.float32)
        sides.append(jnp.where(valid, rows, 0.0).astype(jnp.bfloat16))
    masked = jnp.concatenate(sides, axis=0)
    step = width // 3
    for at in range(0, width, step):
        grad_act[:, at : at + step] = dot(masked, point_weight[at : at + step, :], NT)


def gather_heads(info, blocks, query, key, value, bias):
    frames = query.shape[0] // len(blocks)
    for by, block in enumerate(blocks):
        rows = slice(by * frames, (by + 1) * frames)
        query[rows] = block[0] * jnp.bfloat16(SCALE)
        key[rows] = block[1]
        value[rows] = block[2]
        valid = valid_of((info[0] ^ by) * frames, frames, info[1])
        bias[rows] = jnp.broadcast_to(jnp.where(valid, 0.0, NEG_FILL), (frames, LANES))


def attend_kernel(ways, info, *refs):
    blocks, outs = refs[:ways], refs[ways : 2 * ways]
    attended, log_total, query, key, value, bias, turned = refs[2 * ways :]
    gather_heads(info, blocks, query, key, value, bias)
    total_frames, share = query.shape
    frames = total_frames // ways
    for head in range(share // HEAD_DIM):
        part = slice(head * HEAD_DIM, (head + 1) * HEAD_DIM)
        spread = jnp.concatenate([bias[...]] * (total_frames // LANES), axis=1)
        scores = dot(key[:, part], query[:, part], NT) + spread
        row_max = jnp.max(scores, axis=0, keepdims=True)
        weights = jnp.exp(scores - row_max)
        total = jnp.sum(weights, axis=0, keepdims=True)
        turned[part, :] = dot(value[:, part], weights.astype(jnp.bfloat16), TN) / total
        log_total[head : head + 1, :] = row_max + jnp.log(total)
    attended[...] = turned[...].T.astype(jnp.bfloat16)
    reach = 2 * EDGE
    for by in range(ways):
        other = info[0] ^ by
        before = (info[0] ^ jnp.maximum(other - 1, 0)) * frames + frames - reach
        after = (info[0] ^ jnp.minimum(other + 1, ways - 1)) * frames
        outs[by][:reach] = attended[pl.ds(pl.multiple_of(before, reach), reach), :]
        outs[by][reach : reach + frames] = attended[by * frames : (by + 1) * frames, :]
        outs[by][reach + frames :] = attended[pl.ds(pl.multiple_of(after, reach), reach), :]


def attend_back_kernel(ways, info, *refs):
    blocks, messages = refs[:ways], refs[ways : 2 * ways]
    attended, log_total = refs[2 * ways : 2 * ways + 2]
    outs = refs[2 * ways + 2 : 3 * ways + 2]
    query, key, value, bias, grad, turned = refs[3 * ways + 2 :]
    gather_heads(info, blocks, query, key, value, bias)
    total_frames, share = query.shape
    frames = total_frames // ways
    for by in range(ways):
        grad[by * frames : (by + 1) * frames] = messages[by][:frames, :]
    turned[...] = (grad[...].astype(jnp.float32) * attended[...].astype(jnp.float32)).T
    for head in range(share // HEAD_DIM):
        part = slice(head * HEAD_DIM, (head + 1) * HEAD_DIM)
        delta = jnp.sum(turned[part, :], axis=0, keepdims=True)
        spread = jnp.concatenate([bias[...]] * (total_frames // LANES), axis=1)
        scores = dot(key[:, part], query[:, part], NT) + spread
        probs = jnp.exp(scores - log_total[head : head + 1, :])
        value_grad = dot(probs.astype(jnp.bfloat16), grad[:, part])
        prob_grad = dot(value[:, part], grad[:, part], NT)
        score_grad = (probs * (prob_grad - delta)).astype(jnp.bfloat16)
        key_grad = dot(score_grad, query[:, part])
        turned[part, :] = dot(key[:, part], score_grad, TN) * SCALE
        for by in range(ways):
            rows = slice(by * frames, (by + 1) * frames)
            outs[by][1, :, part] = key_grad[rows].astype(jnp.bfloat16)
            outs[by][2, :, part] = value_grad[rows].astype(jnp.bfloat16)
    query_grad = turned[...].T.astype(jnp.bfloat16)
    for by in range(ways):
        outs[by][0] = query_grad[by * frames : (by + 1) * frames]


def project_kernel(ways, info, *refs):
    blocks = refs[:ways]
    residual, before, after, out_weight, params = refs[ways : ways + 5]
    mixed, conv_in = refs[-3 - ways : -1 - ways]
    messages, attended = refs[-1 - ways : -1], refs[-1]
    halves = refs[ways + 5 : -3 - ways]
    frames, width = residual.shape
    share = width // ways
    reach = 2 * EDGE
    rows = frames + 2 * reach
    for by in range(ways):
        for at in range(ways):

            @pl.when((info[0] ^ by) == at)
            def _():
                attended[:, at * share : (at + 1) * share] = blocks[by][...]

    step = width // 3
    for at in range(0, width, step):
        part = slice(at, at + step)
        mixed[:reach, part] = before[:reach, part].astype(jnp.float32)
        mixed[reach : reach + frames, part] = residual[:, part].astype(jnp.float32)
        mixed[reach + frames :, part] = after[:reach, part].astype(jnp.float32)
        mixed[:, part] += dot(attended[...], out_weight[:, part])

    gain = params[31:32, :]
    first = info[0] * frames - reach

    def band(index, carry):
        at = pl.ds(pl.multiple_of(index * BAND, BAND), BAND)
        normed, _ = moments(mixed[at, :])
        position = first + index * BAND + lax.broadcasted_iota(jnp.int32, (BAND, 1), 0)
        valid = (position >= 0) & (position < info[1])
        conv_in[at, :] = jnp.where(valid, normed * gain, 0.0).astype(jnp.bfloat16)
        return carry

    lax.fori_loop(0, rows // BAND, band, 0)
    for by, message in enumerate(messages):
        lacking = [slot for slot in range(ways) if slot != by]
        for at, slot in enumerate(lacking):
            message[:, at * share : (at + 1) * share] = blocks[slot][reach : reach + frames, :]
        if by < NEAR:
            message[:, width - share :] = halves[by % len(halves)][...]


def stride_of(rows):
    return rows // 8 + 1


def in_columns(ref, rows):
    for at in range(ref.shape[0]):
        ref[at, : rows.shape[0]] = rows[:, at * LANES : (at + 1) * LANES].astype(jnp.float32)


def from_columns(ref, rows):
    return jnp.concatenate([ref[at, rows, :] for at in range(ref.shape[0])], axis=1)


def strided(ref, index, start, stride):
    return ref[index, pl.ds(start, 8, stride=stride), :]


def depthwise(padded, taps, tap_of, out, rows):
    stride = stride_of(rows)

    def column(index, carry):
        part = pl.ds(pl.multiple_of(index * LANES, LANES), LANES)
        cells = [strided(padded, index, at + 1, stride) for at in range(stride + 2 * EDGE - 2)]
        total = [None] * stride
        for offset in range(1, 2 * EDGE):
            tap = tap_of(offset)
            scale = jnp.broadcast_to(taps[tap : tap + 1, part], (8, LANES))
            for at in range(stride):
                term = cells[at + offset - 1] * scale
                total[at] = term if total[at] is None else total[at] + term
        for at in range(stride):
            out[index, pl.ds(at, 8, stride=stride), :] = total[at]
        return carry

    lax.fori_loop(0, out.shape[0], column, 0)


def tap_grads(padded, grad, start, rows, taps):
    stride = rows // 8

    def column(index, carry):
        part = pl.ds(pl.multiple_of(index * LANES, LANES), LANES)
        cells = [
            strided(padded, index, start + at + 1, stride) for at in range(stride + 2 * EDGE - 2)
        ]
        grads = [strided(grad, index, start + at, stride) for at in range(stride)]
        for tap in range(2 * EDGE - 1):
            total = cells[tap] * grads[0]
            for at in range(1, stride):
                total = total + cells[at + tap] * grads[at]
            taps[tap : tap + 1, part] = jnp.sum(total, axis=0, keepdims=True)
        return carry

    lax.fori_loop(0, grad.shape[0], column, 0)


def conv_kernel_body(across, info, conv_in, params, grad_own, grad_edges, *refs):
    count = (len(refs) - 8 + NEAR) // 2
    messages = refs[: count - NEAR]
    conv_act, grad_conv, sums = refs[count - NEAR : count - NEAR + 3]
    halves = refs[count - NEAR + 3 : -5]
    padded, conv, grad_act, bias_sum, gain_sum = refs[-5:]
    frames, width = grad_own.shape
    rows, wide = frames + 2 * EDGE, frames + 4 * EDGE
    in_columns(padded, conv_in[...])
    padded[:, wide:, :] = jnp.zeros((width // LANES, padded.shape[1] - wide, LANES), jnp.float32)
    grad_act[:EDGE] = grad_edges[:EDGE]
    grad_act[EDGE : EDGE + frames] = grad_own[...]
    grad_act[EDGE + frames :] = grad_edges[EDGE:]
    depthwise(padded, params, lambda offset: offset - 1, conv, rows)
    bias, gain = params[32:33, :], params[33:34, :]
    bias_sum[...] = jnp.zeros_like(bias_sum)
    gain_sum[...] = jnp.zeros_like(gain_sum)

    def band(index, carry):
        at = pl.ds(pl.multiple_of(index * BAND, BAND), BAND)
        normed, inv_scale = moments(from_columns(conv, at) + bias)
        scaled = normed * gain
        gate = 0.5 + 0.5 * jnp.tanh(0.5 * scaled)
        conv_act[at, :] = (scaled * gate).astype(jnp.bfloat16)
        grad_scaled = grad_act[at, :] * gate * (1.0 + scaled * (1.0 - gate))
        grad_rows = norm_back(grad_scaled * gain, normed, inv_scale)
        for column in range(width // LANES):
            grad_conv[column, at, :] = grad_rows[:, column * LANES : (column + 1) * LANES]

        @pl.when((index >= EDGE // BAND) & (index < (EDGE + frames) // BAND))
        def _():
            bias_sum[...] += fold(grad_rows)
            gain_sum[...] += fold(grad_scaled * normed)

        return carry

    lax.fori_loop(0, rows // BAND, band, 0)
    sums[0:1, :] = jnp.sum(bias_sum[...], axis=0, keepdims=True)
    sums[1:2, :] = jnp.sum(gain_sum[...], axis=0, keepdims=True)
    half = width // 2
    for by, block in enumerate(halves):
        for at in range(2):

            @pl.when((info[0] ^ by) // across == at)
            def _():
                block[:, :half] = conv_act[EDGE : EDGE + frames, at * half : (at + 1) * half]

        if by >= NEAR:
            block[:, half:] = messages[by - NEAR][...]


def block_out_kernel(info, conv_act, mixed, point_weight, block_out):
    frames, width = block_out.shape
    step = width // 3
    for at in range(0, width, step):
        part = slice(at, at + step)
        block_out[:, part] = (
            mixed[2 * EDGE : 2 * EDGE + frames, part]
            + dot(conv_act[EDGE : EDGE + frames, :], point_weight[:, part])
        ).astype(jnp.bfloat16)


def conv_back_kernel(ways, slim, info, grad_conv, conv_in, params, masked, mixed, out_weight, *refs):
    conv_sums, grad_residual, messages = refs[0], refs[1], refs[2 : 2 + ways]
    padded, padded_in, conv, gain_sum, taps, packed, chosen = refs[2 + ways :]
    frames, width = grad_residual.shape
    share = width // ways
    reached = frames + 2 * EDGE
    padded[:, :reached, :] = grad_conv[...].astype(jnp.bfloat16).astype(jnp.float32)
    padded[:, reached:, :] = jnp.zeros(
        (width // LANES, padded.shape[1] - reached, LANES), jnp.float32
    )
    depthwise(padded, params, lambda offset: 31 - offset, conv, frames)
    gain = params[31:32, :]
    gain_sum[...] = jnp.zeros_like(gain_sum)

    def band(index, carry):
        at = pl.ds(pl.multiple_of(index * BAND, BAND), BAND)
        own_mixed = pl.ds(pl.multiple_of(index * BAND + 2 * EDGE, BAND), BAND)
        valid = valid_of(info[0] * frames + index * BAND, BAND, info[1])
        grad_in = jnp.where(valid, from_columns(conv, at), 0.0)
        normed, inv_scale = moments(mixed[own_mixed, :])
        grad_mixed = norm_back(grad_in * gain, normed, inv_scale)
        gain_sum[...] += fold(grad_in * normed)
        grad_residual[at, :] = (masked[at, :].astype(jnp.float32) + grad_mixed).astype(
            jnp.bfloat16
        )
        return carry

    lax.fori_loop(0, frames // BAND, band, 0)
    for by in range(ways):
        at = pl.ds(pl.multiple_of((info[0] ^ by) * share, share), share)
        messages[by][:frames] = dot(grad_residual[...], out_weight[at, :], NT).astype(jnp.bfloat16)

    in_columns(padded_in, conv_in[...])
    tap_grads(padded_in, grad_conv, EDGE, frames, taps)
    taps[31:32, :] = conv_sums[0:1, :]
    taps[32:33, :] = jnp.sum(gain_sum[...], axis=0, keepdims=True)
    taps[33:34, :] = conv_sums[1:2, :]
    taps[34:, :] = jnp.zeros((EXTRA - 34, width), jnp.float32)
    packed[:frames] = grad_residual[...]
    packed[frames:] = taps[...].astype(jnp.bfloat16)
    for at in range(ways):
        pieces = []
        for start in range(at * slim, width, ways * slim):
            pieces.append(packed[:, start : start + slim])
        chosen[at] = jnp.concatenate(pieces, axis=1)
    for by in range(ways):
        messages[by][frames:] = chosen[info[0] ^ by]


def split_rows(info, parts, terms, sent, kept):
    rows = terms.shape[0] // parts
    for bit in range(2):

        @pl.when(info[2] % 2 == bit)
        def _():
            for at in range(parts // 2):
                own = (2 * at + bit) * rows
                other = (2 * at + 1 - bit) * rows
                kept[at] = terms[own : own + rows, :]
                sent[at] = terms[other : other + rows, :].astype(jnp.bfloat16)


def point_kernel(ways, parts, info, *refs):
    grads, acts, (sent, kept, terms) = refs[:ways], refs[ways : 2 * ways], refs[2 * ways :]
    extent, half = terms.shape
    left = jnp.concatenate([grad[:, grad.shape[1] - extent :] for grad in grads], axis=0)
    right = jnp.concatenate([act[:, :half] for act in acts], axis=0)
    step = terms.shape[1] // 2
    for at in range(0, 2 * step, step):
        part = slice(at, at + step)
        terms[:, part] = dot(left, right[:, part], TN)
    split_rows(info, parts, terms, sent, kept)


def point_sum_kernel(across, info, kept, received, own, other):
    rows = own.shape[0]
    total = kept[0] + received[0].astype(jnp.float32)
    for at in range(2):

        @pl.when(info[0] // across == at)
        def _():
            own[...] = total[at * rows : (at + 1) * rows, :]
            other[...] = total[(1 - at) * rows : (2 - at) * rows, :].astype(jnp.bfloat16)


def weight_kernel(ways, parts, info, *refs):
    grads, rows = refs[:ways], refs[ways : 2 * ways]
    attended, sent, kept, terms = refs[2 * ways :]
    total_frames, share = attended.shape
    frames = total_frames // ways
    width = ways * share
    slim = share // parts
    left = jnp.concatenate([grad[frames : 2 * frames, :] for grad in grads], axis=0)
    for slot in range(ways):
        if slot == 0:
            right = attended[...]
        else:
            pieces = []
            for by in range(ways):
                at = (by ^ slot) - (1 if (by ^ slot) > by else 0)
                first = (width // 2 if by >= NEAR else 0) + at * share
                pieces.append(rows[by][:, first : first + share])
            right = jnp.concatenate(pieces, axis=0)
        terms[:, slot * share : (slot + 1) * share] = dot(left, right, TN)
    small = jnp.zeros((EXTRA, share), jnp.float32)
    for grad in grads:
        small = small + grad[2 * frames :, :].astype(jnp.float32)
    filler = jnp.zeros((LANES - EXTRA, share), jnp.float32)
    terms[:, width:] = jnp.concatenate([small, filler], axis=0).T
    split_rows(info, parts, terms, sent, kept)


def halve_kernel(shift, info, kept, received, sent, still_kept):
    bit = (info[2] >> shift) & 1
    for at in range(sent.shape[0]):
        own, other = 2 * at + bit, 2 * at + 1 - bit
        still_kept[at] = kept[own] + received[own].astype(jnp.float32)
        sent[at] = (kept[other] + received[other].astype(jnp.float32)).astype(jnp.bfloat16)


def finish_kernel(ways, info, kept, received, own, other, weight, taps, vectors, point):
    width = weight.shape[1]
    share, half = width // ways, width // 2
    for at in range(2):

        @pl.when(info[0] // (ways // 2) == at)
        def _():
            point[:, at * half : (at + 1) * half] = own[...]
            point[:, (1 - at) * half : (2 - at) * half] = other[...].astype(jnp.float32)

    total = kept[0] + received[0].astype(jnp.float32)
    for by in range(ways):
        for at in range(ways):

            @pl.when((info[0] ^ by) == at)
            def _():
                weight[:, at * share : (at + 1) * share] = total[:, by * share : (by + 1) * share]

    small = total[:, width:].T
    taps[...] = small[:31]
    vectors[...] = small[31:34]


def swap(block, axis, by):
    return lax.ppermute(block, axis, [(i, i ^ by) for i in range(lax.axis_size(axis))])


def swap_all(blocks, axis, step=1):
    return [blocks[0]] + [swap(block, axis, step * by) for by, block in enumerate(blocks[1:], 1)]


def local(
    residual_in,
    query_rows,
    key_rows,
    value_rows,
    lengths,
    out_weight,
    norm_gain,
    conv_kernel,
    conv_bias,
    conv_gain,
    point_weight,
    grad_out,
):
    ways = lax.axis_size("ctx")
    parts = lax.axis_size("dp")
    own = lax.axis_index("ctx")
    place = lax.axis_index("dp")
    frames, width = residual_in.shape[1:]
    share = width // ways
    slim = share // parts
    heads = HEADS // ways
    every = ways * frames
    across = ways // 2
    broad = width // across
    half = width // 2
    tiles = width // LANES
    bf16, f32 = jnp.bfloat16, jnp.float32
    square = 2 * frames * width * width
    rows_bytes = 2 * frames * width
    reached, wide = frames + 2 * EDGE, frames + 4 * EDGE

    info = jnp.stack([own, lengths[0], place]).astype(jnp.int32)
    params = jnp.concatenate(
        [conv_kernel, norm_gain[None], conv_bias[None], conv_gain[None]], axis=0
    )

    def every_nth(count, group):
        at = jnp.arange(count, dtype=jnp.int32)
        return ((at // slim) * (group * slim) + at % slim)[None]

    by_tiles = share % LANES == 0
    *packed, head, tail = call(
        functools.partial(pack_kernel, ways),
        "pack",
        [((3, frames, share), bf16)] * ways + [((3 * EDGE, width), bf16)] * 2,
        scratch=[((3, frames, width), bf16)],
        semaphores=7,
        far=("in",),
        megabytes=58,
        moved=6 * rows_bytes,
    )(query_rows[0], key_rows[0], value_rows[0], residual_in[0], grad_out[0])
    packed = swap_all(packed, "ctx")

    masked, grad_own, *masked_halves = call(
        functools.partial(mask_kernel, slim),
        "mask",
        [((frames, width), bf16), ((frames, width), f32)] + [((frames, broad), bf16)] * across,
        flops=2 * square,
        moved=6 * rows_bytes + 2 * width * width,
    )(info, grad_out[0], point_weight, every_nth(broad, across))
    packed[1], head, tail, masked_halves = lax.optimization_barrier(
        (packed[1], head, tail, masked_halves)
    )
    steps = [(i, i + 1) for i in range(ways - 1)]
    before = lax.ppermute(tail, "ctx", steps)
    after = lax.ppermute(head, "ctx", [(j, i) for i, j in steps])
    far_halves = [swap(masked_halves[by % across], "ctx", by) for by in range(NEAR, ways)]
    packed, masked = lax.optimization_barrier((packed, masked))
    head_scratch = [((every, share), bf16)] * 3 + [((every, LANES), f32)]
    pair_flops = 2 * heads * every * every * HEAD_DIM
    *returned, attended, log_total = call(
        functools.partial(attend_kernel, ways),
        "attend",
        [((wide, share), bf16)] * ways + [((every, share), bf16), ((heads, every), f32)],
        scratch=head_scratch + [((share, every), f32)],
        flops=8 * pair_flops,
        moved=4 * rows_bytes,
        exps=heads * every * every,
    )(info, *packed)
    returned = swap_all(returned, "ctx")
    grad_edges = call(
        functools.partial(mask_edges_kernel, frames),
        "mask_edges",
        [((2 * EDGE, width), f32)],
        flops=square,
        moved=2 * width * width,
    )(info, before, after, point_weight)[0]
    returned, grad_edges, far_halves = lax.optimization_barrier((returned, grad_edges, far_halves))

    mixed, conv_in, *messages = call(
        functools.partial(project_kernel, ways),
        "project",
        [((wide, width), f32), ((wide, width), bf16)]
        + [((frames, width - share + broad), bf16)] * NEAR
        + [((frames, width - share), bf16)] * (ways - NEAR),
        scratch=[((wide, width), bf16)],
        flops=square,
        moved=6 * rows_bytes + 2 * width * width,
    )(info, *returned, residual_in[0], before, after, out_weight, params, *masked_halves)
    arrived = swap_all(messages[:NEAR], "ctx")

    spread = 8 * stride_of(reached)
    conv_act, grad_conv, conv_sums, *act_halves = call(
        functools.partial(conv_kernel_body, across),
        "conv",
        [
            ((reached, width), bf16),
            ((tiles, reached, LANES), f32),
            ((2, width), f32),
        ]
        + [((frames, half), bf16)] * NEAR
        + [((frames, half + width - share), bf16)] * (ways - NEAR),
        scratch=[
            ((tiles, spread + 2 * EDGE, LANES), f32),
            ((tiles, spread, LANES), f32),
            ((reached, width), f32),
            ((8, width), f32),
            ((8, width), f32),
        ],
        flops=frames * width * 4000,
        moved=6 * rows_bytes,
        exps=frames * width,
    )(info, conv_in, params, grad_own, grad_edges, *messages[NEAR:])
    arrived, act_halves, grad_conv = lax.optimization_barrier((arrived, act_halves, grad_conv))
    act_halves = swap_all(act_halves, "ctx")

    spread = 8 * stride_of(frames)
    grad_residual, *grad_messages = call(
        functools.partial(conv_back_kernel, ways, slim),
        "conv_back",
        [((frames, width), bf16)] + [((2 * frames + EXTRA, share), bf16)] * ways,
        scratch=[
            ((tiles, spread + 2 * EDGE, LANES), f32),
            ((tiles, wide, LANES), f32),
            ((tiles, spread, LANES), f32),
            ((8, width), f32),
            ((EXTRA, width), f32),
            ((frames + EXTRA, width), bf16),
            ((ways, frames + EXTRA, share), bf16),
        ],
        flops=frames * width * 8000,
        moved=8 * rows_bytes + 2 * width * width,
    )(
        info,
        grad_conv,
        conv_in,
        params,
        masked,
        mixed,
        out_weight,
        conv_sums,
    )
    act_halves, grad_messages = lax.optimization_barrier((act_halves, grad_messages))
    messages = arrived + act_halves[NEAR:]
    grad_messages = swap_all(grad_messages, "ctx")

    block_out = call(
        block_out_kernel,
        "block_out",
        [((frames, width), bf16)],
        flops=square,
        moved=4 * rows_bytes + 2 * width * width,
    )(info, conv_act, mixed, point_weight)[0]

    def halve(kept, received, shift):
        extent = (kept.shape[0] // 2,) + kept.shape[1:]
        return call(
            functools.partial(halve_kernel, shift),
            "halve",
            [(extent, bf16), (extent, f32)],
            moved=16 * extent[0] * extent[1] * extent[2],
        )(info, kept, received)

    def reduce(sent, kept, first):
        received = swap(sent, "dp", 2**first)
        for shift in range(first + 1, parts.bit_length() - 1):
            sent, kept = halve(kept, received, shift)
            received = swap(sent, "dp", 2**shift)
        return kept, received

    point_half = (parts // 2, 2 * slim, half)
    point_sent, point_kept = call(
        functools.partial(point_kernel, ways, parts),
        "point_terms",
        [(point_half, bf16), (point_half, f32)],
        scratch=[((broad, half), f32)],
        flops=square,
        moved=8 * rows_bytes,
    )(info, *arrived, *far_halves, *act_halves)
    point_sent, point_kept = halve(point_kept, swap(point_sent, "dp", 1), 1)
    grad_messages, point_sent, block_out = lax.optimization_barrier(
        (grad_messages, point_sent, block_out)
    )
    point_own, point_other = call(
        functools.partial(point_sum_kernel, across),
        "point_sum",
        [((slim, half), f32), ((slim, half), bf16)],
        moved=slim * width * (parts + 8),
    )(info, *reduce(point_sent, point_kept, 1))
    point_other = swap(point_other, "ctx", across)

    extent = width + LANES
    core_half = (parts // 2, slim, extent)
    sent, kept = call(
        functools.partial(weight_kernel, ways, parts),
        "out_terms",
        [(core_half, bf16), (core_half, f32)],
        scratch=[((share, extent), f32)],
        flops=square,
        moved=10 * rows_bytes,
    )(info, *grad_messages, *messages, attended)
    pieces = reduce(sent, kept, 0)
    out_total, taps, vectors, point_total = call(
        functools.partial(finish_kernel, ways),
        "finish",
        [((slim, width), f32), ((31, slim), f32), ((3, slim), f32), ((slim, width), f32)],
        moved=slim * extent * (parts + 8),
    )(info, *pieces, point_own, point_other)

    grad_packed = call(
        functools.partial(attend_back_kernel, ways),
        "attend_back",
        [((3, frames, share), bf16)] * ways,
        scratch=head_scratch + [((every, share), bf16), ((share, every), f32)],
        flops=20 * pair_flops,
        moved=8 * rows_bytes,
        exps=heads * every * every,
    )(info, *packed, *grad_messages, attended, log_total)
    grad_packed = swap_all(grad_packed, "ctx")
    grad_query, grad_key, grad_value = call(
        functools.partial(unpack_kernel if by_tiles else unpack_parts_kernel, ways),
        "unpack",
        [((frames, width), bf16)] * 3,
        semaphores=3 * ways if by_tiles else 0,
        far=("out",) if by_tiles else (),
        moved=6 * rows_bytes,
    )(info, *grad_packed)

    return (
        block_out[None],
        grad_residual[None],
        grad_query[None],
        grad_key[None],
        grad_value[None],
        out_total.T,
        point_total.T,
        taps,
        vectors,
    )


def solution(mesh):
    rows = P("dp", "ctx", None)
    columns = P(None, ("dp", "ctx"))
    in_specs = (rows, rows, rows, rows, P("dp"), P(), P(), P(), P(), P(), P(), rows)
    out_specs = (rows,) * 5 + (columns,) * 4
    return jax.shard_map(local, mesh=mesh, in_specs=in_specs, out_specs=out_specs, check_vma=False)
```

```python
import functools

import jax
import jax.numpy as jnp
from jax import lax
from jax.experimental import pallas as pl
from jax.experimental.pallas import tpu as pltpu
from jax.sharding import PartitionSpec as P

HEADS = 24
HEAD_DIM = 64
SCALE = HEAD_DIM ** (-0.5)

NEG_FILL = -1e30
EPSILON = 1e-05

LANES = 128
EDGE = 16
NEAR = 3
BAND = 16
EXTRA = 48

NN = (((1,), (0,)), ((), ()))
NT = (((1,), (1,)), ((), ()))
TN = (((0,), (0,)), ((), ()))


def dot(left, right, dims=NN):
    return lax.dot_general(left, right, dims, preferred_element_type=jnp.float32)


def call(
    kernel, name, outs, scratch=(), semaphores=0, far=(), megabytes=28, flops=0, moved=0, exps=0
):
    vmem = pl.BlockSpec(memory_space=pltpu.VMEM)
    smem = pl.BlockSpec(memory_space=pltpu.SMEM)
    anywhere = pl.BlockSpec(memory_space=pl.ANY)

    def run(*arrays):
        scratches = [pltpu.VMEM(shape, kind) for shape, kind in scratch]
        if semaphores:
            scratches.append(pltpu.SemaphoreType.DMA((semaphores,)))
        return pl.pallas_call(
            kernel,
            name=name,
            in_specs=[smem if a.ndim == 1 else anywhere if "in" in far else vmem for a in arrays],
            out_specs=[anywhere if "out" in far else vmem] * len(outs),
            out_shape=[jax.ShapeDtypeStruct(shape, kind) for shape, kind in outs],
            scratch_shapes=scratches,
            compiler_params=pltpu.CompilerParams(vmem_limit_bytes=megabytes << 20),
            cost_estimate=pl.CostEstimate(flops=flops, bytes_accessed=moved, transcendentals=exps),
        )(*arrays)

    return run


def valid_of(first, rows, length):
    return first + lax.broadcasted_iota(jnp.int32, (rows, 1), 0) < length


def moments(rows):
    centre = jnp.mean(rows, axis=-1, keepdims=True)
    centred = rows - centre
    inv_scale = lax.rsqrt(jnp.mean(centred * centred, axis=-1, keepdims=True) + EPSILON)
    return centred * inv_scale, inv_scale


def norm_back(grad_normed, normed, inv_scale):
    first_mean = jnp.mean(grad_normed, axis=-1, keepdims=True)
    second_mean = jnp.mean(grad_normed * normed, axis=-1, keepdims=True)
    return inv_scale * (grad_normed - first_mean - normed * second_mean)


def fold(rows):
    total = rows[:8]
    for at in range(8, rows.shape[0], 8):
        total = total + rows[at : at + 8]
    return total


def at_group(info, by, ways, share, visit):
    if share % LANES == 0:
        visit(pl.ds(pl.multiple_of((info[0] ^ by) * share, LANES), share))
        return
    for at in range(ways):

        @pl.when((info[0] ^ by) == at)
        def _():
            visit(slice(at * share, (at + 1) * share))


def pack_kernel(ways, query, key, value, residual, grad_out, *refs):
    blocks, ends, whole, arrived = refs[:ways], refs[ways : ways + 2], refs[-2], refs[-1]
    info = [lax.axis_index("ctx")]
    frames, width = query.shape
    share, reach = width // ways, 2 * EDGE
    pairs = [(rows, whole.at[slot]) for slot, rows in enumerate((query, key, value))]
    for end, tail in zip(ends, (False, True)):
        for rows, start, count in ((residual, 0, reach), (grad_out, reach, EDGE)):
            first = frames - count if tail else 0
            pairs.append((rows.at[pl.ds(first, count)], end.at[pl.ds(start, count)]))
    copies = [
        pltpu.make_async_copy(source, target, arrived.at[at])
        for at, (source, target) in enumerate(pairs)
    ]
    for copy in copies:
        copy.start()
    for slot, copy in enumerate(copies[:3]):
        copy.wait()
        for by in range(ways):

            def visit(lanes):
                blocks[by][slot] = whole[slot, :, lanes]

            at_group(info, by, ways, share, visit)
    for copy in copies[3:]:
        copy.wait()


def unpack_kernel(ways, info, *refs):
    blocks, outs, arrived = refs[:ways], refs[ways:-1], refs[-1]
    share = blocks[0].shape[2]
    copies = []
    for by in range(ways):
        for slot, rows in enumerate(outs):
            lanes = pl.ds(pl.multiple_of((info[0] ^ by) * share, LANES), share)
            copy = pltpu.make_async_copy(
                blocks[by].at[slot], rows.at[:, lanes], arrived.at[len(copies)]
            )
            copy.start()
            copies.append(copy)
    for copy in copies:
        copy.wait()


def unpack_parts_kernel(ways, info, *refs):
    blocks, outs = refs[:ways], refs[ways:]
    share = blocks[0].shape[2]
    for by in range(ways):
        for slot, rows in enumerate(outs):

            def visit(lanes):
                rows[:, lanes] = blocks[by][slot]

            at_group(info, by, ways, share, visit)


def selector(columns, slim, position, width):
    wanted = columns + position * slim
    rows = lax.broadcasted_iota(jnp.int32, (width, columns.shape[1]), 0)
    return jnp.where(rows == wanted, 1.0, 0.0).astype(jnp.bfloat16)


def mask_kernel(slim, info, grad_out, point_weight, columns, masked, grad_act, *halves):
    frames, width = grad_out.shape
    valid = valid_of(info[0] * frames, frames, info[1])
    masked[...] = jnp.where(valid, grad_out[...].astype(jnp.float32), 0.0).astype(jnp.bfloat16)
    step = width // 3
    for at in range(0, width, step):
        grad_act[:, at : at + step] = dot(masked[...], point_weight[at : at + step, :], NT)
    across = len(halves)
    for by in range(across):
        chosen = selector(columns[...], slim, (info[0] % across) ^ by, width)
        halves[by][...] = dot(masked[...], chosen).astype(jnp.bfloat16)


def mask_edges_kernel(frames, info, before, after, point_weight, grad_act):
    width = grad_act.shape[1]
    first = info[0] * frames
    sides = []
    for side, start in ((before, first - EDGE), (after, first + frames)):
        valid = valid_of(start, EDGE, info[1])
        rows = side[2 * EDGE :, :].astype(jnp.float32)
        sides.append(jnp.where(valid, rows, 0.0).astype(jnp.bfloat16))
    masked = jnp.concatenate(sides, axis=0)
    step = width // 3
    for at in range(0, width, step):
        grad_act[:, at : at + step] = dot(masked, point_weight[at : at + step, :], NT)


def gather_heads(info, blocks, query, key, value, bias):
    frames = query.shape[0] // len(blocks)
    for by, block in enumerate(blocks):
        rows = slice(by * frames, (by + 1) * frames)
        query[rows] = block[0] * jnp.bfloat16(SCALE)
        key[rows] = block[1]
        value[rows] = block[2]
        valid = valid_of((info[0] ^ by) * frames, frames, info[1])
        bias[rows] = jnp.broadcast_to(jnp.where(valid, 0.0, NEG_FILL), (frames, LANES))


def attend_kernel(ways, info, *refs):
    blocks, outs = refs[:ways], refs[ways : 2 * ways]
    attended, log_total, query, key, value, bias, turned = refs[2 * ways :]
    gather_heads(info, blocks, query, key, value, bias)
    total_frames, share = query.shape
    frames = total_frames // ways
    for head in range(share // HEAD_DIM):
        part = slice(head * HEAD_DIM, (head + 1) * HEAD_DIM)
        spread = jnp.concatenate([bias[...]] * (total_frames // LANES), axis=1)
        scores = dot(key[:, part], query[:, part], NT) + spread
        row_max = jnp.max(scores, axis=0, keepdims=True)
        weights = jnp.exp(scores - row_max)
        total = jnp.sum(weights, axis=0, keepdims=True)
        turned[part, :] = dot(value[:, part], weights.astype(jnp.bfloat16), TN) / total
        log_total[head : head + 1, :] = row_max + jnp.log(total)
    attended[...] = turned[...].T.astype(jnp.bfloat16)
    reach = 2 * EDGE
    for by in range(ways):
        other = info[0] ^ by
        before = (info[0] ^ jnp.maximum(other - 1, 0)) * frames + frames - reach
        after = (info[0] ^ jnp.minimum(other + 1, ways - 1)) * frames
        outs[by][:reach] = attended[pl.ds(pl.multiple_of(before, reach), reach), :]
        outs[by][reach : reach + frames] = attended[by * frames : (by + 1) * frames, :]
        outs[by][reach + frames :] = attended[pl.ds(pl.multiple_of(after, reach), reach), :]


def attend_back_kernel(ways, info, *refs):
    blocks, messages = refs[:ways], refs[ways : 2 * ways]
    attended, log_total = refs[2 * ways : 2 * ways + 2]
    outs = refs[2 * ways + 2 : 3 * ways + 2]
    query, key, value, bias, grad, turned = refs[3 * ways + 2 :]
    gather_heads(info, blocks, query, key, value, bias)
    total_frames, share = query.shape
    frames = total_frames // ways
    for by in range(ways):
        grad[by * frames : (by + 1) * frames] = messages[by][:frames, :]
    turned[...] = (grad[...].astype(jnp.float32) * attended[...].astype(jnp.float32)).T
    for head in range(share // HEAD_DIM):
        part = slice(head * HEAD_DIM, (head + 1) * HEAD_DIM)
        delta = jnp.sum(turned[part, :], axis=0, keepdims=True)
        spread = jnp.concatenate([bias[...]] * (total_frames // LANES), axis=1)
        scores = dot(key[:, part], query[:, part], NT) + spread
        probs = jnp.exp(scores - log_total[head : head + 1, :])
        value_grad = dot(probs.astype(jnp.bfloat16), grad[:, part])
        prob_grad = dot(value[:, part], grad[:, part], NT)
        score_grad = (probs * (prob_grad - delta)).astype(jnp.bfloat16)
        key_grad = dot(score_grad, query[:, part])
        turned[part, :] = dot(key[:, part], score_grad, TN) * SCALE
        for by in range(ways):
            rows = slice(by * frames, (by + 1) * frames)
            outs[by][1, :, part] = key_grad[rows].astype(jnp.bfloat16)
            outs[by][2, :, part] = value_grad[rows].astype(jnp.bfloat16)
    query_grad = turned[...].T.astype(jnp.bfloat16)
    for by in range(ways):
        outs[by][0] = query_grad[by * frames : (by + 1) * frames]


def gather_kernel(ways, info, *refs):
    blocks, halves, messages = refs[:ways], refs[ways:-ways], refs[-ways:]
    frames, share = halves[0].shape[0], blocks[0].shape[1]
    reach = 2 * EDGE
    for by, message in enumerate(messages):
        lacking = [slot for slot in range(ways) if slot != by]
        for at, slot in enumerate(lacking):
            message[:, at * share : (at + 1) * share] = blocks[slot][reach : reach + frames, :]
        if by < NEAR:
            message[:, (ways - 1) * share :] = halves[by % len(halves)][...]


def project_kernel(ways, info, *refs):
    blocks = refs[:ways]
    residual, before, after, out_weight, params = refs[ways : ways + 5]
    mixed, conv_in, attended = refs[ways + 5 :]
    frames, width = residual.shape
    share = width // ways
    reach = 2 * EDGE
    rows = frames + 2 * reach
    for by in range(ways):
        for at in range(ways):

            @pl.when((info[0] ^ by) == at)
            def _():
                attended[:, at * share : (at + 1) * share] = blocks[by][...]

    step = width // 3
    for at in range(0, width, step):
        part = slice(at, at + step)
        mixed[:reach, part] = before[:reach, part].astype(jnp.float32)
        mixed[reach : reach + frames, part] = residual[:, part].astype(jnp.float32)
        mixed[reach + frames :, part] = after[:reach, part].astype(jnp.float32)
        mixed[:, part] += dot(attended[...], out_weight[:, part])

    gain = params[31:32, :]
    first = info[0] * frames - reach

    def band(index, carry):
        at = pl.ds(pl.multiple_of(index * BAND, BAND), BAND)
        normed, _ = moments(mixed[at, :])
        position = first + index * BAND + lax.broadcasted_iota(jnp.int32, (BAND, 1), 0)
        valid = (position >= 0) & (position < info[1])
        conv_in[at, :] = jnp.where(valid, normed * gain, 0.0).astype(jnp.bfloat16)
        return carry

    lax.fori_loop(0, rows // BAND, band, 0)


def stride_of(rows):
    return rows // 8 + 1


def in_columns(ref, rows):
    for at in range(ref.shape[0]):
        ref[at, : rows.shape[0]] = rows[:, at * LANES : (at + 1) * LANES].astype(jnp.float32)


def from_columns(ref, rows):
    return jnp.concatenate([ref[at, rows, :] for at in range(ref.shape[0])], axis=1)


def strided(ref, index, start, stride):
    return ref[index, pl.ds(start, 8, stride=stride), :]


def depthwise(padded, taps, tap_of, out, rows):
    stride = stride_of(rows)

    def column(index, carry):
        part = pl.ds(pl.multiple_of(index * LANES, LANES), LANES)
        cells = [strided(padded, index, at + 1, stride) for at in range(stride + 2 * EDGE - 2)]
        total = [None] * stride
        for offset in range(1, 2 * EDGE):
            tap = tap_of(offset)
            scale = jnp.broadcast_to(taps[tap : tap + 1, part], (8, LANES))
            for at in range(stride):
                term = cells[at + offset - 1] * scale
                total[at] = term if total[at] is None else total[at] + term
        for at in range(stride):
            out[index, pl.ds(at, 8, stride=stride), :] = total[at]
        return carry

    lax.fori_loop(0, out.shape[0], column, 0)


def tap_grads(padded, grad, start, rows, taps):
    stride = rows // 8

    def column(index, carry):
        part = pl.ds(pl.multiple_of(index * LANES, LANES), LANES)
        cells = [
            strided(padded, index, start + at + 1, stride) for at in range(stride + 2 * EDGE - 2)
        ]
        grads = [strided(grad, index, start + at, stride) for at in range(stride)]
        for tap in range(2 * EDGE - 1):
            total = cells[tap] * grads[0]
            for at in range(1, stride):
                total = total + cells[at + tap] * grads[at]
            taps[tap : tap + 1, part] = jnp.sum(total, axis=0, keepdims=True)
        return carry

    lax.fori_loop(0, grad.shape[0], column, 0)


def conv_kernel_body(across, info, conv_in, params, grad_own, grad_edges, *refs):
    count = (len(refs) - 8 + NEAR) // 2
    messages = refs[: count - NEAR]
    conv_act, grad_conv, sums = refs[count - NEAR : count - NEAR + 3]
    halves = refs[count - NEAR + 3 : -5]
    padded, conv, grad_act, bias_sum, gain_sum = refs[-5:]
    frames, width = grad_own.shape
    rows, wide = frames + 2 * EDGE, frames + 4 * EDGE
    in_columns(padded, conv_in[...])
    padded[:, wide:, :] = jnp.zeros((width // LANES, padded.shape[1] - wide, LANES), jnp.float32)
    grad_act[:EDGE] = grad_edges[:EDGE]
    grad_act[EDGE : EDGE + frames] = grad_own[...]
    grad_act[EDGE + frames :] = grad_edges[EDGE:]
    depthwise(padded, params, lambda offset: offset - 1, conv, rows)
    bias, gain = params[32:33, :], params[33:34, :]
    bias_sum[...] = jnp.zeros_like(bias_sum)
    gain_sum[...] = jnp.zeros_like(gain_sum)

    def band(index, carry):
        at = pl.ds(pl.multiple_of(index * BAND, BAND), BAND)
        normed, inv_scale = moments(from_columns(conv, at) + bias)
        scaled = normed * gain
        gate = 0.5 + 0.5 * jnp.tanh(0.5 * scaled)
        conv_act[at, :] = (scaled * gate).astype(jnp.bfloat16)
        grad_scaled = grad_act[at, :] * gate * (1.0 + scaled * (1.0 - gate))
        grad_rows = norm_back(grad_scaled * gain, normed, inv_scale)
        for column in range(width // LANES):
            grad_conv[column, at, :] = grad_rows[:, column * LANES : (column + 1) * LANES]

        @pl.when((index >= EDGE // BAND) & (index < (EDGE + frames) // BAND))
        def _():
            bias_sum[...] += fold(grad_rows)
            gain_sum[...] += fold(grad_scaled * normed)

        return carry

    lax.fori_loop(0, rows // BAND, band, 0)
    sums[0:1, :] = jnp.sum(bias_sum[...], axis=0, keepdims=True)
    sums[1:2, :] = jnp.sum(gain_sum[...], axis=0, keepdims=True)
    half = width // 2
    for by, block in enumerate(halves):
        for at in range(2):

            @pl.when((info[0] ^ by) // across == at)
            def _():
                block[:, :half] = conv_act[EDGE : EDGE + frames, at * half : (at + 1) * half]

        if by >= NEAR:
            block[:, half:] = messages[by - NEAR][...]


def block_out_kernel(info, conv_act, mixed, point_weight, block_out):
    frames, width = block_out.shape
    step = width // 3
    for at in range(0, width, step):
        part = slice(at, at + step)
        block_out[:, part] = (
            mixed[2 * EDGE : 2 * EDGE + frames, part]
            + dot(conv_act[EDGE : EDGE + frames, :], point_weight[:, part])
        ).astype(jnp.bfloat16)


def conv_back_kernel(ways, slim, info, grad_conv, conv_in, params, masked, mixed, out_weight, *refs):
    conv_sums, grad_residual, messages = refs[0], refs[1], refs[2 : 2 + ways]
    padded, padded_in, conv, gain_sum, taps, packed, chosen = refs[2 + ways :]
    frames, width = grad_residual.shape
    share = width // ways
    reached = frames + 2 * EDGE
    padded[:, :reached, :] = grad_conv[...].astype(jnp.bfloat16).astype(jnp.float32)
    padded[:, reached:, :] = jnp.zeros(
        (width // LANES, padded.shape[1] - reached, LANES), jnp.float32
    )
    depthwise(padded, params, lambda offset: 31 - offset, conv, frames)
    gain = params[31:32, :]
    gain_sum[...] = jnp.zeros_like(gain_sum)

    def band(index, carry):
        at = pl.ds(pl.multiple_of(index * BAND, BAND), BAND)
        own_mixed = pl.ds(pl.multiple_of(index * BAND + 2 * EDGE, BAND), BAND)
        valid = valid_of(info[0] * frames + index * BAND, BAND, info[1])
        grad_in = jnp.where(valid, from_columns(conv, at), 0.0)
        normed, inv_scale = moments(mixed[own_mixed, :])
        grad_mixed = norm_back(grad_in * gain, normed, inv_scale)
        gain_sum[...] += fold(grad_in * normed)
        grad_residual[at, :] = (masked[at, :].astype(jnp.float32) + grad_mixed).astype(
            jnp.bfloat16
        )
        return carry

    lax.fori_loop(0, frames // BAND, band, 0)
    for by in range(ways):
        at = pl.ds(pl.multiple_of((info[0] ^ by) * share, share), share)
        messages[by][:frames] = dot(grad_residual[...], out_weight[at, :], NT).astype(jnp.bfloat16)

    in_columns(padded_in, conv_in[...])
    tap_grads(padded_in, grad_conv, EDGE, frames, taps)
    taps[31:32, :] = conv_sums[0:1, :]
    taps[32:33, :] = jnp.sum(gain_sum[...], axis=0, keepdims=True)
    taps[33:34, :] = conv_sums[1:2, :]
    taps[34:, :] = jnp.zeros((EXTRA - 34, width), jnp.float32)
    packed[:frames] = grad_residual[...]
    packed[frames:] = taps[...].astype(jnp.bfloat16)
    for at in range(ways):
        pieces = []
        for start in range(at * slim, width, ways * slim):
            pieces.append(packed[:, start : start + slim])
        chosen[at] = jnp.concatenate(pieces, axis=1)
    for by in range(ways):
        messages[by][frames:] = chosen[info[0] ^ by]


def split_rows(info, parts, shift, terms, sent, kept):
    rows = terms.shape[0] // parts
    low = (1 << shift) - 1

    def start(at, bit):
        return (((at & ~low) << 1) | (bit << shift) | (at & low)) * rows

    for bit in range(2):

        @pl.when((info[2] >> shift) & 1 == bit)
        def _():
            for at in range(parts // 2):
                own, other = start(at, bit), start(at, 1 - bit)
                kept[at] = terms[own : own + rows, :]
                sent[at] = terms[other : other + rows, :].astype(jnp.bfloat16)


def point_kernel(ways, parts, info, *refs):
    grads, acts, (sent, kept, terms) = refs[:ways], refs[ways : 2 * ways], refs[2 * ways :]
    extent, half = terms.shape
    left = jnp.concatenate([grad[:, grad.shape[1] - extent :] for grad in grads], axis=0)
    right = jnp.concatenate([act[:, :half] for act in acts], axis=0)
    step = terms.shape[1] // 2
    for at in range(0, 2 * step, step):
        part = slice(at, at + step)
        terms[:, part] = dot(left, right[:, part], TN)
    split_rows(info, parts, 1, terms, sent, kept)


def point_sum_kernel(across, info, kept, received, own, other):
    rows = own.shape[0]
    total = kept[0] + received[0].astype(jnp.float32)
    for at in range(2):

        @pl.when(info[0] // across == at)
        def _():
            own[...] = total[at * rows : (at + 1) * rows, :]
            other[...] = total[(1 - at) * rows : (2 - at) * rows, :].astype(jnp.bfloat16)


def weight_kernel(ways, parts, info, *refs):
    grads, rows = refs[:ways], refs[ways : 2 * ways]
    attended, sent, kept, terms = refs[2 * ways :]
    total_frames, share = attended.shape
    frames = total_frames // ways
    width = ways * share
    slim = share // parts
    left = jnp.concatenate([grad[frames : 2 * frames, :] for grad in grads], axis=0)
    for slot in range(ways):
        if slot == 0:
            right = attended[...]
        else:
            pieces = []
            for by in range(ways):
                at = (by ^ slot) - (1 if (by ^ slot) > by else 0)
                first = (width // 2 if by >= NEAR else 0) + at * share
                pieces.append(rows[by][:, first : first + share])
            right = jnp.concatenate(pieces, axis=0)
        terms[:, slot * share : (slot + 1) * share] = dot(left, right, TN)
    small = jnp.zeros((EXTRA, share), jnp.float32)
    for grad in grads:
        small = small + grad[2 * frames :, :].astype(jnp.float32)
    filler = jnp.zeros((LANES - EXTRA, share), jnp.float32)
    terms[:, width:] = jnp.concatenate([small, filler], axis=0).T
    split_rows(info, parts, 0, terms, sent, kept)


def halve_kernel(shift, info, kept, received, sent, still_kept):
    bit = (info[2] >> shift) & 1
    for at in range(sent.shape[0]):
        own, other = 2 * at + bit, 2 * at + 1 - bit
        still_kept[at] = kept[own] + received[own].astype(jnp.float32)
        sent[at] = (kept[other] + received[other].astype(jnp.float32)).astype(jnp.bfloat16)


def finish_kernel(ways, info, kept, received, own, other, weight, taps, vectors, point):
    width = weight.shape[1]
    share, half = width // ways, width // 2
    for at in range(2):

        @pl.when(info[0] // (ways // 2) == at)
        def _():
            point[:, at * half : (at + 1) * half] = own[...]
            point[:, (1 - at) * half : (2 - at) * half] = other[...].astype(jnp.float32)

    total = kept[0] + received[0].astype(jnp.float32)
    for by in range(ways):
        for at in range(ways):

            @pl.when((info[0] ^ by) == at)
            def _():
                weight[:, at * share : (at + 1) * share] = total[:, by * share : (by + 1) * share]

    small = total[:, width:].T
    taps[...] = small[:31]
    vectors[...] = small[31:34]


def swap(block, axis, by):
    return lax.ppermute(block, axis, [(i, i ^ by) for i in range(lax.axis_size(axis))])


def swap_all(blocks, axis, step=1):
    return [blocks[0]] + [swap(block, axis, step * by) for by, block in enumerate(blocks[1:], 1)]


def local(
    residual_in,
    query_rows,
    key_rows,
    value_rows,
    lengths,
    out_weight,
    norm_gain,
    conv_kernel,
    conv_bias,
    conv_gain,
    point_weight,
    grad_out,
):
    ways = lax.axis_size("ctx")
    parts = lax.axis_size("dp")
    own = lax.axis_index("ctx")
    place = lax.axis_index("dp")
    frames, width = residual_in.shape[1:]
    share = width // ways
    slim = share // parts
    heads = HEADS // ways
    every = ways * frames
    across = ways // 2
    broad = width // across
    half = width // 2
    tiles = width // LANES
    bf16, f32 = jnp.bfloat16, jnp.float32
    square = 2 * frames * width * width
    rows_bytes = 2 * frames * width
    reached, wide = frames + 2 * EDGE, frames + 4 * EDGE

    info = jnp.stack([own, lengths[0], place]).astype(jnp.int32)
    params = jnp.concatenate(
        [conv_kernel, norm_gain[None], conv_bias[None], conv_gain[None]], axis=0
    )

    def every_nth(count, group):
        at = jnp.arange(count, dtype=jnp.int32)
        return ((at // slim) * (group * slim) + at % slim)[None]

    by_tiles = share % LANES == 0
    *packed, head, tail = call(
        functools.partial(pack_kernel, ways),
        "pack",
        [((3, frames, share), bf16)] * ways + [((3 * EDGE, width), bf16)] * 2,
        scratch=[((3, frames, width), bf16)],
        semaphores=7,
        far=("in",),
        megabytes=58,
        moved=6 * rows_bytes,
    )(query_rows[0], key_rows[0], value_rows[0], residual_in[0], grad_out[0])
    packed = swap_all(packed, "ctx")

    masked, grad_own, *masked_halves = call(
        functools.partial(mask_kernel, slim),
        "mask",
        [((frames, width), bf16), ((frames, width), f32)] + [((frames, broad), bf16)] * across,
        flops=2 * square,
        moved=6 * rows_bytes + 2 * width * width,
    )(info, grad_out[0], point_weight, every_nth(broad, across))
    packed[1], head, tail, masked = lax.optimization_barrier((packed[1], head, tail, masked))
    steps = [(i, i + 1) for i in range(ways - 1)]
    before = lax.ppermute(tail, "ctx", steps)
    after = lax.ppermute(head, "ctx", [(j, i) for i, j in steps])
    packed, masked, before, after = lax.optimization_barrier((packed, masked, before, after))
    head_scratch = [((every, share), bf16)] * 3 + [((every, LANES), f32)]
    pair_flops = 2 * heads * every * every * HEAD_DIM
    *returned, attended, log_total = call(
        functools.partial(attend_kernel, ways),
        "attend",
        [((wide, share), bf16)] * ways + [((every, share), bf16), ((heads, every), f32)],
        scratch=head_scratch + [((share, every), f32)],
        flops=8 * pair_flops,
        moved=4 * rows_bytes,
        exps=heads * every * every,
    )(info, *packed)
    returned = swap_all(returned, "ctx")
    grad_edges = call(
        functools.partial(mask_edges_kernel, frames),
        "mask_edges",
        [((2 * EDGE, width), f32)],
        flops=square,
        moved=2 * width * width,
    )(info, before, after, point_weight)[0]
    returned, grad_edges = lax.optimization_barrier((returned, grad_edges))
    messages = call(
        functools.partial(gather_kernel, ways),
        "gather",
        [((frames, width - share + broad), bf16)] * NEAR
        + [((frames, width - share), bf16)] * (ways - NEAR),
        moved=8 * rows_bytes,
    )(info, *returned, *masked_halves)
    arrived = swap_all(messages[:NEAR], "ctx")
    far_halves = [swap(masked_halves[by % across], "ctx", by) for by in range(NEAR, ways)]

    returned, messages = lax.optimization_barrier((returned, messages))
    mixed, conv_in = call(
        functools.partial(project_kernel, ways),
        "project",
        [((wide, width), f32), ((wide, width), bf16)],
        scratch=[((wide, width), bf16)],
        flops=square,
        moved=6 * rows_bytes + 2 * width * width,
    )(info, *returned, residual_in[0], before, after, out_weight, params)
    spread = 8 * stride_of(reached)
    conv_act, grad_conv, conv_sums, *act_halves = call(
        functools.partial(conv_kernel_body, across),
        "conv",
        [
            ((reached, width), bf16),
            ((tiles, reached, LANES), f32),
            ((2, width), f32),
        ]
        + [((frames, half), bf16)] * NEAR
        + [((frames, half + width - share), bf16)] * (ways - NEAR),
        scratch=[
            ((tiles, spread + 2 * EDGE, LANES), f32),
            ((tiles, spread, LANES), f32),
            ((reached, width), f32),
            ((8, width), f32),
            ((8, width), f32),
        ],
        flops=frames * width * 4000,
        moved=6 * rows_bytes,
        exps=frames * width,
    )(info, conv_in, params, grad_own, grad_edges, *messages[NEAR:])
    arrived, far_halves, act_halves, grad_conv = lax.optimization_barrier(
        (arrived, far_halves, act_halves, grad_conv)
    )
    act_halves = swap_all(act_halves, "ctx")

    spread = 8 * stride_of(frames)
    grad_residual, *grad_messages = call(
        functools.partial(conv_back_kernel, ways, slim),
        "conv_back",
        [((frames, width), bf16)] + [((2 * frames + EXTRA, share), bf16)] * ways,
        scratch=[
            ((tiles, spread + 2 * EDGE, LANES), f32),
            ((tiles, wide, LANES), f32),
            ((tiles, spread, LANES), f32),
            ((8, width), f32),
            ((EXTRA, width), f32),
            ((frames + EXTRA, width), bf16),
            ((ways, frames + EXTRA, share), bf16),
        ],
        flops=frames * width * 8000,
        moved=8 * rows_bytes + 2 * width * width,
    )(
        info,
        grad_conv,
        conv_in,
        params,
        masked,
        mixed,
        out_weight,
        conv_sums,
    )
    act_halves, grad_messages = lax.optimization_barrier((act_halves, grad_messages))
    messages = arrived + act_halves[NEAR:]
    grad_messages = swap_all(grad_messages, "ctx")

    block_out = call(
        block_out_kernel,
        "block_out",
        [((frames, width), bf16)],
        flops=square,
        moved=4 * rows_bytes + 2 * width * width,
    )(info, conv_act, mixed, point_weight)[0]

    def halve(kept, received, shift):
        extent = (kept.shape[0] // 2,) + kept.shape[1:]
        return call(
            functools.partial(halve_kernel, shift),
            "halve",
            [(extent, bf16), (extent, f32)],
            moved=16 * extent[0] * extent[1] * extent[2],
        )(info, kept, received)

    def reduce(kept, received, first):
        for shift in range(first + 1, parts.bit_length() - 1):
            sent, kept = halve(kept, received, shift)
            received = swap(sent, "dp", 2**shift)
        return kept, received

    point_half = (parts // 2, 2 * slim, half)
    point_sent, point_kept = call(
        functools.partial(point_kernel, ways, parts),
        "point_terms",
        [(point_half, bf16), (point_half, f32)],
        scratch=[((broad, half), f32)],
        flops=square,
        moved=8 * rows_bytes,
    )(info, *arrived, *far_halves, *act_halves)
    point_sent, point_kept = halve(point_kept, swap(point_sent, "dp", 2), 0)
    grad_messages, point_sent, block_out = lax.optimization_barrier(
        (grad_messages, point_sent, block_out)
    )
    point_own, point_other = call(
        functools.partial(point_sum_kernel, across),
        "point_sum",
        [((slim, half), f32), ((slim, half), bf16)],
        moved=slim * width * (parts + 8),
    )(info, *reduce(point_kept, swap(point_sent, "dp", 1), 1))
    point_other = swap(point_other, "ctx", across)

    extent = width + LANES
    core_half = (parts // 2, slim, extent)
    sent, kept = call(
        functools.partial(weight_kernel, ways, parts),
        "out_terms",
        [(core_half, bf16), (core_half, f32)],
        scratch=[((share, extent), f32)],
        flops=square,
        moved=10 * rows_bytes,
    )(info, *grad_messages, *messages, attended)
    pieces = reduce(kept, swap(sent, "dp", 1), 0)
    out_total, taps, vectors, point_total = call(
        functools.partial(finish_kernel, ways),
        "finish",
        [((slim, width), f32), ((31, slim), f32), ((3, slim), f32), ((slim, width), f32)],
        moved=slim * extent * (parts + 8),
    )(info, *pieces, point_own, point_other)

    grad_packed = call(
        functools.partial(attend_back_kernel, ways),
        "attend_back",
        [((3, frames, share), bf16)] * ways,
        scratch=head_scratch + [((every, share), bf16), ((share, every), f32)],
        flops=20 * pair_flops,
        moved=8 * rows_bytes,
        exps=heads * every * every,
    )(info, *packed, *grad_messages, attended, log_total)
    grad_packed = swap_all(grad_packed, "ctx")
    grad_query, grad_key, grad_value = call(
        functools.partial(unpack_kernel if by_tiles else unpack_parts_kernel, ways),
        "unpack",
        [((frames, width), bf16)] * 3,
        semaphores=3 * ways if by_tiles else 0,
        far=("out",) if by_tiles else (),
        moved=6 * rows_bytes,
    )(info, *grad_packed)

    return (
        block_out[None],
        grad_residual[None],
        grad_query[None],
        grad_key[None],
        grad_value[None],
        out_total.T,
        point_total.T,
        taps,
        vectors,
    )


def solution(mesh):
    rows = P("dp", "ctx", None)
    columns = P(None, ("dp", "ctx"))
    in_specs = (rows, rows, rows, rows, P("dp"), P(), P(), P(), P(), P(), P(), rows)
    out_specs = (rows,) * 5 + (columns,) * 4
    return jax.shard_map(local, mesh=mesh, in_specs=in_specs, out_specs=out_specs, check_vma=False)
```

```python
import functools

import jax
import jax.numpy as jnp
from jax import lax
from jax.experimental import pallas as pl
from jax.experimental.pallas import tpu as pltpu
from jax.sharding import PartitionSpec as P

HEADS = 24
HEAD_DIM = 64
SCALE = HEAD_DIM ** (-0.5)

NEG_FILL = -1e30
EPSILON = 1e-05

LANES = 128
EDGE = 16
NEAR = 3
BAND = 16
EXTRA = 48

NN = (((1,), (0,)), ((), ()))
NT = (((1,), (1,)), ((), ()))
TN = (((0,), (0,)), ((), ()))


def dot(left, right, dims=NN):
    return lax.dot_general(left, right, dims, preferred_element_type=jnp.float32)


def call(
    kernel, name, outs, scratch=(), semaphores=0, far=(), megabytes=28, flops=0, moved=0, exps=0
):
    vmem = pl.BlockSpec(memory_space=pltpu.VMEM)
    smem = pl.BlockSpec(memory_space=pltpu.SMEM)
    anywhere = pl.BlockSpec(memory_space=pl.ANY)

    def run(*arrays):
        scratches = [pltpu.VMEM(shape, kind) for shape, kind in scratch]
        if semaphores:
            scratches.append(pltpu.SemaphoreType.DMA((semaphores,)))
        return pl.pallas_call(
            kernel,
            name=name,
            in_specs=[smem if a.ndim == 1 else anywhere if "in" in far else vmem for a in arrays],
            out_specs=[anywhere if "out" in far else vmem] * len(outs),
            out_shape=[jax.ShapeDtypeStruct(shape, kind) for shape, kind in outs],
            scratch_shapes=scratches,
            compiler_params=pltpu.CompilerParams(vmem_limit_bytes=megabytes << 20),
            cost_estimate=pl.CostEstimate(flops=flops, bytes_accessed=moved, transcendentals=exps),
        )(*arrays)

    return run


def valid_of(first, rows, length):
    return first + lax.broadcasted_iota(jnp.int32, (rows, 1), 0) < length


def moments(rows):
    centre = jnp.mean(rows, axis=-1, keepdims=True)
    centred = rows - centre
    inv_scale = lax.rsqrt(jnp.mean(centred * centred, axis=-1, keepdims=True) + EPSILON)
    return centred * inv_scale, inv_scale


def norm_back(grad_normed, normed, inv_scale):
    first_mean = jnp.mean(grad_normed, axis=-1, keepdims=True)
    second_mean = jnp.mean(grad_normed * normed, axis=-1, keepdims=True)
    return inv_scale * (grad_normed - first_mean - normed * second_mean)


def fold(rows):
    total = rows[:8]
    for at in range(8, rows.shape[0], 8):
        total = total + rows[at : at + 8]
    return total


def at_group(info, by, ways, share, visit):
    if share % LANES == 0:
        visit(pl.ds(pl.multiple_of((info[0] ^ by) * share, LANES), share))
        return
    for at in range(ways):

        @pl.when((info[0] ^ by) == at)
        def _():
            visit(slice(at * share, (at + 1) * share))


def neighbours(ways):
    return [by for by in (1, 3, 7, 15) if by < ways]


def edge_rows(frames, at):
    return slice(3 * frames + at * 3 * EDGE, 3 * frames + (at + 1) * 3 * EDGE)


def pack_kernel(ways, query, key, value, residual, grad_out, *refs):
    blocks, whole, ends, arrived = refs[:ways], refs[ways], refs[ways + 1], refs[ways + 2]
    info = [lax.axis_index("ctx")]
    frames, width = query.shape
    share, reach = width // ways, 2 * EDGE
    pairs = [(rows, whole.at[slot]) for slot, rows in enumerate((query, key, value))]
    for side, tail in enumerate((False, True)):
        for rows, start, count in ((residual, 0, reach), (grad_out, reach, EDGE)):
            first = frames - count if tail else 0
            pairs.append((rows.at[pl.ds(first, count)], ends.at[side, pl.ds(start, count)]))
    copies = [
        pltpu.make_async_copy(source, target, arrived.at[at])
        for at, (source, target) in enumerate(pairs)
    ]
    for copy in copies:
        copy.start()
    for slot, copy in enumerate(copies[:3]):
        copy.wait()
        for by in range(ways):

            def visit(lanes):
                blocks[by][slot * frames : (slot + 1) * frames, :] = whole[slot, :, lanes]

            at_group(info, by, ways, share, visit)
    for copy in copies[3:]:
        copy.wait()
    for by in neighbours(ways):
        side = jnp.where((info[0] ^ by) > info[0], 1, 0)
        for at in range(ways):
            blocks[by][edge_rows(frames, at), :] = ends[side, :, at * share : (at + 1) * share]


def unpack_kernel(ways, info, *refs):
    blocks, outs, arrived = refs[:ways], refs[ways:-1], refs[-1]
    share = blocks[0].shape[2]
    copies = []
    for by in range(ways):
        for slot, rows in enumerate(outs):
            lanes = pl.ds(pl.multiple_of((info[0] ^ by) * share, LANES), share)
            copy = pltpu.make_async_copy(
                blocks[by].at[slot], rows.at[:, lanes], arrived.at[len(copies)]
            )
            copy.start()
            copies.append(copy)
    for copy in copies:
        copy.wait()


def unpack_parts_kernel(ways, info, *refs):
    blocks, outs = refs[:ways], refs[ways:]
    share = blocks[0].shape[2]
    for by in range(ways):
        for slot, rows in enumerate(outs):

            def visit(lanes):
                rows[:, lanes] = blocks[by][slot]

            at_group(info, by, ways, share, visit)


def selector(columns, slim, position, width):
    wanted = columns + position * slim
    rows = lax.broadcasted_iota(jnp.int32, (width, columns.shape[1]), 0)
    return jnp.where(rows == wanted, 1.0, 0.0).astype(jnp.bfloat16)


def mask_kernel(slim, info, grad_out, point_weight, columns, masked, grad_act, *halves):
    frames, width = grad_out.shape
    valid = valid_of(info[0] * frames, frames, info[1])
    masked[...] = jnp.where(valid, grad_out[...].astype(jnp.float32), 0.0).astype(jnp.bfloat16)
    step = width // 3
    for at in range(0, width, step):
        grad_act[:, at : at + step] = dot(masked[...], point_weight[at : at + step, :], NT)
    across = len(halves)
    for by in range(across):
        chosen = selector(columns[...], slim, (info[0] % across) ^ by, width)
        halves[by][...] = dot(masked[...], chosen).astype(jnp.bfloat16)


def mask_edges_kernel(frames, info, before, after, point_weight, grad_act):
    width = grad_act.shape[1]
    first = info[0] * frames
    sides = []
    for side, start in ((before, first - EDGE), (after, first + frames)):
        valid = valid_of(start, EDGE, info[1])
        rows = side[2 * EDGE :, :].astype(jnp.float32)
        sides.append(jnp.where(valid, rows, 0.0).astype(jnp.bfloat16))
    masked = jnp.concatenate(sides, axis=0)
    step = width // 3
    for at in range(0, width, step):
        grad_act[:, at : at + step] = dot(masked, point_weight[at : at + step, :], NT)


def gather_heads(info, blocks, query, key, value, bias):
    frames = query.shape[0] // len(blocks)
    for by, block in enumerate(blocks):
        rows = slice(by * frames, (by + 1) * frames)
        query[rows] = block[:frames, :] * jnp.bfloat16(SCALE)
        key[rows] = block[frames : 2 * frames, :]
        value[rows] = block[2 * frames : 3 * frames, :]
        valid = valid_of((info[0] ^ by) * frames, frames, info[1])
        bias[rows] = jnp.broadcast_to(jnp.where(valid, 0.0, NEG_FILL), (frames, LANES))


def attend_kernel(ways, info, *refs):
    blocks, outs = refs[:ways], refs[ways : 2 * ways]
    attended, log_total, before, after, query, key, value, bias, turned = refs[2 * ways :]
    gather_heads(info, blocks, query, key, value, bias)
    total_frames, share = query.shape
    frames = total_frames // ways
    for side, other in ((before, info[0] - 1), (after, info[0] + 1)):
        side[...] = jnp.zeros_like(side)
        for by in neighbours(ways):

            @pl.when((info[0] ^ other) == by)
            def _():
                for at in range(ways):
                    lanes = slice(at * share, (at + 1) * share)
                    side[:, lanes] = blocks[by][edge_rows(frames, at), :]

    for head in range(share // HEAD_DIM):
        part = slice(head * HEAD_DIM, (head + 1) * HEAD_DIM)
        spread = jnp.concatenate([bias[...]] * (total_frames // LANES), axis=1)
        scores = dot(key[:, part], query[:, part], NT) + spread
        row_max = jnp.max(scores, axis=0, keepdims=True)
        weights = jnp.exp(scores - row_max)
        total = jnp.sum(weights, axis=0, keepdims=True)
        turned[part, :] = dot(value[:, part], weights.astype(jnp.bfloat16), TN) / total
        log_total[head : head + 1, :] = row_max + jnp.log(total)
    attended[...] = turned[...].T.astype(jnp.bfloat16)
    reach = 2 * EDGE
    for by in range(ways):
        other = info[0] ^ by
        before = (info[0] ^ jnp.maximum(other - 1, 0)) * frames + frames - reach
        after = (info[0] ^ jnp.minimum(other + 1, ways - 1)) * frames
        outs[by][:reach] = attended[pl.ds(pl.multiple_of(before, reach), reach), :]
        outs[by][reach : reach + frames] = attended[by * frames : (by + 1) * frames, :]
        outs[by][reach + frames :] = attended[pl.ds(pl.multiple_of(after, reach), reach), :]


def attend_back_kernel(ways, info, *refs):
    blocks, messages = refs[:ways], refs[ways : 2 * ways]
    attended, log_total = refs[2 * ways : 2 * ways + 2]
    outs = refs[2 * ways + 2 : 3 * ways + 2]
    query, key, value, bias, grad, turned = refs[3 * ways + 2 :]
    gather_heads(info, blocks, query, key, value, bias)
    total_frames, share = query.shape
    frames = total_frames // ways
    for by in range(ways):
        grad[by * frames : (by + 1) * frames] = messages[by][:frames, :]
    turned[...] = (grad[...].astype(jnp.float32) * attended[...].astype(jnp.float32)).T
    for head in range(share // HEAD_DIM):
        part = slice(head * HEAD_DIM, (head + 1) * HEAD_DIM)
        delta = jnp.sum(turned[part, :], axis=0, keepdims=True)
        spread = jnp.concatenate([bias[...]] * (total_frames // LANES), axis=1)
        scores = dot(key[:, part], query[:, part], NT) + spread
        probs = jnp.exp(scores - log_total[head : head + 1, :])
        value_grad = dot(probs.astype(jnp.bfloat16), grad[:, part])
        prob_grad = dot(value[:, part], grad[:, part], NT)
        score_grad = (probs * (prob_grad - delta)).astype(jnp.bfloat16)
        key_grad = dot(score_grad, query[:, part])
        turned[part, :] = dot(key[:, part], score_grad, TN) * SCALE
        for by in range(ways):
            rows = slice(by * frames, (by + 1) * frames)
            outs[by][1, :, part] = key_grad[rows].astype(jnp.bfloat16)
            outs[by][2, :, part] = value_grad[rows].astype(jnp.bfloat16)
    query_grad = turned[...].T.astype(jnp.bfloat16)
    for by in range(ways):
        outs[by][0] = query_grad[by * frames : (by + 1) * frames]


def gather_kernel(ways, info, *refs):
    blocks, messages = refs[:ways], refs[ways:]
    frames, share, reach = messages[0].shape[0], blocks[0].shape[1], 2 * EDGE
    for by, message in enumerate(messages):
        lacking = [slot for slot in range(ways) if slot != by]
        for at, slot in enumerate(lacking):
            message[:, at * share : (at + 1) * share] = blocks[slot][reach : reach + frames, :]


def project_kernel(ways, info, *refs):
    blocks = refs[:ways]
    residual, before, after, out_weight, params = refs[ways : ways + 5]
    mixed, conv_in, attended = refs[ways + 5 :]
    frames, width = residual.shape
    share = width // ways
    reach = 2 * EDGE
    rows = frames + 2 * reach
    for by in range(ways):
        for at in range(ways):

            @pl.when((info[0] ^ by) == at)
            def _():
                attended[:, at * share : (at + 1) * share] = blocks[by][...]

    step = width // 3
    for at in range(0, width, step):
        part = slice(at, at + step)
        mixed[:reach, part] = before[:reach, part].astype(jnp.float32)
        mixed[reach : reach + frames, part] = residual[:, part].astype(jnp.float32)
        mixed[reach + frames :, part] = after[:reach, part].astype(jnp.float32)
        mixed[:, part] += dot(attended[...], out_weight[:, part])

    gain = params[31:32, :]
    first = info[0] * frames - reach

    def band(index, carry):
        at = pl.ds(pl.multiple_of(index * BAND, BAND), BAND)
        normed, _ = moments(mixed[at, :])
        position = first + index * BAND + lax.broadcasted_iota(jnp.int32, (BAND, 1), 0)
        valid = (position >= 0) & (position < info[1])
        conv_in[at, :] = jnp.where(valid, normed * gain, 0.0).astype(jnp.bfloat16)
        return carry

    lax.fori_loop(0, rows // BAND, band, 0)


def stride_of(rows):
    return rows // 8 + 1


def in_columns(ref, rows):
    for at in range(ref.shape[0]):
        ref[at, : rows.shape[0]] = rows[:, at * LANES : (at + 1) * LANES].astype(jnp.float32)


def from_columns(ref, rows):
    return jnp.concatenate([ref[at, rows, :] for at in range(ref.shape[0])], axis=1)


def strided(ref, index, start, stride):
    return ref[index, pl.ds(start, 8, stride=stride), :]


def depthwise(padded, taps, tap_of, out, rows):
    stride = stride_of(rows)

    def column(index, carry):
        part = pl.ds(pl.multiple_of(index * LANES, LANES), LANES)
        cells = [strided(padded, index, at + 1, stride) for at in range(stride + 2 * EDGE - 2)]
        total = [None] * stride
        for offset in range(1, 2 * EDGE):
            tap = tap_of(offset)
            scale = jnp.broadcast_to(taps[tap : tap + 1, part], (8, LANES))
            for at in range(stride):
                term = cells[at + offset - 1] * scale
                total[at] = term if total[at] is None else total[at] + term
        for at in range(stride):
            out[index, pl.ds(at, 8, stride=stride), :] = total[at]
        return carry

    lax.fori_loop(0, out.shape[0], column, 0)


def tap_grads(padded, grad, start, rows, taps):
    stride = rows // 8

    def column(index, carry):
        part = pl.ds(pl.multiple_of(index * LANES, LANES), LANES)
        cells = [
            strided(padded, index, start + at + 1, stride) for at in range(stride + 2 * EDGE - 2)
        ]
        grads = [strided(grad, index, start + at, stride) for at in range(stride)]
        for tap in range(2 * EDGE - 1):
            total = cells[tap] * grads[0]
            for at in range(1, stride):
                total = total + cells[at + tap] * grads[at]
            taps[tap : tap + 1, part] = jnp.sum(total, axis=0, keepdims=True)
        return carry

    lax.fori_loop(0, grad.shape[0], column, 0)


def conv_kernel_body(across, info, conv_in, params, grad_own, grad_edges, *refs):
    count = (len(refs) - 8 + NEAR) // 2
    messages = refs[: count - NEAR]
    conv_act, grad_conv, sums = refs[count - NEAR : count - NEAR + 3]
    halves = refs[count - NEAR + 3 : -5]
    padded, conv, grad_act, bias_sum, gain_sum = refs[-5:]
    frames, width = grad_own.shape
    rows, wide = frames + 2 * EDGE, frames + 4 * EDGE
    in_columns(padded, conv_in[...])
    padded[:, wide:, :] = jnp.zeros((width // LANES, padded.shape[1] - wide, LANES), jnp.float32)
    grad_act[:EDGE] = grad_edges[:EDGE]
    grad_act[EDGE : EDGE + frames] = grad_own[...]
    grad_act[EDGE + frames :] = grad_edges[EDGE:]
    depthwise(padded, params, lambda offset: offset - 1, conv, rows)
    bias, gain = params[32:33, :], params[33:34, :]
    bias_sum[...] = jnp.zeros_like(bias_sum)
    gain_sum[...] = jnp.zeros_like(gain_sum)

    def band(index, carry):
        at = pl.ds(pl.multiple_of(index * BAND, BAND), BAND)
        normed, inv_scale = moments(from_columns(conv, at) + bias)
        scaled = normed * gain
        gate = 0.5 + 0.5 * jnp.tanh(0.5 * scaled)
        conv_act[at, :] = (scaled * gate).astype(jnp.bfloat16)
        grad_scaled = grad_act[at, :] * gate * (1.0 + scaled * (1.0 - gate))
        grad_rows = norm_back(grad_scaled * gain, normed, inv_scale)
        for column in range(width // LANES):
            grad_conv[column, at, :] = grad_rows[:, column * LANES : (column + 1) * LANES]

        @pl.when((index >= EDGE // BAND) & (index < (EDGE + frames) // BAND))
        def _():
            bias_sum[...] += fold(grad_rows)
            gain_sum[...] += fold(grad_scaled * normed)

        return carry

    lax.fori_loop(0, rows // BAND, band, 0)
    sums[0:1, :] = jnp.sum(bias_sum[...], axis=0, keepdims=True)
    sums[1:2, :] = jnp.sum(gain_sum[...], axis=0, keepdims=True)
    half = width // 2
    for by, block in enumerate(halves):
        for at in range(2):

            @pl.when((info[0] ^ by) // across == at)
            def _():
                block[:, :half] = conv_act[EDGE : EDGE + frames, at * half : (at + 1) * half]

        if by >= NEAR:
            block[:, half:] = messages[by - NEAR][...]


def block_out_kernel(info, conv_act, mixed, point_weight, block_out):
    frames, width = block_out.shape
    step = width // 3
    for at in range(0, width, step):
        part = slice(at, at + step)
        block_out[:, part] = (
            mixed[2 * EDGE : 2 * EDGE + frames, part]
            + dot(conv_act[EDGE : EDGE + frames, :], point_weight[:, part])
        ).astype(jnp.bfloat16)


def conv_back_kernel(ways, slim, info, grad_conv, conv_in, params, masked, mixed, out_weight, *refs):
    conv_sums, grad_residual, messages = refs[0], refs[1], refs[2 : 2 + ways]
    padded, padded_in, conv, gain_sum, taps, packed, chosen = refs[2 + ways :]
    frames, width = grad_residual.shape
    share = width // ways
    reached = frames + 2 * EDGE
    padded[:, :reached, :] = grad_conv[...].astype(jnp.bfloat16).astype(jnp.float32)
    padded[:, reached:, :] = jnp.zeros(
        (width // LANES, padded.shape[1] - reached, LANES), jnp.float32
    )
    depthwise(padded, params, lambda offset: 31 - offset, conv, frames)
    gain = params[31:32, :]
    gain_sum[...] = jnp.zeros_like(gain_sum)

    def band(index, carry):
        at = pl.ds(pl.multiple_of(index * BAND, BAND), BAND)
        own_mixed = pl.ds(pl.multiple_of(index * BAND + 2 * EDGE, BAND), BAND)
        valid = valid_of(info[0] * frames + index * BAND, BAND, info[1])
        grad_in = jnp.where(valid, from_columns(conv, at), 0.0)
        normed, inv_scale = moments(mixed[own_mixed, :])
        grad_mixed = norm_back(grad_in * gain, normed, inv_scale)
        gain_sum[...] += fold(grad_in * normed)
        grad_residual[at, :] = (masked[at, :].astype(jnp.float32) + grad_mixed).astype(
            jnp.bfloat16
        )
        return carry

    lax.fori_loop(0, frames // BAND, band, 0)
    for by in range(ways):
        at = pl.ds(pl.multiple_of((info[0] ^ by) * share, share), share)
        messages[by][:frames] = dot(grad_residual[...], out_weight[at, :], NT).astype(jnp.bfloat16)

    in_columns(padded_in, conv_in[...])
    tap_grads(padded_in, grad_conv, EDGE, frames, taps)
    taps[31:32, :] = conv_sums[0:1, :]
    taps[32:33, :] = jnp.sum(gain_sum[...], axis=0, keepdims=True)
    taps[33:34, :] = conv_sums[1:2, :]
    taps[34:, :] = jnp.zeros((EXTRA - 34, width), jnp.float32)
    packed[:frames] = grad_residual[...]
    packed[frames:] = taps[...].astype(jnp.bfloat16)
    for at in range(ways):
        pieces = []
        for start in range(at * slim, width, ways * slim):
            pieces.append(packed[:, start : start + slim])
        chosen[at] = jnp.concatenate(pieces, axis=1)
    for by in range(ways):
        messages[by][frames:] = chosen[info[0] ^ by]


def split_rows(info, parts, shift, terms, sent, kept):
    rows = terms.shape[0] // parts
    low = (1 << shift) - 1

    def start(at, bit):
        return (((at & ~low) << 1) | (bit << shift) | (at & low)) * rows

    for bit in range(2):

        @pl.when((info[2] >> shift) & 1 == bit)
        def _():
            for at in range(parts // 2):
                own, other = start(at, bit), start(at, 1 - bit)
                kept[at] = terms[own : own + rows, :]
                sent[at] = terms[other : other + rows, :].astype(jnp.bfloat16)


def point_kernel(ways, parts, info, *refs):
    grads, acts, (sent, kept, terms) = refs[:ways], refs[ways : 2 * ways], refs[2 * ways :]
    extent, half = terms.shape
    left = jnp.concatenate([grad[:, grad.shape[1] - extent :] for grad in grads], axis=0)
    right = jnp.concatenate([act[:, :half] for act in acts], axis=0)
    step = terms.shape[1] // 2
    for at in range(0, 2 * step, step):
        part = slice(at, at + step)
        terms[:, part] = dot(left, right[:, part], TN)
    split_rows(info, parts, 1, terms, sent, kept)


def point_sum_kernel(across, info, kept, received, own, other):
    rows = own.shape[0]
    total = kept[0] + received[0].astype(jnp.float32)
    for at in range(2):

        @pl.when(info[0] // across == at)
        def _():
            own[...] = total[at * rows : (at + 1) * rows, :]
            other[...] = total[(1 - at) * rows : (2 - at) * rows, :].astype(jnp.bfloat16)


def weight_kernel(ways, parts, info, *refs):
    grads, rows = refs[:ways], refs[ways : 2 * ways]
    attended, sent, kept, terms = refs[2 * ways :]
    total_frames, share = attended.shape
    frames = total_frames // ways
    width = ways * share
    slim = share // parts
    left = jnp.concatenate([grad[frames : 2 * frames, :] for grad in grads], axis=0)
    for slot in range(ways):
        if slot == 0:
            right = attended[...]
        else:
            pieces = []
            for by in range(ways):
                at = (by ^ slot) - (1 if (by ^ slot) > by else 0)
                first = (width // 2 if by >= NEAR else 0) + at * share
                pieces.append(rows[by][:, first : first + share])
            right = jnp.concatenate(pieces, axis=0)
        terms[:, slot * share : (slot + 1) * share] = dot(left, right, TN)
    small = jnp.zeros((EXTRA, share), jnp.float32)
    for grad in grads:
        small = small + grad[2 * frames :, :].astype(jnp.float32)
    filler = jnp.zeros((LANES - EXTRA, share), jnp.float32)
    terms[:, width:] = jnp.concatenate([small, filler], axis=0).T
    split_rows(info, parts, 0, terms, sent, kept)


def halve_kernel(shift, info, kept, received, sent, still_kept):
    bit = (info[2] >> shift) & 1
    for at in range(sent.shape[0]):
        own, other = 2 * at + bit, 2 * at + 1 - bit
        still_kept[at] = kept[own] + received[own].astype(jnp.float32)
        sent[at] = (kept[other] + received[other].astype(jnp.float32)).astype(jnp.bfloat16)


def finish_kernel(ways, info, kept, received, own, other, weight, taps, vectors, point):
    width = weight.shape[1]
    share, half = width // ways, width // 2
    for at in range(2):

        @pl.when(info[0] // (ways // 2) == at)
        def _():
            point[:, at * half : (at + 1) * half] = own[...]
            point[:, (1 - at) * half : (2 - at) * half] = other[...].astype(jnp.float32)

    total = kept[0] + received[0].astype(jnp.float32)
    for by in range(ways):
        for at in range(ways):

            @pl.when((info[0] ^ by) == at)
            def _():
                weight[:, at * share : (at + 1) * share] = total[:, by * share : (by + 1) * share]

    small = total[:, width:].T
    taps[...] = small[:31]
    vectors[...] = small[31:34]


def swap(block, axis, by):
    return lax.ppermute(block, axis, [(i, i ^ by) for i in range(lax.axis_size(axis))])


def swap_all(blocks, axis, step=1):
    return [blocks[0]] + [swap(block, axis, step * by) for by, block in enumerate(blocks[1:], 1)]


def local(
    residual_in,
    query_rows,
    key_rows,
    value_rows,
    lengths,
    out_weight,
    norm_gain,
    conv_kernel,
    conv_bias,
    conv_gain,
    point_weight,
    grad_out,
):
    ways = lax.axis_size("ctx")
    parts = lax.axis_size("dp")
    own = lax.axis_index("ctx")
    place = lax.axis_index("dp")
    frames, width = residual_in.shape[1:]
    share = width // ways
    slim = share // parts
    heads = HEADS // ways
    every = ways * frames
    across = ways // 2
    broad = width // across
    half = width // 2
    tiles = width // LANES
    bf16, f32 = jnp.bfloat16, jnp.float32
    square = 2 * frames * width * width
    rows_bytes = 2 * frames * width
    reached, wide = frames + 2 * EDGE, frames + 4 * EDGE

    info = jnp.stack([own, lengths[0], place]).astype(jnp.int32)
    params = jnp.concatenate(
        [conv_kernel, norm_gain[None], conv_bias[None], conv_gain[None]], axis=0
    )

    def every_nth(count, group):
        at = jnp.arange(count, dtype=jnp.int32)
        return ((at // slim) * (group * slim) + at % slim)[None]

    by_tiles = share % LANES == 0
    packed_rows = [3 * frames + 3 * EDGE * ways * (by in neighbours(ways)) for by in range(ways)]
    packed = call(
        functools.partial(pack_kernel, ways),
        "pack",
        [((rows, share), bf16) for rows in packed_rows],
        scratch=[((3, frames, width), bf16), ((2, 3 * EDGE, width), bf16)],
        semaphores=7,
        far=("in",),
        megabytes=58,
        moved=6 * rows_bytes,
    )(query_rows[0], key_rows[0], value_rows[0], residual_in[0], grad_out[0])
    packed = swap_all(packed, "ctx")

    masked, grad_own, *masked_halves = call(
        functools.partial(mask_kernel, slim),
        "mask",
        [((frames, width), bf16), ((frames, width), f32)] + [((frames, broad), bf16)] * across,
        flops=2 * square,
        moved=6 * rows_bytes + 2 * width * width,
    )(info, grad_out[0], point_weight, every_nth(broad, across))
    packed[1], masked_halves = lax.optimization_barrier((packed[1], masked_halves))
    masked_halves = swap_all([masked_halves[by % across] for by in range(ways)], "ctx")

    packed, masked = lax.optimization_barrier((packed, masked))
    head_scratch = [((every, share), bf16)] * 3 + [((every, LANES), f32)]
    pair_flops = 2 * heads * every * every * HEAD_DIM
    *returned, attended, log_total, before, after = call(
        functools.partial(attend_kernel, ways),
        "attend",
        [((wide, share), bf16)] * ways + [((every, share), bf16), ((heads, every), f32)]
        + [((3 * EDGE, width), bf16)] * 2,
        scratch=head_scratch + [((share, every), f32)],
        flops=8 * pair_flops,
        moved=4 * rows_bytes,
        exps=heads * every * every,
    )(info, *packed)
    returned, masked_halves[1:NEAR] = lax.optimization_barrier((returned, masked_halves[1:NEAR]))
    returned = swap_all(returned, "ctx")
    grad_edges = call(
        functools.partial(mask_edges_kernel, frames),
        "mask_edges",
        [((2 * EDGE, width), f32)],
        flops=square,
        moved=2 * width * width,
    )(info, before, after, point_weight)[0]
    returned, grad_edges, masked_halves = lax.optimization_barrier(
        (returned, grad_edges, masked_halves)
    )
    messages = call(
        functools.partial(gather_kernel, ways),
        "gather",
        [((frames, width - share), bf16)] * ways,
        moved=8 * rows_bytes,
    )(info, *returned)
    arrived = swap_all(messages[:NEAR], "ctx")

    returned, messages = lax.optimization_barrier((returned, messages))
    mixed, conv_in = call(
        functools.partial(project_kernel, ways),
        "project",
        [((wide, width), f32), ((wide, width), bf16)],
        scratch=[((wide, width), bf16)],
        flops=square,
        moved=6 * rows_bytes + 2 * width * width,
    )(info, *returned, residual_in[0], before, after, out_weight, params)
    spread = 8 * stride_of(reached)
    conv_act, grad_conv, conv_sums, *act_halves = call(
        functools.partial(conv_kernel_body, across),
        "conv",
        [
            ((reached, width), bf16),
            ((tiles, reached, LANES), f32),
            ((2, width), f32),
        ]
        + [((frames, half), bf16)] * NEAR
        + [((frames, half + width - share), bf16)] * (ways - NEAR),
        scratch=[
            ((tiles, spread + 2 * EDGE, LANES), f32),
            ((tiles, spread, LANES), f32),
            ((reached, width), f32),
            ((8, width), f32),
            ((8, width), f32),
        ],
        flops=frames * width * 4000,
        moved=6 * rows_bytes,
        exps=frames * width,
    )(info, conv_in, params, grad_own, grad_edges, *messages[NEAR:])
    arrived, act_halves, grad_conv = lax.optimization_barrier((arrived, act_halves, grad_conv))
    act_halves = swap_all(act_halves, "ctx")

    spread = 8 * stride_of(frames)
    grad_residual, *grad_messages = call(
        functools.partial(conv_back_kernel, ways, slim),
        "conv_back",
        [((frames, width), bf16)] + [((2 * frames + EXTRA, share), bf16)] * ways,
        scratch=[
            ((tiles, spread + 2 * EDGE, LANES), f32),
            ((tiles, wide, LANES), f32),
            ((tiles, spread, LANES), f32),
            ((8, width), f32),
            ((EXTRA, width), f32),
            ((frames + EXTRA, width), bf16),
            ((ways, frames + EXTRA, share), bf16),
        ],
        flops=frames * width * 8000,
        moved=8 * rows_bytes + 2 * width * width,
    )(
        info,
        grad_conv,
        conv_in,
        params,
        masked,
        mixed,
        out_weight,
        conv_sums,
    )
    act_halves, grad_messages = lax.optimization_barrier((act_halves, grad_messages))
    messages = arrived + act_halves[NEAR:]
    grad_messages = swap_all(grad_messages, "ctx")

    block_out = call(
        block_out_kernel,
        "block_out",
        [((frames, width), bf16)],
        flops=square,
        moved=4 * rows_bytes + 2 * width * width,
    )(info, conv_act, mixed, point_weight)[0]

    def halve(kept, received, shift):
        extent = (kept.shape[0] // 2,) + kept.shape[1:]
        return call(
            functools.partial(halve_kernel, shift),
            "halve",
            [(extent, bf16), (extent, f32)],
            moved=16 * extent[0] * extent[1] * extent[2],
        )(info, kept, received)

    def reduce(kept, received, first):
        for shift in range(first + 1, parts.bit_length() - 1):
            sent, kept = halve(kept, received, shift)
            received = swap(sent, "dp", 2**shift)
        return kept, received

    point_half = (parts // 2, 2 * slim, half)
    point_sent, point_kept = call(
        functools.partial(point_kernel, ways, parts),
        "point_terms",
        [(point_half, bf16), (point_half, f32)],
        scratch=[((broad, half), f32)],
        flops=square,
        moved=8 * rows_bytes,
    )(info, *masked_halves, *act_halves)
    point_sent, point_kept = halve(point_kept, swap(point_sent, "dp", 2), 0)
    grad_messages, point_sent, block_out = lax.optimization_barrier(
        (grad_messages, point_sent, block_out)
    )
    late_messages = grad_messages
    point_received = swap(point_sent, "dp", 1)
    for shift in range(2, parts.bit_length() - 1):
        point_sent, point_kept = halve(point_kept, point_received, shift)
        late_messages, point_sent = lax.optimization_barrier((late_messages, point_sent))
        point_received = swap(point_sent, "dp", 2**shift)
    point_own, point_other = call(
        functools.partial(point_sum_kernel, across),
        "point_sum",
        [((slim, half), f32), ((slim, half), bf16)],
        moved=slim * width * (parts + 8),
    )(info, point_kept, point_received)
    point_other = swap(point_other, "ctx", across)

    extent = width + LANES
    core_half = (parts // 2, slim, extent)
    sent, kept = call(
        functools.partial(weight_kernel, ways, parts),
        "out_terms",
        [(core_half, bf16), (core_half, f32)],
        scratch=[((share, extent), f32)],
        flops=square,
        moved=10 * rows_bytes,
    )(info, *grad_messages, *messages, attended)
    pieces = reduce(kept, swap(sent, "dp", 1), 0)
    out_total, taps, vectors, point_total = call(
        functools.partial(finish_kernel, ways),
        "finish",
        [((slim, width), f32), ((31, slim), f32), ((3, slim), f32), ((slim, width), f32)],
        moved=slim * extent * (parts + 8),
    )(info, *pieces, point_own, point_other)

    grad_packed = call(
        functools.partial(attend_back_kernel, ways),
        "attend_back",
        [((3, frames, share), bf16)] * ways,
        scratch=head_scratch + [((every, share), bf16), ((share, every), f32)],
        flops=20 * pair_flops,
        moved=8 * rows_bytes,
        exps=heads * every * every,
    )(info, *packed, *late_messages, attended, log_total)
    grad_packed = swap_all(grad_packed, "ctx")
    grad_query, grad_key, grad_value = call(
        functools.partial(unpack_kernel if by_tiles else unpack_parts_kernel, ways),
        "unpack",
        [((frames, width), bf16)] * 3,
        semaphores=3 * ways if by_tiles else 0,
        far=("out",) if by_tiles else (),
        moved=6 * rows_bytes,
    )(info, *grad_packed)

    return (
        block_out[None],
        grad_residual[None],
        grad_query[None],
        grad_key[None],
        grad_value[None],
        out_total.T,
        point_total.T,
        taps,
        vectors,
    )


def solution(mesh):
    rows = P("dp", "ctx", None)
    columns = P(None, ("dp", "ctx"))
    in_specs = (rows, rows, rows, rows, P("dp"), P(), P(), P(), P(), P(), P(), rows)
    out_specs = (rows,) * 5 + (columns,) * 4
    return jax.shard_map(local, mesh=mesh, in_specs=in_specs, out_specs=out_specs, check_vma=False)
```

```python
import functools

import jax
import jax.numpy as jnp
from jax import lax
from jax.experimental import pallas as pl
from jax.experimental.pallas import tpu as pltpu
from jax.sharding import PartitionSpec as P

HEADS = 24
HEAD_DIM = 64
SCALE = HEAD_DIM ** (-0.5)

NEG_FILL = -1e30
EPSILON = 1e-05

LANES = 128
EDGE = 16
NEAR = 3
BAND = 16
EXTRA = 48

NN = (((1,), (0,)), ((), ()))
NT = (((1,), (1,)), ((), ()))
TN = (((0,), (0,)), ((), ()))


def dot(left, right, dims=NN):
    return lax.dot_general(left, right, dims, preferred_element_type=jnp.float32)


def call(
    kernel, name, outs, scratch=(), semaphores=0, far=(), megabytes=28, flops=0, moved=0, exps=0
):
    vmem = pl.BlockSpec(memory_space=pltpu.VMEM)
    smem = pl.BlockSpec(memory_space=pltpu.SMEM)
    anywhere = pl.BlockSpec(memory_space=pl.ANY)

    def run(*arrays):
        scratches = [pltpu.VMEM(shape, kind) for shape, kind in scratch]
        if semaphores:
            scratches.append(pltpu.SemaphoreType.DMA((semaphores,)))
        return pl.pallas_call(
            kernel,
            name=name,
            in_specs=[smem if a.ndim == 1 else anywhere if "in" in far else vmem for a in arrays],
            out_specs=[anywhere if "out" in far else vmem] * len(outs),
            out_shape=[jax.ShapeDtypeStruct(shape, kind) for shape, kind in outs],
            scratch_shapes=scratches,
            compiler_params=pltpu.CompilerParams(vmem_limit_bytes=megabytes << 20),
            cost_estimate=pl.CostEstimate(flops=flops, bytes_accessed=moved, transcendentals=exps),
        )(*arrays)

    return run


def valid_of(first, rows, length):
    return first + lax.broadcasted_iota(jnp.int32, (rows, 1), 0) < length


def moments(rows):
    centre = jnp.mean(rows, axis=-1, keepdims=True)
    centred = rows - centre
    inv_scale = lax.rsqrt(jnp.mean(centred * centred, axis=-1, keepdims=True) + EPSILON)
    return centred * inv_scale, inv_scale


def norm_back(grad_normed, normed, inv_scale):
    first_mean = jnp.mean(grad_normed, axis=-1, keepdims=True)
    second_mean = jnp.mean(grad_normed * normed, axis=-1, keepdims=True)
    return inv_scale * (grad_normed - first_mean - normed * second_mean)


def fold(rows):
    total = rows[:8]
    for at in range(8, rows.shape[0], 8):
        total = total + rows[at : at + 8]
    return total


def at_group(info, by, ways, share, visit):
    if share % LANES == 0:
        visit(pl.ds(pl.multiple_of((info[0] ^ by) * share, LANES), share))
        return
    for at in range(ways):

        @pl.when((info[0] ^ by) == at)
        def _():
            visit(slice(at * share, (at + 1) * share))


def neighbours(ways):
    return [by for by in (1, 3, 7, 15) if by < ways]


def edge_rows(frames, at):
    return slice(3 * frames + at * 3 * EDGE, 3 * frames + (at + 1) * 3 * EDGE)


def pack_kernel(ways, query, key, value, residual, grad_out, *refs):
    blocks, whole, ends, arrived = refs[:ways], refs[ways], refs[ways + 1], refs[ways + 2]
    info = [lax.axis_index("ctx")]
    frames, width = query.shape
    share, reach = width // ways, 2 * EDGE
    pairs = [(rows, whole.at[slot]) for slot, rows in enumerate((query, key, value))]
    for side, tail in enumerate((False, True)):
        for rows, start, count in ((residual, 0, reach), (grad_out, reach, EDGE)):
            first = frames - count if tail else 0
            pairs.append((rows.at[pl.ds(first, count)], ends.at[side, pl.ds(start, count)]))
    copies = [
        pltpu.make_async_copy(source, target, arrived.at[at])
        for at, (source, target) in enumerate(pairs)
    ]
    for copy in copies:
        copy.start()
    for slot, copy in enumerate(copies[:3]):
        copy.wait()
        for by in range(ways):

            def visit(lanes):
                blocks[by][slot * frames : (slot + 1) * frames, :] = whole[slot, :, lanes]

            at_group(info, by, ways, share, visit)
    for copy in copies[3:]:
        copy.wait()
    for by in neighbours(ways):
        side = jnp.where((info[0] ^ by) > info[0], 1, 0)
        for at in range(ways):
            blocks[by][edge_rows(frames, at), :] = ends[side, :, at * share : (at + 1) * share]


def unpack_kernel(ways, info, *refs):
    blocks, outs, arrived = refs[:ways], refs[ways:-1], refs[-1]
    share = blocks[0].shape[2]
    copies = []
    for by in range(ways):
        for slot, rows in enumerate(outs):
            lanes = pl.ds(pl.multiple_of((info[0] ^ by) * share, LANES), share)
            copy = pltpu.make_async_copy(
                blocks[by].at[slot], rows.at[:, lanes], arrived.at[len(copies)]
            )
            copy.start()
            copies.append(copy)
    for copy in copies:
        copy.wait()


def unpack_parts_kernel(ways, info, *refs):
    blocks, outs = refs[:ways], refs[ways:]
    share = blocks[0].shape[2]
    for by in range(ways):
        for slot, rows in enumerate(outs):

            def visit(lanes):
                rows[:, lanes] = blocks[by][slot]

            at_group(info, by, ways, share, visit)


def selector(columns, slim, position, width):
    wanted = columns + position * slim
    rows = lax.broadcasted_iota(jnp.int32, (width, columns.shape[1]), 0)
    return jnp.where(rows == wanted, 1.0, 0.0).astype(jnp.bfloat16)


def mask_kernel(slim, info, grad_out, point_weight, columns, block, *refs):
    masked, grad_act, own_block, halves = refs[0], refs[1], refs[2], refs[3:]
    own_block[...] = block[...]
    frames, width = grad_out.shape
    valid = valid_of(info[0] * frames, frames, info[1])
    masked[...] = jnp.where(valid, grad_out[...].astype(jnp.float32), 0.0).astype(jnp.bfloat16)
    step = width // 3
    for at in range(0, width, step):
        grad_act[:, at : at + step] = dot(masked[...], point_weight[at : at + step, :], NT)
    across = len(halves)
    for by in range(across):
        chosen = selector(columns[...], slim, (info[0] % across) ^ by, width)
        halves[by][...] = dot(masked[...], chosen).astype(jnp.bfloat16)


def mask_edges_kernel(frames, info, before, after, point_weight, grad_act):
    width = grad_act.shape[1]
    first = info[0] * frames
    sides = []
    for side, start in ((before, first - EDGE), (after, first + frames)):
        valid = valid_of(start, EDGE, info[1])
        rows = side[2 * EDGE :, :].astype(jnp.float32)
        sides.append(jnp.where(valid, rows, 0.0).astype(jnp.bfloat16))
    masked = jnp.concatenate(sides, axis=0)
    step = width // 3
    for at in range(0, width, step):
        grad_act[:, at : at + step] = dot(masked, point_weight[at : at + step, :], NT)


def gather_heads(info, blocks, query, key, value, bias):
    frames = query.shape[0] // len(blocks)
    for by, block in enumerate(blocks):
        rows = slice(by * frames, (by + 1) * frames)
        query[rows] = block[:frames, :] * jnp.bfloat16(SCALE)
        key[rows] = block[frames : 2 * frames, :]
        value[rows] = block[2 * frames : 3 * frames, :]
        valid = valid_of((info[0] ^ by) * frames, frames, info[1])
        bias[rows] = jnp.broadcast_to(jnp.where(valid, 0.0, NEG_FILL), (frames, LANES))


def attend_kernel(ways, info, *refs):
    blocks, outs = refs[:ways], refs[ways : 2 * ways]
    attended, log_total, before, after, query, key, value, bias, turned = refs[2 * ways :]
    gather_heads(info, blocks, query, key, value, bias)
    total_frames, share = query.shape
    frames = total_frames // ways
    for side, other in ((before, info[0] - 1), (after, info[0] + 1)):
        side[...] = jnp.zeros_like(side)
        for by in neighbours(ways):

            @pl.when((info[0] ^ other) == by)
            def _():
                for at in range(ways):
                    lanes = slice(at * share, (at + 1) * share)
                    side[:, lanes] = blocks[by][edge_rows(frames, at), :]

    for head in range(share // HEAD_DIM):
        part = slice(head * HEAD_DIM, (head + 1) * HEAD_DIM)
        spread = jnp.concatenate([bias[...]] * (total_frames // LANES), axis=1)
        scores = dot(key[:, part], query[:, part], NT) + spread
        row_max = jnp.max(scores, axis=0, keepdims=True)
        weights = jnp.exp(scores - row_max)
        total = jnp.sum(weights, axis=0, keepdims=True)
        turned[part, :] = dot(value[:, part], weights.astype(jnp.bfloat16), TN) / total
        log_total[head : head + 1, :] = row_max + jnp.log(total)
    attended[...] = turned[...].T.astype(jnp.bfloat16)
    reach = 2 * EDGE
    for by in range(ways):
        other = info[0] ^ by
        before = (info[0] ^ jnp.maximum(other - 1, 0)) * frames + frames - reach
        after = (info[0] ^ jnp.minimum(other + 1, ways - 1)) * frames
        outs[by][:reach] = attended[pl.ds(pl.multiple_of(before, reach), reach), :]
        outs[by][reach : reach + frames] = attended[by * frames : (by + 1) * frames, :]
        outs[by][reach + frames :] = attended[pl.ds(pl.multiple_of(after, reach), reach), :]


def attend_back_kernel(ways, info, *refs):
    blocks, messages = refs[:ways], refs[ways : 2 * ways]
    attended, log_total = refs[2 * ways : 2 * ways + 2]
    outs = refs[2 * ways + 2 : 3 * ways + 2]
    query, key, value, bias, grad, turned = refs[3 * ways + 2 :]
    gather_heads(info, blocks, query, key, value, bias)
    total_frames, share = query.shape
    frames = total_frames // ways
    for by in range(ways):
        grad[by * frames : (by + 1) * frames] = messages[by][:frames, :]
    turned[...] = (grad[...].astype(jnp.float32) * attended[...].astype(jnp.float32)).T
    for head in range(share // HEAD_DIM):
        part = slice(head * HEAD_DIM, (head + 1) * HEAD_DIM)
        delta = jnp.sum(turned[part, :], axis=0, keepdims=True)
        spread = jnp.concatenate([bias[...]] * (total_frames // LANES), axis=1)
        scores = dot(key[:, part], query[:, part], NT) + spread
        probs = jnp.exp(scores - log_total[head : head + 1, :])
        value_grad = dot(probs.astype(jnp.bfloat16), grad[:, part])
        prob_grad = dot(value[:, part], grad[:, part], NT)
        score_grad = (probs * (prob_grad - delta)).astype(jnp.bfloat16)
        key_grad = dot(score_grad, query[:, part])
        turned[part, :] = dot(key[:, part], score_grad, TN) * SCALE
        for by in range(ways):
            rows = slice(by * frames, (by + 1) * frames)
            outs[by][1, :, part] = key_grad[rows].astype(jnp.bfloat16)
            outs[by][2, :, part] = value_grad[rows].astype(jnp.bfloat16)
    query_grad = turned[...].T.astype(jnp.bfloat16)
    for by in range(ways):
        outs[by][0] = query_grad[by * frames : (by + 1) * frames]


def gather_kernel(ways, info, *refs):
    blocks, messages = refs[:ways], refs[ways:]
    frames, share, reach = messages[0].shape[0], blocks[0].shape[1], 2 * EDGE
    for by, message in enumerate(messages):
        lacking = [slot for slot in range(ways) if slot != by]
        for at, slot in enumerate(lacking):
            message[:, at * share : (at + 1) * share] = blocks[slot][reach : reach + frames, :]


def project_kernel(ways, info, *refs):
    blocks = refs[:ways]
    residual, before, after, out_weight, params = refs[ways : ways + 5]
    mixed, conv_in, attended = refs[ways + 5 :]
    frames, width = residual.shape
    share = width // ways
    reach = 2 * EDGE
    rows = frames + 2 * reach
    for by in range(ways):
        for at in range(ways):

            @pl.when((info[0] ^ by) == at)
            def _():
                attended[:, at * share : (at + 1) * share] = blocks[by][...]

    step = width // 3
    for at in range(0, width, step):
        part = slice(at, at + step)
        mixed[:reach, part] = before[:reach, part].astype(jnp.float32)
        mixed[reach : reach + frames, part] = residual[:, part].astype(jnp.float32)
        mixed[reach + frames :, part] = after[:reach, part].astype(jnp.float32)
        mixed[:, part] += dot(attended[...], out_weight[:, part])

    gain = params[31:32, :]
    first = info[0] * frames - reach

    def band(index, carry):
        at = pl.ds(pl.multiple_of(index * BAND, BAND), BAND)
        normed, _ = moments(mixed[at, :])
        position = first + index * BAND + lax.broadcasted_iota(jnp.int32, (BAND, 1), 0)
        valid = (position >= 0) & (position < info[1])
        conv_in[at, :] = jnp.where(valid, normed * gain, 0.0).astype(jnp.bfloat16)
        return carry

    lax.fori_loop(0, rows // BAND, band, 0)


def stride_of(rows):
    return rows // 8 + 1


def in_columns(ref, rows):
    for at in range(ref.shape[0]):
        ref[at, : rows.shape[0]] = rows[:, at * LANES : (at + 1) * LANES].astype(jnp.float32)


def from_columns(ref, rows):
    return jnp.concatenate([ref[at, rows, :] for at in range(ref.shape[0])], axis=1)


def strided(ref, index, start, stride):
    return ref[index, pl.ds(start, 8, stride=stride), :]


def depthwise(padded, taps, tap_of, out, rows):
    stride = stride_of(rows)

    def column(index, carry):
        part = pl.ds(pl.multiple_of(index * LANES, LANES), LANES)
        cells = [strided(padded, index, at + 1, stride) for at in range(stride + 2 * EDGE - 2)]
        total = [None] * stride
        for offset in range(1, 2 * EDGE):
            tap = tap_of(offset)
            scale = jnp.broadcast_to(taps[tap : tap + 1, part], (8, LANES))
            for at in range(stride):
                term = cells[at + offset - 1] * scale
                total[at] = term if total[at] is None else total[at] + term
        for at in range(stride):
            out[index, pl.ds(at, 8, stride=stride), :] = total[at]
        return carry

    lax.fori_loop(0, out.shape[0], column, 0)


def tap_grads(padded, grad, start, rows, taps):
    stride = rows // 8

    def column(index, carry):
        part = pl.ds(pl.multiple_of(index * LANES, LANES), LANES)
        cells = [
            strided(padded, index, start + at + 1, stride) for at in range(stride + 2 * EDGE - 2)
        ]
        grads = [strided(grad, index, start + at, stride) for at in range(stride)]
        for tap in range(2 * EDGE - 1):
            total = cells[tap] * grads[0]
            for at in range(1, stride):
                total = total + cells[at + tap] * grads[at]
            taps[tap : tap + 1, part] = jnp.sum(total, axis=0, keepdims=True)
        return carry

    lax.fori_loop(0, grad.shape[0], column, 0)


def conv_kernel_body(across, info, conv_in, params, grad_own, grad_edges, *refs):
    conv_act, grad_conv, sums = refs[:3]
    halves = refs[3:-5]
    padded, conv, grad_act, bias_sum, gain_sum = refs[-5:]
    frames, width = grad_own.shape
    rows, wide = frames + 2 * EDGE, frames + 4 * EDGE
    in_columns(padded, conv_in[...])
    padded[:, wide:, :] = jnp.zeros((width // LANES, padded.shape[1] - wide, LANES), jnp.float32)
    grad_act[:EDGE] = grad_edges[:EDGE]
    grad_act[EDGE : EDGE + frames] = grad_own[...]
    grad_act[EDGE + frames :] = grad_edges[EDGE:]
    depthwise(padded, params, lambda offset: offset - 1, conv, rows)
    bias, gain = params[32:33, :], params[33:34, :]
    bias_sum[...] = jnp.zeros_like(bias_sum)
    gain_sum[...] = jnp.zeros_like(gain_sum)

    def band(index, carry):
        at = pl.ds(pl.multiple_of(index * BAND, BAND), BAND)
        normed, inv_scale = moments(from_columns(conv, at) + bias)
        scaled = normed * gain
        gate = 0.5 + 0.5 * jnp.tanh(0.5 * scaled)
        conv_act[at, :] = (scaled * gate).astype(jnp.bfloat16)
        grad_scaled = grad_act[at, :] * gate * (1.0 + scaled * (1.0 - gate))
        grad_rows = norm_back(grad_scaled * gain, normed, inv_scale)
        for column in range(width // LANES):
            grad_conv[column, at, :] = grad_rows[:, column * LANES : (column + 1) * LANES]

        @pl.when((index >= EDGE // BAND) & (index < (EDGE + frames) // BAND))
        def _():
            bias_sum[...] += fold(grad_rows)
            gain_sum[...] += fold(grad_scaled * normed)

        return carry

    lax.fori_loop(0, rows // BAND, band, 0)
    sums[0:1, :] = jnp.sum(bias_sum[...], axis=0, keepdims=True)
    sums[1:2, :] = jnp.sum(gain_sum[...], axis=0, keepdims=True)
    half = width // 2
    for by, block in enumerate(halves):
        for at in range(2):

            @pl.when((info[0] ^ by) // across == at)
            def _():
                block[...] = conv_act[EDGE : EDGE + frames, at * half : (at + 1) * half]


def block_out_kernel(info, conv_act, mixed, point_weight, block_out):
    frames, width = block_out.shape
    step = width // 3
    for at in range(0, width, step):
        part = slice(at, at + step)
        block_out[:, part] = (
            mixed[2 * EDGE : 2 * EDGE + frames, part]
            + dot(conv_act[EDGE : EDGE + frames, :], point_weight[:, part])
        ).astype(jnp.bfloat16)


def conv_back_kernel(ways, slim, info, grad_conv, conv_in, params, masked, mixed, out_weight, *refs):
    conv_sums, grad_residual, messages = refs[0], refs[1], refs[2 : 2 + ways]
    padded, padded_in, conv, gain_sum, taps, packed, chosen = refs[2 + ways :]
    frames, width = grad_residual.shape
    share = width // ways
    reached = frames + 2 * EDGE
    padded[:, :reached, :] = grad_conv[...].astype(jnp.bfloat16).astype(jnp.float32)
    padded[:, reached:, :] = jnp.zeros(
        (width // LANES, padded.shape[1] - reached, LANES), jnp.float32
    )
    depthwise(padded, params, lambda offset: 31 - offset, conv, frames)
    gain = params[31:32, :]
    gain_sum[...] = jnp.zeros_like(gain_sum)

    def band(index, carry):
        at = pl.ds(pl.multiple_of(index * BAND, BAND), BAND)
        own_mixed = pl.ds(pl.multiple_of(index * BAND + 2 * EDGE, BAND), BAND)
        valid = valid_of(info[0] * frames + index * BAND, BAND, info[1])
        grad_in = jnp.where(valid, from_columns(conv, at), 0.0)
        normed, inv_scale = moments(mixed[own_mixed, :])
        grad_mixed = norm_back(grad_in * gain, normed, inv_scale)
        gain_sum[...] += fold(grad_in * normed)
        grad_residual[at, :] = (masked[at, :].astype(jnp.float32) + grad_mixed).astype(
            jnp.bfloat16
        )
        return carry

    lax.fori_loop(0, frames // BAND, band, 0)
    for by in range(ways):
        at = pl.ds(pl.multiple_of((info[0] ^ by) * share, share), share)
        messages[by][:frames] = dot(grad_residual[...], out_weight[at, :], NT).astype(jnp.bfloat16)

    in_columns(padded_in, conv_in[...])
    tap_grads(padded_in, grad_conv, EDGE, frames, taps)
    taps[31:32, :] = conv_sums[0:1, :]
    taps[32:33, :] = jnp.sum(gain_sum[...], axis=0, keepdims=True)
    taps[33:34, :] = conv_sums[1:2, :]
    taps[34:, :] = jnp.zeros((EXTRA - 34, width), jnp.float32)
    packed[:frames] = grad_residual[...]
    packed[frames:] = taps[...].astype(jnp.bfloat16)
    for at in range(ways):
        pieces = []
        for start in range(at * slim, width, ways * slim):
            pieces.append(packed[:, start : start + slim])
        chosen[at] = jnp.concatenate(pieces, axis=1)
    for by in range(ways):
        messages[by][frames:] = chosen[info[0] ^ by]


def split_rows(info, parts, terms, sent, kept):
    rows = terms.shape[0] // parts
    for bit in range(2):

        @pl.when(info[2] % 2 == bit)
        def _():
            for at in range(parts // 2):
                own, other = (2 * at + bit) * rows, (2 * at + 1 - bit) * rows
                kept[at] = terms[own : own + rows, :]
                sent[at] = terms[other : other + rows, :].astype(jnp.bfloat16)


def point_kernel(ways, parts, info, *refs):
    grads, acts, (sent, kept, terms) = refs[:ways], refs[ways : 2 * ways], refs[2 * ways :]
    extent, half = terms.shape
    left = jnp.concatenate([grad[:, grad.shape[1] - extent :] for grad in grads], axis=0)
    right = jnp.concatenate([act[:, :half] for act in acts], axis=0)
    step = terms.shape[1] // 2
    for at in range(0, 2 * step, step):
        part = slice(at, at + step)
        terms[:, part] = dot(left, right[:, part], TN)
    split_rows(info, parts, terms, sent, kept)


def point_sum_kernel(across, info, kept, received, own, other):
    rows = own.shape[0]
    total = kept[0] + received[0].astype(jnp.float32)
    for at in range(2):

        @pl.when(info[0] // across == at)
        def _():
            own[...] = total[at * rows : (at + 1) * rows, :]
            other[...] = total[(1 - at) * rows : (2 - at) * rows, :].astype(jnp.bfloat16)


def weight_kernel(ways, parts, info, *refs):
    grads, rows = refs[:ways], refs[ways : 2 * ways]
    attended, sent, kept, terms = refs[2 * ways :]
    total_frames, share = attended.shape
    frames = total_frames // ways
    width = ways * share
    slim = share // parts
    left = jnp.concatenate([grad[frames : 2 * frames, :] for grad in grads], axis=0)
    for slot in range(ways):
        if slot == 0:
            right = attended[...]
        else:
            pieces = []
            for by in range(ways):
                at = (by ^ slot) - (1 if (by ^ slot) > by else 0)
                pieces.append(rows[by][:, at * share : (at + 1) * share])
            right = jnp.concatenate(pieces, axis=0)
        terms[:, slot * share : (slot + 1) * share] = dot(left, right, TN)
    small = jnp.zeros((EXTRA, share), jnp.float32)
    for grad in grads:
        small = small + grad[2 * frames :, :].astype(jnp.float32)
    filler = jnp.zeros((LANES - EXTRA, share), jnp.float32)
    terms[:, width:] = jnp.concatenate([small, filler], axis=0).T
    split_rows(info, parts, terms, sent, kept)


def halve_kernel(shift, info, kept, received, sent, still_kept):
    bit = (info[2] >> shift) & 1
    for at in range(sent.shape[0]):
        own, other = 2 * at + bit, 2 * at + 1 - bit
        still_kept[at] = kept[own] + received[own].astype(jnp.float32)
        sent[at] = (kept[other] + received[other].astype(jnp.float32)).astype(jnp.bfloat16)


def finish_kernel(ways, info, kept, received, own, other, weight, taps, vectors, point):
    width = weight.shape[1]
    share, half = width // ways, width // 2
    for at in range(2):

        @pl.when(info[0] // (ways // 2) == at)
        def _():
            point[:, at * half : (at + 1) * half] = own[...]
            point[:, (1 - at) * half : (2 - at) * half] = other[...].astype(jnp.float32)

    total = kept[0] + received[0].astype(jnp.float32)
    for by in range(ways):
        for at in range(ways):

            @pl.when((info[0] ^ by) == at)
            def _():
                weight[:, at * share : (at + 1) * share] = total[:, by * share : (by + 1) * share]

    small = total[:, width:].T
    taps[...] = small[:31]
    vectors[...] = small[31:34]


def swap(block, axis, by):
    return lax.ppermute(block, axis, [(i, i ^ by) for i in range(lax.axis_size(axis))])


def swap_all(blocks, axis, step=1):
    return [blocks[0]] + [swap(block, axis, step * by) for by, block in enumerate(blocks[1:], 1)]


def local(
    residual_in,
    query_rows,
    key_rows,
    value_rows,
    lengths,
    out_weight,
    norm_gain,
    conv_kernel,
    conv_bias,
    conv_gain,
    point_weight,
    grad_out,
):
    ways = lax.axis_size("ctx")
    parts = lax.axis_size("dp")
    own = lax.axis_index("ctx")
    place = lax.axis_index("dp")
    frames, width = residual_in.shape[1:]
    share = width // ways
    slim = share // parts
    heads = HEADS // ways
    every = ways * frames
    across = ways // 2
    broad = width // across
    half = width // 2
    tiles = width // LANES
    bf16, f32 = jnp.bfloat16, jnp.float32
    square = 2 * frames * width * width
    rows_bytes = 2 * frames * width
    reached, wide = frames + 2 * EDGE, frames + 4 * EDGE

    info = jnp.stack([own, lengths[0], place]).astype(jnp.int32)
    params = jnp.concatenate(
        [conv_kernel, norm_gain[None], conv_bias[None], conv_gain[None]], axis=0
    )

    def every_nth(count, group):
        at = jnp.arange(count, dtype=jnp.int32)
        return ((at // slim) * (group * slim) + at % slim)[None]

    by_tiles = share % LANES == 0
    packed_rows = [3 * frames + 3 * EDGE * ways * (by in neighbours(ways)) for by in range(ways)]
    packed = call(
        functools.partial(pack_kernel, ways),
        "pack",
        [((rows, share), bf16) for rows in packed_rows],
        scratch=[((3, frames, width), bf16), ((2, 3 * EDGE, width), bf16)],
        semaphores=7,
        far=("in",),
        megabytes=58,
        moved=6 * rows_bytes,
    )(query_rows[0], key_rows[0], value_rows[0], residual_in[0], grad_out[0])
    packed = swap_all(packed, "ctx")

    masked, grad_own, packed[0], *masked_halves = call(
        functools.partial(mask_kernel, slim),
        "mask",
        [((frames, width), bf16), ((frames, width), f32), ((3 * frames, share), bf16)]
        + [((frames, broad), bf16)] * across,
        flops=2 * square,
        moved=6 * rows_bytes + 2 * width * width,
    )(info, grad_out[0], point_weight, every_nth(broad, across), packed[0])
    packed[1], masked_halves = lax.optimization_barrier((packed[1], masked_halves))
    masked_halves = swap_all([masked_halves[by % across] for by in range(ways)], "ctx")

    packed, masked = lax.optimization_barrier((packed, masked))
    head_scratch = [((every, share), bf16)] * 3 + [((every, LANES), f32)]
    pair_flops = 2 * heads * every * every * HEAD_DIM
    *returned, attended, log_total, before, after = call(
        functools.partial(attend_kernel, ways),
        "attend",
        [((wide, share), bf16)] * ways + [((every, share), bf16), ((heads, every), f32)]
        + [((3 * EDGE, width), bf16)] * 2,
        scratch=head_scratch + [((share, every), f32)],
        flops=8 * pair_flops,
        moved=4 * rows_bytes,
        exps=heads * every * every,
    )(info, *packed)
    returned, masked_halves[1:NEAR] = lax.optimization_barrier((returned, masked_halves[1:NEAR]))
    returned = swap_all(returned, "ctx")
    grad_edges = call(
        functools.partial(mask_edges_kernel, frames),
        "mask_edges",
        [((2 * EDGE, width), f32)],
        flops=square,
        moved=2 * width * width,
    )(info, before, after, point_weight)[0]
    returned, grad_edges, masked_halves = lax.optimization_barrier(
        (returned, grad_edges, masked_halves)
    )
    messages = call(
        functools.partial(gather_kernel, ways),
        "gather",
        [((frames, width - share), bf16)] * ways,
        moved=8 * rows_bytes,
    )(info, *returned)
    arrived = swap_all(messages, "ctx")

    returned, messages = lax.optimization_barrier((returned, messages))
    mixed, conv_in = call(
        functools.partial(project_kernel, ways),
        "project",
        [((wide, width), f32), ((wide, width), bf16)],
        scratch=[((wide, width), bf16)],
        flops=square,
        moved=6 * rows_bytes + 2 * width * width,
    )(info, *returned, residual_in[0], before, after, out_weight, params)
    spread = 8 * stride_of(reached)
    conv_act, grad_conv, conv_sums, *act_halves = call(
        functools.partial(conv_kernel_body, across),
        "conv",
        [
            ((reached, width), bf16),
            ((tiles, reached, LANES), f32),
            ((2, width), f32),
        ]
        + [((frames, half), bf16)] * ways,
        scratch=[
            ((tiles, spread + 2 * EDGE, LANES), f32),
            ((tiles, spread, LANES), f32),
            ((reached, width), f32),
            ((8, width), f32),
            ((8, width), f32),
        ],
        flops=frames * width * 4000,
        moved=6 * rows_bytes,
        exps=frames * width,
    )(info, conv_in, params, grad_own, grad_edges)
    near, act_halves = lax.optimization_barrier((arrived[:NEAR], act_halves))
    act_halves = swap_all(act_halves, "ctx")
    far, grad_conv = lax.optimization_barrier((arrived[NEAR:], grad_conv))

    spread = 8 * stride_of(frames)
    grad_residual, *grad_messages = call(
        functools.partial(conv_back_kernel, ways, slim),
        "conv_back",
        [((frames, width), bf16)] + [((2 * frames + EXTRA, share), bf16)] * ways,
        scratch=[
            ((tiles, spread + 2 * EDGE, LANES), f32),
            ((tiles, wide, LANES), f32),
            ((tiles, spread, LANES), f32),
            ((8, width), f32),
            ((EXTRA, width), f32),
            ((frames + EXTRA, width), bf16),
            ((ways, frames + EXTRA, share), bf16),
        ],
        flops=frames * width * 8000,
        moved=8 * rows_bytes + 2 * width * width,
    )(
        info,
        grad_conv,
        conv_in,
        params,
        masked,
        mixed,
        out_weight,
        conv_sums,
    )
    act_halves, grad_messages = lax.optimization_barrier((act_halves, grad_messages))
    messages = near + far
    grad_messages = swap_all(grad_messages, "ctx")

    block_out = call(
        block_out_kernel,
        "block_out",
        [((frames, width), bf16)],
        flops=square,
        moved=4 * rows_bytes + 2 * width * width,
    )(info, conv_act, mixed, point_weight)[0]

    def halve(kept, received, shift):
        extent = (kept.shape[0] // 2,) + kept.shape[1:]
        return call(
            functools.partial(halve_kernel, shift),
            "halve",
            [(extent, bf16), (extent, f32)],
            moved=16 * extent[0] * extent[1] * extent[2],
        )(info, kept, received)

    grad_messages[1], act_halves = lax.optimization_barrier((grad_messages[1], act_halves))
    point_half = (parts // 2, 2 * slim, half)
    point_sent, point_kept = call(
        functools.partial(point_kernel, ways, parts),
        "point_terms",
        [(point_half, bf16), (point_half, f32)],
        scratch=[((broad, half), f32)],
        flops=square,
        moved=8 * rows_bytes,
    )(info, *masked_halves, *act_halves)
    grad_messages, point_sent, block_out = lax.optimization_barrier(
        (grad_messages, point_sent, block_out)
    )
    extent = width + LANES
    core_half = (parts // 2, slim, extent)
    sent, kept = call(
        functools.partial(weight_kernel, ways, parts),
        "out_terms",
        [(core_half, bf16), (core_half, f32)],
        scratch=[((share, extent), f32)],
        flops=square,
        moved=10 * rows_bytes,
    )(info, *grad_messages, *messages, attended)
    received, point_received = swap(sent, "dp", 1), swap(point_sent, "dp", 1)
    for shift in range(1, parts.bit_length() - 1):
        point_sent, point_kept = halve(point_kept, point_received, shift)
        sent, kept = halve(kept, received, shift)
        point_received = swap(point_sent, "dp", 2**shift)
        received = swap(sent, "dp", 2**shift)

    point_own, point_other = call(
        functools.partial(point_sum_kernel, across),
        "point_sum",
        [((slim, half), f32), ((slim, half), bf16)],
        moved=slim * width * (parts + 8),
    )(info, point_kept, point_received)
    point_other = swap(point_other, "ctx", across)

    out_total, taps, vectors, point_total = call(
        functools.partial(finish_kernel, ways),
        "finish",
        [((slim, width), f32), ((31, slim), f32), ((3, slim), f32), ((slim, width), f32)],
        moved=slim * extent * (parts + 8),
    )(info, kept, received, point_own, point_other)

    grad_packed = call(
        functools.partial(attend_back_kernel, ways),
        "attend_back",
        [((3, frames, share), bf16)] * ways,
        scratch=head_scratch + [((every, share), bf16), ((share, every), f32)],
        flops=20 * pair_flops,
        moved=8 * rows_bytes,
        exps=heads * every * every,
    )(info, *packed, *grad_messages, attended, log_total)
    grad_packed = swap_all(grad_packed, "ctx")
    grad_query, grad_key, grad_value = call(
        functools.partial(unpack_kernel if by_tiles else unpack_parts_kernel, ways),
        "unpack",
        [((frames, width), bf16)] * 3,
        semaphores=3 * ways if by_tiles else 0,
        far=("out",) if by_tiles else (),
        moved=6 * rows_bytes,
    )(info, *grad_packed)

    return (
        block_out[None],
        grad_residual[None],
        grad_query[None],
        grad_key[None],
        grad_value[None],
        out_total.T,
        point_total.T,
        taps,
        vectors,
    )


def solution(mesh):
    rows = P("dp", "ctx", None)
    columns = P(None, ("dp", "ctx"))
    in_specs = (rows, rows, rows, rows, P("dp"), P(), P(), P(), P(), P(), P(), rows)
    out_specs = (rows,) * 5 + (columns,) * 4
    return jax.shard_map(local, mesh=mesh, in_specs=in_specs, out_specs=out_specs, check_vma=False)
```

```python
import functools

import jax
import jax.numpy as jnp
from jax import lax
from jax.experimental import pallas as pl
from jax.experimental.pallas import tpu as pltpu
from jax.sharding import PartitionSpec as P

HEADS = 24
HEAD_DIM = 64
SCALE = HEAD_DIM ** (-0.5)

NEG_FILL = -1e30
EPSILON = 1e-05

LANES = 128
EDGE = 16
NEAR = 3
BAND = 16
EXTRA = 48

NN = (((1,), (0,)), ((), ()))
NT = (((1,), (1,)), ((), ()))
TN = (((0,), (0,)), ((), ()))


def dot(left, right, dims=NN):
    return lax.dot_general(left, right, dims, preferred_element_type=jnp.float32)


def call(
    kernel, name, outs, scratch=(), semaphores=0, far=(), megabytes=28, flops=0, moved=0, exps=0
):
    vmem = pl.BlockSpec(memory_space=pltpu.VMEM)
    smem = pl.BlockSpec(memory_space=pltpu.SMEM)
    anywhere = pl.BlockSpec(memory_space=pl.ANY)

    def run(*arrays):
        scratches = [pltpu.VMEM(shape, kind) for shape, kind in scratch]
        if semaphores:
            scratches.append(pltpu.SemaphoreType.DMA((semaphores,)))
        return pl.pallas_call(
            kernel,
            name=name,
            in_specs=[smem if a.ndim == 1 else anywhere if "in" in far else vmem for a in arrays],
            out_specs=[anywhere if "out" in far else vmem] * len(outs),
            out_shape=[jax.ShapeDtypeStruct(shape, kind) for shape, kind in outs],
            scratch_shapes=scratches,
            compiler_params=pltpu.CompilerParams(vmem_limit_bytes=megabytes << 20),
            cost_estimate=pl.CostEstimate(flops=flops, bytes_accessed=moved, transcendentals=exps),
        )(*arrays)

    return run


def valid_of(first, rows, length):
    return first + lax.broadcasted_iota(jnp.int32, (rows, 1), 0) < length


def moments(rows):
    centre = jnp.mean(rows, axis=-1, keepdims=True)
    centred = rows - centre
    inv_scale = lax.rsqrt(jnp.mean(centred * centred, axis=-1, keepdims=True) + EPSILON)
    return centred * inv_scale, inv_scale


def norm_back(grad_normed, normed, inv_scale):
    first_mean = jnp.mean(grad_normed, axis=-1, keepdims=True)
    second_mean = jnp.mean(grad_normed * normed, axis=-1, keepdims=True)
    return inv_scale * (grad_normed - first_mean - normed * second_mean)


def fold(rows):
    total = rows[:8]
    for at in range(8, rows.shape[0], 8):
        total = total + rows[at : at + 8]
    return total


def at_group(info, by, ways, share, visit):
    if share % LANES == 0:
        visit(pl.ds(pl.multiple_of((info[0] ^ by) * share, LANES), share))
        return
    for at in range(ways):

        @pl.when((info[0] ^ by) == at)
        def _():
            visit(slice(at * share, (at + 1) * share))


def neighbours(ways):
    return [by for by in (1, 3, 7, 15) if by < ways]


def edge_rows(frames, at):
    return slice(3 * frames + at * 3 * EDGE, 3 * frames + (at + 1) * 3 * EDGE)


def pack_kernel(ways, query, key, value, residual, grad_out, *refs):
    blocks, whole, ends, arrived = refs[:ways], refs[ways], refs[ways + 1], refs[ways + 2]
    info = [lax.axis_index("ctx")]
    frames, width = query.shape
    share, reach = width // ways, 2 * EDGE
    pairs = [(rows, whole.at[slot]) for slot, rows in enumerate((query, key, value))]
    for side, tail in enumerate((False, True)):
        for rows, start, count in ((residual, 0, reach), (grad_out, reach, EDGE)):
            first = frames - count if tail else 0
            pairs.append((rows.at[pl.ds(first, count)], ends.at[side, pl.ds(start, count)]))
    copies = [
        pltpu.make_async_copy(source, target, arrived.at[at])
        for at, (source, target) in enumerate(pairs)
    ]
    for copy in copies:
        copy.start()
    for slot, copy in enumerate(copies[:3]):
        copy.wait()
        for by in range(ways):

            def visit(lanes):
                blocks[by][slot * frames : (slot + 1) * frames, :] = whole[slot, :, lanes]

            at_group(info, by, ways, share, visit)
    for copy in copies[3:]:
        copy.wait()
    for by in neighbours(ways):
        side = jnp.where((info[0] ^ by) > info[0], 1, 0)
        for at in range(ways):
            blocks[by][edge_rows(frames, at), :] = ends[side, :, at * share : (at + 1) * share]


def unpack_kernel(ways, info, *refs):
    blocks, outs, arrived = refs[:ways], refs[ways:-1], refs[-1]
    share = blocks[0].shape[2]
    copies = []
    for by in range(ways):
        for slot, rows in enumerate(outs):
            lanes = pl.ds(pl.multiple_of((info[0] ^ by) * share, LANES), share)
            copy = pltpu.make_async_copy(
                blocks[by].at[slot], rows.at[:, lanes], arrived.at[len(copies)]
            )
            copy.start()
            copies.append(copy)
    for copy in copies:
        copy.wait()


def unpack_parts_kernel(ways, info, *refs):
    blocks, outs = refs[:ways], refs[ways:]
    share = blocks[0].shape[2]
    for by in range(ways):
        for slot, rows in enumerate(outs):

            def visit(lanes):
                rows[:, lanes] = blocks[by][slot]

            at_group(info, by, ways, share, visit)


def mask_kernel(lower, info, grad_out, point_weight, block, *refs):
    masked, grad_act, own_block, halves = refs[0], refs[1], refs[2], refs[3:]
    own_block[...] = block[...]
    frames, width = grad_out.shape
    valid = valid_of(info[0] * frames, frames, info[1])
    masked[...] = jnp.where(valid, grad_out[...].astype(jnp.float32), 0.0).astype(jnp.bfloat16)
    step = width // 3
    for at in range(0, width, step):
        grad_act[:, at : at + step] = dot(masked[...], point_weight[at : at + step, :], NT)
    quarter = width // 4
    for by, half in enumerate(halves):
        for at in range(2):
            start = (2 * at + ((info[2] // lower) ^ by) % 2) * quarter
            lanes = pl.ds(pl.multiple_of(start, LANES), quarter)
            half[:, at * quarter : (at + 1) * quarter] = masked[:, lanes]


def mask_edges_kernel(frames, info, before, after, point_weight, grad_act):
    width = grad_act.shape[1]
    first = info[0] * frames
    sides = []
    for side, start in ((before, first - EDGE), (after, first + frames)):
        valid = valid_of(start, EDGE, info[1])
        rows = side[2 * EDGE :, :].astype(jnp.float32)
        sides.append(jnp.where(valid, rows, 0.0).astype(jnp.bfloat16))
    masked = jnp.concatenate(sides, axis=0)
    step = width // 3
    for at in range(0, width, step):
        grad_act[:, at : at + step] = dot(masked, point_weight[at : at + step, :], NT)


def gather_heads(info, blocks, query, key, value, bias):
    frames = query.shape[0] // len(blocks)
    for by, block in enumerate(blocks):
        rows = slice(by * frames, (by + 1) * frames)
        query[rows] = block[:frames, :] * jnp.bfloat16(SCALE)
        key[rows] = block[frames : 2 * frames, :]
        value[rows] = block[2 * frames : 3 * frames, :]
        valid = valid_of((info[0] ^ by) * frames, frames, info[1])
        bias[rows] = jnp.broadcast_to(jnp.where(valid, 0.0, NEG_FILL), (frames, LANES))


def attend_kernel(ways, info, *refs):
    blocks, outs = refs[:ways], refs[ways : 2 * ways]
    attended, log_total, before, after, query, key, value, bias, turned = refs[2 * ways :]
    gather_heads(info, blocks, query, key, value, bias)
    total_frames, share = query.shape
    frames = total_frames // ways
    for side, other in ((before, info[0] - 1), (after, info[0] + 1)):
        side[...] = jnp.zeros_like(side)
        for by in neighbours(ways):

            @pl.when((info[0] ^ other) == by)
            def _():
                for at in range(ways):
                    lanes = slice(at * share, (at + 1) * share)
                    side[:, lanes] = blocks[by][edge_rows(frames, at), :]

    for head in range(share // HEAD_DIM):
        part = slice(head * HEAD_DIM, (head + 1) * HEAD_DIM)
        spread = jnp.concatenate([bias[...]] * (total_frames // LANES), axis=1)
        scores = dot(key[:, part], query[:, part], NT) + spread
        row_max = jnp.max(scores, axis=0, keepdims=True)
        weights = jnp.exp(scores - row_max)
        total = jnp.sum(weights, axis=0, keepdims=True)
        turned[part, :] = dot(value[:, part], weights.astype(jnp.bfloat16), TN) / total
        log_total[head : head + 1, :] = row_max + jnp.log(total)
    attended[...] = turned[...].T.astype(jnp.bfloat16)
    reach = 2 * EDGE
    for by in range(ways):
        other = info[0] ^ by
        before = (info[0] ^ jnp.maximum(other - 1, 0)) * frames + frames - reach
        after = (info[0] ^ jnp.minimum(other + 1, ways - 1)) * frames
        outs[by][:reach] = attended[pl.ds(pl.multiple_of(before, reach), reach), :]
        outs[by][reach : reach + frames] = attended[by * frames : (by + 1) * frames, :]
        outs[by][reach + frames :] = attended[pl.ds(pl.multiple_of(after, reach), reach), :]


def attend_back_kernel(ways, info, *refs):
    blocks, messages = refs[:ways], refs[ways : 2 * ways]
    attended, log_total = refs[2 * ways : 2 * ways + 2]
    outs = refs[2 * ways + 2 : 3 * ways + 2]
    query, key, value, bias, grad, turned = refs[3 * ways + 2 :]
    gather_heads(info, blocks, query, key, value, bias)
    total_frames, share = query.shape
    frames = total_frames // ways
    for by in range(ways):
        grad[by * frames : (by + 1) * frames] = messages[by][:frames, :]
    turned[...] = (grad[...].astype(jnp.float32) * attended[...].astype(jnp.float32)).T
    for head in range(share // HEAD_DIM):
        part = slice(head * HEAD_DIM, (head + 1) * HEAD_DIM)
        delta = jnp.sum(turned[part, :], axis=0, keepdims=True)
        spread = jnp.concatenate([bias[...]] * (total_frames // LANES), axis=1)
        scores = dot(key[:, part], query[:, part], NT) + spread
        probs = jnp.exp(scores - log_total[head : head + 1, :])
        value_grad = dot(probs.astype(jnp.bfloat16), grad[:, part])
        prob_grad = dot(value[:, part], grad[:, part], NT)
        score_grad = (probs * (prob_grad - delta)).astype(jnp.bfloat16)
        key_grad = dot(score_grad, query[:, part])
        turned[part, :] = dot(key[:, part], score_grad, TN) * SCALE
        for by in range(ways):
            rows = slice(by * frames, (by + 1) * frames)
            outs[by][1, :, part] = key_grad[rows].astype(jnp.bfloat16)
            outs[by][2, :, part] = value_grad[rows].astype(jnp.bfloat16)
    query_grad = turned[...].T.astype(jnp.bfloat16)
    for by in range(ways):
        outs[by][0] = query_grad[by * frames : (by + 1) * frames]


def gather_kernel(ways, info, *refs):
    blocks, messages = refs[:ways], refs[ways:]
    frames, share, reach = messages[0].shape[0], blocks[0].shape[1], 2 * EDGE
    for by, message in enumerate(messages):
        lacking = [slot for slot in range(ways) if slot != by]
        for at, slot in enumerate(lacking):
            message[:, at * share : (at + 1) * share] = blocks[slot][reach : reach + frames, :]


def project_kernel(ways, info, *refs):
    blocks = refs[:ways]
    residual, before, after, out_weight, params = refs[ways : ways + 5]
    mixed, conv_in, attended = refs[ways + 5 :]
    frames, width = residual.shape
    share = width // ways
    reach = 2 * EDGE
    rows = frames + 2 * reach
    for by in range(ways):
        for at in range(ways):

            @pl.when((info[0] ^ by) == at)
            def _():
                attended[:, at * share : (at + 1) * share] = blocks[by][...]

    step = width // 3
    for at in range(0, width, step):
        part = slice(at, at + step)
        mixed[:reach, part] = before[:reach, part].astype(jnp.float32)
        mixed[reach : reach + frames, part] = residual[:, part].astype(jnp.float32)
        mixed[reach + frames :, part] = after[:reach, part].astype(jnp.float32)
        mixed[:, part] += dot(attended[...], out_weight[:, part])

    gain = params[31:32, :]
    first = info[0] * frames - reach

    def band(index, carry):
        at = pl.ds(pl.multiple_of(index * BAND, BAND), BAND)
        normed, _ = moments(mixed[at, :])
        position = first + index * BAND + lax.broadcasted_iota(jnp.int32, (BAND, 1), 0)
        valid = (position >= 0) & (position < info[1])
        conv_in[at, :] = jnp.where(valid, normed * gain, 0.0).astype(jnp.bfloat16)
        return carry

    lax.fori_loop(0, rows // BAND, band, 0)


def stride_of(rows):
    return rows // 8 + 1


def in_columns(ref, rows):
    for at in range(ref.shape[0]):
        ref[at, : rows.shape[0]] = rows[:, at * LANES : (at + 1) * LANES].astype(jnp.float32)


def from_columns(ref, rows):
    return jnp.concatenate([ref[at, rows, :] for at in range(ref.shape[0])], axis=1)


def strided(ref, index, start, stride):
    return ref[index, pl.ds(start, 8, stride=stride), :]


def depthwise(padded, taps, tap_of, out, rows):
    stride = stride_of(rows)

    def column(index, carry):
        part = pl.ds(pl.multiple_of(index * LANES, LANES), LANES)
        cells = [strided(padded, index, at + 1, stride) for at in range(stride + 2 * EDGE - 2)]
        total = [None] * stride
        for offset in range(1, 2 * EDGE):
            tap = tap_of(offset)
            scale = jnp.broadcast_to(taps[tap : tap + 1, part], (8, LANES))
            for at in range(stride):
                term = cells[at + offset - 1] * scale
                total[at] = term if total[at] is None else total[at] + term
        for at in range(stride):
            out[index, pl.ds(at, 8, stride=stride), :] = total[at]
        return carry

    lax.fori_loop(0, out.shape[0], column, 0)


def tap_grads(padded, grad, start, rows, taps):
    stride = rows // 8

    def column(index, carry):
        part = pl.ds(pl.multiple_of(index * LANES, LANES), LANES)
        cells = [
            strided(padded, index, start + at + 1, stride) for at in range(stride + 2 * EDGE - 2)
        ]
        grads = [strided(grad, index, start + at, stride) for at in range(stride)]
        for tap in range(2 * EDGE - 1):
            total = cells[tap] * grads[0]
            for at in range(1, stride):
                total = total + cells[at + tap] * grads[at]
            taps[tap : tap + 1, part] = jnp.sum(total, axis=0, keepdims=True)
        return carry

    lax.fori_loop(0, grad.shape[0], column, 0)


def conv_kernel_body(lower, info, conv_in, params, grad_own, grad_edges, *refs):
    conv_act, grad_conv, sums = refs[:3]
    halves = refs[3:-5]
    padded, conv, grad_act, bias_sum, gain_sum = refs[-5:]
    frames, width = grad_own.shape
    rows, wide = frames + 2 * EDGE, frames + 4 * EDGE
    in_columns(padded, conv_in[...])
    padded[:, wide:, :] = jnp.zeros((width // LANES, padded.shape[1] - wide, LANES), jnp.float32)
    grad_act[:EDGE] = grad_edges[:EDGE]
    grad_act[EDGE : EDGE + frames] = grad_own[...]
    grad_act[EDGE + frames :] = grad_edges[EDGE:]
    depthwise(padded, params, lambda offset: offset - 1, conv, rows)
    bias, gain = params[32:33, :], params[33:34, :]
    bias_sum[...] = jnp.zeros_like(bias_sum)
    gain_sum[...] = jnp.zeros_like(gain_sum)

    def band(index, carry):
        at = pl.ds(pl.multiple_of(index * BAND, BAND), BAND)
        normed, inv_scale = moments(from_columns(conv, at) + bias)
        scaled = normed * gain
        gate = 0.5 + 0.5 * jnp.tanh(0.5 * scaled)
        conv_act[at, :] = (scaled * gate).astype(jnp.bfloat16)
        grad_scaled = grad_act[at, :] * gate * (1.0 + scaled * (1.0 - gate))
        grad_rows = norm_back(grad_scaled * gain, normed, inv_scale)
        for column in range(width // LANES):
            grad_conv[column, at, :] = grad_rows[:, column * LANES : (column + 1) * LANES]

        @pl.when((index >= EDGE // BAND) & (index < (EDGE + frames) // BAND))
        def _():
            bias_sum[...] += fold(grad_rows)
            gain_sum[...] += fold(grad_scaled * normed)

        return carry

    lax.fori_loop(0, rows // BAND, band, 0)
    sums[0:1, :] = jnp.sum(bias_sum[...], axis=0, keepdims=True)
    sums[1:2, :] = jnp.sum(gain_sum[...], axis=0, keepdims=True)
    half = width // 2
    for by, block in enumerate(halves):
        start = ((info[2] // (2 * lower)) ^ by) * half
        block[...] = conv_act[EDGE : EDGE + frames, pl.ds(pl.multiple_of(start, LANES), half)]


def block_out_kernel(info, conv_act, mixed, point_weight, block_out):
    frames, width = block_out.shape
    step = width // 3
    for at in range(0, width, step):
        part = slice(at, at + step)
        block_out[:, part] = (
            mixed[2 * EDGE : 2 * EDGE + frames, part]
            + dot(conv_act[EDGE : EDGE + frames, :], point_weight[:, part])
        ).astype(jnp.bfloat16)


def conv_back_kernel(ways, slim, info, grad_conv, conv_in, params, masked, mixed, out_weight, *refs):
    conv_sums, grad_residual, messages = refs[0], refs[1], refs[2 : 2 + ways]
    padded, padded_in, conv, gain_sum, taps, packed, chosen = refs[2 + ways :]
    frames, width = grad_residual.shape
    share = width // ways
    reached = frames + 2 * EDGE
    padded[:, :reached, :] = grad_conv[...].astype(jnp.bfloat16).astype(jnp.float32)
    padded[:, reached:, :] = jnp.zeros(
        (width // LANES, padded.shape[1] - reached, LANES), jnp.float32
    )
    depthwise(padded, params, lambda offset: 31 - offset, conv, frames)
    gain = params[31:32, :]
    gain_sum[...] = jnp.zeros_like(gain_sum)

    def band(index, carry):
        at = pl.ds(pl.multiple_of(index * BAND, BAND), BAND)
        own_mixed = pl.ds(pl.multiple_of(index * BAND + 2 * EDGE, BAND), BAND)
        valid = valid_of(info[0] * frames + index * BAND, BAND, info[1])
        grad_in = jnp.where(valid, from_columns(conv, at), 0.0)
        normed, inv_scale = moments(mixed[own_mixed, :])
        grad_mixed = norm_back(grad_in * gain, normed, inv_scale)
        gain_sum[...] += fold(grad_in * normed)
        grad_residual[at, :] = (masked[at, :].astype(jnp.float32) + grad_mixed).astype(
            jnp.bfloat16
        )
        return carry

    lax.fori_loop(0, frames // BAND, band, 0)
    for by in range(ways):
        at = pl.ds(pl.multiple_of((info[0] ^ by) * share, share), share)
        messages[by][:frames] = dot(grad_residual[...], out_weight[at, :], NT).astype(jnp.bfloat16)

    in_columns(padded_in, conv_in[...])
    tap_grads(padded_in, grad_conv, EDGE, frames, taps)
    taps[31:32, :] = conv_sums[0:1, :]
    taps[32:33, :] = jnp.sum(gain_sum[...], axis=0, keepdims=True)
    taps[33:34, :] = conv_sums[1:2, :]
    taps[34:, :] = jnp.zeros((EXTRA - 34, width), jnp.float32)
    packed[:frames] = grad_residual[...]
    packed[frames:] = taps[...].astype(jnp.bfloat16)
    for at in range(ways):
        pieces = []
        for start in range(at * slim, width, ways * slim):
            pieces.append(packed[:, start : start + slim])
        chosen[at] = jnp.concatenate(pieces, axis=1)
    for by in range(ways):
        messages[by][frames:] = chosen[info[0] ^ by]


def split_rows(info, parts, terms, sent, kept):
    rows = terms.shape[0] // parts
    for bit in range(2):

        @pl.when(info[2] % 2 == bit)
        def _():
            for at in range(parts // 2):
                own, other = (2 * at + bit) * rows, (2 * at + 1 - bit) * rows
                kept[at] = terms[own : own + rows, :]
                sent[at] = terms[other : other + rows, :].astype(jnp.bfloat16)


def point_kernel(shift, info, *refs):
    grads, acts, (sent, kept, terms) = refs[:4], refs[4:8], refs[8:]
    left = jnp.concatenate([grad[...] for grad in grads], axis=0)
    right = jnp.concatenate([act[...] for act in acts], axis=0)
    step = terms.shape[1] // 2
    for at in range(0, 2 * step, step):
        part = slice(at, at + step)
        terms[:, part] = dot(left, right[:, part], TN)
    pieces, slim = kept.shape[0], kept.shape[1] // 2
    for bit in range(2):

        @pl.when(((info[2] >> shift) & 1) == bit)
        def _():
            for at in range(pieces):
                for side in range(2):
                    base = side * 2 * pieces * slim
                    own = base + (bit * pieces + at) * slim
                    other = base + ((1 - bit) * pieces + at) * slim
                    rows = slice(side * slim, (side + 1) * slim)
                    kept[at, rows, :] = terms[own : own + slim, :]
                    sent[at, rows, :] = terms[other : other + slim, :].astype(jnp.bfloat16)


def point_sum_kernel(shift, info, kept, received, own, other):
    rows = own.shape[0]
    total = kept[0] + received[0].astype(jnp.float32)
    for at in range(2):

        @pl.when(((info[2] >> shift) & 1) == at)
        def _():
            own[...] = total[at * rows : (at + 1) * rows, :]
            other[...] = total[(1 - at) * rows : (2 - at) * rows, :].astype(jnp.bfloat16)


def weight_kernel(ways, parts, info, *refs):
    grads, rows = refs[:ways], refs[ways : 2 * ways]
    attended, sent, kept, terms = refs[2 * ways :]
    total_frames, share = attended.shape
    frames = total_frames // ways
    width = ways * share
    slim = share // parts
    left = jnp.concatenate([grad[frames : 2 * frames, :] for grad in grads], axis=0)
    for slot in range(ways):
        if slot == 0:
            right = attended[...]
        else:
            pieces = []
            for by in range(ways):
                at = (by ^ slot) - (1 if (by ^ slot) > by else 0)
                pieces.append(rows[by][:, at * share : (at + 1) * share])
            right = jnp.concatenate(pieces, axis=0)
        terms[:, slot * share : (slot + 1) * share] = dot(left, right, TN)
    small = jnp.zeros((EXTRA, share), jnp.float32)
    for grad in grads:
        small = small + grad[2 * frames :, :].astype(jnp.float32)
    filler = jnp.zeros((LANES - EXTRA, share), jnp.float32)
    terms[:, width:] = jnp.concatenate([small, filler], axis=0).T
    split_rows(info, parts, terms, sent, kept)


def halve_kernel(axis, shift, alternate, info, kept, received, sent, still_kept):
    bit = (info[axis] >> shift) & 1
    count = sent.shape[0]
    for at in range(count):
        if alternate:
            own, other = 2 * at + bit, 2 * at + 1 - bit
        else:
            own, other = bit * count + at, (1 - bit) * count + at
        still_kept[at] = kept[own] + received[own].astype(jnp.float32)
        sent[at] = (kept[other] + received[other].astype(jnp.float32)).astype(jnp.bfloat16)


def finish_kernel(ways, shift, info, kept, received, own, other, weight, taps, vectors, point):
    width = weight.shape[1]
    share, half = width // ways, width // 2
    for at in range(2):

        @pl.when(((info[2] >> shift) & 1) == at)
        def _():
            point[:, at * half : (at + 1) * half] = own[...]
            point[:, (1 - at) * half : (2 - at) * half] = other[...].astype(jnp.float32)

    total = kept[0] + received[0].astype(jnp.float32)
    for by in range(ways):
        for at in range(ways):

            @pl.when((info[0] ^ by) == at)
            def _():
                weight[:, at * share : (at + 1) * share] = total[:, by * share : (by + 1) * share]

    small = total[:, width:].T
    taps[...] = small[:31]
    vectors[...] = small[31:34]


def swap(block, axis, by):
    return lax.ppermute(block, axis, [(i, i ^ by) for i in range(lax.axis_size(axis))])


def swap_all(blocks, axis, step=1):
    return [blocks[0]] + [swap(block, axis, step * by) for by, block in enumerate(blocks[1:], 1)]


def local(
    residual_in,
    query_rows,
    key_rows,
    value_rows,
    lengths,
    out_weight,
    norm_gain,
    conv_kernel,
    conv_bias,
    conv_gain,
    point_weight,
    grad_out,
):
    ways = lax.axis_size("ctx")
    parts = lax.axis_size("dp")
    own = lax.axis_index("ctx")
    place = lax.axis_index("dp")
    frames, width = residual_in.shape[1:]
    share = width // ways
    slim = share // parts
    heads = HEADS // ways
    every = ways * frames
    lower = parts // 4
    half = width // 2
    tiles = width // LANES
    bf16, f32 = jnp.bfloat16, jnp.float32
    square = 2 * frames * width * width
    rows_bytes = 2 * frames * width
    reached, wide = frames + 2 * EDGE, frames + 4 * EDGE

    info = jnp.stack([own, lengths[0], place]).astype(jnp.int32)
    params = jnp.concatenate(
        [conv_kernel, norm_gain[None], conv_bias[None], conv_gain[None]], axis=0
    )

    by_tiles = share % LANES == 0
    packed_rows = [3 * frames + 3 * EDGE * ways * (by in neighbours(ways)) for by in range(ways)]
    packed = call(
        functools.partial(pack_kernel, ways),
        "pack",
        [((rows, share), bf16) for rows in packed_rows],
        scratch=[((3, frames, width), bf16), ((2, 3 * EDGE, width), bf16)],
        semaphores=7,
        far=("in",),
        megabytes=58,
        moved=6 * rows_bytes,
    )(query_rows[0], key_rows[0], value_rows[0], residual_in[0], grad_out[0])
    packed = swap_all(packed, "ctx")

    masked, grad_own, packed[0], *masked_halves = call(
        functools.partial(mask_kernel, lower),
        "mask",
        [((frames, width), bf16), ((frames, width), f32), ((3 * frames, share), bf16)]
        + [((frames, half), bf16)] * 2,
        flops=2 * square,
        moved=6 * rows_bytes + 2 * width * width,
    )(info, grad_out[0], point_weight, packed[0])
    packed[1], masked_halves = lax.optimization_barrier((packed[1], masked_halves))
    masked_halves = swap_all([masked_halves[by % 2] for by in range(4)], "dp", lower)

    packed, masked = lax.optimization_barrier((packed, masked))
    head_scratch = [((every, share), bf16)] * 3 + [((every, LANES), f32)]
    pair_flops = 2 * heads * every * every * HEAD_DIM
    *returned, attended, log_total, before, after = call(
        functools.partial(attend_kernel, ways),
        "attend",
        [((wide, share), bf16)] * ways + [((every, share), bf16), ((heads, every), f32)]
        + [((3 * EDGE, width), bf16)] * 2,
        scratch=head_scratch + [((share, every), f32)],
        flops=8 * pair_flops,
        moved=4 * rows_bytes,
        exps=heads * every * every,
    )(info, *packed)
    returned, masked_halves[1] = lax.optimization_barrier((returned, masked_halves[1]))
    returned = swap_all(returned, "ctx")
    grad_edges = call(
        functools.partial(mask_edges_kernel, frames),
        "mask_edges",
        [((2 * EDGE, width), f32)],
        flops=square,
        moved=2 * width * width,
    )(info, before, after, point_weight)[0]
    returned, grad_edges, masked_halves = lax.optimization_barrier(
        (returned, grad_edges, masked_halves)
    )
    messages = call(
        functools.partial(gather_kernel, ways),
        "gather",
        [((frames, width - share), bf16)] * ways,
        moved=8 * rows_bytes,
    )(info, *returned)
    arrived = swap_all(messages, "ctx")

    returned, messages = lax.optimization_barrier((returned, messages))
    mixed, conv_in = call(
        functools.partial(project_kernel, ways),
        "project",
        [((wide, width), f32), ((wide, width), bf16)],
        scratch=[((wide, width), bf16)],
        flops=square,
        moved=6 * rows_bytes + 2 * width * width,
    )(info, *returned, residual_in[0], before, after, out_weight, params)
    spread = 8 * stride_of(reached)
    conv_act, grad_conv, conv_sums, *act_halves = call(
        functools.partial(conv_kernel_body, lower),
        "conv",
        [
            ((reached, width), bf16),
            ((tiles, reached, LANES), f32),
            ((2, width), f32),
        ]
        + [((frames, half), bf16)] * 2,
        scratch=[
            ((tiles, spread + 2 * EDGE, LANES), f32),
            ((tiles, spread, LANES), f32),
            ((reached, width), f32),
            ((8, width), f32),
            ((8, width), f32),
        ],
        flops=frames * width * 4000,
        moved=6 * rows_bytes,
        exps=frames * width,
    )(info, conv_in, params, grad_own, grad_edges)
    near, act_halves = lax.optimization_barrier((arrived[:NEAR], act_halves))
    act_halves = swap_all([act_halves[by // 2] for by in range(4)], "dp", lower)
    far, grad_conv = lax.optimization_barrier((arrived[NEAR:], grad_conv))

    spread = 8 * stride_of(frames)
    grad_residual, *grad_messages = call(
        functools.partial(conv_back_kernel, ways, slim),
        "conv_back",
        [((frames, width), bf16)] + [((2 * frames + EXTRA, share), bf16)] * ways,
        scratch=[
            ((tiles, spread + 2 * EDGE, LANES), f32),
            ((tiles, wide, LANES), f32),
            ((tiles, spread, LANES), f32),
            ((8, width), f32),
            ((EXTRA, width), f32),
            ((frames + EXTRA, width), bf16),
            ((ways, frames + EXTRA, share), bf16),
        ],
        flops=frames * width * 8000,
        moved=8 * rows_bytes + 2 * width * width,
    )(
        info,
        grad_conv,
        conv_in,
        params,
        masked,
        mixed,
        out_weight,
        conv_sums,
    )
    act_halves, grad_messages[NEAR:] = lax.optimization_barrier(
        (act_halves, grad_messages[NEAR:])
    )
    messages = near + far
    grad_messages = swap_all(grad_messages, "ctx")

    block_out = call(
        block_out_kernel,
        "block_out",
        [((frames, width), bf16)],
        flops=square,
        moved=4 * rows_bytes + 2 * width * width,
    )(info, conv_act, mixed, point_weight)[0]

    def halve(kept, received, axis, shift, alternate):
        extent = (kept.shape[0] // 2,) + kept.shape[1:]
        return call(
            functools.partial(halve_kernel, 0 if axis == "ctx" else 2, shift, alternate),
            "halve",
            [(extent, bf16), (extent, f32)],
            moved=16 * extent[0] * extent[1] * extent[2],
        )(info, kept, received)

    grad_messages[1], act_halves = lax.optimization_barrier((grad_messages[1], act_halves))
    bits = [("dp", shift) for shift in reversed(range(lower.bit_length() - 1))]
    bits += [("ctx", shift) for shift in reversed(range(ways.bit_length() - 1))]
    point_half = (lower * ways // 2, 2 * slim, half)
    point_sent, point_kept = call(
        functools.partial(point_kernel, bits[0][1]),
        "point_terms",
        [(point_half, bf16), (point_half, f32)],
        scratch=[((half, half), f32)],
        flops=square,
        moved=8 * rows_bytes,
    )(info, *masked_halves, *act_halves)
    grad_messages, point_sent, block_out = lax.optimization_barrier(
        (grad_messages, point_sent, block_out)
    )
    extent = width + LANES
    core_half = (parts // 2, slim, extent)
    sent, kept = call(
        functools.partial(weight_kernel, ways, parts),
        "out_terms",
        [(core_half, bf16), (core_half, f32)],
        scratch=[((share, extent), f32)],
        flops=square,
        moved=10 * rows_bytes,
    )(info, *grad_messages, *messages, attended)
    received = swap(sent, "dp", 1)
    for shift in range(1, parts.bit_length() - 1):
        sent, kept = halve(kept, received, "dp", shift, True)
        received = swap(sent, "dp", 2**shift)

    point_received = swap(point_sent, bits[0][0], 2 ** bits[0][1])
    for axis, shift in bits[1:]:
        point_sent, point_kept = halve(point_kept, point_received, axis, shift, False)
        point_received = swap(point_sent, axis, 2**shift)
    layer_bit = (parts // 2).bit_length() - 1
    point_own, point_other = call(
        functools.partial(point_sum_kernel, layer_bit),
        "point_sum",
        [((slim, half), f32), ((slim, half), bf16)],
        moved=slim * width * (parts + 8),
    )(info, point_kept, point_received)
    point_other = swap(point_other, "dp", parts // 2)

    out_total, taps, vectors, point_total = call(
        functools.partial(finish_kernel, ways, layer_bit),
        "finish",
        [((slim, width), f32), ((31, slim), f32), ((3, slim), f32), ((slim, width), f32)],
        moved=slim * extent * (parts + 8),
    )(info, kept, received, point_own, point_other)

    grad_packed = call(
        functools.partial(attend_back_kernel, ways),
        "attend_back",
        [((3, frames, share), bf16)] * ways,
        scratch=head_scratch + [((every, share), bf16), ((share, every), f32)],
        flops=20 * pair_flops,
        moved=8 * rows_bytes,
        exps=heads * every * every,
    )(info, *packed, *grad_messages, attended, log_total)
    grad_packed = swap_all(grad_packed, "ctx")
    grad_query, grad_key, grad_value = call(
        functools.partial(unpack_kernel if by_tiles else unpack_parts_kernel, ways),
        "unpack",
        [((frames, width), bf16)] * 3,
        semaphores=3 * ways if by_tiles else 0,
        far=("out",) if by_tiles else (),
        moved=6 * rows_bytes,
    )(info, *grad_packed)

    return (
        block_out[None],
        grad_residual[None],
        grad_query[None],
        grad_key[None],
        grad_value[None],
        out_total.T,
        point_total.T,
        taps,
        vectors,
    )


def solution(mesh):
    rows = P("dp", "ctx", None)
    columns = P(None, ("dp", "ctx"))
    in_specs = (rows, rows, rows, rows, P("dp"), P(), P(), P(), P(), P(), P(), rows)
    out_specs = (rows,) * 5 + (columns,) * 4
    return jax.shard_map(local, mesh=mesh, in_specs=in_specs, out_specs=out_specs, check_vma=False)
```

```python
import functools

import jax
import jax.numpy as jnp
from jax import lax
from jax.experimental import pallas as pl
from jax.experimental.pallas import tpu as pltpu
from jax.sharding import PartitionSpec as P

HEADS = 24
HEAD_DIM = 64
SCALE = HEAD_DIM ** (-0.5)

NEG_FILL = -1e30
EPSILON = 1e-05

LANES = 128
EDGE = 16
NEAR = 3
BAND = 16
EXTRA = 48

NN = (((1,), (0,)), ((), ()))
NT = (((1,), (1,)), ((), ()))
TN = (((0,), (0,)), ((), ()))


def dot(left, right, dims=NN):
    return lax.dot_general(left, right, dims, preferred_element_type=jnp.float32)


def call(
    kernel, name, outs, scratch=(), semaphores=0, far=(), megabytes=28, flops=0, moved=0, exps=0
):
    vmem = pl.BlockSpec(memory_space=pltpu.VMEM)
    smem = pl.BlockSpec(memory_space=pltpu.SMEM)
    anywhere = pl.BlockSpec(memory_space=pl.ANY)

    def run(*arrays):
        scratches = [pltpu.VMEM(shape, kind) for shape, kind in scratch]
        if semaphores:
            scratches.append(pltpu.SemaphoreType.DMA((semaphores,)))
        return pl.pallas_call(
            kernel,
            name=name,
            in_specs=[smem if a.ndim == 1 else anywhere if "in" in far else vmem for a in arrays],
            out_specs=[anywhere if "out" in far else vmem] * len(outs),
            out_shape=[jax.ShapeDtypeStruct(shape, kind) for shape, kind in outs],
            scratch_shapes=scratches,
            compiler_params=pltpu.CompilerParams(vmem_limit_bytes=megabytes << 20),
            cost_estimate=pl.CostEstimate(flops=flops, bytes_accessed=moved, transcendentals=exps),
        )(*arrays)

    return run


def valid_of(first, rows, length):
    return first + lax.broadcasted_iota(jnp.int32, (rows, 1), 0) < length


def moments(rows):
    centre = jnp.mean(rows, axis=-1, keepdims=True)
    centred = rows - centre
    inv_scale = lax.rsqrt(jnp.mean(centred * centred, axis=-1, keepdims=True) + EPSILON)
    return centred * inv_scale, inv_scale


def norm_back(grad_normed, normed, inv_scale):
    first_mean = jnp.mean(grad_normed, axis=-1, keepdims=True)
    second_mean = jnp.mean(grad_normed * normed, axis=-1, keepdims=True)
    return inv_scale * (grad_normed - first_mean - normed * second_mean)


def fold(rows):
    total = rows[:8]
    for at in range(8, rows.shape[0], 8):
        total = total + rows[at : at + 8]
    return total


def at_group(info, by, ways, share, visit):
    if share % LANES == 0:
        visit(pl.ds(pl.multiple_of((info[0] ^ by) * share, LANES), share))
        return
    for at in range(ways):

        @pl.when((info[0] ^ by) == at)
        def _():
            visit(slice(at * share, (at + 1) * share))


def neighbours(ways):
    return [by for by in (1, 3, 7, 15) if by < ways]


def edge_rows(frames, at):
    return slice(3 * frames + at * 3 * EDGE, 3 * frames + (at + 1) * 3 * EDGE)


def pack_kernel(ways, query, key, value, residual, grad_out, *refs):
    blocks, whole, ends, arrived = refs[:ways], refs[ways], refs[ways + 1], refs[ways + 2]
    info = [lax.axis_index("ctx")]
    frames, width = query.shape
    share, reach = width // ways, 2 * EDGE
    pairs = [(rows, whole.at[slot]) for slot, rows in enumerate((query, key, value))]
    for side, tail in enumerate((False, True)):
        for rows, start, count in ((residual, 0, reach), (grad_out, reach, EDGE)):
            first = frames - count if tail else 0
            pairs.append((rows.at[pl.ds(first, count)], ends.at[side, pl.ds(start, count)]))
    copies = [
        pltpu.make_async_copy(source, target, arrived.at[at])
        for at, (source, target) in enumerate(pairs)
    ]
    for copy in copies:
        copy.start()
    for slot, copy in enumerate(copies[:3]):
        copy.wait()
        for by in range(ways):

            def visit(lanes):
                blocks[by][slot * frames : (slot + 1) * frames, :] = whole[slot, :, lanes]

            at_group(info, by, ways, share, visit)
    for copy in copies[3:]:
        copy.wait()
    for by in neighbours(ways):
        side = jnp.where((info[0] ^ by) > info[0], 1, 0)
        for at in range(ways):
            blocks[by][edge_rows(frames, at), :] = ends[side, :, at * share : (at + 1) * share]


def unpack_kernel(ways, info, *refs):
    blocks, outs, arrived = refs[:ways], refs[ways:-1], refs[-1]
    share = blocks[0].shape[2]
    copies = []
    for by in range(ways):
        for slot, rows in enumerate(outs):
            lanes = pl.ds(pl.multiple_of((info[0] ^ by) * share, LANES), share)
            copy = pltpu.make_async_copy(
                blocks[by].at[slot], rows.at[:, lanes], arrived.at[len(copies)]
            )
            copy.start()
            copies.append(copy)
    for copy in copies:
        copy.wait()


def unpack_parts_kernel(ways, info, *refs):
    blocks, outs = refs[:ways], refs[ways:]
    share = blocks[0].shape[2]
    for by in range(ways):
        for slot, rows in enumerate(outs):

            def visit(lanes):
                rows[:, lanes] = blocks[by][slot]

            at_group(info, by, ways, share, visit)


def mask_kernel(lower, info, grad_out, point_weight, block, *refs):
    masked, grad_act, own_block, halves = refs[0], refs[1], refs[2], refs[3:]
    own_block[...] = block[...]
    frames, width = grad_out.shape
    valid = valid_of(info[0] * frames, frames, info[1])
    masked[...] = jnp.where(valid, grad_out[...].astype(jnp.float32), 0.0).astype(jnp.bfloat16)
    step = width // 3
    for at in range(0, width, step):
        grad_act[:, at : at + step] = dot(masked[...], point_weight[at : at + step, :], NT)
    quarter = width // 4
    for by, half in enumerate(halves):
        for at in range(2):
            start = (2 * at + ((info[2] // lower) ^ by) % 2) * quarter
            lanes = pl.ds(pl.multiple_of(start, LANES), quarter)
            half[:, at * quarter : (at + 1) * quarter] = masked[:, lanes]


def mask_edges_kernel(frames, info, before, after, point_weight, grad_act):
    width = grad_act.shape[1]
    first = info[0] * frames
    sides = []
    for side, start in ((before, first - EDGE), (after, first + frames)):
        valid = valid_of(start, EDGE, info[1])
        rows = side[2 * EDGE :, :].astype(jnp.float32)
        sides.append(jnp.where(valid, rows, 0.0).astype(jnp.bfloat16))
    masked = jnp.concatenate(sides, axis=0)
    step = width // 3
    for at in range(0, width, step):
        grad_act[:, at : at + step] = dot(masked, point_weight[at : at + step, :], NT)


def gather_heads(info, blocks, query, key, value, bias):
    frames = query.shape[0] // len(blocks)
    for by, block in enumerate(blocks):
        rows = slice(by * frames, (by + 1) * frames)
        query[rows] = block[:frames, :] * jnp.bfloat16(SCALE)
        key[rows] = block[frames : 2 * frames, :]
        value[rows] = block[2 * frames : 3 * frames, :]
        valid = valid_of((info[0] ^ by) * frames, frames, info[1])
        bias[rows] = jnp.broadcast_to(jnp.where(valid, 0.0, NEG_FILL), (frames, LANES))


def attend_kernel(ways, info, *refs):
    blocks, outs = refs[:ways], refs[ways : 2 * ways]
    attended, log_total, before, after, query, key, value, bias, turned = refs[2 * ways :]
    gather_heads(info, blocks, query, key, value, bias)
    total_frames, share = query.shape
    frames = total_frames // ways
    for side, other in ((before, info[0] - 1), (after, info[0] + 1)):
        side[...] = jnp.zeros_like(side)
        for by in neighbours(ways):

            @pl.when((info[0] ^ other) == by)
            def _():
                for at in range(ways):
                    lanes = slice(at * share, (at + 1) * share)
                    side[:, lanes] = blocks[by][edge_rows(frames, at), :]

    for head in range(share // HEAD_DIM):
        part = slice(head * HEAD_DIM, (head + 1) * HEAD_DIM)
        spread = jnp.concatenate([bias[...]] * (total_frames // LANES), axis=1)
        scores = dot(key[:, part], query[:, part], NT) + spread
        row_max = jnp.max(scores, axis=0, keepdims=True)
        weights = jnp.exp(scores - row_max)
        total = jnp.sum(weights, axis=0, keepdims=True)
        turned[part, :] = dot(value[:, part], weights.astype(jnp.bfloat16), TN) / total
        log_total[head : head + 1, :] = row_max + jnp.log(total)
    attended[...] = turned[...].T.astype(jnp.bfloat16)
    reach = 2 * EDGE
    for by in range(ways):
        other = info[0] ^ by
        before = (info[0] ^ jnp.maximum(other - 1, 0)) * frames + frames - reach
        after = (info[0] ^ jnp.minimum(other + 1, ways - 1)) * frames
        outs[by][:reach] = attended[pl.ds(pl.multiple_of(before, reach), reach), :]
        outs[by][reach : reach + frames] = attended[by * frames : (by + 1) * frames, :]
        outs[by][reach + frames :] = attended[pl.ds(pl.multiple_of(after, reach), reach), :]


def attend_back_kernel(ways, info, *refs):
    blocks, messages = refs[:ways], refs[ways : 2 * ways]
    attended, log_total = refs[2 * ways : 2 * ways + 2]
    outs = refs[2 * ways + 2 : 3 * ways + 2]
    query, key, value, bias, grad, turned = refs[3 * ways + 2 :]
    gather_heads(info, blocks, query, key, value, bias)
    total_frames, share = query.shape
    frames = total_frames // ways
    for by in range(ways):
        grad[by * frames : (by + 1) * frames] = messages[by][:frames, :]
    turned[...] = (grad[...].astype(jnp.float32) * attended[...].astype(jnp.float32)).T
    for head in range(share // HEAD_DIM):
        part = slice(head * HEAD_DIM, (head + 1) * HEAD_DIM)
        delta = jnp.sum(turned[part, :], axis=0, keepdims=True)
        spread = jnp.concatenate([bias[...]] * (total_frames // LANES), axis=1)
        scores = dot(key[:, part], query[:, part], NT) + spread
        probs = jnp.exp(scores - log_total[head : head + 1, :])
        value_grad = dot(probs.astype(jnp.bfloat16), grad[:, part])
        prob_grad = dot(value[:, part], grad[:, part], NT)
        score_grad = (probs * (prob_grad - delta)).astype(jnp.bfloat16)
        key_grad = dot(score_grad, query[:, part])
        turned[part, :] = dot(key[:, part], score_grad, TN) * SCALE
        for by in range(ways):
            rows = slice(by * frames, (by + 1) * frames)
            outs[by][1, :, part] = key_grad[rows].astype(jnp.bfloat16)
            outs[by][2, :, part] = value_grad[rows].astype(jnp.bfloat16)
    query_grad = turned[...].T.astype(jnp.bfloat16)
    for by in range(ways):
        outs[by][0] = query_grad[by * frames : (by + 1) * frames]


def gather_kernel(ways, info, *refs):
    blocks, messages = refs[:ways], refs[ways:]
    frames, share, reach = messages[0].shape[0], blocks[0].shape[1], 2 * EDGE
    for by, message in enumerate(messages):
        lacking = [slot for slot in range(ways) if slot != by]
        for at, slot in enumerate(lacking):
            message[:, at * share : (at + 1) * share] = blocks[slot][reach : reach + frames, :]


def project_kernel(ways, info, *refs):
    blocks = refs[:ways]
    residual, before, after, out_weight, params = refs[ways : ways + 5]
    mixed, conv_in, attended = refs[ways + 5 :]
    frames, width = residual.shape
    share = width // ways
    reach = 2 * EDGE
    rows = frames + 2 * reach
    for by in range(ways):
        for at in range(ways):

            @pl.when((info[0] ^ by) == at)
            def _():
                attended[:, at * share : (at + 1) * share] = blocks[by][...]

    step = width // 3
    for at in range(0, width, step):
        part = slice(at, at + step)
        mixed[:reach, part] = before[:reach, part].astype(jnp.float32)
        mixed[reach : reach + frames, part] = residual[:, part].astype(jnp.float32)
        mixed[reach + frames :, part] = after[:reach, part].astype(jnp.float32)
        mixed[:, part] += dot(attended[...], out_weight[:, part])

    gain = params[31:32, :]
    first = info[0] * frames - reach

    def band(index, carry):
        at = pl.ds(pl.multiple_of(index * BAND, BAND), BAND)
        normed, _ = moments(mixed[at, :])
        position = first + index * BAND + lax.broadcasted_iota(jnp.int32, (BAND, 1), 0)
        valid = (position >= 0) & (position < info[1])
        conv_in[at, :] = jnp.where(valid, normed * gain, 0.0).astype(jnp.bfloat16)
        return carry

    lax.fori_loop(0, rows // BAND, band, 0)


def stride_of(rows):
    return rows // 8 + 1


def in_columns(ref, rows):
    for at in range(ref.shape[0]):
        ref[at, : rows.shape[0]] = rows[:, at * LANES : (at + 1) * LANES].astype(jnp.float32)


def from_columns(ref, rows):
    return jnp.concatenate([ref[at, rows, :] for at in range(ref.shape[0])], axis=1)


def strided(ref, index, start, stride):
    return ref[index, pl.ds(start, 8, stride=stride), :]


def depthwise(padded, taps, tap_of, out, rows):
    stride = stride_of(rows)

    def column(index, carry):
        part = pl.ds(pl.multiple_of(index * LANES, LANES), LANES)
        cells = [strided(padded, index, at + 1, stride) for at in range(stride + 2 * EDGE - 2)]
        total = [None] * stride
        for offset in range(1, 2 * EDGE):
            tap = tap_of(offset)
            scale = jnp.broadcast_to(taps[tap : tap + 1, part], (8, LANES))
            for at in range(stride):
                term = cells[at + offset - 1] * scale
                total[at] = term if total[at] is None else total[at] + term
        for at in range(stride):
            out[index, pl.ds(at, 8, stride=stride), :] = total[at]
        return carry

    lax.fori_loop(0, out.shape[0], column, 0)


def tap_grads(padded, grad, start, rows, taps):
    stride = rows // 8

    def column(index, carry):
        part = pl.ds(pl.multiple_of(index * LANES, LANES), LANES)
        cells = [
            strided(padded, index, start + at + 1, stride) for at in range(stride + 2 * EDGE - 2)
        ]
        grads = [strided(grad, index, start + at, stride) for at in range(stride)]
        for tap in range(2 * EDGE - 1):
            total = cells[tap] * grads[0]
            for at in range(1, stride):
                total = total + cells[at + tap] * grads[at]
            taps[tap : tap + 1, part] = jnp.sum(total, axis=0, keepdims=True)
        return carry

    lax.fori_loop(0, grad.shape[0], column, 0)


def conv_kernel_body(lower, info, conv_in, params, grad_own, grad_edges, *refs):
    conv_act, grad_conv, sums = refs[:3]
    halves = refs[3:-5]
    padded, conv, grad_act, bias_sum, gain_sum = refs[-5:]
    frames, width = grad_own.shape
    rows, wide = frames + 2 * EDGE, frames + 4 * EDGE
    in_columns(padded, conv_in[...])
    padded[:, wide:, :] = jnp.zeros((width // LANES, padded.shape[1] - wide, LANES), jnp.float32)
    grad_act[:EDGE] = grad_edges[:EDGE]
    grad_act[EDGE : EDGE + frames] = grad_own[...]
    grad_act[EDGE + frames :] = grad_edges[EDGE:]
    depthwise(padded, params, lambda offset: offset - 1, conv, rows)
    bias, gain = params[32:33, :], params[33:34, :]
    bias_sum[...] = jnp.zeros_like(bias_sum)
    gain_sum[...] = jnp.zeros_like(gain_sum)

    def band(index, carry):
        at = pl.ds(pl.multiple_of(index * BAND, BAND), BAND)
        normed, inv_scale = moments(from_columns(conv, at) + bias)
        scaled = normed * gain
        gate = 0.5 + 0.5 * jnp.tanh(0.5 * scaled)
        conv_act[at, :] = (scaled * gate).astype(jnp.bfloat16)
        grad_scaled = grad_act[at, :] * gate * (1.0 + scaled * (1.0 - gate))
        grad_rows = norm_back(grad_scaled * gain, normed, inv_scale)
        for column in range(width // LANES):
            grad_conv[column, at, :] = grad_rows[:, column * LANES : (column + 1) * LANES]

        @pl.when((index >= EDGE // BAND) & (index < (EDGE + frames) // BAND))
        def _():
            bias_sum[...] += fold(grad_rows)
            gain_sum[...] += fold(grad_scaled * normed)

        return carry

    lax.fori_loop(0, rows // BAND, band, 0)
    sums[0:1, :] = jnp.sum(bias_sum[...], axis=0, keepdims=True)
    sums[1:2, :] = jnp.sum(gain_sum[...], axis=0, keepdims=True)
    half = width // 2
    for by, block in enumerate(halves):
        start = ((info[2] // (2 * lower)) ^ by) * half
        block[...] = conv_act[EDGE : EDGE + frames, pl.ds(pl.multiple_of(start, LANES), half)]


def block_out_kernel(info, conv_act, mixed, point_weight, block_out):
    frames, width = block_out.shape
    step = width // 3
    for at in range(0, width, step):
        part = slice(at, at + step)
        block_out[:, part] = (
            mixed[2 * EDGE : 2 * EDGE + frames, part]
            + dot(conv_act[EDGE : EDGE + frames, :], point_weight[:, part])
        ).astype(jnp.bfloat16)


def conv_back_kernel(ways, slim, info, grad_conv, conv_in, params, masked, mixed, out_weight, *refs):
    conv_sums, grad_residual, messages = refs[0], refs[1], refs[2 : 2 + ways]
    padded, padded_in, conv, gain_sum, taps, packed, chosen = refs[2 + ways :]
    frames, width = grad_residual.shape
    share = width // ways
    reached = frames + 2 * EDGE
    padded[:, :reached, :] = grad_conv[...].astype(jnp.bfloat16).astype(jnp.float32)
    padded[:, reached:, :] = jnp.zeros(
        (width // LANES, padded.shape[1] - reached, LANES), jnp.float32
    )
    depthwise(padded, params, lambda offset: 31 - offset, conv, frames)
    gain = params[31:32, :]
    gain_sum[...] = jnp.zeros_like(gain_sum)

    def band(index, carry):
        at = pl.ds(pl.multiple_of(index * BAND, BAND), BAND)
        own_mixed = pl.ds(pl.multiple_of(index * BAND + 2 * EDGE, BAND), BAND)
        valid = valid_of(info[0] * frames + index * BAND, BAND, info[1])
        grad_in = jnp.where(valid, from_columns(conv, at), 0.0)
        normed, inv_scale = moments(mixed[own_mixed, :])
        grad_mixed = norm_back(grad_in * gain, normed, inv_scale)
        gain_sum[...] += fold(grad_in * normed)
        grad_residual[at, :] = (masked[at, :].astype(jnp.float32) + grad_mixed).astype(
            jnp.bfloat16
        )
        return carry

    lax.fori_loop(0, frames // BAND, band, 0)
    for by in range(ways):
        at = pl.ds(pl.multiple_of((info[0] ^ by) * share, share), share)
        messages[by][:frames] = dot(grad_residual[...], out_weight[at, :], NT).astype(jnp.bfloat16)

    in_columns(padded_in, conv_in[...])
    tap_grads(padded_in, grad_conv, EDGE, frames, taps)
    taps[31:32, :] = conv_sums[0:1, :]
    taps[32:33, :] = jnp.sum(gain_sum[...], axis=0, keepdims=True)
    taps[33:34, :] = conv_sums[1:2, :]
    taps[34:, :] = jnp.zeros((EXTRA - 34, width), jnp.float32)
    packed[:frames] = grad_residual[...]
    packed[frames:] = taps[...].astype(jnp.bfloat16)
    for at in range(ways):
        pieces = []
        for start in range(at * slim, width, ways * slim):
            pieces.append(packed[:, start : start + slim])
        chosen[at] = jnp.concatenate(pieces, axis=1)
    for by in range(ways):
        messages[by][frames:] = chosen[info[0] ^ by]


def split_rows(info, parts, terms, sent, kept):
    rows = terms.shape[0] // parts
    for bit in range(2):

        @pl.when(info[2] % 2 == bit)
        def _():
            for at in range(parts // 2):
                own, other = (2 * at + bit) * rows, (2 * at + 1 - bit) * rows
                kept[at] = terms[own : own + rows, :]
                sent[at] = terms[other : other + rows, :].astype(jnp.bfloat16)


def point_kernel(shift, info, *refs):
    grads, acts, (sent, kept, terms) = refs[:4], refs[4:8], refs[8:]
    left = jnp.concatenate([grad[...] for grad in grads], axis=0)
    right = jnp.concatenate([act[...] for act in acts], axis=0)
    step = terms.shape[1] // 2
    for at in range(0, 2 * step, step):
        part = slice(at, at + step)
        terms[:, part] = dot(left, right[:, part], TN)
    pieces, slim = kept.shape[0], kept.shape[1] // 2
    for bit in range(2):

        @pl.when(((info[2] >> shift) & 1) == bit)
        def _():
            for at in range(pieces):
                for side in range(2):
                    base = side * 2 * pieces * slim
                    own = base + (bit * pieces + at) * slim
                    other = base + ((1 - bit) * pieces + at) * slim
                    rows = slice(side * slim, (side + 1) * slim)
                    kept[at, rows, :] = terms[own : own + slim, :]
                    sent[at, rows, :] = terms[other : other + slim, :].astype(jnp.bfloat16)


def spread_kernel(info, kept, received, own, *blocks):
    own[...] = kept[info[0]] + received[info[0]].astype(jnp.float32)
    for by, block in enumerate(blocks, 1):
        at = info[0] ^ by
        block[...] = (kept[at] + received[at].astype(jnp.float32)).astype(jnp.bfloat16)


def point_sum_kernel(shift, info, *refs):
    blocks, (own, other) = refs[:-2], refs[-2:]
    rows = own.shape[0]
    total = blocks[0][...]
    for block in blocks[1:]:
        total = total + block[...].astype(jnp.float32)
    for at in range(2):

        @pl.when(((info[2] >> shift) & 1) == at)
        def _():
            own[...] = total[at * rows : (at + 1) * rows, :]
            other[...] = total[(1 - at) * rows : (2 - at) * rows, :].astype(jnp.bfloat16)


def weight_kernel(ways, parts, info, *refs):
    grads, rows = refs[:ways], refs[ways : 2 * ways]
    attended, sent, kept, terms = refs[2 * ways :]
    total_frames, share = attended.shape
    frames = total_frames // ways
    width = ways * share
    slim = share // parts
    left = jnp.concatenate([grad[frames : 2 * frames, :] for grad in grads], axis=0)
    for slot in range(ways):
        if slot == 0:
            right = attended[...]
        else:
            pieces = []
            for by in range(ways):
                at = (by ^ slot) - (1 if (by ^ slot) > by else 0)
                pieces.append(rows[by][:, at * share : (at + 1) * share])
            right = jnp.concatenate(pieces, axis=0)
        terms[:, slot * share : (slot + 1) * share] = dot(left, right, TN)
    small = jnp.zeros((EXTRA, share), jnp.float32)
    for grad in grads:
        small = small + grad[2 * frames :, :].astype(jnp.float32)
    filler = jnp.zeros((LANES - EXTRA, share), jnp.float32)
    terms[:, width:] = jnp.concatenate([small, filler], axis=0).T
    split_rows(info, parts, terms, sent, kept)


def halve_kernel(axis, shift, alternate, info, kept, received, sent, still_kept):
    bit = (info[axis] >> shift) & 1
    count = sent.shape[0]
    for at in range(count):
        if alternate:
            own, other = 2 * at + bit, 2 * at + 1 - bit
        else:
            own, other = bit * count + at, (1 - bit) * count + at
        still_kept[at] = kept[own] + received[own].astype(jnp.float32)
        sent[at] = (kept[other] + received[other].astype(jnp.float32)).astype(jnp.bfloat16)


def finish_kernel(ways, shift, info, kept, received, own, other, weight, taps, vectors, point):
    width = weight.shape[1]
    share, half = width // ways, width // 2
    for at in range(2):

        @pl.when(((info[2] >> shift) & 1) == at)
        def _():
            point[:, at * half : (at + 1) * half] = own[...]
            point[:, (1 - at) * half : (2 - at) * half] = other[...].astype(jnp.float32)

    total = kept[0] + received[0].astype(jnp.float32)
    for by in range(ways):
        for at in range(ways):

            @pl.when((info[0] ^ by) == at)
            def _():
                weight[:, at * share : (at + 1) * share] = total[:, by * share : (by + 1) * share]

    small = total[:, width:].T
    taps[...] = small[:31]
    vectors[...] = small[31:34]


def swap(block, axis, by):
    return lax.ppermute(block, axis, [(i, i ^ by) for i in range(lax.axis_size(axis))])


def swap_all(blocks, axis, step=1):
    return [blocks[0]] + [swap(block, axis, step * by) for by, block in enumerate(blocks[1:], 1)]


def local(
    residual_in,
    query_rows,
    key_rows,
    value_rows,
    lengths,
    out_weight,
    norm_gain,
    conv_kernel,
    conv_bias,
    conv_gain,
    point_weight,
    grad_out,
):
    ways = lax.axis_size("ctx")
    parts = lax.axis_size("dp")
    own = lax.axis_index("ctx")
    place = lax.axis_index("dp")
    frames, width = residual_in.shape[1:]
    share = width // ways
    slim = share // parts
    heads = HEADS // ways
    every = ways * frames
    lower = parts // 4
    half = width // 2
    tiles = width // LANES
    bf16, f32 = jnp.bfloat16, jnp.float32
    square = 2 * frames * width * width
    rows_bytes = 2 * frames * width
    reached, wide = frames + 2 * EDGE, frames + 4 * EDGE

    info = jnp.stack([own, lengths[0], place]).astype(jnp.int32)
    params = jnp.concatenate(
        [conv_kernel, norm_gain[None], conv_bias[None], conv_gain[None]], axis=0
    )

    by_tiles = share % LANES == 0
    packed_rows = [3 * frames + 3 * EDGE * ways * (by in neighbours(ways)) for by in range(ways)]
    packed = call(
        functools.partial(pack_kernel, ways),
        "pack",
        [((rows, share), bf16) for rows in packed_rows],
        scratch=[((3, frames, width), bf16), ((2, 3 * EDGE, width), bf16)],
        semaphores=7,
        far=("in",),
        megabytes=58,
        moved=6 * rows_bytes,
    )(query_rows[0], key_rows[0], value_rows[0], residual_in[0], grad_out[0])
    packed = swap_all(packed, "ctx")

    masked, grad_own, packed[0], *masked_halves = call(
        functools.partial(mask_kernel, lower),
        "mask",
        [((frames, width), bf16), ((frames, width), f32), ((3 * frames, share), bf16)]
        + [((frames, half), bf16)] * 2,
        flops=2 * square,
        moved=6 * rows_bytes + 2 * width * width,
    )(info, grad_out[0], point_weight, packed[0])
    packed[1], masked_halves = lax.optimization_barrier((packed[1], masked_halves))
    masked_halves = swap_all([masked_halves[by % 2] for by in range(4)], "dp", lower)

    packed, masked = lax.optimization_barrier((packed, masked))
    head_scratch = [((every, share), bf16)] * 3 + [((every, LANES), f32)]
    pair_flops = 2 * heads * every * every * HEAD_DIM
    *returned, attended, log_total, before, after = call(
        functools.partial(attend_kernel, ways),
        "attend",
        [((wide, share), bf16)] * ways + [((every, share), bf16), ((heads, every), f32)]
        + [((3 * EDGE, width), bf16)] * 2,
        scratch=head_scratch + [((share, every), f32)],
        flops=8 * pair_flops,
        moved=4 * rows_bytes,
        exps=heads * every * every,
    )(info, *packed)
    returned, masked_halves[1:3] = lax.optimization_barrier((returned, masked_halves[1:3]))
    returned = swap_all(returned, "ctx")
    grad_edges = call(
        functools.partial(mask_edges_kernel, frames),
        "mask_edges",
        [((2 * EDGE, width), f32)],
        flops=square,
        moved=2 * width * width,
    )(info, before, after, point_weight)[0]
    returned, grad_edges, masked_halves = lax.optimization_barrier(
        (returned, grad_edges, masked_halves)
    )
    messages = call(
        functools.partial(gather_kernel, ways),
        "gather",
        [((frames, width - share), bf16)] * ways,
        moved=8 * rows_bytes,
    )(info, *returned)
    arrived = swap_all(messages, "ctx")

    returned, messages = lax.optimization_barrier((returned, messages))
    mixed, conv_in = call(
        functools.partial(project_kernel, ways),
        "project",
        [((wide, width), f32), ((wide, width), bf16)],
        scratch=[((wide, width), bf16)],
        flops=square,
        moved=6 * rows_bytes + 2 * width * width,
    )(info, *returned, residual_in[0], before, after, out_weight, params)
    spread = 8 * stride_of(reached)
    conv_act, grad_conv, conv_sums, *act_halves = call(
        functools.partial(conv_kernel_body, lower),
        "conv",
        [
            ((reached, width), bf16),
            ((tiles, reached, LANES), f32),
            ((2, width), f32),
        ]
        + [((frames, half), bf16)] * 2,
        scratch=[
            ((tiles, spread + 2 * EDGE, LANES), f32),
            ((tiles, spread, LANES), f32),
            ((reached, width), f32),
            ((8, width), f32),
            ((8, width), f32),
        ],
        flops=frames * width * 4000,
        moved=6 * rows_bytes,
        exps=frames * width,
    )(info, conv_in, params, grad_own, grad_edges)
    near, act_halves = lax.optimization_barrier((arrived[:NEAR], act_halves))
    act_halves = swap_all([act_halves[by // 2] for by in range(4)], "dp", lower)
    far, grad_conv = lax.optimization_barrier((arrived[NEAR:], grad_conv))

    spread = 8 * stride_of(frames)
    grad_residual, *grad_messages = call(
        functools.partial(conv_back_kernel, ways, slim),
        "conv_back",
        [((frames, width), bf16)] + [((2 * frames + EXTRA, share), bf16)] * ways,
        scratch=[
            ((tiles, spread + 2 * EDGE, LANES), f32),
            ((tiles, wide, LANES), f32),
            ((tiles, spread, LANES), f32),
            ((8, width), f32),
            ((EXTRA, width), f32),
            ((frames + EXTRA, width), bf16),
            ((ways, frames + EXTRA, share), bf16),
        ],
        flops=frames * width * 8000,
        moved=8 * rows_bytes + 2 * width * width,
    )(
        info,
        grad_conv,
        conv_in,
        params,
        masked,
        mixed,
        out_weight,
        conv_sums,
    )
    act_halves[1], grad_messages[NEAR:] = lax.optimization_barrier(
        (act_halves[1], grad_messages[NEAR:])
    )
    act_halves, conv_act = lax.optimization_barrier((act_halves, conv_act))
    messages = near + far
    grad_messages = swap_all(grad_messages, "ctx")

    block_out = call(
        block_out_kernel,
        "block_out",
        [((frames, width), bf16)],
        flops=square,
        moved=4 * rows_bytes + 2 * width * width,
    )(info, conv_act, mixed, point_weight)[0]

    def halve(kept, received, axis, shift, alternate):
        extent = (kept.shape[0] // 2,) + kept.shape[1:]
        return call(
            functools.partial(halve_kernel, 0 if axis == "ctx" else 2, shift, alternate),
            "halve",
            [(extent, bf16), (extent, f32)],
            moved=16 * extent[0] * extent[1] * extent[2],
        )(info, kept, received)

    grad_messages[1], act_halves = lax.optimization_barrier((grad_messages[1], act_halves))
    bits = list(reversed(range(lower.bit_length() - 1)))
    point_half = (lower * ways // 2, 2 * slim, half)
    point_sent, point_kept = call(
        functools.partial(point_kernel, bits[0]),
        "point_terms",
        [(point_half, bf16), (point_half, f32)],
        scratch=[((half, half), f32)],
        flops=square,
        moved=8 * rows_bytes,
    )(info, *masked_halves, *act_halves)
    grad_messages, point_sent, block_out = lax.optimization_barrier(
        (grad_messages, point_sent, block_out)
    )
    extent = width + LANES
    core_half = (parts // 2, slim, extent)
    sent, kept = call(
        functools.partial(weight_kernel, ways, parts),
        "out_terms",
        [(core_half, bf16), (core_half, f32)],
        scratch=[((share, extent), f32)],
        flops=square,
        moved=10 * rows_bytes,
    )(info, *grad_messages, *messages, attended)
    received = swap(sent, "dp", 1)
    for shift in range(1, parts.bit_length() - 1):
        sent, kept = halve(kept, received, "dp", shift, True)
        received = swap(sent, "dp", 2**shift)

    point_received = swap(point_sent, "dp", 2 ** bits[0])
    for shift in bits[1:]:
        point_sent, point_kept = halve(point_kept, point_received, "dp", shift, False)
        point_received = swap(point_sent, "dp", 2**shift)
    pieces = call(
        spread_kernel,
        "spread",
        [((2 * slim, half), f32)] + [((2 * slim, half), bf16)] * (ways - 1),
        moved=slim * width * 6 * ways,
    )(info, point_kept, point_received)
    pieces = swap_all(pieces, "ctx")
    grad_packed = call(
        functools.partial(attend_back_kernel, ways),
        "attend_back",
        [((3, frames, share), bf16)] * ways,
        scratch=head_scratch + [((every, share), bf16), ((share, every), f32)],
        flops=20 * pair_flops,
        moved=8 * rows_bytes,
        exps=heads * every * every,
    )(info, *packed, *grad_messages, attended, log_total)
    pieces, grad_packed = lax.optimization_barrier((pieces, grad_packed))
    grad_packed = swap_all(grad_packed, "ctx")
    layer_bit = (parts // 2).bit_length() - 1
    point_own, point_other = call(
        functools.partial(point_sum_kernel, layer_bit),
        "point_sum",
        [((slim, half), f32), ((slim, half), bf16)],
        moved=slim * width * (parts + 8),
    )(info, *pieces)
    point_other = swap(point_other, "dp", parts // 2)

    out_total, taps, vectors, point_total = call(
        functools.partial(finish_kernel, ways, layer_bit),
        "finish",
        [((slim, width), f32), ((31, slim), f32), ((3, slim), f32), ((slim, width), f32)],
        moved=slim * extent * (parts + 8),
    )(info, kept, received, point_own, point_other)

    grad_query, grad_key, grad_value = call(
        functools.partial(unpack_kernel if by_tiles else unpack_parts_kernel, ways),
        "unpack",
        [((frames, width), bf16)] * 3,
        semaphores=3 * ways if by_tiles else 0,
        far=("out",) if by_tiles else (),
        moved=6 * rows_bytes,
    )(info, *grad_packed)

    return (
        block_out[None],
        grad_residual[None],
        grad_query[None],
        grad_key[None],
        grad_value[None],
        out_total.T,
        point_total.T,
        taps,
        vectors,
    )


def solution(mesh):
    rows = P("dp", "ctx", None)
    columns = P(None, ("dp", "ctx"))
    in_specs = (rows, rows, rows, rows, P("dp"), P(), P(), P(), P(), P(), P(), rows)
    out_specs = (rows,) * 5 + (columns,) * 4
    return jax.shard_map(local, mesh=mesh, in_specs=in_specs, out_specs=out_specs, check_vma=False)
```

```python
import functools

import jax
import jax.numpy as jnp
from jax import lax
from jax.experimental import pallas as pl
from jax.experimental.pallas import tpu as pltpu
from jax.sharding import PartitionSpec as P

HEADS = 24
HEAD_DIM = 64
SCALE = HEAD_DIM ** (-0.5)

NEG_FILL = -1e30
EPSILON = 1e-05

LANES = 128
EDGE = 16
NEAR = 3
BAND = 16
EXTRA = 48

NN = (((1,), (0,)), ((), ()))
NT = (((1,), (1,)), ((), ()))
TN = (((0,), (0,)), ((), ()))


def dot(left, right, dims=NN):
    return lax.dot_general(left, right, dims, preferred_element_type=jnp.float32)


def call(
    kernel, name, outs, scratch=(), semaphores=0, far=(), megabytes=28, flops=0, moved=0, exps=0
):
    vmem = pl.BlockSpec(memory_space=pltpu.VMEM)
    smem = pl.BlockSpec(memory_space=pltpu.SMEM)
    anywhere = pl.BlockSpec(memory_space=pl.ANY)

    def run(*arrays):
        scratches = [pltpu.VMEM(shape, kind) for shape, kind in scratch]
        if semaphores:
            scratches.append(pltpu.SemaphoreType.DMA((semaphores,)))
        return pl.pallas_call(
            kernel,
            name=name,
            in_specs=[smem if a.ndim == 1 else anywhere if "in" in far else vmem for a in arrays],
            out_specs=[anywhere if "out" in far else vmem] * len(outs),
            out_shape=[jax.ShapeDtypeStruct(shape, kind) for shape, kind in outs],
            scratch_shapes=scratches,
            compiler_params=pltpu.CompilerParams(vmem_limit_bytes=megabytes << 20),
            cost_estimate=pl.CostEstimate(flops=flops, bytes_accessed=moved, transcendentals=exps),
        )(*arrays)

    return run


def valid_of(first, rows, length):
    return first + lax.broadcasted_iota(jnp.int32, (rows, 1), 0) < length


def moments(rows):
    centre = jnp.mean(rows, axis=-1, keepdims=True)
    centred = rows - centre
    inv_scale = lax.rsqrt(jnp.mean(centred * centred, axis=-1, keepdims=True) + EPSILON)
    return centred * inv_scale, inv_scale


def norm_back(grad_normed, normed, inv_scale):
    first_mean = jnp.mean(grad_normed, axis=-1, keepdims=True)
    second_mean = jnp.mean(grad_normed * normed, axis=-1, keepdims=True)
    return inv_scale * (grad_normed - first_mean - normed * second_mean)


def fold(rows):
    total = rows[:8]
    for at in range(8, rows.shape[0], 8):
        total = total + rows[at : at + 8]
    return total


def at_group(info, by, ways, share, visit):
    if share % LANES == 0:
        visit(pl.ds(pl.multiple_of((info[0] ^ by) * share, LANES), share))
        return
    for at in range(ways):

        @pl.when((info[0] ^ by) == at)
        def _():
            visit(slice(at * share, (at + 1) * share))


def neighbours(ways):
    return [by for by in (1, 3, 7, 15) if by < ways]


def edge_rows(frames, at):
    return slice(3 * frames + at * 3 * EDGE, 3 * frames + (at + 1) * 3 * EDGE)


def pack_kernel(ways, query, key, value, residual, grad_out, *refs):
    blocks, whole, ends, arrived = refs[:ways], refs[ways], refs[ways + 1], refs[ways + 2]
    info = [lax.axis_index("ctx")]
    frames, width = query.shape
    share, reach = width // ways, 2 * EDGE
    pairs = [(rows, whole.at[slot]) for slot, rows in enumerate((query, key, value))]
    for side, tail in enumerate((False, True)):
        for rows, start, count in ((residual, 0, reach), (grad_out, reach, EDGE)):
            first = frames - count if tail else 0
            pairs.append((rows.at[pl.ds(first, count)], ends.at[side, pl.ds(start, count)]))
    copies = [
        pltpu.make_async_copy(source, target, arrived.at[at])
        for at, (source, target) in enumerate(pairs)
    ]
    for copy in copies:
        copy.start()
    for slot, copy in enumerate(copies[:3]):
        copy.wait()
        for by in range(ways):

            def visit(lanes):
                blocks[by][slot * frames : (slot + 1) * frames, :] = whole[slot, :, lanes]

            at_group(info, by, ways, share, visit)
    for copy in copies[3:]:
        copy.wait()
    for by in neighbours(ways):
        side = jnp.where((info[0] ^ by) > info[0], 1, 0)
        for at in range(ways):
            blocks[by][edge_rows(frames, at), :] = ends[side, :, at * share : (at + 1) * share]


def unpack_kernel(ways, info, *refs):
    blocks, outs, arrived = refs[:ways], refs[ways:-1], refs[-1]
    share = blocks[0].shape[2]
    copies = []
    for by in range(ways):
        for slot, rows in enumerate(outs):
            lanes = pl.ds(pl.multiple_of((info[0] ^ by) * share, LANES), share)
            copy = pltpu.make_async_copy(
                blocks[by].at[slot], rows.at[:, lanes], arrived.at[len(copies)]
            )
            copy.start()
            copies.append(copy)
    for copy in copies:
        copy.wait()


def unpack_parts_kernel(ways, info, *refs):
    blocks, outs = refs[:ways], refs[ways:]
    share = blocks[0].shape[2]
    for by in range(ways):
        for slot, rows in enumerate(outs):

            def visit(lanes):
                rows[:, lanes] = blocks[by][slot]

            at_group(info, by, ways, share, visit)


def mask_kernel(lower, info, grad_out, masked, *halves):
    frames, width = grad_out.shape
    valid = valid_of(info[0] * frames, frames, info[1])
    masked[...] = jnp.where(valid, grad_out[...].astype(jnp.float32), 0.0).astype(jnp.bfloat16)
    quarter = width // 4
    for by, half in enumerate(halves):
        for at in range(2):
            start = (2 * at + ((info[2] // lower) ^ by) % 2) * quarter
            lanes = pl.ds(pl.multiple_of(start, LANES), quarter)
            half[:, at * quarter : (at + 1) * quarter] = masked[:, lanes]


def grad_act_kernel(info, masked, point_weight, block, grad_act, own_block):
    own_block[...] = block[...]
    width = masked.shape[1]
    step = width // 3
    for at in range(0, width, step):
        grad_act[:, at : at + step] = dot(masked[...], point_weight[at : at + step, :], NT)


def mask_edges_kernel(frames, info, before, after, point_weight, grad_act):
    width = grad_act.shape[1]
    first = info[0] * frames
    sides = []
    for side, start in ((before, first - EDGE), (after, first + frames)):
        valid = valid_of(start, EDGE, info[1])
        rows = side[2 * EDGE :, :].astype(jnp.float32)
        sides.append(jnp.where(valid, rows, 0.0).astype(jnp.bfloat16))
    masked = jnp.concatenate(sides, axis=0)
    step = width // 3
    for at in range(0, width, step):
        grad_act[:, at : at + step] = dot(masked, point_weight[at : at + step, :], NT)


def gather_heads(info, blocks, query, key, value, bias):
    frames = query.shape[0] // len(blocks)
    for by, block in enumerate(blocks):
        rows = slice(by * frames, (by + 1) * frames)
        query[rows] = block[:frames, :] * jnp.bfloat16(SCALE)
        key[rows] = block[frames : 2 * frames, :]
        value[rows] = block[2 * frames : 3 * frames, :]
        valid = valid_of((info[0] ^ by) * frames, frames, info[1])
        bias[rows] = jnp.broadcast_to(jnp.where(valid, 0.0, NEG_FILL), (frames, LANES))


def attend_kernel(ways, info, *refs):
    blocks, outs = refs[:ways], refs[ways : 2 * ways]
    attended, log_total, before, after, query, key, value, bias, turned = refs[2 * ways :]
    gather_heads(info, blocks, query, key, value, bias)
    total_frames, share = query.shape
    frames = total_frames // ways
    for side, other in ((before, info[0] - 1), (after, info[0] + 1)):
        side[...] = jnp.zeros_like(side)
        for by in neighbours(ways):

            @pl.when((info[0] ^ other) == by)
            def _():
                for at in range(ways):
                    lanes = slice(at * share, (at + 1) * share)
                    side[:, lanes] = blocks[by][edge_rows(frames, at), :]

    for head in range(share // HEAD_DIM):
        part = slice(head * HEAD_DIM, (head + 1) * HEAD_DIM)
        spread = jnp.concatenate([bias[...]] * (total_frames // LANES), axis=1)
        scores = dot(key[:, part], query[:, part], NT) + spread
        row_max = jnp.max(scores, axis=0, keepdims=True)
        weights = jnp.exp(scores - row_max)
        total = jnp.sum(weights, axis=0, keepdims=True)
        turned[part, :] = dot(value[:, part], weights.astype(jnp.bfloat16), TN) / total
        log_total[head : head + 1, :] = row_max + jnp.log(total)
    attended[...] = turned[...].T.astype(jnp.bfloat16)
    reach = 2 * EDGE
    for by in range(ways):
        other = info[0] ^ by
        before = (info[0] ^ jnp.maximum(other - 1, 0)) * frames + frames - reach
        after = (info[0] ^ jnp.minimum(other + 1, ways - 1)) * frames
        outs[by][:reach] = attended[pl.ds(pl.multiple_of(before, reach), reach), :]
        outs[by][reach : reach + frames] = attended[by * frames : (by + 1) * frames, :]
        outs[by][reach + frames :] = attended[pl.ds(pl.multiple_of(after, reach), reach), :]


def attend_back_kernel(ways, info, *refs):
    blocks, messages = refs[:ways], refs[ways : 2 * ways]
    attended, log_total = refs[2 * ways : 2 * ways + 2]
    outs = refs[2 * ways + 2 : 3 * ways + 2]
    query, key, value, bias, grad, turned = refs[3 * ways + 2 :]
    gather_heads(info, blocks, query, key, value, bias)
    total_frames, share = query.shape
    frames = total_frames // ways
    for by in range(ways):
        grad[by * frames : (by + 1) * frames] = messages[by][:frames, :]
    turned[...] = (grad[...].astype(jnp.float32) * attended[...].astype(jnp.float32)).T
    for head in range(share // HEAD_DIM):
        part = slice(head * HEAD_DIM, (head + 1) * HEAD_DIM)
        delta = jnp.sum(turned[part, :], axis=0, keepdims=True)
        spread = jnp.concatenate([bias[...]] * (total_frames // LANES), axis=1)
        scores = dot(key[:, part], query[:, part], NT) + spread
        probs = jnp.exp(scores - log_total[head : head + 1, :])
        value_grad = dot(probs.astype(jnp.bfloat16), grad[:, part])
        prob_grad = dot(value[:, part], grad[:, part], NT)
        score_grad = (probs * (prob_grad - delta)).astype(jnp.bfloat16)
        key_grad = dot(score_grad, query[:, part])
        turned[part, :] = dot(key[:, part], score_grad, TN) * SCALE
        for by in range(ways):
            rows = slice(by * frames, (by + 1) * frames)
            outs[by][1, :, part] = key_grad[rows].astype(jnp.bfloat16)
            outs[by][2, :, part] = value_grad[rows].astype(jnp.bfloat16)
    query_grad = turned[...].T.astype(jnp.bfloat16)
    for by in range(ways):
        outs[by][0] = query_grad[by * frames : (by + 1) * frames]


def gather_kernel(ways, info, *refs):
    blocks, messages = refs[:ways], refs[ways:]
    frames, share, reach = messages[0].shape[0], blocks[0].shape[1], 2 * EDGE
    for by, message in enumerate(messages):
        lacking = [slot for slot in range(ways) if slot != by]
        for at, slot in enumerate(lacking):
            message[:, at * share : (at + 1) * share] = blocks[slot][reach : reach + frames, :]


def project_kernel(ways, info, *refs):
    blocks = refs[:ways]
    residual, before, after, out_weight, params = refs[ways : ways + 5]
    mixed, conv_in, attended = refs[ways + 5 :]
    frames, width = residual.shape
    share = width // ways
    reach = 2 * EDGE
    rows = frames + 2 * reach
    for by in range(ways):
        for at in range(ways):

            @pl.when((info[0] ^ by) == at)
            def _():
                attended[:, at * share : (at + 1) * share] = blocks[by][...]

    step = width // 3
    for at in range(0, width, step):
        part = slice(at, at + step)
        mixed[:reach, part] = before[:reach, part].astype(jnp.float32)
        mixed[reach : reach + frames, part] = residual[:, part].astype(jnp.float32)
        mixed[reach + frames :, part] = after[:reach, part].astype(jnp.float32)
        mixed[:, part] += dot(attended[...], out_weight[:, part])

    gain = params[31:32, :]
    first = info[0] * frames - reach

    def band(index, carry):
        at = pl.ds(pl.multiple_of(index * BAND, BAND), BAND)
        normed, _ = moments(mixed[at, :])
        position = first + index * BAND + lax.broadcasted_iota(jnp.int32, (BAND, 1), 0)
        valid = (position >= 0) & (position < info[1])
        conv_in[at, :] = jnp.where(valid, normed * gain, 0.0).astype(jnp.bfloat16)
        return carry

    lax.fori_loop(0, rows // BAND, band, 0)


def stride_of(rows):
    return rows // 8 + 1


def in_columns(ref, rows):
    for at in range(ref.shape[0]):
        ref[at, : rows.shape[0]] = rows[:, at * LANES : (at + 1) * LANES].astype(jnp.float32)


def from_columns(ref, rows):
    return jnp.concatenate([ref[at, rows, :] for at in range(ref.shape[0])], axis=1)


def strided(ref, index, start, stride):
    return ref[index, pl.ds(start, 8, stride=stride), :]


def depthwise(padded, taps, tap_of, out, rows):
    stride = stride_of(rows)

    def column(index, carry):
        part = pl.ds(pl.multiple_of(index * LANES, LANES), LANES)
        cells = [strided(padded, index, at + 1, stride) for at in range(stride + 2 * EDGE - 2)]
        total = [None] * stride
        for offset in range(1, 2 * EDGE):
            tap = tap_of(offset)
            scale = jnp.broadcast_to(taps[tap : tap + 1, part], (8, LANES))
            for at in range(stride):
                term = cells[at + offset - 1] * scale
                total[at] = term if total[at] is None else total[at] + term
        for at in range(stride):
            out[index, pl.ds(at, 8, stride=stride), :] = total[at]
        return carry

    lax.fori_loop(0, out.shape[0], column, 0)


def tap_grads(padded, grad, start, rows, taps):
    stride = rows // 8

    def column(index, carry):
        part = pl.ds(pl.multiple_of(index * LANES, LANES), LANES)
        cells = [
            strided(padded, index, start + at + 1, stride) for at in range(stride + 2 * EDGE - 2)
        ]
        grads = [strided(grad, index, start + at, stride) for at in range(stride)]
        for tap in range(2 * EDGE - 1):
            total = cells[tap] * grads[0]
            for at in range(1, stride):
                total = total + cells[at + tap] * grads[at]
            taps[tap : tap + 1, part] = jnp.sum(total, axis=0, keepdims=True)
        return carry

    lax.fori_loop(0, grad.shape[0], column, 0)


def conv_kernel_body(lower, info, conv_in, params, grad_own, grad_edges, *refs):
    conv_act, grad_conv, sums = refs[:3]
    halves = refs[3:-5]
    padded, conv, grad_act, bias_sum, gain_sum = refs[-5:]
    frames, width = grad_own.shape
    rows, wide = frames + 2 * EDGE, frames + 4 * EDGE
    in_columns(padded, conv_in[...])
    padded[:, wide:, :] = jnp.zeros((width // LANES, padded.shape[1] - wide, LANES), jnp.float32)
    grad_act[:EDGE] = grad_edges[:EDGE]
    grad_act[EDGE : EDGE + frames] = grad_own[...]
    grad_act[EDGE + frames :] = grad_edges[EDGE:]
    depthwise(padded, params, lambda offset: offset - 1, conv, rows)
    bias, gain = params[32:33, :], params[33:34, :]
    bias_sum[...] = jnp.zeros_like(bias_sum)
    gain_sum[...] = jnp.zeros_like(gain_sum)

    def band(index, carry):
        at = pl.ds(pl.multiple_of(index * BAND, BAND), BAND)
        normed, inv_scale = moments(from_columns(conv, at) + bias)
        scaled = normed * gain
        gate = 0.5 + 0.5 * jnp.tanh(0.5 * scaled)
        conv_act[at, :] = (scaled * gate).astype(jnp.bfloat16)
        grad_scaled = grad_act[at, :] * gate * (1.0 + scaled * (1.0 - gate))
        grad_rows = norm_back(grad_scaled * gain, normed, inv_scale)
        for column in range(width // LANES):
            grad_conv[column, at, :] = grad_rows[:, column * LANES : (column + 1) * LANES]

        @pl.when((index >= EDGE // BAND) & (index < (EDGE + frames) // BAND))
        def _():
            bias_sum[...] += fold(grad_rows)
            gain_sum[...] += fold(grad_scaled * normed)

        return carry

    lax.fori_loop(0, rows // BAND, band, 0)
    sums[0:1, :] = jnp.sum(bias_sum[...], axis=0, keepdims=True)
    sums[1:2, :] = jnp.sum(gain_sum[...], axis=0, keepdims=True)
    half = width // 2
    for by, block in enumerate(halves):
        start = ((info[2] // (2 * lower)) ^ by) * half
        block[...] = conv_act[EDGE : EDGE + frames, pl.ds(pl.multiple_of(start, LANES), half)]


def block_out_kernel(info, conv_act, mixed, point_weight, block_out):
    frames, width = block_out.shape
    step = width // 3
    for at in range(0, width, step):
        part = slice(at, at + step)
        block_out[:, part] = (
            mixed[2 * EDGE : 2 * EDGE + frames, part]
            + dot(conv_act[EDGE : EDGE + frames, :], point_weight[:, part])
        ).astype(jnp.bfloat16)


def conv_back_kernel(ways, slim, info, grad_conv, conv_in, params, masked, mixed, out_weight, *refs):
    conv_sums, grad_residual, messages = refs[0], refs[1], refs[2 : 2 + ways]
    padded, padded_in, conv, gain_sum, taps, packed, chosen = refs[2 + ways :]
    frames, width = grad_residual.shape
    share = width // ways
    reached = frames + 2 * EDGE
    padded[:, :reached, :] = grad_conv[...].astype(jnp.bfloat16).astype(jnp.float32)
    padded[:, reached:, :] = jnp.zeros(
        (width // LANES, padded.shape[1] - reached, LANES), jnp.float32
    )
    depthwise(padded, params, lambda offset: 31 - offset, conv, frames)
    gain = params[31:32, :]
    gain_sum[...] = jnp.zeros_like(gain_sum)

    def band(index, carry):
        at = pl.ds(pl.multiple_of(index * BAND, BAND), BAND)
        own_mixed = pl.ds(pl.multiple_of(index * BAND + 2 * EDGE, BAND), BAND)
        valid = valid_of(info[0] * frames + index * BAND, BAND, info[1])
        grad_in = jnp.where(valid, from_columns(conv, at), 0.0)
        normed, inv_scale = moments(mixed[own_mixed, :])
        grad_mixed = norm_back(grad_in * gain, normed, inv_scale)
        gain_sum[...] += fold(grad_in * normed)
        grad_residual[at, :] = (masked[at, :].astype(jnp.float32) + grad_mixed).astype(
            jnp.bfloat16
        )
        return carry

    lax.fori_loop(0, frames // BAND, band, 0)
    for by in range(ways):
        at = pl.ds(pl.multiple_of((info[0] ^ by) * share, share), share)
        messages[by][:frames] = dot(grad_residual[...], out_weight[at, :], NT).astype(jnp.bfloat16)

    in_columns(padded_in, conv_in[...])
    tap_grads(padded_in, grad_conv, EDGE, frames, taps)
    taps[31:32, :] = conv_sums[0:1, :]
    taps[32:33, :] = jnp.sum(gain_sum[...], axis=0, keepdims=True)
    taps[33:34, :] = conv_sums[1:2, :]
    taps[34:, :] = jnp.zeros((EXTRA - 34, width), jnp.float32)
    packed[:frames] = grad_residual[...]
    packed[frames:] = taps[...].astype(jnp.bfloat16)
    for at in range(ways):
        pieces = []
        for start in range(at * slim, width, ways * slim):
            pieces.append(packed[:, start : start + slim])
        chosen[at] = jnp.concatenate(pieces, axis=1)
    for by in range(ways):
        messages[by][frames:] = chosen[info[0] ^ by]


def split_rows(info, parts, terms, sent, kept):
    rows = terms.shape[0] // parts
    for bit in range(2):

        @pl.when(info[2] % 2 == bit)
        def _():
            for at in range(parts // 2):
                own, other = (2 * at + bit) * rows, (2 * at + 1 - bit) * rows
                kept[at] = terms[own : own + rows, :]
                sent[at] = terms[other : other + rows, :].astype(jnp.bfloat16)


def point_kernel(shift, info, *refs):
    grads, acts, (sent, kept, terms) = refs[:4], refs[4:8], refs[8:]
    left = jnp.concatenate([grad[...] for grad in grads], axis=0)
    right = jnp.concatenate([act[...] for act in acts], axis=0)
    step = terms.shape[1] // 2
    for at in range(0, 2 * step, step):
        part = slice(at, at + step)
        terms[:, part] = dot(left, right[:, part], TN)
    pieces, slim = kept.shape[0], kept.shape[1] // 2
    for bit in range(2):

        @pl.when(((info[2] >> shift) & 1) == bit)
        def _():
            for at in range(pieces):
                for side in range(2):
                    base = side * 2 * pieces * slim
                    own = base + (bit * pieces + at) * slim
                    other = base + ((1 - bit) * pieces + at) * slim
                    rows = slice(side * slim, (side + 1) * slim)
                    kept[at, rows, :] = terms[own : own + slim, :]
                    sent[at, rows, :] = terms[other : other + slim, :].astype(jnp.bfloat16)


def spread_kernel(info, kept, received, own, *blocks):
    own[...] = kept[info[0]] + received[info[0]].astype(jnp.float32)
    for by, block in enumerate(blocks, 1):
        at = info[0] ^ by
        block[...] = (kept[at] + received[at].astype(jnp.float32)).astype(jnp.bfloat16)


def point_sum_kernel(shift, info, *refs):
    blocks, (own, other) = refs[:-2], refs[-2:]
    rows = own.shape[0]
    total = blocks[0][...]
    for block in blocks[1:]:
        total = total + block[...].astype(jnp.float32)
    for at in range(2):

        @pl.when(((info[2] >> shift) & 1) == at)
        def _():
            own[...] = total[at * rows : (at + 1) * rows, :]
            other[...] = total[(1 - at) * rows : (2 - at) * rows, :].astype(jnp.bfloat16)


def weight_kernel(ways, parts, info, *refs):
    grads, rows = refs[:ways], refs[ways : 2 * ways]
    attended, sent, kept, terms = refs[2 * ways :]
    total_frames, share = attended.shape
    frames = total_frames // ways
    width = ways * share
    slim = share // parts
    left = jnp.concatenate([grad[frames : 2 * frames, :] for grad in grads], axis=0)
    for slot in range(ways):
        if slot == 0:
            right = attended[...]
        else:
            pieces = []
            for by in range(ways):
                at = (by ^ slot) - (1 if (by ^ slot) > by else 0)
                pieces.append(rows[by][:, at * share : (at + 1) * share])
            right = jnp.concatenate(pieces, axis=0)
        terms[:, slot * share : (slot + 1) * share] = dot(left, right, TN)
    small = jnp.zeros((EXTRA, share), jnp.float32)
    for grad in grads:
        small = small + grad[2 * frames :, :].astype(jnp.float32)
    filler = jnp.zeros((LANES - EXTRA, share), jnp.float32)
    terms[:, width:] = jnp.concatenate([small, filler], axis=0).T
    split_rows(info, parts, terms, sent, kept)


def halve_kernel(axis, shift, alternate, info, kept, received, sent, still_kept):
    bit = (info[axis] >> shift) & 1
    count = sent.shape[0]
    for at in range(count):
        if alternate:
            own, other = 2 * at + bit, 2 * at + 1 - bit
        else:
            own, other = bit * count + at, (1 - bit) * count + at
        still_kept[at] = kept[own] + received[own].astype(jnp.float32)
        sent[at] = (kept[other] + received[other].astype(jnp.float32)).astype(jnp.bfloat16)


def finish_kernel(ways, shift, info, kept, received, own, other, weight, taps, vectors, point):
    width = weight.shape[1]
    share, half = width // ways, width // 2
    for at in range(2):

        @pl.when(((info[2] >> shift) & 1) == at)
        def _():
            point[:, at * half : (at + 1) * half] = own[...]
            point[:, (1 - at) * half : (2 - at) * half] = other[...].astype(jnp.float32)

    total = kept[0] + received[0].astype(jnp.float32)
    for by in range(ways):
        for at in range(ways):

            @pl.when((info[0] ^ by) == at)
            def _():
                weight[:, at * share : (at + 1) * share] = total[:, by * share : (by + 1) * share]

    small = total[:, width:].T
    taps[...] = small[:31]
    vectors[...] = small[31:34]


def swap(block, axis, by):
    return lax.ppermute(block, axis, [(i, i ^ by) for i in range(lax.axis_size(axis))])


def swap_all(blocks, axis, step=1):
    return [blocks[0]] + [swap(block, axis, step * by) for by, block in enumerate(blocks[1:], 1)]


def local(
    residual_in,
    query_rows,
    key_rows,
    value_rows,
    lengths,
    out_weight,
    norm_gain,
    conv_kernel,
    conv_bias,
    conv_gain,
    point_weight,
    grad_out,
):
    ways = lax.axis_size("ctx")
    parts = lax.axis_size("dp")
    own = lax.axis_index("ctx")
    place = lax.axis_index("dp")
    frames, width = residual_in.shape[1:]
    share = width // ways
    slim = share // parts
    heads = HEADS // ways
    every = ways * frames
    lower = parts // 4
    half = width // 2
    tiles = width // LANES
    bf16, f32 = jnp.bfloat16, jnp.float32
    square = 2 * frames * width * width
    rows_bytes = 2 * frames * width
    reached, wide = frames + 2 * EDGE, frames + 4 * EDGE

    info = jnp.stack([own, lengths[0], place]).astype(jnp.int32)
    params = jnp.concatenate(
        [conv_kernel, norm_gain[None], conv_bias[None], conv_gain[None]], axis=0
    )

    by_tiles = share % LANES == 0
    packed_rows = [3 * frames + 3 * EDGE * ways * (by in neighbours(ways)) for by in range(ways)]
    packed = call(
        functools.partial(pack_kernel, ways),
        "pack",
        [((rows, share), bf16) for rows in packed_rows],
        scratch=[((3, frames, width), bf16), ((2, 3 * EDGE, width), bf16)],
        semaphores=7,
        far=("in",),
        megabytes=58,
        moved=6 * rows_bytes,
    )(query_rows[0], key_rows[0], value_rows[0], residual_in[0], grad_out[0])
    packed = swap_all(packed, "ctx")

    masked, *masked_halves = call(
        functools.partial(mask_kernel, lower),
        "mask",
        [((frames, width), bf16)] + [((frames, half), bf16)] * 2,
        moved=4 * rows_bytes,
    )(info, grad_out[0])
    masked_halves = swap_all([masked_halves[by % 2] for by in range(4)], "dp", lower)
    grad_own, packed[0] = call(
        grad_act_kernel,
        "grad_act",
        [((frames, width), f32), ((3 * frames, share), bf16)],
        flops=square,
        moved=6 * rows_bytes + 2 * width * width,
    )(info, masked, point_weight, packed[0])

    packed, grad_own = lax.optimization_barrier((packed, grad_own))
    head_scratch = [((every, share), bf16)] * 3 + [((every, LANES), f32)]
    pair_flops = 2 * heads * every * every * HEAD_DIM
    *returned, attended, log_total, before, after = call(
        functools.partial(attend_kernel, ways),
        "attend",
        [((wide, share), bf16)] * ways + [((every, share), bf16), ((heads, every), f32)]
        + [((3 * EDGE, width), bf16)] * 2,
        scratch=head_scratch + [((share, every), f32)],
        flops=8 * pair_flops,
        moved=4 * rows_bytes,
        exps=heads * every * every,
    )(info, *packed)
    returned, masked_halves[1:3] = lax.optimization_barrier((returned, masked_halves[1:3]))
    returned = swap_all(returned, "ctx")
    grad_edges = call(
        functools.partial(mask_edges_kernel, frames),
        "mask_edges",
        [((2 * EDGE, width), f32)],
        flops=square,
        moved=2 * width * width,
    )(info, before, after, point_weight)[0]
    returned, grad_edges, masked_halves = lax.optimization_barrier(
        (returned, grad_edges, masked_halves)
    )
    messages = call(
        functools.partial(gather_kernel, ways),
        "gather",
        [((frames, width - share), bf16)] * ways,
        moved=8 * rows_bytes,
    )(info, *returned)
    arrived = swap_all(messages, "ctx")

    returned, messages = lax.optimization_barrier((returned, messages))
    mixed, conv_in = call(
        functools.partial(project_kernel, ways),
        "project",
        [((wide, width), f32), ((wide, width), bf16)],
        scratch=[((wide, width), bf16)],
        flops=square,
        moved=6 * rows_bytes + 2 * width * width,
    )(info, *returned, residual_in[0], before, after, out_weight, params)
    spread = 8 * stride_of(reached)
    conv_act, grad_conv, conv_sums, *act_halves = call(
        functools.partial(conv_kernel_body, lower),
        "conv",
        [
            ((reached, width), bf16),
            ((tiles, reached, LANES), f32),
            ((2, width), f32),
        ]
        + [((frames, half), bf16)] * 2,
        scratch=[
            ((tiles, spread + 2 * EDGE, LANES), f32),
            ((tiles, spread, LANES), f32),
            ((reached, width), f32),
            ((8, width), f32),
            ((8, width), f32),
        ],
        flops=frames * width * 4000,
        moved=6 * rows_bytes,
        exps=frames * width,
    )(info, conv_in, params, grad_own, grad_edges)
    near, act_halves = lax.optimization_barrier((arrived[:NEAR], act_halves))
    act_halves = swap_all([act_halves[by // 2] for by in range(4)], "dp", lower)
    far, grad_conv = lax.optimization_barrier((arrived[NEAR:], grad_conv))

    spread = 8 * stride_of(frames)
    grad_residual, *grad_messages = call(
        functools.partial(conv_back_kernel, ways, slim),
        "conv_back",
        [((frames, width), bf16)] + [((2 * frames + EXTRA, share), bf16)] * ways,
        scratch=[
            ((tiles, spread + 2 * EDGE, LANES), f32),
            ((tiles, wide, LANES), f32),
            ((tiles, spread, LANES), f32),
            ((8, width), f32),
            ((EXTRA, width), f32),
            ((frames + EXTRA, width), bf16),
            ((ways, frames + EXTRA, share), bf16),
        ],
        flops=frames * width * 8000,
        moved=8 * rows_bytes + 2 * width * width,
    )(
        info,
        grad_conv,
        conv_in,
        params,
        masked,
        mixed,
        out_weight,
        conv_sums,
    )
    act_halves[1], grad_messages[NEAR:] = lax.optimization_barrier(
        (act_halves[1], grad_messages[NEAR:])
    )
    act_halves, conv_act = lax.optimization_barrier((act_halves, conv_act))
    messages = near + far
    grad_messages = swap_all(grad_messages, "ctx")

    block_out = call(
        block_out_kernel,
        "block_out",
        [((frames, width), bf16)],
        flops=square,
        moved=4 * rows_bytes + 2 * width * width,
    )(info, conv_act, mixed, point_weight)[0]

    def halve(kept, received, axis, shift, alternate):
        extent = (kept.shape[0] // 2,) + kept.shape[1:]
        return call(
            functools.partial(halve_kernel, 0 if axis == "ctx" else 2, shift, alternate),
            "halve",
            [(extent, bf16), (extent, f32)],
            moved=16 * extent[0] * extent[1] * extent[2],
        )(info, kept, received)

    grad_messages[1], act_halves = lax.optimization_barrier((grad_messages[1], act_halves))
    bits = list(reversed(range(lower.bit_length() - 1)))
    point_half = (lower * ways // 2, 2 * slim, half)
    point_sent, point_kept = call(
        functools.partial(point_kernel, bits[0]),
        "point_terms",
        [(point_half, bf16), (point_half, f32)],
        scratch=[((half, half), f32)],
        flops=square,
        moved=8 * rows_bytes,
    )(info, *masked_halves, *act_halves)
    grad_messages, point_sent, block_out = lax.optimization_barrier(
        (grad_messages, point_sent, block_out)
    )
    extent = width + LANES
    core_half = (parts // 2, slim, extent)
    sent, kept = call(
        functools.partial(weight_kernel, ways, parts),
        "out_terms",
        [(core_half, bf16), (core_half, f32)],
        scratch=[((share, extent), f32)],
        flops=square,
        moved=10 * rows_bytes,
    )(info, *grad_messages, *messages, attended)
    received = swap(sent, "dp", 1)
    for shift in range(1, parts.bit_length() - 1):
        sent, kept = halve(kept, received, "dp", shift, True)
        received = swap(sent, "dp", 2**shift)

    point_received = swap(point_sent, "dp", 2 ** bits[0])
    for shift in bits[1:]:
        point_sent, point_kept = halve(point_kept, point_received, "dp", shift, False)
        point_received = swap(point_sent, "dp", 2**shift)
    pieces = call(
        spread_kernel,
        "spread",
        [((2 * slim, half), f32)] + [((2 * slim, half), bf16)] * (ways - 1),
        moved=slim * width * 6 * ways,
    )(info, point_kept, point_received)
    pieces = swap_all(pieces, "ctx")
    grad_packed = call(
        functools.partial(attend_back_kernel, ways),
        "attend_back",
        [((3, frames, share), bf16)] * ways,
        scratch=head_scratch + [((every, share), bf16), ((share, every), f32)],
        flops=20 * pair_flops,
        moved=8 * rows_bytes,
        exps=heads * every * every,
    )(info, *packed, *grad_messages, attended, log_total)
    pieces, grad_packed = lax.optimization_barrier((pieces, grad_packed))
    grad_packed = swap_all(grad_packed, "ctx")
    layer_bit = (parts // 2).bit_length() - 1
    point_own, point_other = call(
        functools.partial(point_sum_kernel, layer_bit),
        "point_sum",
        [((slim, half), f32), ((slim, half), bf16)],
        moved=slim * width * (parts + 8),
    )(info, *pieces)
    point_other = swap(point_other, "dp", parts // 2)

    out_total, taps, vectors, point_total = call(
        functools.partial(finish_kernel, ways, layer_bit),
        "finish",
        [((slim, width), f32), ((31, slim), f32), ((3, slim), f32), ((slim, width), f32)],
        moved=slim * extent * (parts + 8),
    )(info, kept, received, point_own, point_other)

    grad_query, grad_key, grad_value = call(
        functools.partial(unpack_kernel if by_tiles else unpack_parts_kernel, ways),
        "unpack",
        [((frames, width), bf16)] * 3,
        semaphores=3 * ways if by_tiles else 0,
        far=("out",) if by_tiles else (),
        moved=6 * rows_bytes,
    )(info, *grad_packed)

    return (
        block_out[None],
        grad_residual[None],
        grad_query[None],
        grad_key[None],
        grad_value[None],
        out_total.T,
        point_total.T,
        taps,
        vectors,
    )


def solution(mesh):
    rows = P("dp", "ctx", None)
    columns = P(None, ("dp", "ctx"))
    in_specs = (rows, rows, rows, rows, P("dp"), P(), P(), P(), P(), P(), P(), rows)
    out_specs = (rows,) * 5 + (columns,) * 4
    return jax.shard_map(local, mesh=mesh, in_specs=in_specs, out_specs=out_specs, check_vma=False)
```

```python
import functools

import jax
import jax.numpy as jnp
from jax import lax
from jax.experimental import pallas as pl
from jax.experimental.pallas import tpu as pltpu
from jax.sharding import PartitionSpec as P

HEADS = 24
HEAD_DIM = 64
SCALE = HEAD_DIM ** (-0.5)

NEG_FILL = -1e30
EPSILON = 1e-05

LANES = 128
EDGE = 16
NEAR = 3
BAND = 16
EXTRA = 48

NN = (((1,), (0,)), ((), ()))
NT = (((1,), (1,)), ((), ()))
TN = (((0,), (0,)), ((), ()))


def dot(left, right, dims=NN):
    return lax.dot_general(left, right, dims, preferred_element_type=jnp.float32)


def call(
    kernel, name, outs, scratch=(), semaphores=0, far=(), megabytes=28, flops=0, moved=0, exps=0
):
    vmem = pl.BlockSpec(memory_space=pltpu.VMEM)
    smem = pl.BlockSpec(memory_space=pltpu.SMEM)
    anywhere = pl.BlockSpec(memory_space=pl.ANY)

    def run(*arrays):
        scratches = [pltpu.VMEM(shape, kind) for shape, kind in scratch]
        if semaphores:
            scratches.append(pltpu.SemaphoreType.DMA((semaphores,)))
        return pl.pallas_call(
            kernel,
            name=name,
            in_specs=[smem if a.ndim == 1 else anywhere if "in" in far else vmem for a in arrays],
            out_specs=[anywhere if "out" in far else vmem] * len(outs),
            out_shape=[jax.ShapeDtypeStruct(shape, kind) for shape, kind in outs],
            scratch_shapes=scratches,
            compiler_params=pltpu.CompilerParams(vmem_limit_bytes=megabytes << 20),
            cost_estimate=pl.CostEstimate(flops=flops, bytes_accessed=moved, transcendentals=exps),
        )(*arrays)

    return run


def valid_of(first, rows, length):
    return first + lax.broadcasted_iota(jnp.int32, (rows, 1), 0) < length


def moments(rows):
    centre = jnp.mean(rows, axis=-1, keepdims=True)
    centred = rows - centre
    inv_scale = lax.rsqrt(jnp.mean(centred * centred, axis=-1, keepdims=True) + EPSILON)
    return centred * inv_scale, inv_scale


def norm_back(grad_normed, normed, inv_scale):
    first_mean = jnp.mean(grad_normed, axis=-1, keepdims=True)
    second_mean = jnp.mean(grad_normed * normed, axis=-1, keepdims=True)
    return inv_scale * (grad_normed - first_mean - normed * second_mean)


def fold(rows):
    total = rows[:8]
    for at in range(8, rows.shape[0], 8):
        total = total + rows[at : at + 8]
    return total


def at_group(info, by, ways, share, visit):
    if share % LANES == 0:
        visit(pl.ds(pl.multiple_of((info[0] ^ by) * share, LANES), share))
        return
    for at in range(ways):

        @pl.when((info[0] ^ by) == at)
        def _():
            visit(slice(at * share, (at + 1) * share))


def neighbours(ways):
    return [by for by in (1, 3, 7, 15) if by < ways]


def edge_rows(frames, at):
    return slice(3 * frames + at * 3 * EDGE, 3 * frames + (at + 1) * 3 * EDGE)


def pack_kernel(ways, query, key, value, residual, grad_out, *refs):
    blocks, whole, ends, arrived = refs[:ways], refs[ways], refs[ways + 1], refs[ways + 2]
    info = [lax.axis_index("ctx")]
    frames, width = query.shape
    share, reach = width // ways, 2 * EDGE
    pairs = [(rows, whole.at[slot]) for slot, rows in enumerate((query, key, value))]
    for side, tail in enumerate((False, True)):
        for rows, start, count in ((residual, 0, reach), (grad_out, reach, EDGE)):
            first = frames - count if tail else 0
            pairs.append((rows.at[pl.ds(first, count)], ends.at[side, pl.ds(start, count)]))
    copies = [
        pltpu.make_async_copy(source, target, arrived.at[at])
        for at, (source, target) in enumerate(pairs)
    ]
    for copy in copies:
        copy.start()
    for slot, copy in enumerate(copies[:3]):
        copy.wait()
        for by in range(ways):

            def visit(lanes):
                blocks[by][slot * frames : (slot + 1) * frames, :] = whole[slot, :, lanes]

            at_group(info, by, ways, share, visit)
    for copy in copies[3:]:
        copy.wait()
    for by in neighbours(ways):
        side = jnp.where((info[0] ^ by) > info[0], 1, 0)
        for at in range(ways):
            blocks[by][edge_rows(frames, at), :] = ends[side, :, at * share : (at + 1) * share]


def unpack_kernel(ways, info, *refs):
    blocks, outs, arrived = refs[:ways], refs[ways:-1], refs[-1]
    share = blocks[0].shape[2]
    copies = []
    for by in range(ways):
        for slot, rows in enumerate(outs):
            lanes = pl.ds(pl.multiple_of((info[0] ^ by) * share, LANES), share)
            copy = pltpu.make_async_copy(
                blocks[by].at[slot], rows.at[:, lanes], arrived.at[len(copies)]
            )
            copy.start()
            copies.append(copy)
    for copy in copies:
        copy.wait()


def unpack_parts_kernel(ways, info, *refs):
    blocks, outs = refs[:ways], refs[ways:]
    share = blocks[0].shape[2]
    for by in range(ways):
        for slot, rows in enumerate(outs):

            def visit(lanes):
                rows[:, lanes] = blocks[by][slot]

            at_group(info, by, ways, share, visit)


def mask_kernel(lower, info, grad_out, masked, *halves):
    frames, width = grad_out.shape
    valid = valid_of(info[0] * frames, frames, info[1])
    masked[...] = jnp.where(valid, grad_out[...].astype(jnp.float32), 0.0).astype(jnp.bfloat16)
    quarter = width // 4
    for by, half in enumerate(halves):
        for at in range(2):
            start = (2 * at + ((info[2] // lower) ^ by) % 2) * quarter
            lanes = pl.ds(pl.multiple_of(start, LANES), quarter)
            half[:, at * quarter : (at + 1) * quarter] = masked[:, lanes]


def grad_act_kernel(info, masked, point_weight, block, grad_act, own_block):
    own_block[...] = block[...]
    width = masked.shape[1]
    step = width // 3
    for at in range(0, width, step):
        grad_act[:, at : at + step] = dot(masked[...], point_weight[at : at + step, :], NT)


def mask_edges_kernel(frames, info, before, after, point_weight, grad_act):
    width = grad_act.shape[1]
    first = info[0] * frames
    sides = []
    for side, start in ((before, first - EDGE), (after, first + frames)):
        valid = valid_of(start, EDGE, info[1])
        rows = side[2 * EDGE :, :].astype(jnp.float32)
        sides.append(jnp.where(valid, rows, 0.0).astype(jnp.bfloat16))
    masked = jnp.concatenate(sides, axis=0)
    step = width // 3
    for at in range(0, width, step):
        grad_act[:, at : at + step] = dot(masked, point_weight[at : at + step, :], NT)


def gather_heads(info, blocks, query, key, value, bias):
    frames = query.shape[0] // len(blocks)
    for by, block in enumerate(blocks):
        rows = slice(by * frames, (by + 1) * frames)
        query[rows] = block[:frames, :] * jnp.bfloat16(SCALE)
        key[rows] = block[frames : 2 * frames, :]
        value[rows] = block[2 * frames : 3 * frames, :]
        valid = valid_of((info[0] ^ by) * frames, frames, info[1])
        bias[rows] = jnp.broadcast_to(jnp.where(valid, 0.0, NEG_FILL), (frames, LANES))


def attend_kernel(ways, info, *refs):
    blocks, outs = refs[:ways], refs[ways : 2 * ways]
    attended, log_total, before, after, query, key, value, bias, turned = refs[2 * ways :]
    gather_heads(info, blocks, query, key, value, bias)
    total_frames, share = query.shape
    frames = total_frames // ways
    for side, other in ((before, info[0] - 1), (after, info[0] + 1)):
        side[...] = jnp.zeros_like(side)
        for by in neighbours(ways):

            @pl.when((info[0] ^ other) == by)
            def _():
                for at in range(ways):
                    lanes = slice(at * share, (at + 1) * share)
                    side[:, lanes] = blocks[by][edge_rows(frames, at), :]

    for head in range(share // HEAD_DIM):
        part = slice(head * HEAD_DIM, (head + 1) * HEAD_DIM)
        spread = jnp.concatenate([bias[...]] * (total_frames // LANES), axis=1)
        scores = dot(key[:, part], query[:, part], NT) + spread
        row_max = jnp.max(scores, axis=0, keepdims=True)
        weights = jnp.exp(scores - row_max)
        total = jnp.sum(weights, axis=0, keepdims=True)
        turned[part, :] = dot(value[:, part], weights.astype(jnp.bfloat16), TN) / total
        log_total[head : head + 1, :] = row_max + jnp.log(total)
    attended[...] = turned[...].T.astype(jnp.bfloat16)
    reach = 2 * EDGE
    for by in range(ways):
        other = info[0] ^ by
        before = (info[0] ^ jnp.maximum(other - 1, 0)) * frames + frames - reach
        after = (info[0] ^ jnp.minimum(other + 1, ways - 1)) * frames
        outs[by][:reach] = attended[pl.ds(pl.multiple_of(before, reach), reach), :]
        outs[by][reach : reach + frames] = attended[by * frames : (by + 1) * frames, :]
        outs[by][reach + frames :] = attended[pl.ds(pl.multiple_of(after, reach), reach), :]


def attend_back_kernel(ways, info, *refs):
    blocks, messages = refs[:ways], refs[ways : 2 * ways]
    attended, log_total = refs[2 * ways : 2 * ways + 2]
    outs = refs[2 * ways + 2 : 3 * ways + 2]
    query, key, value, bias, grad, turned = refs[3 * ways + 2 :]
    gather_heads(info, blocks, query, key, value, bias)
    total_frames, share = query.shape
    frames = total_frames // ways
    for by in range(ways):
        grad[by * frames : (by + 1) * frames] = messages[by][:frames, :]
    turned[...] = (grad[...].astype(jnp.float32) * attended[...].astype(jnp.float32)).T
    for head in range(share // HEAD_DIM):
        part = slice(head * HEAD_DIM, (head + 1) * HEAD_DIM)
        delta = jnp.sum(turned[part, :], axis=0, keepdims=True)
        spread = jnp.concatenate([bias[...]] * (total_frames // LANES), axis=1)
        scores = dot(key[:, part], query[:, part], NT) + spread
        probs = jnp.exp(scores - log_total[head : head + 1, :])
        value_grad = dot(probs.astype(jnp.bfloat16), grad[:, part])
        prob_grad = dot(value[:, part], grad[:, part], NT)
        score_grad = (probs * (prob_grad - delta)).astype(jnp.bfloat16)
        key_grad = dot(score_grad, query[:, part])
        turned[part, :] = dot(key[:, part], score_grad, TN) * SCALE
        for by in range(ways):
            rows = slice(by * frames, (by + 1) * frames)
            outs[by][1, :, part] = key_grad[rows].astype(jnp.bfloat16)
            outs[by][2, :, part] = value_grad[rows].astype(jnp.bfloat16)
    query_grad = turned[...].T.astype(jnp.bfloat16)
    for by in range(ways):
        outs[by][0] = query_grad[by * frames : (by + 1) * frames]


def gather_kernel(ways, info, *refs):
    blocks, messages = refs[:ways], refs[ways:]
    frames, share, reach = messages[0].shape[0], blocks[0].shape[1], 2 * EDGE
    for by, message in enumerate(messages):
        lacking = [slot for slot in range(ways) if slot != by]
        for at, slot in enumerate(lacking):
            message[:, at * share : (at + 1) * share] = blocks[slot][reach : reach + frames, :]


def project_kernel(ways, info, *refs):
    blocks = refs[:ways]
    residual, before, after, out_weight, params = refs[ways : ways + 5]
    mixed, conv_in, attended = refs[ways + 5 :]
    frames, width = residual.shape
    share = width // ways
    reach = 2 * EDGE
    rows = frames + 2 * reach
    for by in range(ways):
        for at in range(ways):

            @pl.when((info[0] ^ by) == at)
            def _():
                attended[:, at * share : (at + 1) * share] = blocks[by][...]

    step = width // 3
    for at in range(0, width, step):
        part = slice(at, at + step)
        mixed[:reach, part] = before[:reach, part].astype(jnp.float32)
        mixed[reach : reach + frames, part] = residual[:, part].astype(jnp.float32)
        mixed[reach + frames :, part] = after[:reach, part].astype(jnp.float32)
        mixed[:, part] += dot(attended[...], out_weight[:, part])

    gain = params[31:32, :]
    first = info[0] * frames - reach

    def band(index, carry):
        at = pl.ds(pl.multiple_of(index * BAND, BAND), BAND)
        normed, _ = moments(mixed[at, :])
        position = first + index * BAND + lax.broadcasted_iota(jnp.int32, (BAND, 1), 0)
        valid = (position >= 0) & (position < info[1])
        conv_in[at, :] = jnp.where(valid, normed * gain, 0.0).astype(jnp.bfloat16)
        return carry

    lax.fori_loop(0, rows // BAND, band, 0, unroll=2)


def stride_of(rows):
    return rows // 8 + 1


def in_columns(ref, rows):
    for at in range(ref.shape[0]):
        ref[at, : rows.shape[0]] = rows[:, at * LANES : (at + 1) * LANES].astype(jnp.float32)


def from_columns(ref, rows):
    return jnp.concatenate([ref[at, rows, :] for at in range(ref.shape[0])], axis=1)


def strided(ref, index, start, stride):
    return ref[index, pl.ds(start, 8, stride=stride), :]


def depthwise(padded, taps, tap_of, out, rows):
    stride = stride_of(rows)

    def column(index, carry):
        part = pl.ds(pl.multiple_of(index * LANES, LANES), LANES)
        cells = [strided(padded, index, at + 1, stride) for at in range(stride + 2 * EDGE - 2)]
        total = [None] * stride
        for offset in range(1, 2 * EDGE):
            tap = tap_of(offset)
            scale = jnp.broadcast_to(taps[tap : tap + 1, part], (8, LANES))
            for at in range(stride):
                term = cells[at + offset - 1] * scale
                total[at] = term if total[at] is None else total[at] + term
        for at in range(stride):
            out[index, pl.ds(at, 8, stride=stride), :] = total[at]
        return carry

    lax.fori_loop(0, out.shape[0], column, 0)


def tap_grads(padded, grad, start, rows, taps):
    stride = rows // 8

    def column(index, carry):
        part = pl.ds(pl.multiple_of(index * LANES, LANES), LANES)
        cells = [
            strided(padded, index, start + at + 1, stride) for at in range(stride + 2 * EDGE - 2)
        ]
        grads = [strided(grad, index, start + at, stride) for at in range(stride)]
        for tap in range(2 * EDGE - 1):
            total = cells[tap] * grads[0]
            for at in range(1, stride):
                total = total + cells[at + tap] * grads[at]
            taps[tap : tap + 1, part] = jnp.sum(total, axis=0, keepdims=True)
        return carry

    lax.fori_loop(0, grad.shape[0], column, 0)


def conv_kernel_body(lower, info, conv_in, params, grad_own, grad_edges, *refs):
    conv_act, grad_conv, sums = refs[:3]
    halves = refs[3:-5]
    padded, conv, grad_act, bias_sum, gain_sum = refs[-5:]
    frames, width = grad_own.shape
    rows, wide = frames + 2 * EDGE, frames + 4 * EDGE
    in_columns(padded, conv_in[...])
    padded[:, wide:, :] = jnp.zeros((width // LANES, padded.shape[1] - wide, LANES), jnp.float32)
    grad_act[:EDGE] = grad_edges[:EDGE]
    grad_act[EDGE : EDGE + frames] = grad_own[...]
    grad_act[EDGE + frames :] = grad_edges[EDGE:]
    depthwise(padded, params, lambda offset: offset - 1, conv, rows)
    bias, gain = params[32:33, :], params[33:34, :]
    bias_sum[...] = jnp.zeros_like(bias_sum)
    gain_sum[...] = jnp.zeros_like(gain_sum)

    def band(index, carry):
        at = pl.ds(pl.multiple_of(index * BAND, BAND), BAND)
        normed, inv_scale = moments(from_columns(conv, at) + bias)
        scaled = normed * gain
        gate = 0.5 + 0.5 * jnp.tanh(0.5 * scaled)
        conv_act[at, :] = (scaled * gate).astype(jnp.bfloat16)
        grad_scaled = grad_act[at, :] * gate * (1.0 + scaled * (1.0 - gate))
        grad_rows = norm_back(grad_scaled * gain, normed, inv_scale)
        for column in range(width // LANES):
            grad_conv[column, at, :] = grad_rows[:, column * LANES : (column + 1) * LANES]

        @pl.when((index >= EDGE // BAND) & (index < (EDGE + frames) // BAND))
        def _():
            bias_sum[...] += fold(grad_rows)
            gain_sum[...] += fold(grad_scaled * normed)

        return carry

    lax.fori_loop(0, rows // BAND, band, 0, unroll=2)
    sums[0:1, :] = jnp.sum(bias_sum[...], axis=0, keepdims=True)
    sums[1:2, :] = jnp.sum(gain_sum[...], axis=0, keepdims=True)
    half = width // 2
    for by, block in enumerate(halves):
        start = ((info[2] // (2 * lower)) ^ by) * half
        block[...] = conv_act[EDGE : EDGE + frames, pl.ds(pl.multiple_of(start, LANES), half)]


def block_out_kernel(info, conv_act, mixed, point_weight, block_out):
    frames, width = block_out.shape
    step = width // 3
    for at in range(0, width, step):
        part = slice(at, at + step)
        block_out[:, part] = (
            mixed[2 * EDGE : 2 * EDGE + frames, part]
            + dot(conv_act[EDGE : EDGE + frames, :], point_weight[:, part])
        ).astype(jnp.bfloat16)


def conv_back_kernel(ways, slim, info, grad_conv, conv_in, params, masked, mixed, out_weight, *refs):
    conv_sums, grad_residual, messages = refs[0], refs[1], refs[2 : 2 + ways]
    padded, padded_in, conv, gain_sum, taps, packed, chosen = refs[2 + ways :]
    frames, width = grad_residual.shape
    share = width // ways
    reached = frames + 2 * EDGE
    padded[:, :reached, :] = grad_conv[...].astype(jnp.bfloat16).astype(jnp.float32)
    padded[:, reached:, :] = jnp.zeros(
        (width // LANES, padded.shape[1] - reached, LANES), jnp.float32
    )
    depthwise(padded, params, lambda offset: 31 - offset, conv, frames)
    gain = params[31:32, :]
    gain_sum[...] = jnp.zeros_like(gain_sum)

    def band(index, carry):
        at = pl.ds(pl.multiple_of(index * BAND, BAND), BAND)
        own_mixed = pl.ds(pl.multiple_of(index * BAND + 2 * EDGE, BAND), BAND)
        valid = valid_of(info[0] * frames + index * BAND, BAND, info[1])
        grad_in = jnp.where(valid, from_columns(conv, at), 0.0)
        normed, inv_scale = moments(mixed[own_mixed, :])
        grad_mixed = norm_back(grad_in * gain, normed, inv_scale)
        gain_sum[...] += fold(grad_in * normed)
        grad_residual[at, :] = (masked[at, :].astype(jnp.float32) + grad_mixed).astype(
            jnp.bfloat16
        )
        return carry

    lax.fori_loop(0, frames // BAND, band, 0, unroll=2)
    for by in range(ways):
        at = pl.ds(pl.multiple_of((info[0] ^ by) * share, share), share)
        messages[by][:frames] = dot(grad_residual[...], out_weight[at, :], NT).astype(jnp.bfloat16)

    in_columns(padded_in, conv_in[...])
    tap_grads(padded_in, grad_conv, EDGE, frames, taps)
    taps[31:32, :] = conv_sums[0:1, :]
    taps[32:33, :] = jnp.sum(gain_sum[...], axis=0, keepdims=True)
    taps[33:34, :] = conv_sums[1:2, :]
    taps[34:, :] = jnp.zeros((EXTRA - 34, width), jnp.float32)
    packed[:frames] = grad_residual[...]
    packed[frames:] = taps[...].astype(jnp.bfloat16)
    for at in range(ways):
        pieces = []
        for start in range(at * slim, width, ways * slim):
            pieces.append(packed[:, start : start + slim])
        chosen[at] = jnp.concatenate(pieces, axis=1)
    for by in range(ways):
        messages[by][frames:] = chosen[info[0] ^ by]


def split_rows(info, parts, terms, sent, kept):
    rows = terms.shape[0] // parts
    for bit in range(2):

        @pl.when(info[2] % 2 == bit)
        def _():
            for at in range(parts // 2):
                own, other = (2 * at + bit) * rows, (2 * at + 1 - bit) * rows
                kept[at] = terms[own : own + rows, :]
                sent[at] = terms[other : other + rows, :].astype(jnp.bfloat16)


def point_kernel(shift, info, *refs):
    grads, acts, (sent, kept, terms) = refs[:4], refs[4:8], refs[8:]
    left = jnp.concatenate([grad[...] for grad in grads], axis=0)
    right = jnp.concatenate([act[...] for act in acts], axis=0)
    step = terms.shape[1] // 2
    for at in range(0, 2 * step, step):
        part = slice(at, at + step)
        terms[:, part] = dot(left, right[:, part], TN)
    pieces, slim = kept.shape[0], kept.shape[1] // 2
    for bit in range(2):

        @pl.when(((info[2] >> shift) & 1) == bit)
        def _():
            for at in range(pieces):
                for side in range(2):
                    base = side * 2 * pieces * slim
                    own = base + (bit * pieces + at) * slim
                    other = base + ((1 - bit) * pieces + at) * slim
                    rows = slice(side * slim, (side + 1) * slim)
                    kept[at, rows, :] = terms[own : own + slim, :]
                    sent[at, rows, :] = terms[other : other + slim, :].astype(jnp.bfloat16)


def spread_kernel(info, kept, received, own, *blocks):
    own[...] = kept[info[0]] + received[info[0]].astype(jnp.float32)
    for by, block in enumerate(blocks, 1):
        at = info[0] ^ by
        block[...] = (kept[at] + received[at].astype(jnp.float32)).astype(jnp.bfloat16)


def point_sum_kernel(shift, info, *refs):
    blocks, (own, other) = refs[:-2], refs[-2:]
    rows = own.shape[0]
    total = blocks[0][...]
    for block in blocks[1:]:
        total = total + block[...].astype(jnp.float32)
    for at in range(2):

        @pl.when(((info[2] >> shift) & 1) == at)
        def _():
            own[...] = total[at * rows : (at + 1) * rows, :]
            other[...] = total[(1 - at) * rows : (2 - at) * rows, :].astype(jnp.bfloat16)


def weight_kernel(ways, parts, info, *refs):
    grads, rows = refs[:ways], refs[ways : 2 * ways]
    attended, sent, kept, terms = refs[2 * ways :]
    total_frames, share = attended.shape
    frames = total_frames // ways
    width = ways * share
    slim = share // parts
    left = jnp.concatenate([grad[frames : 2 * frames, :] for grad in grads], axis=0)
    for slot in range(ways):
        if slot == 0:
            right = attended[...]
        else:
            pieces = []
            for by in range(ways):
                at = (by ^ slot) - (1 if (by ^ slot) > by else 0)
                pieces.append(rows[by][:, at * share : (at + 1) * share])
            right = jnp.concatenate(pieces, axis=0)
        terms[:, slot * share : (slot + 1) * share] = dot(left, right, TN)
    small = jnp.zeros((EXTRA, share), jnp.float32)
    for grad in grads:
        small = small + grad[2 * frames :, :].astype(jnp.float32)
    filler = jnp.zeros((LANES - EXTRA, share), jnp.float32)
    terms[:, width:] = jnp.concatenate([small, filler], axis=0).T
    split_rows(info, parts, terms, sent, kept)


def halve_kernel(axis, shift, alternate, info, kept, received, sent, still_kept):
    bit = (info[axis] >> shift) & 1
    count = sent.shape[0]
    for at in range(count):
        if alternate:
            own, other = 2 * at + bit, 2 * at + 1 - bit
        else:
            own, other = bit * count + at, (1 - bit) * count + at
        still_kept[at] = kept[own] + received[own].astype(jnp.float32)
        sent[at] = (kept[other] + received[other].astype(jnp.float32)).astype(jnp.bfloat16)


def finish_kernel(ways, shift, info, kept, received, own, other, weight, taps, vectors, point):
    width = weight.shape[1]
    share, half = width // ways, width // 2
    for at in range(2):

        @pl.when(((info[2] >> shift) & 1) == at)
        def _():
            point[:, at * half : (at + 1) * half] = own[...]
            point[:, (1 - at) * half : (2 - at) * half] = other[...].astype(jnp.float32)

    total = kept[0] + received[0].astype(jnp.float32)
    for by in range(ways):
        for at in range(ways):

            @pl.when((info[0] ^ by) == at)
            def _():
                weight[:, at * share : (at + 1) * share] = total[:, by * share : (by + 1) * share]

    small = total[:, width:].T
    taps[...] = small[:31]
    vectors[...] = small[31:34]


def swap(block, axis, by):
    return lax.ppermute(block, axis, [(i, i ^ by) for i in range(lax.axis_size(axis))])


def swap_all(blocks, axis, step=1):
    return [blocks[0]] + [swap(block, axis, step * by) for by, block in enumerate(blocks[1:], 1)]


def local(
    residual_in,
    query_rows,
    key_rows,
    value_rows,
    lengths,
    out_weight,
    norm_gain,
    conv_kernel,
    conv_bias,
    conv_gain,
    point_weight,
    grad_out,
):
    ways = lax.axis_size("ctx")
    parts = lax.axis_size("dp")
    own = lax.axis_index("ctx")
    place = lax.axis_index("dp")
    frames, width = residual_in.shape[1:]
    share = width // ways
    slim = share // parts
    heads = HEADS // ways
    every = ways * frames
    lower = parts // 4
    half = width // 2
    tiles = width // LANES
    bf16, f32 = jnp.bfloat16, jnp.float32
    square = 2 * frames * width * width
    rows_bytes = 2 * frames * width
    reached, wide = frames + 2 * EDGE, frames + 4 * EDGE

    info = jnp.stack([own, lengths[0], place]).astype(jnp.int32)
    params = jnp.concatenate(
        [conv_kernel, norm_gain[None], conv_bias[None], conv_gain[None]], axis=0
    )

    by_tiles = share % LANES == 0
    packed_rows = [3 * frames + 3 * EDGE * ways * (by in neighbours(ways)) for by in range(ways)]
    packed = call(
        functools.partial(pack_kernel, ways),
        "pack",
        [((rows, share), bf16) for rows in packed_rows],
        scratch=[((3, frames, width), bf16), ((2, 3 * EDGE, width), bf16)],
        semaphores=7,
        far=("in",),
        megabytes=58,
        moved=6 * rows_bytes,
    )(query_rows[0], key_rows[0], value_rows[0], residual_in[0], grad_out[0])
    packed = swap_all(packed, "ctx")

    masked, *masked_halves = call(
        functools.partial(mask_kernel, lower),
        "mask",
        [((frames, width), bf16)] + [((frames, half), bf16)] * 2,
        moved=4 * rows_bytes,
    )(info, grad_out[0])
    masked_halves = swap_all([masked_halves[by % 2] for by in range(4)], "dp", lower)
    grad_own, packed[0] = call(
        grad_act_kernel,
        "grad_act",
        [((frames, width), f32), ((3 * frames, share), bf16)],
        flops=square,
        moved=6 * rows_bytes + 2 * width * width,
    )(info, masked, point_weight, packed[0])

    packed, grad_own = lax.optimization_barrier((packed, grad_own))
    head_scratch = [((every, share), bf16)] * 3 + [((every, LANES), f32)]
    pair_flops = 2 * heads * every * every * HEAD_DIM
    *returned, attended, log_total, before, after = call(
        functools.partial(attend_kernel, ways),
        "attend",
        [((wide, share), bf16)] * ways + [((every, share), bf16), ((heads, every), f32)]
        + [((3 * EDGE, width), bf16)] * 2,
        scratch=head_scratch + [((share, every), f32)],
        flops=8 * pair_flops,
        moved=4 * rows_bytes,
        exps=heads * every * every,
    )(info, *packed)
    returned, masked_halves[1:3] = lax.optimization_barrier((returned, masked_halves[1:3]))
    returned = swap_all(returned, "ctx")
    grad_edges = call(
        functools.partial(mask_edges_kernel, frames),
        "mask_edges",
        [((2 * EDGE, width), f32)],
        flops=square,
        moved=2 * width * width,
    )(info, before, after, point_weight)[0]
    returned, grad_edges, masked_halves = lax.optimization_barrier(
        (returned, grad_edges, masked_halves)
    )
    messages = call(
        functools.partial(gather_kernel, ways),
        "gather",
        [((frames, width - share), bf16)] * ways,
        moved=8 * rows_bytes,
    )(info, *returned)
    arrived = swap_all(messages, "ctx")

    returned, messages = lax.optimization_barrier((returned, messages))
    mixed, conv_in = call(
        functools.partial(project_kernel, ways),
        "project",
        [((wide, width), f32), ((wide, width), bf16)],
        scratch=[((wide, width), bf16)],
        flops=square,
        moved=6 * rows_bytes + 2 * width * width,
    )(info, *returned, residual_in[0], before, after, out_weight, params)
    spread = 8 * stride_of(reached)
    conv_act, grad_conv, conv_sums, *act_halves = call(
        functools.partial(conv_kernel_body, lower),
        "conv",
        [
            ((reached, width), bf16),
            ((tiles, reached, LANES), f32),
            ((2, width), f32),
        ]
        + [((frames, half), bf16)] * 2,
        scratch=[
            ((tiles, spread + 2 * EDGE, LANES), f32),
            ((tiles, spread, LANES), f32),
            ((reached, width), f32),
            ((8, width), f32),
            ((8, width), f32),
        ],
        flops=frames * width * 4000,
        moved=6 * rows_bytes,
        exps=frames * width,
    )(info, conv_in, params, grad_own, grad_edges)
    near, act_halves = lax.optimization_barrier((arrived[:NEAR], act_halves))
    act_halves = swap_all([act_halves[by // 2] for by in range(4)], "dp", lower)
    far, grad_conv = lax.optimization_barrier((arrived[NEAR:], grad_conv))

    spread = 8 * stride_of(frames)
    grad_residual, *grad_messages = call(
        functools.partial(conv_back_kernel, ways, slim),
        "conv_back",
        [((frames, width), bf16)] + [((2 * frames + EXTRA, share), bf16)] * ways,
        scratch=[
            ((tiles, spread + 2 * EDGE, LANES), f32),
            ((tiles, wide, LANES), f32),
            ((tiles, spread, LANES), f32),
            ((8, width), f32),
            ((EXTRA, width), f32),
            ((frames + EXTRA, width), bf16),
            ((ways, frames + EXTRA, share), bf16),
        ],
        flops=frames * width * 8000,
        moved=8 * rows_bytes + 2 * width * width,
    )(
        info,
        grad_conv,
        conv_in,
        params,
        masked,
        mixed,
        out_weight,
        conv_sums,
    )
    act_halves[1], grad_messages[NEAR:] = lax.optimization_barrier(
        (act_halves[1], grad_messages[NEAR:])
    )
    act_halves, conv_act = lax.optimization_barrier((act_halves, conv_act))
    messages = near + far
    grad_messages = swap_all(grad_messages, "ctx")

    block_out = call(
        block_out_kernel,
        "block_out",
        [((frames, width), bf16)],
        flops=square,
        moved=4 * rows_bytes + 2 * width * width,
    )(info, conv_act, mixed, point_weight)[0]

    def halve(kept, received, axis, shift, alternate):
        extent = (kept.shape[0] // 2,) + kept.shape[1:]
        return call(
            functools.partial(halve_kernel, 0 if axis == "ctx" else 2, shift, alternate),
            "halve",
            [(extent, bf16), (extent, f32)],
            moved=16 * extent[0] * extent[1] * extent[2],
        )(info, kept, received)

    grad_messages[1], act_halves = lax.optimization_barrier((grad_messages[1], act_halves))
    bits = list(reversed(range(lower.bit_length() - 1)))
    point_half = (lower * ways // 2, 2 * slim, half)
    point_sent, point_kept = call(
        functools.partial(point_kernel, bits[0]),
        "point_terms",
        [(point_half, bf16), (point_half, f32)],
        scratch=[((half, half), f32)],
        flops=square,
        moved=8 * rows_bytes,
    )(info, *masked_halves, *act_halves)
    grad_messages, point_sent, block_out = lax.optimization_barrier(
        (grad_messages, point_sent, block_out)
    )
    extent = width + LANES
    core_half = (parts // 2, slim, extent)
    sent, kept = call(
        functools.partial(weight_kernel, ways, parts),
        "out_terms",
        [(core_half, bf16), (core_half, f32)],
        scratch=[((share, extent), f32)],
        flops=square,
        moved=10 * rows_bytes,
    )(info, *grad_messages, *messages, attended)
    received = swap(sent, "dp", 1)
    for shift in range(1, parts.bit_length() - 1):
        sent, kept = halve(kept, received, "dp", shift, True)
        received = swap(sent, "dp", 2**shift)

    point_received = swap(point_sent, "dp", 2 ** bits[0])
    for shift in bits[1:]:
        point_sent, point_kept = halve(point_kept, point_received, "dp", shift, False)
        point_received = swap(point_sent, "dp", 2**shift)
    pieces = call(
        spread_kernel,
        "spread",
        [((2 * slim, half), f32)] + [((2 * slim, half), bf16)] * (ways - 1),
        moved=slim * width * 6 * ways,
    )(info, point_kept, point_received)
    pieces = swap_all(pieces, "ctx")
    grad_packed = call(
        functools.partial(attend_back_kernel, ways),
        "attend_back",
        [((3, frames, share), bf16)] * ways,
        scratch=head_scratch + [((every, share), bf16), ((share, every), f32)],
        flops=20 * pair_flops,
        moved=8 * rows_bytes,
        exps=heads * every * every,
    )(info, *packed, *grad_messages, attended, log_total)
    pieces, grad_packed = lax.optimization_barrier((pieces, grad_packed))
    grad_packed = swap_all(grad_packed, "ctx")
    layer_bit = (parts // 2).bit_length() - 1
    point_own, point_other = call(
        functools.partial(point_sum_kernel, layer_bit),
        "point_sum",
        [((slim, half), f32), ((slim, half), bf16)],
        moved=slim * width * (parts + 8),
    )(info, *pieces)
    point_other = swap(point_other, "dp", parts // 2)

    out_total, taps, vectors, point_total = call(
        functools.partial(finish_kernel, ways, layer_bit),
        "finish",
        [((slim, width), f32), ((31, slim), f32), ((3, slim), f32), ((slim, width), f32)],
        moved=slim * extent * (parts + 8),
    )(info, kept, received, point_own, point_other)

    grad_packed, out_total, point_total = lax.optimization_barrier(
        (grad_packed, out_total, point_total)
    )
    grad_query, grad_key, grad_value = call(
        functools.partial(unpack_kernel if by_tiles else unpack_parts_kernel, ways),
        "unpack",
        [((frames, width), bf16)] * 3,
        semaphores=3 * ways if by_tiles else 0,
        far=("out",) if by_tiles else (),
        moved=6 * rows_bytes,
    )(info, *grad_packed)

    return (
        block_out[None],
        grad_residual[None],
        grad_query[None],
        grad_key[None],
        grad_value[None],
        out_total.T,
        point_total.T,
        taps,
        vectors,
    )


def solution(mesh):
    rows = P("dp", "ctx", None)
    columns = P(None, ("dp", "ctx"))
    in_specs = (rows, rows, rows, rows, P("dp"), P(), P(), P(), P(), P(), P(), rows)
    out_specs = (rows,) * 5 + (columns,) * 4
    return jax.shard_map(local, mesh=mesh, in_specs=in_specs, out_specs=out_specs, check_vma=False)
```

```python
import functools

import jax
import jax.numpy as jnp
from jax import lax
from jax.experimental import pallas as pl
from jax.experimental.pallas import tpu as pltpu
from jax.sharding import PartitionSpec as P

HEADS = 24
HEAD_DIM = 64
SCALE = HEAD_DIM ** (-0.5)

NEG_FILL = -1e30
EPSILON = 1e-05

LANES = 128
EDGE = 16
NEAR = 3
BAND = 16
EXTRA = 48

NN = (((1,), (0,)), ((), ()))
NT = (((1,), (1,)), ((), ()))
TN = (((0,), (0,)), ((), ()))


def dot(left, right, dims=NN):
    return lax.dot_general(left, right, dims, preferred_element_type=jnp.float32)


def call(
    kernel, name, outs, scratch=(), semaphores=0, far=(), megabytes=28, flops=0, moved=0, exps=0
):
    vmem = pl.BlockSpec(memory_space=pltpu.VMEM)
    smem = pl.BlockSpec(memory_space=pltpu.SMEM)
    anywhere = pl.BlockSpec(memory_space=pl.ANY)

    def run(*arrays):
        scratches = [pltpu.VMEM(shape, kind) for shape, kind in scratch]
        if semaphores:
            scratches.append(pltpu.SemaphoreType.DMA((semaphores,)))
        return pl.pallas_call(
            kernel,
            name=name,
            in_specs=[smem if a.ndim == 1 else anywhere if "in" in far else vmem for a in arrays],
            out_specs=[anywhere if "out" in far else vmem] * len(outs),
            out_shape=[jax.ShapeDtypeStruct(shape, kind) for shape, kind in outs],
            scratch_shapes=scratches,
            compiler_params=pltpu.CompilerParams(vmem_limit_bytes=megabytes << 20),
            cost_estimate=pl.CostEstimate(flops=flops, bytes_accessed=moved, transcendentals=exps),
        )(*arrays)

    return run


def valid_of(first, rows, length):
    return first + lax.broadcasted_iota(jnp.int32, (rows, 1), 0) < length


def moments(rows):
    centre = jnp.mean(rows, axis=-1, keepdims=True)
    centred = rows - centre
    inv_scale = lax.rsqrt(jnp.mean(centred * centred, axis=-1, keepdims=True) + EPSILON)
    return centred * inv_scale, inv_scale


def norm_back(grad_normed, normed, inv_scale):
    first_mean = jnp.mean(grad_normed, axis=-1, keepdims=True)
    second_mean = jnp.mean(grad_normed * normed, axis=-1, keepdims=True)
    return inv_scale * (grad_normed - first_mean - normed * second_mean)


def fold(rows):
    total = rows[:8]
    for at in range(8, rows.shape[0], 8):
        total = total + rows[at : at + 8]
    return total


def at_group(info, by, ways, share, visit):
    if share % LANES == 0:
        visit(pl.ds(pl.multiple_of((info[0] ^ by) * share, LANES), share))
        return
    for at in range(ways):

        @pl.when((info[0] ^ by) == at)
        def _():
            visit(slice(at * share, (at + 1) * share))


def neighbours(ways):
    return [by for by in (1, 3, 7, 15) if by < ways]


def edge_rows(frames, at):
    return slice(3 * frames + at * 3 * EDGE, 3 * frames + (at + 1) * 3 * EDGE)


def pack_kernel(ways, query, key, value, residual, grad_out, *refs):
    blocks, whole, ends, arrived = refs[:ways], refs[ways], refs[ways + 1], refs[ways + 2]
    info = [lax.axis_index("ctx")]
    frames, width = query.shape
    share, reach = width // ways, 2 * EDGE
    pairs = [(rows, whole.at[slot]) for slot, rows in enumerate((query, key, value))]
    for side, tail in enumerate((False, True)):
        for rows, start, count in ((residual, 0, reach), (grad_out, reach, EDGE)):
            first = frames - count if tail else 0
            pairs.append((rows.at[pl.ds(first, count)], ends.at[side, pl.ds(start, count)]))
    copies = [
        pltpu.make_async_copy(source, target, arrived.at[at])
        for at, (source, target) in enumerate(pairs)
    ]
    for copy in copies:
        copy.start()
    for slot, copy in enumerate(copies[:3]):
        copy.wait()
        for by in range(ways):

            def visit(lanes):
                blocks[by][slot * frames : (slot + 1) * frames, :] = whole[slot, :, lanes]

            at_group(info, by, ways, share, visit)
    for copy in copies[3:]:
        copy.wait()
    for by in neighbours(ways):
        side = jnp.where((info[0] ^ by) > info[0], 1, 0)
        for at in range(ways):
            blocks[by][edge_rows(frames, at), :] = ends[side, :, at * share : (at + 1) * share]


def unpack_kernel(ways, info, *refs):
    blocks, outs, arrived = refs[:ways], refs[ways:-1], refs[-1]
    share = blocks[0].shape[2]
    copies = []
    for by in range(ways):
        for slot, rows in enumerate(outs):
            lanes = pl.ds(pl.multiple_of((info[0] ^ by) * share, LANES), share)
            copy = pltpu.make_async_copy(
                blocks[by].at[slot], rows.at[:, lanes], arrived.at[len(copies)]
            )
            copy.start()
            copies.append(copy)
    for copy in copies:
        copy.wait()


def unpack_parts_kernel(ways, info, *refs):
    blocks, outs = refs[:ways], refs[ways:]
    share = blocks[0].shape[2]
    for by in range(ways):
        for slot, rows in enumerate(outs):

            def visit(lanes):
                rows[:, lanes] = blocks[by][slot]

            at_group(info, by, ways, share, visit)


def mask_kernel(lower, info, grad_out, masked, *halves):
    frames, width = grad_out.shape
    valid = valid_of(info[0] * frames, frames, info[1])
    masked[...] = jnp.where(valid, grad_out[...].astype(jnp.float32), 0.0).astype(jnp.bfloat16)
    quarter = width // 4
    for by, half in enumerate(halves):
        for at in range(2):
            start = (2 * at + ((info[2] // lower) ^ by) % 2) * quarter
            lanes = pl.ds(pl.multiple_of(start, LANES), quarter)
            half[:, at * quarter : (at + 1) * quarter] = masked[:, lanes]


def grad_act_kernel(info, masked, point_weight, block, grad_act, own_block):
    own_block[...] = block[...]
    width = masked.shape[1]
    step = width // 3
    for at in range(0, width, step):
        grad_act[:, at : at + step] = dot(masked[...], point_weight[at : at + step, :], NT)


def mask_edges_kernel(frames, info, before, after, point_weight, grad_act):
    width = grad_act.shape[1]
    first = info[0] * frames
    sides = []
    for side, start in ((before, first - EDGE), (after, first + frames)):
        valid = valid_of(start, EDGE, info[1])
        rows = side[2 * EDGE :, :].astype(jnp.float32)
        sides.append(jnp.where(valid, rows, 0.0).astype(jnp.bfloat16))
    masked = jnp.concatenate(sides, axis=0)
    step = width // 3
    for at in range(0, width, step):
        grad_act[:, at : at + step] = dot(masked, point_weight[at : at + step, :], NT)


def gather_heads(info, blocks, query, key, value, bias):
    frames = query.shape[0] // len(blocks)
    for by, block in enumerate(blocks):
        rows = slice(by * frames, (by + 1) * frames)
        query[rows] = block[:frames, :] * jnp.bfloat16(SCALE)
        key[rows] = block[frames : 2 * frames, :]
        value[rows] = block[2 * frames : 3 * frames, :]
        valid = valid_of((info[0] ^ by) * frames, frames, info[1])
        bias[rows] = jnp.broadcast_to(jnp.where(valid, 0.0, NEG_FILL), (frames, LANES))


def attend_kernel(ways, info, *refs):
    blocks, outs = refs[:ways], refs[ways : 2 * ways]
    attended, log_total, before, after, query, key, value, bias, turned = refs[2 * ways :]
    gather_heads(info, blocks, query, key, value, bias)
    total_frames, share = query.shape
    frames = total_frames // ways
    for side, other in ((before, info[0] - 1), (after, info[0] + 1)):
        side[...] = jnp.zeros_like(side)
        for by in neighbours(ways):

            @pl.when((info[0] ^ other) == by)
            def _():
                for at in range(ways):
                    lanes = slice(at * share, (at + 1) * share)
                    side[:, lanes] = blocks[by][edge_rows(frames, at), :]

    for head in range(share // HEAD_DIM):
        part = slice(head * HEAD_DIM, (head + 1) * HEAD_DIM)
        spread = jnp.concatenate([bias[...]] * (total_frames // LANES), axis=1)
        scores = dot(key[:, part], query[:, part], NT) + spread
        row_max = jnp.max(scores, axis=0, keepdims=True)
        weights = jnp.exp(scores - row_max)
        total = jnp.sum(weights, axis=0, keepdims=True)
        turned[part, :] = dot(value[:, part], weights.astype(jnp.bfloat16), TN) / total
        log_total[head : head + 1, :] = row_max + jnp.log(total)
    attended[...] = turned[...].T.astype(jnp.bfloat16)
    reach = 2 * EDGE
    for by in range(ways):
        other = info[0] ^ by
        before = (info[0] ^ jnp.maximum(other - 1, 0)) * frames + frames - reach
        after = (info[0] ^ jnp.minimum(other + 1, ways - 1)) * frames
        outs[by][:reach] = attended[pl.ds(pl.multiple_of(before, reach), reach), :]
        outs[by][reach : reach + frames] = attended[by * frames : (by + 1) * frames, :]
        outs[by][reach + frames :] = attended[pl.ds(pl.multiple_of(after, reach), reach), :]


def attend_back_kernel(ways, info, *refs):
    blocks, messages = refs[:ways], refs[ways : 2 * ways]
    attended, log_total = refs[2 * ways : 2 * ways + 2]
    outs = refs[2 * ways + 2 : 3 * ways + 2]
    query, key, value, bias, grad, turned = refs[3 * ways + 2 :]
    gather_heads(info, blocks, query, key, value, bias)
    total_frames, share = query.shape
    frames = total_frames // ways
    for by in range(ways):
        grad[by * frames : (by + 1) * frames] = messages[by][:frames, :]
    turned[...] = (grad[...].astype(jnp.float32) * attended[...].astype(jnp.float32)).T
    for head in range(share // HEAD_DIM):
        part = slice(head * HEAD_DIM, (head + 1) * HEAD_DIM)
        delta = jnp.sum(turned[part, :], axis=0, keepdims=True)
        spread = jnp.concatenate([bias[...]] * (total_frames // LANES), axis=1)
        scores = dot(key[:, part], query[:, part], NT) + spread
        probs = jnp.exp(scores - log_total[head : head + 1, :])
        value_grad = dot(probs.astype(jnp.bfloat16), grad[:, part])
        prob_grad = dot(value[:, part], grad[:, part], NT)
        score_grad = (probs * (prob_grad - delta)).astype(jnp.bfloat16)
        key_grad = dot(score_grad, query[:, part])
        turned[part, :] = dot(key[:, part], score_grad, TN) * SCALE
        for by in range(ways):
            rows = slice(by * frames, (by + 1) * frames)
            outs[by][1, :, part] = key_grad[rows].astype(jnp.bfloat16)
            outs[by][2, :, part] = value_grad[rows].astype(jnp.bfloat16)
    query_grad = turned[...].T.astype(jnp.bfloat16)
    for by in range(ways):
        outs[by][0] = query_grad[by * frames : (by + 1) * frames]


def gather_kernel(ways, info, *refs):
    blocks, messages = refs[:ways], refs[ways:]
    frames, share, reach = messages[0].shape[0], blocks[0].shape[1], 2 * EDGE
    for by, message in enumerate(messages):
        lacking = [slot for slot in range(ways) if slot != by]
        for at, slot in enumerate(lacking):
            message[:, at * share : (at + 1) * share] = blocks[slot][reach : reach + frames, :]


def project_kernel(ways, info, *refs):
    blocks = refs[:ways]
    residual, before, after, out_weight, params = refs[ways : ways + 5]
    mixed, conv_in, attended = refs[ways + 5 :]
    frames, width = residual.shape
    share = width // ways
    reach = 2 * EDGE
    rows = frames + 2 * reach
    for by in range(ways):
        for at in range(ways):

            @pl.when((info[0] ^ by) == at)
            def _():
                attended[:, at * share : (at + 1) * share] = blocks[by][...]

    step = width // 3
    for at in range(0, width, step):
        part = slice(at, at + step)
        mixed[:reach, part] = before[:reach, part].astype(jnp.float32)
        mixed[reach : reach + frames, part] = residual[:, part].astype(jnp.float32)
        mixed[reach + frames :, part] = after[:reach, part].astype(jnp.float32)
        mixed[:, part] += dot(attended[...], out_weight[:, part])

    gain = params[31:32, :]
    first = info[0] * frames - reach

    def band(index, carry):
        at = pl.ds(pl.multiple_of(index * BAND, BAND), BAND)
        normed, _ = moments(mixed[at, :])
        position = first + index * BAND + lax.broadcasted_iota(jnp.int32, (BAND, 1), 0)
        valid = (position >= 0) & (position < info[1])
        conv_in[at, :] = jnp.where(valid, normed * gain, 0.0).astype(jnp.bfloat16)
        return carry

    lax.fori_loop(0, rows // BAND, band, 0, unroll=4)


def stride_of(rows):
    return rows // 8 + 1


def in_columns(ref, rows):
    for at in range(ref.shape[0]):
        ref[at, : rows.shape[0]] = rows[:, at * LANES : (at + 1) * LANES].astype(jnp.float32)


def from_columns(ref, rows):
    return jnp.concatenate([ref[at, rows, :] for at in range(ref.shape[0])], axis=1)


def strided(ref, index, start, stride):
    return ref[index, pl.ds(start, 8, stride=stride), :]


def depthwise(padded, taps, tap_of, out, rows):
    stride = stride_of(rows)

    def column(index, carry):
        part = pl.ds(pl.multiple_of(index * LANES, LANES), LANES)
        cells = [strided(padded, index, at + 1, stride) for at in range(stride + 2 * EDGE - 2)]
        total = [None] * stride
        for offset in range(1, 2 * EDGE):
            tap = tap_of(offset)
            scale = jnp.broadcast_to(taps[tap : tap + 1, part], (8, LANES))
            for at in range(stride):
                term = cells[at + offset - 1] * scale
                total[at] = term if total[at] is None else total[at] + term
        for at in range(stride):
            out[index, pl.ds(at, 8, stride=stride), :] = total[at]
        return carry

    lax.fori_loop(0, out.shape[0], column, 0)


def tap_grads(padded, grad, start, rows, taps):
    stride = rows // 8

    def column(index, carry):
        part = pl.ds(pl.multiple_of(index * LANES, LANES), LANES)
        cells = [
            strided(padded, index, start + at + 1, stride) for at in range(stride + 2 * EDGE - 2)
        ]
        grads = [strided(grad, index, start + at, stride) for at in range(stride)]
        for tap in range(2 * EDGE - 1):
            total = cells[tap] * grads[0]
            for at in range(1, stride):
                total = total + cells[at + tap] * grads[at]
            taps[tap : tap + 1, part] = jnp.sum(total, axis=0, keepdims=True)
        return carry

    lax.fori_loop(0, grad.shape[0], column, 0)


def conv_kernel_body(lower, info, conv_in, params, grad_own, grad_edges, *refs):
    conv_act, grad_conv, sums = refs[:3]
    halves = refs[3:-5]
    padded, conv, grad_act, bias_sum, gain_sum = refs[-5:]
    frames, width = grad_own.shape
    rows, wide = frames + 2 * EDGE, frames + 4 * EDGE
    in_columns(padded, conv_in[...])
    padded[:, wide:, :] = jnp.zeros((width // LANES, padded.shape[1] - wide, LANES), jnp.float32)
    grad_act[:EDGE] = grad_edges[:EDGE]
    grad_act[EDGE : EDGE + frames] = grad_own[...]
    grad_act[EDGE + frames :] = grad_edges[EDGE:]
    depthwise(padded, params, lambda offset: offset - 1, conv, rows)
    bias, gain = params[32:33, :], params[33:34, :]
    bias_sum[...] = jnp.zeros_like(bias_sum)
    gain_sum[...] = jnp.zeros_like(gain_sum)

    def band(index, inner):
        at = pl.ds(pl.multiple_of(index * BAND, BAND), BAND)
        normed, inv_scale = moments(from_columns(conv, at) + bias)
        scaled = normed * gain
        gate = 0.5 + 0.5 * jnp.tanh(0.5 * scaled)
        conv_act[at, :] = (scaled * gate).astype(jnp.bfloat16)
        grad_scaled = grad_act[at, :] * gate * (1.0 + scaled * (1.0 - gate))
        grad_rows = norm_back(grad_scaled * gain, normed, inv_scale)
        for column in range(width // LANES):
            grad_conv[column, at, :] = grad_rows[:, column * LANES : (column + 1) * LANES]

        if inner:
            bias_sum[...] += fold(grad_rows)
            gain_sum[...] += fold(grad_scaled * normed)

    def inner_band(index, carry):
        band(index, True)
        return carry

    for index in range(EDGE // BAND):
        band(index, False)
        band((EDGE + frames) // BAND + index, False)
    lax.fori_loop(EDGE // BAND, (EDGE + frames) // BAND, inner_band, 0, unroll=2)
    sums[0:1, :] = jnp.sum(bias_sum[...], axis=0, keepdims=True)
    sums[1:2, :] = jnp.sum(gain_sum[...], axis=0, keepdims=True)
    half = width // 2
    for by, block in enumerate(halves):
        start = ((info[2] // (2 * lower)) ^ by) * half
        block[...] = conv_act[EDGE : EDGE + frames, pl.ds(pl.multiple_of(start, LANES), half)]


def block_out_kernel(info, conv_act, mixed, point_weight, block_out):
    frames, width = block_out.shape
    step = width // 3
    for at in range(0, width, step):
        part = slice(at, at + step)
        block_out[:, part] = (
            mixed[2 * EDGE : 2 * EDGE + frames, part]
            + dot(conv_act[EDGE : EDGE + frames, :], point_weight[:, part])
        ).astype(jnp.bfloat16)


def conv_back_kernel(ways, slim, info, grad_conv, conv_in, params, masked, mixed, out_weight, *refs):
    conv_sums, grad_residual, messages = refs[0], refs[1], refs[2 : 2 + ways]
    padded, padded_in, conv, gain_sum, taps, packed, chosen = refs[2 + ways :]
    frames, width = grad_residual.shape
    share = width // ways
    reached = frames + 2 * EDGE
    padded[:, :reached, :] = grad_conv[...].astype(jnp.bfloat16).astype(jnp.float32)
    padded[:, reached:, :] = jnp.zeros(
        (width // LANES, padded.shape[1] - reached, LANES), jnp.float32
    )
    depthwise(padded, params, lambda offset: 31 - offset, conv, frames)
    gain = params[31:32, :]
    gain_sum[...] = jnp.zeros_like(gain_sum)

    def band(index, carry):
        at = pl.ds(pl.multiple_of(index * BAND, BAND), BAND)
        own_mixed = pl.ds(pl.multiple_of(index * BAND + 2 * EDGE, BAND), BAND)
        valid = valid_of(info[0] * frames + index * BAND, BAND, info[1])
        grad_in = jnp.where(valid, from_columns(conv, at), 0.0)
        normed, inv_scale = moments(mixed[own_mixed, :])
        grad_mixed = norm_back(grad_in * gain, normed, inv_scale)
        gain_sum[...] += fold(grad_in * normed)
        grad_residual[at, :] = (masked[at, :].astype(jnp.float32) + grad_mixed).astype(
            jnp.bfloat16
        )
        return carry

    lax.fori_loop(0, frames // BAND, band, 0, unroll=4)
    for by in range(ways):
        at = pl.ds(pl.multiple_of((info[0] ^ by) * share, share), share)
        messages[by][:frames] = dot(grad_residual[...], out_weight[at, :], NT).astype(jnp.bfloat16)

    in_columns(padded_in, conv_in[...])
    tap_grads(padded_in, grad_conv, EDGE, frames, taps)
    taps[31:32, :] = conv_sums[0:1, :]
    taps[32:33, :] = jnp.sum(gain_sum[...], axis=0, keepdims=True)
    taps[33:34, :] = conv_sums[1:2, :]
    taps[34:, :] = jnp.zeros((EXTRA - 34, width), jnp.float32)
    packed[:frames] = grad_residual[...]
    packed[frames:] = taps[...].astype(jnp.bfloat16)
    for at in range(ways):
        pieces = []
        for start in range(at * slim, width, ways * slim):
            pieces.append(packed[:, start : start + slim])
        chosen[at] = jnp.concatenate(pieces, axis=1)
    for by in range(ways):
        messages[by][frames:] = chosen[info[0] ^ by]


def split_rows(info, parts, terms, sent, kept):
    rows = terms.shape[0] // parts
    for bit in range(2):

        @pl.when(info[2] % 2 == bit)
        def _():
            for at in range(parts // 2):
                own, other = (2 * at + bit) * rows, (2 * at + 1 - bit) * rows
                kept[at] = terms[own : own + rows, :]
                sent[at] = terms[other : other + rows, :].astype(jnp.bfloat16)


def point_kernel(shift, info, *refs):
    grads, acts, (sent, kept, terms) = refs[:4], refs[4:8], refs[8:]
    left = jnp.concatenate([grad[...] for grad in grads], axis=0)
    right = jnp.concatenate([act[...] for act in acts], axis=0)
    step = terms.shape[1] // 2
    for at in range(0, 2 * step, step):
        part = slice(at, at + step)
        terms[:, part] = dot(left, right[:, part], TN)
    pieces, slim = kept.shape[0], kept.shape[1] // 2
    for bit in range(2):

        @pl.when(((info[2] >> shift) & 1) == bit)
        def _():
            for at in range(pieces):
                for side in range(2):
                    base = side * 2 * pieces * slim
                    own = base + (bit * pieces + at) * slim
                    other = base + ((1 - bit) * pieces + at) * slim
                    rows = slice(side * slim, (side + 1) * slim)
                    kept[at, rows, :] = terms[own : own + slim, :]
                    sent[at, rows, :] = terms[other : other + slim, :].astype(jnp.bfloat16)


def spread_kernel(info, kept, received, own, *blocks):
    own[...] = kept[info[0]] + received[info[0]].astype(jnp.float32)
    for by, block in enumerate(blocks, 1):
        at = info[0] ^ by
        block[...] = (kept[at] + received[at].astype(jnp.float32)).astype(jnp.bfloat16)


def point_sum_kernel(shift, info, *refs):
    blocks, (own, other) = refs[:-2], refs[-2:]
    rows = own.shape[0]
    total = blocks[0][...]
    for block in blocks[1:]:
        total = total + block[...].astype(jnp.float32)
    for at in range(2):

        @pl.when(((info[2] >> shift) & 1) == at)
        def _():
            own[...] = total[at * rows : (at + 1) * rows, :]
            other[...] = total[(1 - at) * rows : (2 - at) * rows, :].astype(jnp.bfloat16)


def weight_kernel(ways, parts, info, *refs):
    grads, rows = refs[:ways], refs[ways : 2 * ways]
    attended, sent, kept, terms = refs[2 * ways :]
    total_frames, share = attended.shape
    frames = total_frames // ways
    width = ways * share
    slim = share // parts
    left = jnp.concatenate([grad[frames : 2 * frames, :] for grad in grads], axis=0)
    for slot in range(ways):
        if slot == 0:
            right = attended[...]
        else:
            pieces = []
            for by in range(ways):
                at = (by ^ slot) - (1 if (by ^ slot) > by else 0)
                pieces.append(rows[by][:, at * share : (at + 1) * share])
            right = jnp.concatenate(pieces, axis=0)
        terms[:, slot * share : (slot + 1) * share] = dot(left, right, TN)
    small = jnp.zeros((EXTRA, share), jnp.float32)
    for grad in grads:
        small = small + grad[2 * frames :, :].astype(jnp.float32)
    filler = jnp.zeros((LANES - EXTRA, share), jnp.float32)
    terms[:, width:] = jnp.concatenate([small, filler], axis=0).T
    split_rows(info, parts, terms, sent, kept)


def halve_kernel(axis, shift, alternate, info, kept, received, sent, still_kept):
    bit = (info[axis] >> shift) & 1
    count = sent.shape[0]
    for at in range(count):
        if alternate:
            own, other = 2 * at + bit, 2 * at + 1 - bit
        else:
            own, other = bit * count + at, (1 - bit) * count + at
        still_kept[at] = kept[own] + received[own].astype(jnp.float32)
        sent[at] = (kept[other] + received[other].astype(jnp.float32)).astype(jnp.bfloat16)


def finish_kernel(ways, shift, info, kept, received, own, other, weight, taps, vectors, point):
    width = weight.shape[1]
    share, half = width // ways, width // 2
    for at in range(2):

        @pl.when(((info[2] >> shift) & 1) == at)
        def _():
            point[:, at * half : (at + 1) * half] = own[...]
            point[:, (1 - at) * half : (2 - at) * half] = other[...].astype(jnp.float32)

    total = kept[0] + received[0].astype(jnp.float32)
    for by in range(ways):
        for at in range(ways):

            @pl.when((info[0] ^ by) == at)
            def _():
                weight[:, at * share : (at + 1) * share] = total[:, by * share : (by + 1) * share]

    small = total[:, width:].T
    taps[...] = small[:31]
    vectors[...] = small[31:34]


def swap(block, axis, by):
    return lax.ppermute(block, axis, [(i, i ^ by) for i in range(lax.axis_size(axis))])


def swap_all(blocks, axis, step=1):
    return [blocks[0]] + [swap(block, axis, step * by) for by, block in enumerate(blocks[1:], 1)]


def local(
    residual_in,
    query_rows,
    key_rows,
    value_rows,
    lengths,
    out_weight,
    norm_gain,
    conv_kernel,
    conv_bias,
    conv_gain,
    point_weight,
    grad_out,
):
    ways = lax.axis_size("ctx")
    parts = lax.axis_size("dp")
    own = lax.axis_index("ctx")
    place = lax.axis_index("dp")
    frames, width = residual_in.shape[1:]
    share = width // ways
    slim = share // parts
    heads = HEADS // ways
    every = ways * frames
    lower = parts // 4
    half = width // 2
    tiles = width // LANES
    bf16, f32 = jnp.bfloat16, jnp.float32
    square = 2 * frames * width * width
    rows_bytes = 2 * frames * width
    reached, wide = frames + 2 * EDGE, frames + 4 * EDGE

    info = jnp.stack([own, lengths[0], place]).astype(jnp.int32)
    params = jnp.concatenate(
        [conv_kernel, norm_gain[None], conv_bias[None], conv_gain[None]], axis=0
    )

    by_tiles = share % LANES == 0
    packed_rows = [3 * frames + 3 * EDGE * ways * (by in neighbours(ways)) for by in range(ways)]
    packed = call(
        functools.partial(pack_kernel, ways),
        "pack",
        [((rows, share), bf16) for rows in packed_rows],
        scratch=[((3, frames, width), bf16), ((2, 3 * EDGE, width), bf16)],
        semaphores=7,
        far=("in",),
        megabytes=58,
        moved=6 * rows_bytes,
    )(query_rows[0], key_rows[0], value_rows[0], residual_in[0], grad_out[0])
    packed = swap_all(packed, "ctx")

    masked, *masked_halves = call(
        functools.partial(mask_kernel, lower),
        "mask",
        [((frames, width), bf16)] + [((frames, half), bf16)] * 2,
        moved=4 * rows_bytes,
    )(info, grad_out[0])
    masked_halves = swap_all([masked_halves[by % 2] for by in range(4)], "dp", lower)
    grad_own, packed[0] = call(
        grad_act_kernel,
        "grad_act",
        [((frames, width), f32), ((3 * frames, share), bf16)],
        flops=square,
        moved=6 * rows_bytes + 2 * width * width,
    )(info, masked, point_weight, packed[0])

    packed, grad_own = lax.optimization_barrier((packed, grad_own))
    head_scratch = [((every, share), bf16)] * 3 + [((every, LANES), f32)]
    pair_flops = 2 * heads * every * every * HEAD_DIM
    *returned, attended, log_total, before, after = call(
        functools.partial(attend_kernel, ways),
        "attend",
        [((wide, share), bf16)] * ways + [((every, share), bf16), ((heads, every), f32)]
        + [((3 * EDGE, width), bf16)] * 2,
        scratch=head_scratch + [((share, every), f32)],
        flops=8 * pair_flops,
        moved=4 * rows_bytes,
        exps=heads * every * every,
    )(info, *packed)
    returned, masked_halves[1:3] = lax.optimization_barrier((returned, masked_halves[1:3]))
    returned = swap_all(returned, "ctx")
    grad_edges = call(
        functools.partial(mask_edges_kernel, frames),
        "mask_edges",
        [((2 * EDGE, width), f32)],
        flops=square,
        moved=2 * width * width,
    )(info, before, after, point_weight)[0]
    returned, grad_edges, masked_halves = lax.optimization_barrier(
        (returned, grad_edges, masked_halves)
    )
    messages = call(
        functools.partial(gather_kernel, ways),
        "gather",
        [((frames, width - share), bf16)] * ways,
        moved=8 * rows_bytes,
    )(info, *returned)
    arrived = swap_all(messages, "ctx")

    returned, messages = lax.optimization_barrier((returned, messages))
    mixed, conv_in = call(
        functools.partial(project_kernel, ways),
        "project",
        [((wide, width), f32), ((wide, width), bf16)],
        scratch=[((wide, width), bf16)],
        flops=square,
        moved=6 * rows_bytes + 2 * width * width,
    )(info, *returned, residual_in[0], before, after, out_weight, params)
    spread = 8 * stride_of(reached)
    conv_act, grad_conv, conv_sums, *act_halves = call(
        functools.partial(conv_kernel_body, lower),
        "conv",
        [
            ((reached, width), bf16),
            ((tiles, reached, LANES), f32),
            ((2, width), f32),
        ]
        + [((frames, half), bf16)] * 2,
        scratch=[
            ((tiles, spread + 2 * EDGE, LANES), f32),
            ((tiles, spread, LANES), f32),
            ((reached, width), f32),
            ((8, width), f32),
            ((8, width), f32),
        ],
        flops=frames * width * 4000,
        moved=6 * rows_bytes,
        exps=frames * width,
    )(info, conv_in, params, grad_own, grad_edges)
    near, act_halves = lax.optimization_barrier((arrived[:NEAR], act_halves))
    act_halves = swap_all([act_halves[by // 2] for by in range(4)], "dp", lower)
    far, grad_conv = lax.optimization_barrier((arrived[NEAR:], grad_conv))

    spread = 8 * stride_of(frames)
    grad_residual, *grad_messages = call(
        functools.partial(conv_back_kernel, ways, slim),
        "conv_back",
        [((frames, width), bf16)] + [((2 * frames + EXTRA, share), bf16)] * ways,
        scratch=[
            ((tiles, spread + 2 * EDGE, LANES), f32),
            ((tiles, wide, LANES), f32),
            ((tiles, spread, LANES), f32),
            ((8, width), f32),
            ((EXTRA, width), f32),
            ((frames + EXTRA, width), bf16),
            ((ways, frames + EXTRA, share), bf16),
        ],
        flops=frames * width * 8000,
        moved=8 * rows_bytes + 2 * width * width,
    )(
        info,
        grad_conv,
        conv_in,
        params,
        masked,
        mixed,
        out_weight,
        conv_sums,
    )
    act_halves[1], grad_messages[NEAR:] = lax.optimization_barrier(
        (act_halves[1], grad_messages[NEAR:])
    )
    act_halves, conv_act = lax.optimization_barrier((act_halves, conv_act))
    messages = near + far
    grad_messages = swap_all(grad_messages, "ctx")

    block_out = call(
        block_out_kernel,
        "block_out",
        [((frames, width), bf16)],
        flops=square,
        moved=4 * rows_bytes + 2 * width * width,
    )(info, conv_act, mixed, point_weight)[0]

    def halve(kept, received, axis, shift, alternate):
        extent = (kept.shape[0] // 2,) + kept.shape[1:]
        return call(
            functools.partial(halve_kernel, 0 if axis == "ctx" else 2, shift, alternate),
            "halve",
            [(extent, bf16), (extent, f32)],
            moved=16 * extent[0] * extent[1] * extent[2],
        )(info, kept, received)

    grad_messages[1], act_halves = lax.optimization_barrier((grad_messages[1], act_halves))
    bits = list(reversed(range(lower.bit_length() - 1)))
    point_half = (lower * ways // 2, 2 * slim, half)
    point_sent, point_kept = call(
        functools.partial(point_kernel, bits[0]),
        "point_terms",
        [(point_half, bf16), (point_half, f32)],
        scratch=[((half, half), f32)],
        flops=square,
        moved=8 * rows_bytes,
    )(info, *masked_halves, *act_halves)
    grad_messages, point_sent, block_out = lax.optimization_barrier(
        (grad_messages, point_sent, block_out)
    )
    extent = width + LANES
    core_half = (parts // 2, slim, extent)
    sent, kept = call(
        functools.partial(weight_kernel, ways, parts),
        "out_terms",
        [(core_half, bf16), (core_half, f32)],
        scratch=[((share, extent), f32)],
        flops=square,
        moved=10 * rows_bytes,
    )(info, *grad_messages, *messages, attended)
    received = swap(sent, "dp", 1)
    for shift in range(1, parts.bit_length() - 1):
        sent, kept = halve(kept, received, "dp", shift, True)
        received = swap(sent, "dp", 2**shift)

    point_received = swap(point_sent, "dp", 2 ** bits[0])
    for shift in bits[1:]:
        point_sent, point_kept = halve(point_kept, point_received, "dp", shift, False)
        point_received = swap(point_sent, "dp", 2**shift)
    pieces = call(
        spread_kernel,
        "spread",
        [((2 * slim, half), f32)] + [((2 * slim, half), bf16)] * (ways - 1),
        moved=slim * width * 6 * ways,
    )(info, point_kept, point_received)
    pieces = swap_all(pieces, "ctx")
    grad_packed = call(
        functools.partial(attend_back_kernel, ways),
        "attend_back",
        [((3, frames, share), bf16)] * ways,
        scratch=head_scratch + [((every, share), bf16), ((share, every), f32)],
        flops=20 * pair_flops,
        moved=8 * rows_bytes,
        exps=heads * every * every,
    )(info, *packed, *grad_messages, attended, log_total)
    pieces, grad_packed = lax.optimization_barrier((pieces, grad_packed))
    grad_packed = swap_all(grad_packed, "ctx")
    layer_bit = (parts // 2).bit_length() - 1
    point_own, point_other = call(
        functools.partial(point_sum_kernel, layer_bit),
        "point_sum",
        [((slim, half), f32), ((slim, half), bf16)],
        moved=slim * width * (parts + 8),
    )(info, *pieces)
    point_other = swap(point_other, "dp", parts // 2)

    out_total, taps, vectors, point_total = call(
        functools.partial(finish_kernel, ways, layer_bit),
        "finish",
        [((slim, width), f32), ((31, slim), f32), ((3, slim), f32), ((slim, width), f32)],
        moved=slim * extent * (parts + 8),
    )(info, kept, received, point_own, point_other)

    grad_query, grad_key, grad_value = call(
        functools.partial(unpack_kernel if by_tiles else unpack_parts_kernel, ways),
        "unpack",
        [((frames, width), bf16)] * 3,
        semaphores=3 * ways if by_tiles else 0,
        far=("out",) if by_tiles else (),
        moved=6 * rows_bytes,
    )(info, *grad_packed)

    return (
        block_out[None],
        grad_residual[None],
        grad_query[None],
        grad_key[None],
        grad_value[None],
        out_total.T,
        point_total.T,
        taps,
        vectors,
    )


def solution(mesh):
    rows = P("dp", "ctx", None)
    columns = P(None, ("dp", "ctx"))
    in_specs = (rows, rows, rows, rows, P("dp"), P(), P(), P(), P(), P(), P(), rows)
    out_specs = (rows,) * 5 + (columns,) * 4
    return jax.shard_map(local, mesh=mesh, in_specs=in_specs, out_specs=out_specs, check_vma=False)
```

```python
import functools

import jax
import jax.numpy as jnp
from jax import lax
from jax.experimental import pallas as pl
from jax.experimental.pallas import tpu as pltpu
from jax.sharding import PartitionSpec as P

HEADS = 24
HEAD_DIM = 64
SCALE = HEAD_DIM ** (-0.5)

NEG_FILL = -1e30
EPSILON = 1e-05

LANES = 128
EDGE = 16
NEAR = 3
BAND = 16
EXTRA = 48

NN = (((1,), (0,)), ((), ()))
NT = (((1,), (1,)), ((), ()))
TN = (((0,), (0,)), ((), ()))


def dot(left, right, dims=NN):
    return lax.dot_general(left, right, dims, preferred_element_type=jnp.float32)


def call(
    kernel, name, outs, scratch=(), semaphores=0, far=(), megabytes=28, flops=0, moved=0, exps=0
):
    vmem = pl.BlockSpec(memory_space=pltpu.VMEM)
    smem = pl.BlockSpec(memory_space=pltpu.SMEM)
    anywhere = pl.BlockSpec(memory_space=pl.ANY)

    def run(*arrays):
        scratches = [pltpu.VMEM(shape, kind) for shape, kind in scratch]
        if semaphores:
            scratches.append(pltpu.SemaphoreType.DMA((semaphores,)))
        return pl.pallas_call(
            kernel,
            name=name,
            in_specs=[smem if a.ndim == 1 else anywhere if "in" in far else vmem for a in arrays],
            out_specs=[anywhere if "out" in far else vmem] * len(outs),
            out_shape=[jax.ShapeDtypeStruct(shape, kind) for shape, kind in outs],
            scratch_shapes=scratches,
            compiler_params=pltpu.CompilerParams(vmem_limit_bytes=megabytes << 20),
            cost_estimate=pl.CostEstimate(flops=flops, bytes_accessed=moved, transcendentals=exps),
        )(*arrays)

    return run


def valid_of(first, rows, length):
    return first + lax.broadcasted_iota(jnp.int32, (rows, 1), 0) < length


def moments(rows):
    centre = jnp.mean(rows, axis=-1, keepdims=True)
    centred = rows - centre
    inv_scale = lax.rsqrt(jnp.mean(centred * centred, axis=-1, keepdims=True) + EPSILON)
    return centred * inv_scale, inv_scale


def norm_back(grad_normed, normed, inv_scale):
    first_mean = jnp.mean(grad_normed, axis=-1, keepdims=True)
    second_mean = jnp.mean(grad_normed * normed, axis=-1, keepdims=True)
    return inv_scale * (grad_normed - first_mean - normed * second_mean)


def fold(rows):
    total = rows[:8]
    for at in range(8, rows.shape[0], 8):
        total = total + rows[at : at + 8]
    return total


def at_group(info, by, ways, share, visit):
    if share % LANES == 0:
        visit(pl.ds(pl.multiple_of((info[0] ^ by) * share, LANES), share))
        return
    for at in range(ways):

        @pl.when((info[0] ^ by) == at)
        def _():
            visit(slice(at * share, (at + 1) * share))


def neighbours(ways):
    return [by for by in (1, 3, 7, 15) if by < ways]


def edge_rows(frames, at):
    return slice(3 * frames + at * 3 * EDGE, 3 * frames + (at + 1) * 3 * EDGE)


def pack_kernel(ways, query, key, value, residual, grad_out, *refs):
    blocks, whole, ends, arrived = refs[:ways], refs[ways], refs[ways + 1], refs[ways + 2]
    info = [lax.axis_index("ctx")]
    frames, width = query.shape
    share, reach = width // ways, 2 * EDGE
    pairs = [(rows, whole.at[slot]) for slot, rows in enumerate((query, key, value))]
    for side, tail in enumerate((False, True)):
        for rows, start, count in ((residual, 0, reach), (grad_out, reach, EDGE)):
            first = frames - count if tail else 0
            pairs.append((rows.at[pl.ds(first, count)], ends.at[side, pl.ds(start, count)]))
    copies = [
        pltpu.make_async_copy(source, target, arrived.at[at])
        for at, (source, target) in enumerate(pairs)
    ]
    for copy in copies:
        copy.start()
    for slot, copy in enumerate(copies[:3]):
        copy.wait()
        for by in range(ways):

            def visit(lanes):
                blocks[by][slot * frames : (slot + 1) * frames, :] = whole[slot, :, lanes]

            at_group(info, by, ways, share, visit)
    for copy in copies[3:]:
        copy.wait()
    for by in neighbours(ways):
        side = jnp.where((info[0] ^ by) > info[0], 1, 0)
        for at in range(ways):
            blocks[by][edge_rows(frames, at), :] = ends[side, :, at * share : (at + 1) * share]


def unpack_kernel(ways, info, *refs):
    blocks, outs, arrived = refs[:ways], refs[ways:-1], refs[-1]
    share = blocks[0].shape[2]
    copies = []
    for by in range(ways):
        for slot, rows in enumerate(outs):
            lanes = pl.ds(pl.multiple_of((info[0] ^ by) * share, LANES), share)
            copy = pltpu.make_async_copy(
                blocks[by].at[slot], rows.at[:, lanes], arrived.at[len(copies)]
            )
            copy.start()
            copies.append(copy)
    for copy in copies:
        copy.wait()


def unpack_parts_kernel(ways, info, *refs):
    blocks, outs = refs[:ways], refs[ways:]
    share = blocks[0].shape[2]
    for by in range(ways):
        for slot, rows in enumerate(outs):

            def visit(lanes):
                rows[:, lanes] = blocks[by][slot]

            at_group(info, by, ways, share, visit)


def mask_kernel(lower, info, grad_out, masked, *halves):
    frames, width = grad_out.shape
    valid = valid_of(info[0] * frames, frames, info[1])
    masked[...] = jnp.where(valid, grad_out[...].astype(jnp.float32), 0.0).astype(jnp.bfloat16)
    quarter = width // 4
    for by, half in enumerate(halves):
        for at in range(2):
            start = (2 * at + ((info[2] // lower) ^ by) % 2) * quarter
            lanes = pl.ds(pl.multiple_of(start, LANES), quarter)
            half[:, at * quarter : (at + 1) * quarter] = masked[:, lanes]


def grad_act_kernel(info, masked, point_weight, block, grad_act, own_block):
    own_block[...] = block[...]
    width = masked.shape[1]
    step = width // 3
    for at in range(0, width, step):
        grad_act[:, at : at + step] = dot(masked[...], point_weight[at : at + step, :], NT)


def mask_edges_kernel(frames, info, before, after, point_weight, grad_act):
    width = grad_act.shape[1]
    first = info[0] * frames
    sides = []
    for side, start in ((before, first - EDGE), (after, first + frames)):
        valid = valid_of(start, EDGE, info[1])
        rows = side[2 * EDGE :, :].astype(jnp.float32)
        sides.append(jnp.where(valid, rows, 0.0).astype(jnp.bfloat16))
    masked = jnp.concatenate(sides, axis=0)
    step = width // 3
    for at in range(0, width, step):
        grad_act[:, at : at + step] = dot(masked, point_weight[at : at + step, :], NT)


def gather_heads(info, blocks, query, key, value, bias):
    frames = query.shape[0] // len(blocks)
    for by, block in enumerate(blocks):
        rows = slice(by * frames, (by + 1) * frames)
        query[rows] = block[:frames, :] * jnp.bfloat16(SCALE)
        key[rows] = block[frames : 2 * frames, :]
        value[rows] = block[2 * frames : 3 * frames, :]
        valid = valid_of((info[0] ^ by) * frames, frames, info[1])
        bias[rows] = jnp.broadcast_to(jnp.where(valid, 0.0, NEG_FILL), (frames, LANES))


def attend_kernel(ways, info, *refs):
    blocks, outs = refs[:ways], refs[ways : 2 * ways]
    attended, log_total, before, after, query, key, value, bias, turned = refs[2 * ways :]
    gather_heads(info, blocks, query, key, value, bias)
    total_frames, share = query.shape
    frames = total_frames // ways
    for side, other in ((before, info[0] - 1), (after, info[0] + 1)):
        side[...] = jnp.zeros_like(side)
        for by in neighbours(ways):

            @pl.when((info[0] ^ other) == by)
            def _():
                for at in range(ways):
                    lanes = slice(at * share, (at + 1) * share)
                    side[:, lanes] = blocks[by][edge_rows(frames, at), :]

    for head in range(share // HEAD_DIM):
        part = slice(head * HEAD_DIM, (head + 1) * HEAD_DIM)
        spread = jnp.concatenate([bias[...]] * (total_frames // LANES), axis=1)
        scores = dot(key[:, part], query[:, part], NT) + spread
        row_max = jnp.max(scores, axis=0, keepdims=True)
        weights = jnp.exp(scores - row_max)
        total = jnp.sum(weights, axis=0, keepdims=True)
        turned[part, :] = dot(value[:, part], weights.astype(jnp.bfloat16), TN) / total
        log_total[head : head + 1, :] = row_max + jnp.log(total)
    attended[...] = turned[...].T.astype(jnp.bfloat16)
    reach = 2 * EDGE
    for by in range(ways):
        other = info[0] ^ by
        before = (info[0] ^ jnp.maximum(other - 1, 0)) * frames + frames - reach
        after = (info[0] ^ jnp.minimum(other + 1, ways - 1)) * frames
        outs[by][:reach] = attended[pl.ds(pl.multiple_of(before, reach), reach), :]
        outs[by][reach : reach + frames] = attended[by * frames : (by + 1) * frames, :]
        outs[by][reach + frames :] = attended[pl.ds(pl.multiple_of(after, reach), reach), :]


def attend_back_kernel(ways, info, *refs):
    blocks, messages = refs[:ways], refs[ways : 2 * ways]
    attended, log_total = refs[2 * ways : 2 * ways + 2]
    outs = refs[2 * ways + 2 : 3 * ways + 2]
    query, key, value, bias, grad, turned = refs[3 * ways + 2 :]
    gather_heads(info, blocks, query, key, value, bias)
    total_frames, share = query.shape
    frames = total_frames // ways
    for by in range(ways):
        grad[by * frames : (by + 1) * frames] = messages[by][:frames, :]
    turned[...] = (grad[...].astype(jnp.float32) * attended[...].astype(jnp.float32)).T
    for head in range(share // HEAD_DIM):
        part = slice(head * HEAD_DIM, (head + 1) * HEAD_DIM)
        delta = jnp.sum(turned[part, :], axis=0, keepdims=True)
        spread = jnp.concatenate([bias[...]] * (total_frames // LANES), axis=1)
        scores = dot(key[:, part], query[:, part], NT) + spread
        probs = jnp.exp(scores - log_total[head : head + 1, :])
        value_grad = dot(probs.astype(jnp.bfloat16), grad[:, part])
        prob_grad = dot(value[:, part], grad[:, part], NT)
        score_grad = (probs * (prob_grad - delta)).astype(jnp.bfloat16)
        key_grad = dot(score_grad, query[:, part])
        turned[part, :] = dot(key[:, part], score_grad, TN) * SCALE
        for by in range(ways):
            rows = slice(by * frames, (by + 1) * frames)
            outs[by][1, :, part] = key_grad[rows].astype(jnp.bfloat16)
            outs[by][2, :, part] = value_grad[rows].astype(jnp.bfloat16)
    query_grad = turned[...].T.astype(jnp.bfloat16)
    for by in range(ways):
        outs[by][0] = query_grad[by * frames : (by + 1) * frames]


def gather_kernel(ways, info, *refs):
    blocks, messages = refs[:ways], refs[ways:]
    frames, share, reach = messages[0].shape[0], blocks[0].shape[1], 2 * EDGE
    for by, message in enumerate(messages):
        lacking = [slot for slot in range(ways) if slot != by]
        for at, slot in enumerate(lacking):
            message[:, at * share : (at + 1) * share] = blocks[slot][reach : reach + frames, :]


def project_kernel(ways, info, *refs):
    blocks = refs[:ways]
    residual, before, after, out_weight, params = refs[ways : ways + 5]
    mixed, conv_in, attended = refs[ways + 5 :]
    frames, width = residual.shape
    share = width // ways
    reach = 2 * EDGE
    rows = frames + 2 * reach
    for by in range(ways):
        for at in range(ways):

            @pl.when((info[0] ^ by) == at)
            def _():
                attended[:, at * share : (at + 1) * share] = blocks[by][...]

    step = width // 3
    for at in range(0, width, step):
        part = slice(at, at + step)
        mixed[:reach, part] = before[:reach, part].astype(jnp.float32)
        mixed[reach : reach + frames, part] = residual[:, part].astype(jnp.float32)
        mixed[reach + frames :, part] = after[:reach, part].astype(jnp.float32)
        mixed[:, part] += dot(attended[...], out_weight[:, part])

    gain = params[31:32, :]
    first = info[0] * frames - reach

    def band(index, carry):
        at = pl.ds(pl.multiple_of(index * BAND, BAND), BAND)
        normed, _ = moments(mixed[at, :])
        position = first + index * BAND + lax.broadcasted_iota(jnp.int32, (BAND, 1), 0)
        valid = (position >= 0) & (position < info[1])
        conv_in[at, :] = jnp.where(valid, normed * gain, 0.0).astype(jnp.bfloat16)
        return carry

    lax.fori_loop(0, rows // BAND, band, 0, unroll=4)


def stride_of(rows):
    return rows // 8 + 1


def in_columns(ref, rows):
    for at in range(ref.shape[0]):
        ref[at, : rows.shape[0]] = rows[:, at * LANES : (at + 1) * LANES].astype(jnp.float32)


def from_columns(ref, rows):
    return jnp.concatenate([ref[at, rows, :] for at in range(ref.shape[0])], axis=1)


def strided(ref, index, start, stride):
    return ref[index, pl.ds(start, 8, stride=stride), :]


def depthwise(padded, taps, tap_of, out, rows):
    stride = stride_of(rows)

    def column(index, carry):
        part = pl.ds(pl.multiple_of(index * LANES, LANES), LANES)
        cells = [strided(padded, index, at + 1, stride) for at in range(stride + 2 * EDGE - 2)]
        total = [None] * stride
        for offset in range(1, 2 * EDGE):
            tap = tap_of(offset)
            scale = jnp.broadcast_to(taps[tap : tap + 1, part], (8, LANES))
            for at in range(stride):
                term = cells[at + offset - 1] * scale
                total[at] = term if total[at] is None else total[at] + term
        for at in range(stride):
            out[index, pl.ds(at, 8, stride=stride), :] = total[at]
        return carry

    lax.fori_loop(0, out.shape[0], column, 0)


def tap_grads(padded, grad, start, rows, taps):
    stride = rows // 8

    def column(index, carry):
        part = pl.ds(pl.multiple_of(index * LANES, LANES), LANES)
        cells = [
            strided(padded, index, start + at + 1, stride) for at in range(stride + 2 * EDGE - 2)
        ]
        grads = [strided(grad, index, start + at, stride) for at in range(stride)]
        for tap in range(2 * EDGE - 1):
            total = cells[tap] * grads[0]
            for at in range(1, stride):
                total = total + cells[at + tap] * grads[at]
            taps[tap : tap + 1, part] = jnp.sum(total, axis=0, keepdims=True)
        return carry

    lax.fori_loop(0, grad.shape[0], column, 0)


def conv_kernel_body(lower, info, conv_in, params, grad_own, grad_edges, *refs):
    conv_act, grad_conv, sums = refs[:3]
    halves = refs[3:-5]
    padded, conv, grad_act, bias_sum, gain_sum = refs[-5:]
    frames, width = grad_own.shape
    rows, wide = frames + 2 * EDGE, frames + 4 * EDGE
    in_columns(padded, conv_in[...])
    padded[:, wide:, :] = jnp.zeros((width // LANES, padded.shape[1] - wide, LANES), jnp.float32)
    grad_act[:EDGE] = grad_edges[:EDGE]
    grad_act[EDGE : EDGE + frames] = grad_own[...]
    grad_act[EDGE + frames :] = grad_edges[EDGE:]
    depthwise(padded, params, lambda offset: offset - 1, conv, rows)
    bias, gain = params[32:33, :], params[33:34, :]
    bias_sum[...] = jnp.zeros_like(bias_sum)
    gain_sum[...] = jnp.zeros_like(gain_sum)

    def band(index, inner):
        at = pl.ds(pl.multiple_of(index * BAND, BAND), BAND)
        normed, inv_scale = moments(from_columns(conv, at) + bias)
        scaled = normed * gain
        gate = 0.5 + 0.5 * jnp.tanh(0.5 * scaled)
        conv_act[at, :] = (scaled * gate).astype(jnp.bfloat16)
        grad_scaled = grad_act[at, :] * gate * (1.0 + scaled * (1.0 - gate))
        grad_rows = norm_back(grad_scaled * gain, normed, inv_scale)
        for column in range(width // LANES):
            grad_conv[column, at, :] = grad_rows[:, column * LANES : (column + 1) * LANES]

        if inner:
            bias_sum[...] += fold(grad_rows)
            gain_sum[...] += fold(grad_scaled * normed)

    def inner_band(index, carry):
        band(index, True)
        return carry

    for index in range(EDGE // BAND):
        band(index, False)
        band((EDGE + frames) // BAND + index, False)
    lax.fori_loop(EDGE // BAND, (EDGE + frames) // BAND, inner_band, 0, unroll=2)
    sums[0:1, :] = jnp.sum(bias_sum[...], axis=0, keepdims=True)
    sums[1:2, :] = jnp.sum(gain_sum[...], axis=0, keepdims=True)
    half = width // 2
    for by, block in enumerate(halves):
        start = ((info[2] // (2 * lower)) ^ by) * half
        block[...] = conv_act[EDGE : EDGE + frames, pl.ds(pl.multiple_of(start, LANES), half)]


def block_out_kernel(info, conv_act, mixed, point_weight, block_out):
    frames, width = block_out.shape
    step = width // 3
    for at in range(0, width, step):
        part = slice(at, at + step)
        block_out[:, part] = (
            mixed[2 * EDGE : 2 * EDGE + frames, part]
            + dot(conv_act[EDGE : EDGE + frames, :], point_weight[:, part])
        ).astype(jnp.bfloat16)


def conv_back_kernel(ways, slim, info, grad_conv, conv_in, params, masked, mixed, out_weight, *refs):
    conv_sums, grad_residual, messages = refs[0], refs[1], refs[2 : 2 + ways]
    padded, padded_in, conv, gain_sum, taps, packed, chosen = refs[2 + ways :]
    frames, width = grad_residual.shape
    share = width // ways
    reached = frames + 2 * EDGE
    padded[:, :reached, :] = grad_conv[...].astype(jnp.bfloat16).astype(jnp.float32)
    padded[:, reached:, :] = jnp.zeros(
        (width // LANES, padded.shape[1] - reached, LANES), jnp.float32
    )
    depthwise(padded, params, lambda offset: 31 - offset, conv, frames)
    gain = params[31:32, :]
    gain_sum[...] = jnp.zeros_like(gain_sum)

    def band(index, carry):
        at = pl.ds(pl.multiple_of(index * BAND, BAND), BAND)
        own_mixed = pl.ds(pl.multiple_of(index * BAND + 2 * EDGE, BAND), BAND)
        valid = valid_of(info[0] * frames + index * BAND, BAND, info[1])
        grad_in = jnp.where(valid, from_columns(conv, at), 0.0)
        normed, inv_scale = moments(mixed[own_mixed, :])
        grad_mixed = norm_back(grad_in * gain, normed, inv_scale)
        gain_sum[...] += fold(grad_in * normed)
        grad_residual[at, :] = (masked[at, :].astype(jnp.float32) + grad_mixed).astype(
            jnp.bfloat16
        )
        return carry

    lax.fori_loop(0, frames // BAND, band, 0, unroll=4)
    for by in range(ways):
        at = pl.ds(pl.multiple_of((info[0] ^ by) * share, share), share)
        messages[by][:frames] = dot(grad_residual[...], out_weight[at, :], NT).astype(jnp.bfloat16)

    in_columns(padded_in, conv_in[...])
    tap_grads(padded_in, grad_conv, EDGE, frames, taps)
    taps[31:32, :] = conv_sums[0:1, :]
    taps[32:33, :] = jnp.sum(gain_sum[...], axis=0, keepdims=True)
    taps[33:34, :] = conv_sums[1:2, :]
    taps[34:, :] = jnp.zeros((EXTRA - 34, width), jnp.float32)
    packed[:frames] = grad_residual[...]
    packed[frames:] = taps[...].astype(jnp.bfloat16)
    for at in range(ways):
        pieces = []
        for start in range(at * slim, width, ways * slim):
            pieces.append(packed[:, start : start + slim])
        chosen[at] = jnp.concatenate(pieces, axis=1)
    for by in range(ways):
        messages[by][frames:] = chosen[info[0] ^ by]


def split_rows(info, parts, terms, sent, kept):
    rows = terms.shape[0] // parts
    for bit in range(2):

        @pl.when(info[2] % 2 == bit)
        def _():
            for at in range(parts // 2):
                own, other = (2 * at + bit) * rows, (2 * at + 1 - bit) * rows
                kept[at] = terms[own : own + rows, :]
                sent[at] = terms[other : other + rows, :].astype(jnp.bfloat16)


def point_kernel(shift, info, *refs):
    grads, acts, (sent, kept, terms) = refs[:4], refs[4:8], refs[8:]
    left = jnp.concatenate([grad[...] for grad in grads], axis=0)
    right = jnp.concatenate([act[...] for act in acts], axis=0)
    step = terms.shape[1] // 2
    for at in range(0, 2 * step, step):
        part = slice(at, at + step)
        terms[:, part] = dot(left, right[:, part], TN)
    pieces, slim = kept.shape[0], kept.shape[1] // 2
    for bit in range(2):

        @pl.when(((info[2] >> shift) & 1) == bit)
        def _():
            for at in range(pieces):
                for side in range(2):
                    base = side * 2 * pieces * slim
                    own = base + (bit * pieces + at) * slim
                    other = base + ((1 - bit) * pieces + at) * slim
                    rows = slice(side * slim, (side + 1) * slim)
                    kept[at, rows, :] = terms[own : own + slim, :]
                    sent[at, rows, :] = terms[other : other + slim, :].astype(jnp.bfloat16)


def spread_kernel(info, kept, received, own, *blocks):
    own[...] = kept[info[0]] + received[info[0]].astype(jnp.float32)
    for by, block in enumerate(blocks, 1):
        at = info[0] ^ by
        block[...] = (kept[at] + received[at].astype(jnp.float32)).astype(jnp.bfloat16)


def point_sum_kernel(shift, info, *refs):
    blocks, (own, other) = refs[:-2], refs[-2:]
    rows = own.shape[0]
    total = blocks[0][...]
    for block in blocks[1:]:
        total = total + block[...].astype(jnp.float32)
    for at in range(2):

        @pl.when(((info[2] >> shift) & 1) == at)
        def _():
            own[...] = total[at * rows : (at + 1) * rows, :]
            other[...] = total[(1 - at) * rows : (2 - at) * rows, :].astype(jnp.bfloat16)


def weight_kernel(ways, parts, info, *refs):
    grads, rows = refs[:ways], refs[ways : 2 * ways]
    attended, sent, kept, terms = refs[2 * ways :]
    total_frames, share = attended.shape
    frames = total_frames // ways
    width = ways * share
    slim = share // parts
    left = jnp.concatenate([grad[frames : 2 * frames, :] for grad in grads], axis=0)
    for slot in range(ways):
        if slot == 0:
            right = attended[...]
        else:
            pieces = []
            for by in range(ways):
                at = (by ^ slot) - (1 if (by ^ slot) > by else 0)
                pieces.append(rows[by][:, at * share : (at + 1) * share])
            right = jnp.concatenate(pieces, axis=0)
        terms[:, slot * share : (slot + 1) * share] = dot(left, right, TN)
    small = jnp.zeros((EXTRA, share), jnp.float32)
    for grad in grads:
        small = small + grad[2 * frames :, :].astype(jnp.float32)
    filler = jnp.zeros((LANES - EXTRA, share), jnp.float32)
    terms[:, width:] = jnp.concatenate([small, filler], axis=0).T
    split_rows(info, parts, terms, sent, kept)


def halve_kernel(axis, shift, alternate, info, kept, received, sent, still_kept):
    bit = (info[axis] >> shift) & 1
    count = sent.shape[0]
    for at in range(count):
        if alternate:
            own, other = 2 * at + bit, 2 * at + 1 - bit
        else:
            own, other = bit * count + at, (1 - bit) * count + at
        still_kept[at] = kept[own] + received[own].astype(jnp.float32)
        sent[at] = (kept[other] + received[other].astype(jnp.float32)).astype(jnp.bfloat16)


def finish_kernel(ways, shift, info, kept, received, own, other, weight, taps, vectors, point):
    width = weight.shape[1]
    share, half = width // ways, width // 2
    for at in range(2):

        @pl.when(((info[2] >> shift) & 1) == at)
        def _():
            point[:, at * half : (at + 1) * half] = own[...]
            point[:, (1 - at) * half : (2 - at) * half] = other[...].astype(jnp.float32)

    total = kept[0] + received[0].astype(jnp.float32)
    for by in range(ways):
        for at in range(ways):

            @pl.when((info[0] ^ by) == at)
            def _():
                weight[:, at * share : (at + 1) * share] = total[:, by * share : (by + 1) * share]

    small = total[:, width:].T
    taps[...] = small[:31]
    vectors[...] = small[31:34]


def swap(block, axis, by):
    return lax.ppermute(block, axis, [(i, i ^ by) for i in range(lax.axis_size(axis))])


def swap_all(blocks, axis, step=1):
    return [blocks[0]] + [swap(block, axis, step * by) for by, block in enumerate(blocks[1:], 1)]


def local(
    residual_in,
    query_rows,
    key_rows,
    value_rows,
    lengths,
    out_weight,
    norm_gain,
    conv_kernel,
    conv_bias,
    conv_gain,
    point_weight,
    grad_out,
):
    ways = lax.axis_size("ctx")
    parts = lax.axis_size("dp")
    own = lax.axis_index("ctx")
    place = lax.axis_index("dp")
    frames, width = residual_in.shape[1:]
    share = width // ways
    slim = share // parts
    heads = HEADS // ways
    every = ways * frames
    lower = parts // 4
    half = width // 2
    tiles = width // LANES
    bf16, f32 = jnp.bfloat16, jnp.float32
    square = 2 * frames * width * width
    rows_bytes = 2 * frames * width
    reached, wide = frames + 2 * EDGE, frames + 4 * EDGE

    info = jnp.stack([own, lengths[0], place]).astype(jnp.int32)
    params = jnp.concatenate(
        [conv_kernel, norm_gain[None], conv_bias[None], conv_gain[None]], axis=0
    )

    by_tiles = share % LANES == 0
    packed_rows = [3 * frames + 3 * EDGE * ways * (by in neighbours(ways)) for by in range(ways)]
    packed = call(
        functools.partial(pack_kernel, ways),
        "pack",
        [((rows, share), bf16) for rows in packed_rows],
        scratch=[((3, frames, width), bf16), ((2, 3 * EDGE, width), bf16)],
        semaphores=7,
        far=("in",),
        megabytes=58,
        moved=6 * rows_bytes,
    )(query_rows[0], key_rows[0], value_rows[0], residual_in[0], grad_out[0])
    packed = swap_all(packed, "ctx")

    masked, *masked_halves = call(
        functools.partial(mask_kernel, lower),
        "mask",
        [((frames, width), bf16)] + [((frames, half), bf16)] * 2,
        moved=4 * rows_bytes,
    )(info, grad_out[0])
    masked_halves = swap_all([masked_halves[by % 2] for by in range(4)], "dp", lower)
    grad_own, packed[0] = call(
        grad_act_kernel,
        "grad_act",
        [((frames, width), f32), ((3 * frames, share), bf16)],
        flops=square,
        moved=6 * rows_bytes + 2 * width * width,
    )(info, masked, point_weight, packed[0])

    packed, grad_own = lax.optimization_barrier((packed, grad_own))
    head_scratch = [((every, share), bf16)] * 3 + [((every, LANES), f32)]
    pair_flops = 2 * heads * every * every * HEAD_DIM
    *returned, attended, log_total, before, after = call(
        functools.partial(attend_kernel, ways),
        "attend",
        [((wide, share), bf16)] * ways + [((every, share), bf16), ((heads, every), f32)]
        + [((3 * EDGE, width), bf16)] * 2,
        scratch=head_scratch + [((share, every), f32)],
        flops=8 * pair_flops,
        moved=4 * rows_bytes,
        exps=heads * every * every,
    )(info, *packed)
    returned, masked_halves[1:3] = lax.optimization_barrier((returned, masked_halves[1:3]))
    returned = swap_all(returned, "ctx")
    grad_edges = call(
        functools.partial(mask_edges_kernel, frames),
        "mask_edges",
        [((2 * EDGE, width), f32)],
        flops=square,
        moved=2 * width * width,
    )(info, before, after, point_weight)[0]
    returned, grad_edges, masked_halves = lax.optimization_barrier(
        (returned, grad_edges, masked_halves)
    )
    messages = call(
        functools.partial(gather_kernel, ways),
        "gather",
        [((frames, width - share), bf16)] * ways,
        moved=8 * rows_bytes,
    )(info, *returned)
    arrived = swap_all(messages, "ctx")

    returned, messages = lax.optimization_barrier((returned, messages))
    mixed, conv_in = call(
        functools.partial(project_kernel, ways),
        "project",
        [((wide, width), f32), ((wide, width), bf16)],
        scratch=[((wide, width), bf16)],
        flops=square,
        moved=6 * rows_bytes + 2 * width * width,
    )(info, *returned, residual_in[0], before, after, out_weight, params)
    spread = 8 * stride_of(reached)
    conv_act, grad_conv, conv_sums, *act_halves = call(
        functools.partial(conv_kernel_body, lower),
        "conv",
        [
            ((reached, width), bf16),
            ((tiles, reached, LANES), f32),
            ((2, width), f32),
        ]
        + [((frames, half), bf16)] * 2,
        scratch=[
            ((tiles, spread + 2 * EDGE, LANES), f32),
            ((tiles, spread, LANES), f32),
            ((reached, width), f32),
            ((8, width), f32),
            ((8, width), f32),
        ],
        flops=frames * width * 4000,
        moved=6 * rows_bytes,
        exps=frames * width,
    )(info, conv_in, params, grad_own, grad_edges)
    near, act_last = lax.optimization_barrier((arrived[:NEAR], act_halves[1]))
    act_halves = swap_all([act_halves[0], act_halves[0], act_halves[1], act_last], "dp", lower)
    far, grad_conv = lax.optimization_barrier((arrived[NEAR:], grad_conv))

    spread = 8 * stride_of(frames)
    grad_residual, *grad_messages = call(
        functools.partial(conv_back_kernel, ways, slim),
        "conv_back",
        [((frames, width), bf16)] + [((2 * frames + EXTRA, share), bf16)] * ways,
        scratch=[
            ((tiles, spread + 2 * EDGE, LANES), f32),
            ((tiles, wide, LANES), f32),
            ((tiles, spread, LANES), f32),
            ((8, width), f32),
            ((EXTRA, width), f32),
            ((frames + EXTRA, width), bf16),
            ((ways, frames + EXTRA, share), bf16),
        ],
        flops=frames * width * 8000,
        moved=8 * rows_bytes + 2 * width * width,
    )(
        info,
        grad_conv,
        conv_in,
        params,
        masked,
        mixed,
        out_weight,
        conv_sums,
    )
    act_halves[1], grad_messages[NEAR:] = lax.optimization_barrier(
        (act_halves[1], grad_messages[NEAR:])
    )
    act_halves, conv_act = lax.optimization_barrier((act_halves, conv_act))
    messages = near + far
    grad_messages = swap_all(grad_messages, "ctx")

    block_out = call(
        block_out_kernel,
        "block_out",
        [((frames, width), bf16)],
        flops=square,
        moved=4 * rows_bytes + 2 * width * width,
    )(info, conv_act, mixed, point_weight)[0]

    def halve(kept, received, axis, shift, alternate):
        extent = (kept.shape[0] // 2,) + kept.shape[1:]
        return call(
            functools.partial(halve_kernel, 0 if axis == "ctx" else 2, shift, alternate),
            "halve",
            [(extent, bf16), (extent, f32)],
            moved=16 * extent[0] * extent[1] * extent[2],
        )(info, kept, received)

    grad_messages[1], act_halves = lax.optimization_barrier((grad_messages[1], act_halves))
    bits = list(reversed(range(lower.bit_length() - 1)))
    point_half = (lower * ways // 2, 2 * slim, half)
    point_sent, point_kept = call(
        functools.partial(point_kernel, bits[0]),
        "point_terms",
        [(point_half, bf16), (point_half, f32)],
        scratch=[((half, half), f32)],
        flops=square,
        moved=8 * rows_bytes,
    )(info, *masked_halves, *act_halves)
    grad_messages, point_sent, block_out = lax.optimization_barrier(
        (grad_messages, point_sent, block_out)
    )
    extent = width + LANES
    core_half = (parts // 2, slim, extent)
    sent, kept = call(
        functools.partial(weight_kernel, ways, parts),
        "out_terms",
        [(core_half, bf16), (core_half, f32)],
        scratch=[((share, extent), f32)],
        flops=square,
        moved=10 * rows_bytes,
    )(info, *grad_messages, *messages, attended)
    received = swap(sent, "dp", 1)
    for shift in range(1, parts.bit_length() - 1):
        sent, kept = halve(kept, received, "dp", shift, True)
        received = swap(sent, "dp", 2**shift)

    point_received = swap(point_sent, "dp", 2 ** bits[0])
    for shift in bits[1:]:
        point_sent, point_kept = halve(point_kept, point_received, "dp", shift, False)
        point_received = swap(point_sent, "dp", 2**shift)
    pieces = call(
        spread_kernel,
        "spread",
        [((2 * slim, half), f32)] + [((2 * slim, half), bf16)] * (ways - 1),
        moved=slim * width * 6 * ways,
    )(info, point_kept, point_received)
    pieces = swap_all(pieces, "ctx")
    grad_packed = call(
        functools.partial(attend_back_kernel, ways),
        "attend_back",
        [((3, frames, share), bf16)] * ways,
        scratch=head_scratch + [((every, share), bf16), ((share, every), f32)],
        flops=20 * pair_flops,
        moved=8 * rows_bytes,
        exps=heads * every * every,
    )(info, *packed, *grad_messages, attended, log_total)
    pieces, grad_packed = lax.optimization_barrier((pieces, grad_packed))
    grad_packed = swap_all(grad_packed, "ctx")
    layer_bit = (parts // 2).bit_length() - 1
    point_own, point_other = call(
        functools.partial(point_sum_kernel, layer_bit),
        "point_sum",
        [((slim, half), f32), ((slim, half), bf16)],
        moved=slim * width * (parts + 8),
    )(info, *pieces)
    point_other = swap(point_other, "dp", parts // 2)

    out_total, taps, vectors, point_total = call(
        functools.partial(finish_kernel, ways, layer_bit),
        "finish",
        [((slim, width), f32), ((31, slim), f32), ((3, slim), f32), ((slim, width), f32)],
        moved=slim * extent * (parts + 8),
    )(info, kept, received, point_own, point_other)

    grad_query, grad_key, grad_value = call(
        functools.partial(unpack_kernel if by_tiles else unpack_parts_kernel, ways),
        "unpack",
        [((frames, width), bf16)] * 3,
        semaphores=3 * ways if by_tiles else 0,
        far=("out",) if by_tiles else (),
        moved=6 * rows_bytes,
    )(info, *grad_packed)

    return (
        block_out[None],
        grad_residual[None],
        grad_query[None],
        grad_key[None],
        grad_value[None],
        out_total.T,
        point_total.T,
        taps,
        vectors,
    )


def solution(mesh):
    rows = P("dp", "ctx", None)
    columns = P(None, ("dp", "ctx"))
    in_specs = (rows, rows, rows, rows, P("dp"), P(), P(), P(), P(), P(), P(), rows)
    out_specs = (rows,) * 5 + (columns,) * 4
    return jax.shard_map(local, mesh=mesh, in_specs=in_specs, out_specs=out_specs, check_vma=False)
```

```python
import functools

import jax
import jax.numpy as jnp
from jax import lax
from jax.experimental import pallas as pl
from jax.experimental.pallas import tpu as pltpu
from jax.sharding import PartitionSpec as P

HEADS = 24
HEAD_DIM = 64
SCALE = HEAD_DIM ** (-0.5)

NEG_FILL = -1e30
EPSILON = 1e-05

LANES = 128
EDGE = 16
NEAR = 3
BAND = 16
EXTRA = 48

NN = (((1,), (0,)), ((), ()))
NT = (((1,), (1,)), ((), ()))
TN = (((0,), (0,)), ((), ()))


def dot(left, right, dims=NN):
    return lax.dot_general(left, right, dims, preferred_element_type=jnp.float32)


def call(
    kernel, name, outs, scratch=(), semaphores=0, far=(), megabytes=28, flops=0, moved=0, exps=0
):
    vmem = pl.BlockSpec(memory_space=pltpu.VMEM)
    smem = pl.BlockSpec(memory_space=pltpu.SMEM)
    anywhere = pl.BlockSpec(memory_space=pl.ANY)

    def run(*arrays):
        scratches = [pltpu.VMEM(shape, kind) for shape, kind in scratch]
        if semaphores:
            scratches.append(pltpu.SemaphoreType.DMA((semaphores,)))
        return pl.pallas_call(
            kernel,
            name=name,
            in_specs=[smem if a.ndim == 1 else anywhere if "in" in far else vmem for a in arrays],
            out_specs=[anywhere if "out" in far else vmem] * len(outs),
            out_shape=[jax.ShapeDtypeStruct(shape, kind) for shape, kind in outs],
            scratch_shapes=scratches,
            compiler_params=pltpu.CompilerParams(vmem_limit_bytes=megabytes << 20),
            cost_estimate=pl.CostEstimate(flops=flops, bytes_accessed=moved, transcendentals=exps),
        )(*arrays)

    return run


def valid_of(first, rows, length):
    return first + lax.broadcasted_iota(jnp.int32, (rows, 1), 0) < length


def moments(rows):
    centre = jnp.mean(rows, axis=-1, keepdims=True)
    centred = rows - centre
    inv_scale = lax.rsqrt(jnp.mean(centred * centred, axis=-1, keepdims=True) + EPSILON)
    return centred * inv_scale, inv_scale


def norm_back(grad_normed, normed, inv_scale):
    first_mean = jnp.mean(grad_normed, axis=-1, keepdims=True)
    second_mean = jnp.mean(grad_normed * normed, axis=-1, keepdims=True)
    return inv_scale * (grad_normed - first_mean - normed * second_mean)


def fold(rows):
    total = rows[:8]
    for at in range(8, rows.shape[0], 8):
        total = total + rows[at : at + 8]
    return total


def at_group(info, by, ways, share, visit):
    if share % LANES == 0:
        visit(pl.ds(pl.multiple_of((info[0] ^ by) * share, LANES), share))
        return
    for at in range(ways):

        @pl.when((info[0] ^ by) == at)
        def _():
            visit(slice(at * share, (at + 1) * share))


def neighbours(ways):
    return [by for by in (1, 3, 7, 15) if by < ways]


def edge_rows(frames, at):
    return slice(3 * frames + at * 3 * EDGE, 3 * frames + (at + 1) * 3 * EDGE)


def pack_kernel(ways, query, key, value, residual, grad_out, *refs):
    blocks, whole, ends, arrived = refs[:ways], refs[ways], refs[ways + 1], refs[ways + 2]
    info = [lax.axis_index("ctx")]
    frames, width = query.shape
    share, reach = width // ways, 2 * EDGE
    pairs = [(rows, whole.at[slot]) for slot, rows in enumerate((query, key, value))]
    for side, tail in enumerate((False, True)):
        for rows, start, count in ((residual, 0, reach), (grad_out, reach, EDGE)):
            first = frames - count if tail else 0
            pairs.append((rows.at[pl.ds(first, count)], ends.at[side, pl.ds(start, count)]))
    copies = [
        pltpu.make_async_copy(source, target, arrived.at[at])
        for at, (source, target) in enumerate(pairs)
    ]
    for copy in copies:
        copy.start()
    for slot, copy in enumerate(copies[:3]):
        copy.wait()
        for by in range(ways):

            def visit(lanes):
                blocks[by][slot * frames : (slot + 1) * frames, :] = whole[slot, :, lanes]

            at_group(info, by, ways, share, visit)
    for copy in copies[3:]:
        copy.wait()
    for by in neighbours(ways):
        side = jnp.where((info[0] ^ by) > info[0], 1, 0)
        for at in range(ways):
            blocks[by][edge_rows(frames, at), :] = ends[side, :, at * share : (at + 1) * share]


def unpack_kernel(ways, info, *refs):
    blocks, outs, arrived = refs[:ways], refs[ways:-1], refs[-1]
    share = blocks[0].shape[2]
    copies = []
    for by in range(ways):
        for slot, rows in enumerate(outs):
            lanes = pl.ds(pl.multiple_of((info[0] ^ by) * share, LANES), share)
            copy = pltpu.make_async_copy(
                blocks[by].at[slot], rows.at[:, lanes], arrived.at[len(copies)]
            )
            copy.start()
            copies.append(copy)
    for copy in copies:
        copy.wait()


def unpack_parts_kernel(ways, info, *refs):
    blocks, outs = refs[:ways], refs[ways:]
    share = blocks[0].shape[2]
    for by in range(ways):
        for slot, rows in enumerate(outs):

            def visit(lanes):
                rows[:, lanes] = blocks[by][slot]

            at_group(info, by, ways, share, visit)


def mask_kernel(lower, info, grad_out, masked, *halves):
    frames, width = grad_out.shape
    valid = valid_of(info[0] * frames, frames, info[1])
    masked[...] = jnp.where(valid, grad_out[...].astype(jnp.float32), 0.0).astype(jnp.bfloat16)
    quarter = width // 4
    for by, half in enumerate(halves):
        for at in range(2):
            start = (2 * at + ((info[2] // lower) ^ by) % 2) * quarter
            lanes = pl.ds(pl.multiple_of(start, LANES), quarter)
            half[:, at * quarter : (at + 1) * quarter] = masked[:, lanes]


def grad_act_kernel(info, masked, point_weight, block, grad_act, own_block):
    own_block[...] = block[...]
    width = masked.shape[1]
    step = width // 3
    for at in range(0, width, step):
        grad_act[:, at : at + step] = dot(masked[...], point_weight[at : at + step, :], NT)


def mask_edges_kernel(frames, info, before, after, point_weight, grad_act):
    width = grad_act.shape[1]
    first = info[0] * frames
    sides = []
    for side, start in ((before, first - EDGE), (after, first + frames)):
        valid = valid_of(start, EDGE, info[1])
        rows = side[2 * EDGE :, :].astype(jnp.float32)
        sides.append(jnp.where(valid, rows, 0.0).astype(jnp.bfloat16))
    masked = jnp.concatenate(sides, axis=0)
    step = width // 3
    for at in range(0, width, step):
        grad_act[:, at : at + step] = dot(masked, point_weight[at : at + step, :], NT)


def gather_heads(info, blocks, query, key, value, bias):
    frames = query.shape[0] // len(blocks)
    for by, block in enumerate(blocks):
        rows = slice(by * frames, (by + 1) * frames)
        query[rows] = block[:frames, :] * jnp.bfloat16(SCALE)
        key[rows] = block[frames : 2 * frames, :]
        value[rows] = block[2 * frames : 3 * frames, :]
        valid = valid_of((info[0] ^ by) * frames, frames, info[1])
        bias[rows] = jnp.broadcast_to(jnp.where(valid, 0.0, NEG_FILL), (frames, LANES))


def attend_kernel(ways, info, *refs):
    blocks, outs = refs[:ways], refs[ways : 2 * ways]
    attended, log_total, before, after, query, key, value, bias, turned = refs[2 * ways :]
    gather_heads(info, blocks, query, key, value, bias)
    total_frames, share = query.shape
    frames = total_frames // ways
    for side, other in ((before, info[0] - 1), (after, info[0] + 1)):
        side[...] = jnp.zeros_like(side)
        for by in neighbours(ways):

            @pl.when((info[0] ^ other) == by)
            def _():
                for at in range(ways):
                    lanes = slice(at * share, (at + 1) * share)
                    side[:, lanes] = blocks[by][edge_rows(frames, at), :]

    for head in range(share // HEAD_DIM):
        part = slice(head * HEAD_DIM, (head + 1) * HEAD_DIM)
        spread = jnp.concatenate([bias[...]] * (total_frames // LANES), axis=1)
        scores = dot(key[:, part], query[:, part], NT) + spread
        row_max = jnp.max(scores, axis=0, keepdims=True)
        weights = jnp.exp(scores - row_max)
        total = jnp.sum(weights, axis=0, keepdims=True)
        turned[part, :] = dot(value[:, part], weights.astype(jnp.bfloat16), TN) * (1.0 / total)
        log_total[head : head + 1, :] = row_max + jnp.log(total)
    attended[...] = turned[...].T.astype(jnp.bfloat16)
    reach = 2 * EDGE
    for by in range(ways):
        other = info[0] ^ by
        before = (info[0] ^ jnp.maximum(other - 1, 0)) * frames + frames - reach
        after = (info[0] ^ jnp.minimum(other + 1, ways - 1)) * frames
        outs[by][:reach] = attended[pl.ds(pl.multiple_of(before, reach), reach), :]
        outs[by][reach : reach + frames] = attended[by * frames : (by + 1) * frames, :]
        outs[by][reach + frames :] = attended[pl.ds(pl.multiple_of(after, reach), reach), :]


def attend_back_kernel(ways, info, *refs):
    blocks, messages = refs[:ways], refs[ways : 2 * ways]
    attended, log_total = refs[2 * ways : 2 * ways + 2]
    outs = refs[2 * ways + 2 : 3 * ways + 2]
    query, key, value, bias, grad, turned = refs[3 * ways + 2 :]
    gather_heads(info, blocks, query, key, value, bias)
    total_frames, share = query.shape
    frames = total_frames // ways
    for by in range(ways):
        grad[by * frames : (by + 1) * frames] = messages[by][:frames, :]
    turned[...] = (grad[...].astype(jnp.float32) * attended[...].astype(jnp.float32)).T
    for head in range(share // HEAD_DIM):
        part = slice(head * HEAD_DIM, (head + 1) * HEAD_DIM)
        delta = jnp.sum(turned[part, :], axis=0, keepdims=True)
        spread = jnp.concatenate([bias[...]] * (total_frames // LANES), axis=1)
        scores = dot(key[:, part], query[:, part], NT) + spread
        probs = jnp.exp(scores - log_total[head : head + 1, :])
        value_grad = dot(probs.astype(jnp.bfloat16), grad[:, part])
        prob_grad = dot(value[:, part], grad[:, part], NT)
        score_grad = (probs * (prob_grad - delta)).astype(jnp.bfloat16)
        key_grad = dot(score_grad, query[:, part])
        turned[part, :] = dot(key[:, part], score_grad, TN) * SCALE
        for by in range(ways):
            rows = slice(by * frames, (by + 1) * frames)
            outs[by][1, :, part] = key_grad[rows].astype(jnp.bfloat16)
            outs[by][2, :, part] = value_grad[rows].astype(jnp.bfloat16)
    query_grad = turned[...].T.astype(jnp.bfloat16)
    for by in range(ways):
        outs[by][0] = query_grad[by * frames : (by + 1) * frames]


def gather_kernel(ways, info, *refs):
    blocks, messages = refs[:ways], refs[ways:]
    frames, share, reach = messages[0].shape[0], blocks[0].shape[1], 2 * EDGE
    for by, message in enumerate(messages):
        lacking = [slot for slot in range(ways) if slot != by]
        for at, slot in enumerate(lacking):
            message[:, at * share : (at + 1) * share] = blocks[slot][reach : reach + frames, :]


def project_kernel(ways, info, *refs):
    blocks = refs[:ways]
    residual, before, after, out_weight, params = refs[ways : ways + 5]
    mixed, conv_in, attended = refs[ways + 5 :]
    frames, width = residual.shape
    share = width // ways
    reach = 2 * EDGE
    rows = frames + 2 * reach
    for by in range(ways):
        for at in range(ways):

            @pl.when((info[0] ^ by) == at)
            def _():
                attended[:, at * share : (at + 1) * share] = blocks[by][...]

    step = width // 3
    for at in range(0, width, step):
        part = slice(at, at + step)
        mixed[:reach, part] = before[:reach, part].astype(jnp.float32)
        mixed[reach : reach + frames, part] = residual[:, part].astype(jnp.float32)
        mixed[reach + frames :, part] = after[:reach, part].astype(jnp.float32)
        mixed[:, part] += dot(attended[...], out_weight[:, part])

    gain = params[31:32, :]
    first = info[0] * frames - reach

    def band(index, carry):
        at = pl.ds(pl.multiple_of(index * BAND, BAND), BAND)
        normed, _ = moments(mixed[at, :])
        position = first + index * BAND + lax.broadcasted_iota(jnp.int32, (BAND, 1), 0)
        valid = (position >= 0) & (position < info[1])
        conv_in[at, :] = jnp.where(valid, normed * gain, 0.0).astype(jnp.bfloat16)
        return carry

    lax.fori_loop(0, rows // BAND, band, 0, unroll=4)


def stride_of(rows):
    return rows // 8 + 1


def in_columns(ref, rows):
    for at in range(ref.shape[0]):
        ref[at, : rows.shape[0]] = rows[:, at * LANES : (at + 1) * LANES].astype(jnp.float32)


def from_columns(ref, rows):
    return jnp.concatenate([ref[at, rows, :] for at in range(ref.shape[0])], axis=1)


def strided(ref, index, start, stride):
    return ref[index, pl.ds(start, 8, stride=stride), :]


def depthwise(padded, taps, tap_of, out, rows):
    stride = stride_of(rows)

    def column(index, carry):
        part = pl.ds(pl.multiple_of(index * LANES, LANES), LANES)
        cells = [strided(padded, index, at + 1, stride) for at in range(stride + 2 * EDGE - 2)]
        total = [None] * stride
        for offset in range(1, 2 * EDGE):
            tap = tap_of(offset)
            scale = jnp.broadcast_to(taps[tap : tap + 1, part], (8, LANES))
            for at in range(stride):
                term = cells[at + offset - 1] * scale
                total[at] = term if total[at] is None else total[at] + term
        for at in range(stride):
            out[index, pl.ds(at, 8, stride=stride), :] = total[at]
        return carry

    lax.fori_loop(0, out.shape[0], column, 0)


def tap_grads(padded, grad, start, rows, taps):
    stride = rows // 8

    def column(index, carry):
        part = pl.ds(pl.multiple_of(index * LANES, LANES), LANES)
        cells = [
            strided(padded, index, start + at + 1, stride) for at in range(stride + 2 * EDGE - 2)
        ]
        grads = [strided(grad, index, start + at, stride) for at in range(stride)]
        for tap in range(2 * EDGE - 1):
            total = cells[tap] * grads[0]
            for at in range(1, stride):
                total = total + cells[at + tap] * grads[at]
            taps[tap : tap + 1, part] = jnp.sum(total, axis=0, keepdims=True)
        return carry

    lax.fori_loop(0, grad.shape[0], column, 0)


def conv_kernel_body(lower, info, conv_in, params, grad_own, grad_edges, *refs):
    conv_act, grad_conv, sums = refs[:3]
    halves = refs[3:-5]
    padded, conv, grad_act, bias_sum, gain_sum = refs[-5:]
    frames, width = grad_own.shape
    rows, wide = frames + 2 * EDGE, frames + 4 * EDGE
    in_columns(padded, conv_in[...])
    padded[:, wide:, :] = jnp.zeros((width // LANES, padded.shape[1] - wide, LANES), jnp.float32)
    grad_act[:EDGE] = grad_edges[:EDGE]
    grad_act[EDGE : EDGE + frames] = grad_own[...]
    grad_act[EDGE + frames :] = grad_edges[EDGE:]
    depthwise(padded, params, lambda offset: offset - 1, conv, rows)
    bias, gain = params[32:33, :], params[33:34, :]
    bias_sum[...] = jnp.zeros_like(bias_sum)
    gain_sum[...] = jnp.zeros_like(gain_sum)

    def band(index, inner):
        at = pl.ds(pl.multiple_of(index * BAND, BAND), BAND)
        normed, inv_scale = moments(from_columns(conv, at) + bias)
        scaled = normed * gain
        gate = 0.5 + 0.5 * jnp.tanh(0.5 * scaled)
        conv_act[at, :] = (scaled * gate).astype(jnp.bfloat16)
        grad_scaled = grad_act[at, :] * gate * (1.0 + scaled * (1.0 - gate))
        grad_rows = norm_back(grad_scaled * gain, normed, inv_scale)
        for column in range(width // LANES):
            grad_conv[column, at, :] = grad_rows[:, column * LANES : (column + 1) * LANES]

        if inner:
            bias_sum[...] += fold(grad_rows)
            gain_sum[...] += fold(grad_scaled * normed)

    def inner_band(index, carry):
        band(index, True)
        return carry

    for index in range(EDGE // BAND):
        band(index, False)
        band((EDGE + frames) // BAND + index, False)
    lax.fori_loop(EDGE // BAND, (EDGE + frames) // BAND, inner_band, 0, unroll=4)
    sums[0:1, :] = jnp.sum(bias_sum[...], axis=0, keepdims=True)
    sums[1:2, :] = jnp.sum(gain_sum[...], axis=0, keepdims=True)
    half = width // 2
    for by, block in enumerate(halves):
        start = ((info[2] // (2 * lower)) ^ by) * half
        block[...] = conv_act[EDGE : EDGE + frames, pl.ds(pl.multiple_of(start, LANES), half)]


def block_out_kernel(info, conv_act, mixed, point_weight, block_out):
    frames, width = block_out.shape
    step = width // 3
    for at in range(0, width, step):
        part = slice(at, at + step)
        block_out[:, part] = (
            mixed[2 * EDGE : 2 * EDGE + frames, part]
            + dot(conv_act[EDGE : EDGE + frames, :], point_weight[:, part])
        ).astype(jnp.bfloat16)


def conv_back_kernel(ways, slim, info, grad_conv, conv_in, params, masked, mixed, out_weight, *refs):
    conv_sums, grad_residual, messages = refs[0], refs[1], refs[2 : 2 + ways]
    padded, padded_in, conv, gain_sum, taps, packed, chosen = refs[2 + ways :]
    frames, width = grad_residual.shape
    share = width // ways
    reached = frames + 2 * EDGE
    padded[:, :reached, :] = grad_conv[...].astype(jnp.bfloat16).astype(jnp.float32)
    padded[:, reached:, :] = jnp.zeros(
        (width // LANES, padded.shape[1] - reached, LANES), jnp.float32
    )
    depthwise(padded, params, lambda offset: 31 - offset, conv, frames)
    gain = params[31:32, :]
    gain_sum[...] = jnp.zeros_like(gain_sum)

    def band(index, carry):
        at = pl.ds(pl.multiple_of(index * BAND, BAND), BAND)
        own_mixed = pl.ds(pl.multiple_of(index * BAND + 2 * EDGE, BAND), BAND)
        valid = valid_of(info[0] * frames + index * BAND, BAND, info[1])
        grad_in = jnp.where(valid, from_columns(conv, at), 0.0)
        normed, inv_scale = moments(mixed[own_mixed, :])
        grad_mixed = norm_back(grad_in * gain, normed, inv_scale)
        gain_sum[...] += fold(grad_in * normed)
        grad_residual[at, :] = (masked[at, :].astype(jnp.float32) + grad_mixed).astype(
            jnp.bfloat16
        )
        return carry

    lax.fori_loop(0, frames // BAND, band, 0, unroll=4)
    for by in range(ways):
        at = pl.ds(pl.multiple_of((info[0] ^ by) * share, share), share)
        messages[by][:frames] = dot(grad_residual[...], out_weight[at, :], NT).astype(jnp.bfloat16)

    in_columns(padded_in, conv_in[...])
    tap_grads(padded_in, grad_conv, EDGE, frames, taps)
    taps[31:32, :] = conv_sums[0:1, :]
    taps[32:33, :] = jnp.sum(gain_sum[...], axis=0, keepdims=True)
    taps[33:34, :] = conv_sums[1:2, :]
    taps[34:, :] = jnp.zeros((EXTRA - 34, width), jnp.float32)
    packed[:frames] = grad_residual[...]
    packed[frames:] = taps[...].astype(jnp.bfloat16)
    for at in range(ways):
        pieces = []
        for start in range(at * slim, width, ways * slim):
            pieces.append(packed[:, start : start + slim])
        chosen[at] = jnp.concatenate(pieces, axis=1)
    for by in range(ways):
        messages[by][frames:] = chosen[info[0] ^ by]


def split_rows(info, parts, terms, sent, kept):
    rows = terms.shape[0] // parts
    for bit in range(2):

        @pl.when(info[2] % 2 == bit)
        def _():
            for at in range(parts // 2):
                own, other = (2 * at + bit) * rows, (2 * at + 1 - bit) * rows
                kept[at] = terms[own : own + rows, :]
                sent[at] = terms[other : other + rows, :].astype(jnp.bfloat16)


def point_kernel(shift, info, *refs):
    grads, acts, (sent, kept, terms) = refs[:4], refs[4:8], refs[8:]
    left = jnp.concatenate([grad[...] for grad in grads], axis=0)
    right = jnp.concatenate([act[...] for act in acts], axis=0)
    step = terms.shape[1] // 2
    for at in range(0, 2 * step, step):
        part = slice(at, at + step)
        terms[:, part] = dot(left, right[:, part], TN)
    pieces, slim = kept.shape[0], kept.shape[1] // 2
    for bit in range(2):

        @pl.when(((info[2] >> shift) & 1) == bit)
        def _():
            for at in range(pieces):
                for side in range(2):
                    base = side * 2 * pieces * slim
                    own = base + (bit * pieces + at) * slim
                    other = base + ((1 - bit) * pieces + at) * slim
                    rows = slice(side * slim, (side + 1) * slim)
                    kept[at, rows, :] = terms[own : own + slim, :]
                    sent[at, rows, :] = terms[other : other + slim, :].astype(jnp.bfloat16)


def spread_kernel(info, kept, received, own, *blocks):
    own[...] = kept[info[0]] + received[info[0]].astype(jnp.float32)
    for by, block in enumerate(blocks, 1):
        at = info[0] ^ by
        block[...] = (kept[at] + received[at].astype(jnp.float32)).astype(jnp.bfloat16)


def point_sum_kernel(shift, info, *refs):
    blocks, (own, other) = refs[:-2], refs[-2:]
    rows = own.shape[0]
    total = blocks[0][...]
    for block in blocks[1:]:
        total = total + block[...].astype(jnp.float32)
    for at in range(2):

        @pl.when(((info[2] >> shift) & 1) == at)
        def _():
            own[...] = total[at * rows : (at + 1) * rows, :]
            other[...] = total[(1 - at) * rows : (2 - at) * rows, :].astype(jnp.bfloat16)


def weight_kernel(ways, parts, info, *refs):
    grads, rows = refs[:ways], refs[ways : 2 * ways]
    attended, sent, kept, terms = refs[2 * ways :]
    total_frames, share = attended.shape
    frames = total_frames // ways
    width = ways * share
    slim = share // parts
    left = jnp.concatenate([grad[frames : 2 * frames, :] for grad in grads], axis=0)
    for slot in range(ways):
        if slot == 0:
            right = attended[...]
        else:
            pieces = []
            for by in range(ways):
                at = (by ^ slot) - (1 if (by ^ slot) > by else 0)
                pieces.append(rows[by][:, at * share : (at + 1) * share])
            right = jnp.concatenate(pieces, axis=0)
        terms[:, slot * share : (slot + 1) * share] = dot(left, right, TN)
    small = jnp.zeros((EXTRA, share), jnp.float32)
    for grad in grads:
        small = small + grad[2 * frames :, :].astype(jnp.float32)
    filler = jnp.zeros((LANES - EXTRA, share), jnp.float32)
    terms[:, width:] = jnp.concatenate([small, filler], axis=0).T
    split_rows(info, parts, terms, sent, kept)


def halve_kernel(axis, shift, alternate, info, kept, received, sent, still_kept):
    bit = (info[axis] >> shift) & 1
    count = sent.shape[0]
    for at in range(count):
        if alternate:
            own, other = 2 * at + bit, 2 * at + 1 - bit
        else:
            own, other = bit * count + at, (1 - bit) * count + at
        still_kept[at] = kept[own] + received[own].astype(jnp.float32)
        sent[at] = (kept[other] + received[other].astype(jnp.float32)).astype(jnp.bfloat16)


def finish_kernel(ways, shift, info, kept, received, own, other, weight, taps, vectors, point):
    width = weight.shape[1]
    share, half = width // ways, width // 2
    for at in range(2):

        @pl.when(((info[2] >> shift) & 1) == at)
        def _():
            point[:, at * half : (at + 1) * half] = own[...]
            point[:, (1 - at) * half : (2 - at) * half] = other[...].astype(jnp.float32)

    total = kept[0] + received[0].astype(jnp.float32)
    for by in range(ways):
        for at in range(ways):

            @pl.when((info[0] ^ by) == at)
            def _():
                weight[:, at * share : (at + 1) * share] = total[:, by * share : (by + 1) * share]

    small = total[:, width:].T
    taps[...] = small[:31]
    vectors[...] = small[31:34]


def swap(block, axis, by):
    return lax.ppermute(block, axis, [(i, i ^ by) for i in range(lax.axis_size(axis))])


def swap_all(blocks, axis, step=1):
    return [blocks[0]] + [swap(block, axis, step * by) for by, block in enumerate(blocks[1:], 1)]


def local(
    residual_in,
    query_rows,
    key_rows,
    value_rows,
    lengths,
    out_weight,
    norm_gain,
    conv_kernel,
    conv_bias,
    conv_gain,
    point_weight,
    grad_out,
):
    ways = lax.axis_size("ctx")
    parts = lax.axis_size("dp")
    own = lax.axis_index("ctx")
    place = lax.axis_index("dp")
    frames, width = residual_in.shape[1:]
    share = width // ways
    slim = share // parts
    heads = HEADS // ways
    every = ways * frames
    lower = parts // 4
    half = width // 2
    tiles = width // LANES
    bf16, f32 = jnp.bfloat16, jnp.float32
    square = 2 * frames * width * width
    rows_bytes = 2 * frames * width
    reached, wide = frames + 2 * EDGE, frames + 4 * EDGE

    info = jnp.stack([own, lengths[0], place]).astype(jnp.int32)
    params = jnp.concatenate(
        [conv_kernel, norm_gain[None], conv_bias[None], conv_gain[None]], axis=0
    )

    by_tiles = share % LANES == 0
    packed_rows = [3 * frames + 3 * EDGE * ways * (by in neighbours(ways)) for by in range(ways)]
    packed = call(
        functools.partial(pack_kernel, ways),
        "pack",
        [((rows, share), bf16) for rows in packed_rows],
        scratch=[((3, frames, width), bf16), ((2, 3 * EDGE, width), bf16)],
        semaphores=7,
        far=("in",),
        megabytes=58,
        moved=6 * rows_bytes,
    )(query_rows[0], key_rows[0], value_rows[0], residual_in[0], grad_out[0])
    packed = swap_all(packed, "ctx")

    masked, *masked_halves = call(
        functools.partial(mask_kernel, lower),
        "mask",
        [((frames, width), bf16)] + [((frames, half), bf16)] * 2,
        moved=4 * rows_bytes,
    )(info, grad_out[0])
    masked_halves = swap_all([masked_halves[by % 2] for by in range(4)], "dp", lower)
    grad_own, packed[0] = call(
        grad_act_kernel,
        "grad_act",
        [((frames, width), f32), ((3 * frames, share), bf16)],
        flops=square,
        moved=6 * rows_bytes + 2 * width * width,
    )(info, masked, point_weight, packed[0])

    packed, grad_own = lax.optimization_barrier((packed, grad_own))
    head_scratch = [((every, share), bf16)] * 3 + [((every, LANES), f32)]
    pair_flops = 2 * heads * every * every * HEAD_DIM
    *returned, attended, log_total, before, after = call(
        functools.partial(attend_kernel, ways),
        "attend",
        [((wide, share), bf16)] * ways + [((every, share), bf16), ((heads, every), f32)]
        + [((3 * EDGE, width), bf16)] * 2,
        scratch=head_scratch + [((share, every), f32)],
        flops=8 * pair_flops,
        moved=4 * rows_bytes,
        exps=heads * every * every,
    )(info, *packed)
    returned, masked_halves[1:3] = lax.optimization_barrier((returned, masked_halves[1:3]))
    returned = swap_all(returned, "ctx")
    grad_edges = call(
        functools.partial(mask_edges_kernel, frames),
        "mask_edges",
        [((2 * EDGE, width), f32)],
        flops=square,
        moved=2 * width * width,
    )(info, before, after, point_weight)[0]
    returned, grad_edges, masked_halves = lax.optimization_barrier(
        (returned, grad_edges, masked_halves)
    )
    messages = call(
        functools.partial(gather_kernel, ways),
        "gather",
        [((frames, width - share), bf16)] * ways,
        moved=8 * rows_bytes,
    )(info, *returned)
    arrived = swap_all(messages, "ctx")

    returned, messages = lax.optimization_barrier((returned, messages))
    mixed, conv_in = call(
        functools.partial(project_kernel, ways),
        "project",
        [((wide, width), f32), ((wide, width), bf16)],
        scratch=[((wide, width), bf16)],
        flops=square,
        moved=6 * rows_bytes + 2 * width * width,
    )(info, *returned, residual_in[0], before, after, out_weight, params)
    spread = 8 * stride_of(reached)
    conv_act, grad_conv, conv_sums, *act_halves = call(
        functools.partial(conv_kernel_body, lower),
        "conv",
        [
            ((reached, width), bf16),
            ((tiles, reached, LANES), f32),
            ((2, width), f32),
        ]
        + [((frames, half), bf16)] * 2,
        scratch=[
            ((tiles, spread + 2 * EDGE, LANES), f32),
            ((tiles, spread, LANES), f32),
            ((reached, width), f32),
            ((8, width), f32),
            ((8, width), f32),
        ],
        flops=frames * width * 4000,
        moved=6 * rows_bytes,
        exps=frames * width,
    )(info, conv_in, params, grad_own, grad_edges)
    near, act_halves = lax.optimization_barrier((arrived[:NEAR], act_halves))
    act_halves = swap_all([act_halves[by // 2] for by in range(4)], "dp", lower)
    far, grad_conv = lax.optimization_barrier((arrived[NEAR:], grad_conv))

    spread = 8 * stride_of(frames)
    grad_residual, *grad_messages = call(
        functools.partial(conv_back_kernel, ways, slim),
        "conv_back",
        [((frames, width), bf16)] + [((2 * frames + EXTRA, share), bf16)] * ways,
        scratch=[
            ((tiles, spread + 2 * EDGE, LANES), f32),
            ((tiles, wide, LANES), f32),
            ((tiles, spread, LANES), f32),
            ((8, width), f32),
            ((EXTRA, width), f32),
            ((frames + EXTRA, width), bf16),
            ((ways, frames + EXTRA, share), bf16),
        ],
        flops=frames * width * 8000,
        moved=8 * rows_bytes + 2 * width * width,
    )(
        info,
        grad_conv,
        conv_in,
        params,
        masked,
        mixed,
        out_weight,
        conv_sums,
    )
    act_halves[1], grad_messages[NEAR:] = lax.optimization_barrier(
        (act_halves[1], grad_messages[NEAR:])
    )
    act_halves, conv_act = lax.optimization_barrier((act_halves, conv_act))
    messages = near + far
    grad_messages = swap_all(grad_messages, "ctx")

    block_out = call(
        block_out_kernel,
        "block_out",
        [((frames, width), bf16)],
        flops=square,
        moved=4 * rows_bytes + 2 * width * width,
    )(info, conv_act, mixed, point_weight)[0]

    def halve(kept, received, axis, shift, alternate):
        extent = (kept.shape[0] // 2,) + kept.shape[1:]
        return call(
            functools.partial(halve_kernel, 0 if axis == "ctx" else 2, shift, alternate),
            "halve",
            [(extent, bf16), (extent, f32)],
            moved=16 * extent[0] * extent[1] * extent[2],
        )(info, kept, received)

    grad_messages[1], act_halves = lax.optimization_barrier((grad_messages[1], act_halves))
    bits = list(reversed(range(lower.bit_length() - 1)))
    point_half = (lower * ways // 2, 2 * slim, half)
    point_sent, point_kept = call(
        functools.partial(point_kernel, bits[0]),
        "point_terms",
        [(point_half, bf16), (point_half, f32)],
        scratch=[((half, half), f32)],
        flops=square,
        moved=8 * rows_bytes,
    )(info, *masked_halves, *act_halves)
    grad_messages, point_sent, block_out = lax.optimization_barrier(
        (grad_messages, point_sent, block_out)
    )
    extent = width + LANES
    core_half = (parts // 2, slim, extent)
    sent, kept = call(
        functools.partial(weight_kernel, ways, parts),
        "out_terms",
        [(core_half, bf16), (core_half, f32)],
        scratch=[((share, extent), f32)],
        flops=square,
        moved=10 * rows_bytes,
    )(info, *grad_messages, *messages, attended)
    received = swap(sent, "dp", 1)
    for shift in range(1, parts.bit_length() - 1):
        sent, kept = halve(kept, received, "dp", shift, True)
        received = swap(sent, "dp", 2**shift)

    point_received = swap(point_sent, "dp", 2 ** bits[0])
    for shift in bits[1:]:
        point_sent, point_kept = halve(point_kept, point_received, "dp", shift, False)
        point_received = swap(point_sent, "dp", 2**shift)
    pieces = call(
        spread_kernel,
        "spread",
        [((2 * slim, half), f32)] + [((2 * slim, half), bf16)] * (ways - 1),
        moved=slim * width * 6 * ways,
    )(info, point_kept, point_received)
    pieces = swap_all(pieces, "ctx")
    grad_packed = call(
        functools.partial(attend_back_kernel, ways),
        "attend_back",
        [((3, frames, share), bf16)] * ways,
        scratch=head_scratch + [((every, share), bf16), ((share, every), f32)],
        flops=20 * pair_flops,
        moved=8 * rows_bytes,
        exps=heads * every * every,
    )(info, *packed, *grad_messages, attended, log_total)
    pieces, grad_packed = lax.optimization_barrier((pieces, grad_packed))
    grad_packed = swap_all(grad_packed, "ctx")
    layer_bit = (parts // 2).bit_length() - 1
    point_own, point_other = call(
        functools.partial(point_sum_kernel, layer_bit),
        "point_sum",
        [((slim, half), f32), ((slim, half), bf16)],
        moved=slim * width * (parts + 8),
    )(info, *pieces)
    point_other = swap(point_other, "dp", parts // 2)

    out_total, taps, vectors, point_total = call(
        functools.partial(finish_kernel, ways, layer_bit),
        "finish",
        [((slim, width), f32), ((31, slim), f32), ((3, slim), f32), ((slim, width), f32)],
        moved=slim * extent * (parts + 8),
    )(info, kept, received, point_own, point_other)

    grad_query, grad_key, grad_value = call(
        functools.partial(unpack_kernel if by_tiles else unpack_parts_kernel, ways),
        "unpack",
        [((frames, width), bf16)] * 3,
        semaphores=3 * ways if by_tiles else 0,
        far=("out",) if by_tiles else (),
        moved=6 * rows_bytes,
    )(info, *grad_packed)

    return (
        block_out[None],
        grad_residual[None],
        grad_query[None],
        grad_key[None],
        grad_value[None],
        out_total.T,
        point_total.T,
        taps,
        vectors,
    )


def solution(mesh):
    rows = P("dp", "ctx", None)
    columns = P(None, ("dp", "ctx"))
    in_specs = (rows, rows, rows, rows, P("dp"), P(), P(), P(), P(), P(), P(), rows)
    out_specs = (rows,) * 5 + (columns,) * 4
    return jax.shard_map(local, mesh=mesh, in_specs=in_specs, out_specs=out_specs, check_vma=False)
```
